32 devices in a mesh: dp: 8 (over z, x), mp: 4 (over y, core).
Axes of the slice: x: 2, y: 2, z: 4, core: 2. Of those that a mesh axis runs over, the one named last changes fastest.
Arguments:
- inputs: bfloat16 [4096, 768], P(('dp', 'mp')), may hold values from -30 to 30, as said below
- attention_gain: float32 [768], replicated, may hold values from 0.1 to 1.9
- query_weight: bfloat16 [768, 768], P(None, 'mp'), may hold values from -0.21875 to 0.21875
- key_weight: bfloat16 [768, 768], P(None, 'mp'), may hold values from -0.21875 to 0.21875
- value_weight: bfloat16 [768, 768], P(None, 'mp'), may hold values from -0.21875 to 0.21875
- out_weight: bfloat16 [768, 768], P('mp'), may hold values from -3 to 3
- bias_table: float32 [32, 12], P(None, 'mp'), may hold values from -4 to 4
- feedforward_gain: float32 [768], replicated, may hold values from 0.1 to 1.9
- gate_weight: bfloat16 [768, 2048], P(None, 'mp'), may hold values from -0.21875 to 0.21875
- up_weight: bfloat16 [768, 2048], P(None, 'mp'), may hold values from -0.21875 to 0.21875
- down_weight: bfloat16 [2048, 768], P('mp'), may hold values from -0.125 to 0.125
- segment: int32 [4096], replicated, may hold values from 0 to 12, as said below
- bucket: int32 [2047], replicated, may hold values from 0 to 31, as said below
- cotangent: bfloat16 [4096, 768], P(('dp', 'mp')), may hold values from -6 to 6
Outputs:
- layer_out: bfloat16 [4096, 768], P(('dp', 'mp'))
- input_grad: bfloat16 [4096, 768], P(('dp', 'mp'))
- attention_gain_grad: float32 [768], replicated
- query_grad: float32 [768, 768], P(None, 'mp')
- key_grad: float32 [768, 768], P(None, 'mp')
- value_grad: float32 [768, 768], P(None, 'mp')
- out_grad: float32 [768, 768], P('mp')
- table_grad: float32 [32, 12], P(None, 'mp')
- feedforward_gain_grad: float32 [768], replicated
- gate_grad: float32 [768, 2048], P(None, 'mp')
- up_grad: float32 [768, 2048], P(None, 'mp')
- down_grad: float32 [2048, 768], P('mp')
The draws below stay inside these ranges and needn't reach their ends.
Inputs may be any that keep to these rules, and one draw needn't show every extreme that they name: `inputs`: values of order one; rows and columns differ in scale. `segment`: equal values mark one sequence and never fall along the rows. Each sequence is either all 1024 rows of two neighbouring aligned blocks of 512 rows, or one of two sequences that together fill one aligned block, each of them 512 // 4 to 384 rows. Entry 1023 + d is the bucket of offset d (key row minus query row); it is under 32 // 2 for d <= 0 and 16 or more for d > 0, and never falls as |d| grows on either side.
All inputs are finite; a program needn't handle non-finite values.
Results may differ from the reference program's by a relative error of at most 0.02.
Values may be sent and summed in bfloat16 or wider, within the bound.
No kernel may reach another device: no remote copies, remote signals or barrier semaphores. Data moves between devices by JAX's collectives and lax.ppermute only.
A program may use at most 128 MiB of HBM per device.

```python
import math
import jax
import jax.numpy as jnp
from jax import lax

D = 768
HEADS = 12
HEAD = 64
FF = 2048
BUCKETS = 32
TOK_DEV = 512
TOKENS = 4096


def draw_inputs(key, part):
    noise_key, row_key, col_key = jax.random.split(key, 3)
    base = jnp.clip(jax.random.normal(noise_key, (TOKENS, D), jnp.float32), -5.0, 5.0)
    row_scale = jnp.exp(jax.random.uniform(row_key, (TOKENS, 1), jnp.float32, math.log(0.3), math.log(3.0)))
    col_scale = jnp.exp(jax.random.uniform(col_key, (1, D), jnp.float32, math.log(0.5), math.log(2.0)))
    return (base * row_scale * col_scale).astype(jnp.bfloat16)


def draw_segment(key, part):
    blocks = TOKENS // TOK_DEV
    bit_key, middle_key, split_key = jax.random.split(key, 3)
    bits = jax.random.randint(bit_key, (blocks + 1,), 0, 2, dtype=jnp.int32)
    middle = blocks // 2 - jax.random.randint(middle_key, (), 0, 2, dtype=jnp.int32)
    splits = jax.random.randint(split_key, (blocks,), TOK_DEV // 4, 3 * TOK_DEV // 4 + 1, dtype=jnp.int32)
    edges = jnp.arange(blocks + 1, dtype=jnp.int32)
    before = jnp.concatenate([jnp.zeros((1,), jnp.int32), bits[:-1]])
    crossed = bits * (1 - before)
    forced = (edges == 1) | (edges == middle) | (edges == blocks - 1)
    beside = (edges == 0) | (edges == 2) | (edges == middle - 1) | (edges == middle + 1) | (edges == blocks - 2) | (edges == blocks)
    crossed = jnp.where(forced, 1, jnp.where(beside, 0, crossed)).astype(jnp.int32)
    rows_all = jnp.arange(TOKENS, dtype=jnp.int32)
    owner = rows_all // TOK_DEV
    within = rows_all % TOK_DEV
    left_cross = crossed[owner]
    right_cross = crossed[owner + 1]
    short_id = 2 * owner + (within >= splits[owner]).astype(jnp.int32)
    return jnp.where(left_cross == 1, 2 * (owner - 1), jnp.where(right_cross == 1, 2 * owner, short_id)).astype(jnp.int32)


def draw_bucket(key, part):
    longest = 2 * TOK_DEV
    half = BUCKETS // 2
    divisor = half * (half - 1) // 2
    steps_all = jnp.arange(half - 1, dtype=jnp.int32)
    tops = 1 + (steps_all + 1) * max(longest - half, 0) // divisor
    gaps = 1 + jax.random.randint(key, (half - 1,), 0, tops, dtype=jnp.int32)
    bounds = jnp.cumsum(gaps).astype(jnp.int32)
    offsets = jnp.arange(4 * TOK_DEV - 1, dtype=jnp.int32) - (2 * TOK_DEV - 1)
    distance = jnp.abs(offsets)
    counted = jnp.sum((bounds[None, :] <= distance[:, None]).astype(jnp.int32), axis=1)
    return (counted + half * (offsets > 0).astype(jnp.int32)).astype(jnp.int32)


def level_of(own_key, extent, cuts, smallest, high):
    factor_of = 1.0
    for dim, shards_of in cuts:
        steps = jax.random.uniform(jax.random.fold_in(jax.random.fold_in(own_key, 6), dim), (shards_of,), jnp.float32, smallest / len(cuts), high / len(cuts))
        factor_of = factor_of * jnp.repeat(jnp.exp(steps), extent[dim] // shards_of).reshape((-1,) + (1,) * (len(extent) - 1 - dim))
    return factor_of


def centred(own_key, shape, scale, bound, shards=(), held_as=jnp.bfloat16):
    values = scale * jax.random.normal(own_key, shape, jnp.float32)
    if shards:
        values = values * level_of(own_key, shape, shards, -0.22, 0.18)
    return jnp.clip(values, -bound, bound).astype(held_as)


def setup_inputs(seed: int = 0) -> dict:
    streams_of = jax.random.split(jax.random.key(seed), 15)
    inputs = draw_inputs(jax.random.fold_in(streams_of[14], 71), 0)
    attention_gain = jnp.clip(1.0 + 0.18 * jax.random.normal(streams_of[1], (D,), jnp.float32), 0.1, 1.9)
    query_weight = centred(streams_of[2], (D, HEADS * HEAD), D ** -0.5, 0.21875, ((1, 4),))
    key_weight = centred(streams_of[3], (D, HEADS * HEAD), D ** -0.5, 0.21875, ((1, 4),))
    value_weight = centred(streams_of[4], (D, HEADS * HEAD), D ** -0.5, 0.21875, ((1, 4),))
    out_weight = centred(streams_of[5], (HEADS * HEAD, D), (max(1, HEADS * HEAD // 192)) ** -0.5, 3.0, ((0, 4),))
    bias_table = centred(streams_of[6], (BUCKETS, HEADS), 1.0, 4.0, ((1, 4),), jnp.float32)
    feedforward_gain = jnp.clip(1.0 + 0.18 * jax.random.normal(streams_of[7], (D,), jnp.float32), 0.1, 1.9)
    gate_weight = centred(streams_of[8], (D, FF), D ** -0.5, 0.21875, ((1, 4),))
    up_weight = centred(streams_of[9], (D, FF), D ** -0.5, 0.21875, ((1, 4),))
    down_weight = centred(streams_of[10], (FF, D), FF ** -0.5, 0.125, ((0, 4),))
    segment = draw_segment(jax.random.fold_in(streams_of[14], 71), 0)
    bucket = draw_bucket(jax.random.fold_in(streams_of[14], 71), 0)
    cotangent = centred(streams_of[13], (TOKENS, D), 1.0, 6.0, ((0, 32),))
    return dict(inputs=inputs, attention_gain=attention_gain, query_weight=query_weight, key_weight=key_weight, value_weight=value_weight, out_weight=out_weight, bias_table=bias_table, feedforward_gain=feedforward_gain, gate_weight=gate_weight, up_weight=up_weight, down_weight=down_weight, segment=segment, bucket=bucket, cotangent=cotangent)


@jax.custom_vjp
def low(v):
    return lax.optimization_barrier(v.astype(jnp.bfloat16)).astype(jnp.float32)

@jax.custom_vjp
def low_back(v):
    return v

def low_keep(v):
    return (low(v), None)

def low_pass(kept, grad):
    return (grad,)

def back_keep(v):
    return (v, None)

def back_low(kept, grad):
    return (low(grad),)
low.defvjp(low_keep, low_pass)
low_back.defvjp(back_keep, back_low)

def rounded_both(values):
    return low(low_back(values))

def norm_rows(values, gain):
    return values * lax.rsqrt(lax.optimization_barrier(jnp.mean(values * values, axis=-1, keepdims=True)) + 1e-06) * gain

def window_attend(queries, keys, values, offset_bias, segment):
    exact = lax.Precision.HIGHEST
    count = queries.shape[0] // TOK_DEV
    rows_idx = jnp.arange(TOK_DEV, dtype=jnp.int32)
    cols_idx = jnp.arange(3 * TOK_DEV, dtype=jnp.int32)
    offset_index = cols_idx[None, :] - rows_idx[:, None] + TOK_DEV - 1
    bias_full = jnp.transpose(offset_bias[offset_index], (2, 0, 1))
    blank = jnp.zeros((TOK_DEV, HEADS, HEAD), queries.dtype)
    key_padded = jnp.concatenate([blank, keys, blank], axis=0)
    value_padded = jnp.concatenate([blank, values, blank], axis=0)
    outside = jnp.full((TOK_DEV,), -1, jnp.int32)
    segment_padded = jnp.concatenate([outside, segment, outside], axis=0)

    def single_block(device):
        start = (device * TOK_DEV).astype(jnp.int32)
        query_rows = lax.dynamic_slice_in_dim(queries, start, TOK_DEV)
        key_rows = lax.dynamic_slice_in_dim(key_padded, start, 3 * TOK_DEV)
        value_rows = lax.dynamic_slice_in_dim(value_padded, start, 3 * TOK_DEV)
        query_segment = lax.dynamic_slice_in_dim(segment, start, TOK_DEV)
        key_segment = lax.dynamic_slice_in_dim(segment_padded, start, 3 * TOK_DEV)
        scores = jnp.einsum('qhd,khd->hqk', query_rows, key_rows, precision=exact) * HEAD ** (-0.5) + bias_full
        scores = low_back(scores)
        allowed = query_segment[:, None] == key_segment[None, :]
        scores = jnp.where(allowed[None], scores, -1e+30)
        probs = low(jax.nn.softmax(scores, axis=-1))
        return jnp.einsum('hqk,khd->qhd', probs, value_rows, precision=exact)
    mixed = lax.map(jax.checkpoint(single_block), jnp.arange(count, dtype=jnp.int32))
    return mixed.reshape(queries.shape[0], HEADS, HEAD)

def reference(inputs, attention_gain, query_weight, key_weight, value_weight, out_weight, bias_table, feedforward_gain, gate_weight, up_weight, down_weight, segment, bucket, cotangent):
    exact = lax.Precision.HIGHEST

    def forward(features, gain_one, w_query, w_key, w_value, w_out, table, gain_two, w_gate, w_up, w_down):
        normed = low(norm_rows(features, gain_one))
        queries = rounded_both(jnp.dot(normed, w_query, precision=exact))
        keys = rounded_both(jnp.dot(normed, w_key, precision=exact))
        values = rounded_both(jnp.dot(normed, w_value, precision=exact))
        offset_bias = table[bucket]
        mixed = window_attend(queries.reshape(-1, HEADS, HEAD), keys.reshape(-1, HEADS, HEAD), values.reshape(-1, HEADS, HEAD), offset_bias, segment)
        mixed = rounded_both(mixed.reshape(-1, HEADS * HEAD))
        hidden = features + low_back(jnp.dot(mixed, w_out, precision=exact))
        second = low(norm_rows(hidden, gain_two))
        gate = low_back(jnp.dot(second, w_gate, precision=exact))
        up = low_back(jnp.dot(second, w_up, precision=exact))
        act = low(jax.nn.gelu(gate, approximate=True) * up)
        return hidden + low_back(jnp.dot(act, w_down, precision=exact))
    floats = (inputs.astype(jnp.float32), attention_gain.astype(jnp.float32), query_weight.astype(jnp.float32), key_weight.astype(jnp.float32), value_weight.astype(jnp.float32), out_weight.astype(jnp.float32), bias_table.astype(jnp.float32), feedforward_gain.astype(jnp.float32), gate_weight.astype(jnp.float32), up_weight.astype(jnp.float32), down_weight.astype(jnp.float32))
    result, pullback = jax.vjp(forward, *floats)
    grads = pullback(cotangent.astype(jnp.float32))
    return (result.astype(jnp.bfloat16), grads[0].astype(jnp.bfloat16), grads[1], grads[2], grads[3], grads[4], grads[5], grads[6], grads[7], grads[8], grads[9], grads[10])
```

```python
import jax
import jax.numpy as jnp
from jax import lax
from jax.experimental import pallas as pl
from jax.experimental.pallas import tpu as pltpu
from jax.sharding import PartitionSpec as P

HEAD = 64
LOW = jnp.bfloat16
F32 = jnp.float32
CHUNK = 128
SPAN = 2048
NEG = -1e30
ROOT = 0.7978845608
CUBE = 0.044715
VMEM = pl.BlockSpec(memory_space=pltpu.VMEM)
SMEM = pl.BlockSpec(memory_space=pltpu.SMEM)


def dot_nn(a, b):
    return lax.dot_general(a, b, (((1,), (0,)), ((), ())), preferred_element_type=F32)


def dot_nt(a, b):
    return lax.dot_general(a, b, (((1,), (1,)), ((), ())), preferred_element_type=F32)


def dot_tn(a, b):
    return lax.dot_general(a, b, (((0,), (0,)), ((), ())), preferred_element_type=F32)


def call(kernel, outs, ins, scratch=(), smem=1, limit=48):
    return pl.pallas_call(
        kernel,
        out_shape=outs,
        in_specs=[SMEM] * smem + [VMEM] * (len(ins) - smem),
        out_specs=[VMEM] * len(outs),
        scratch_shapes=list(scratch),
        compiler_params=pltpu.CompilerParams(vmem_limit_bytes=limit * 1024 * 1024),
    )(*ins)


def shape(dims, dtype):
    return jax.ShapeDtypeStruct(dims, dtype)


def head_lanes(width, h):
    lane = lax.broadcasted_iota(jnp.int32, (1, width), 1)
    return (lane >= h * HEAD) & (lane < (h + 1) * HEAD)


def keep_head(values, h):
    return jnp.where(head_lanes(values.shape[-1], h), values, jnp.zeros_like(values))


def rows_norm(values):
    return lax.rsqrt(jnp.mean(values * values, axis=-1, keepdims=True) + 1e-06)


def aligned(start):
    return pl.ds(pl.multiple_of(start, CHUNK), CHUNK)


def bias_kernel(bucket_ref, flipped_ref, table_ref, bias_ref, bias_t_ref):
    heads = bias_ref.shape[0]
    buckets = table_ref.shape[0]
    for source, target in ((bucket_ref, bias_ref), (flipped_ref, bias_t_ref)):
        which = lax.broadcasted_iota(jnp.int32, (buckets, SPAN), 0)
        onehot = (source[...] == which).astype(F32)
        for h in range(heads):
            rows = jnp.sum(onehot * table_ref[:, h : h + 1], axis=0, keepdims=True)
            count = 1
            while count < 8:
                rows = jnp.concatenate([rows, pltpu.roll(rows, count, 1)], axis=0)
                count *= 2
            target[h, 0:8, :] = rows
            while count < CHUNK:
                target[h, count : 2 * count, :] = pltpu.roll(target[h, 0:count, :], count, 1)
                count *= 2


def fold_diagonals(tile):
    rows, cols = tile.shape
    while rows > 1:
        rows //= 2
        tile = tile[:rows] + pltpu.roll(tile[rows:], cols - rows, 1)
    return tile


def attend_chunk(q, keys, values, bias_of, allowed):
    heads = q.shape[-1] // HEAD
    total = jnp.zeros(q.shape, F32)
    tops, sums = [], []
    for h in range(heads):
        scores = dot_nt(keep_head(q, h), keys) + bias_of(h)
        if allowed is not None:
            scores = jnp.where(allowed, scores, NEG)
        top = jnp.max(scores, axis=-1, keepdims=True)
        weights = jnp.exp(scores - top)
        tops.append(top)
        sums.append(jnp.sum(weights, axis=-1, keepdims=True))
        total = total + dot_nn(weights.astype(LOW), keep_head(values, h))
    return total, tops, sums


def pack_columns(columns, offset=0, base=None, width=CHUNK):
    rows = columns[0].shape[0]
    lane = lax.broadcasted_iota(jnp.int32, (rows, width), 1)
    out = jnp.zeros((rows, width), F32) if base is None else base
    for k, column in enumerate(columns):
        out = jnp.where(lane == offset + k, column, out)
    return out


def by_head(columns, width):
    lane = lax.broadcasted_iota(jnp.int32, (columns[0].shape[0], width), 1)
    out = columns[0]
    for h in range(1, len(columns)):
        out = jnp.where(lane >= h * HEAD, columns[h], out)
    return out


def own_kernel(
    info,
    x0,
    x1,
    x2,
    x3,
    gain,
    wq,
    wk,
    wv,
    bias,
    seg_col,
    seg_row,
    x_all,
    normed_ref,
    q_ref,
    k_ref,
    v_ref,
    acc_ref,
    stat_ref,
):
    y, c = info[0], info[1]
    width = wq.shape[1]
    heads = width // HEAD
    window = x_all.shape[0]
    for piece, place in ((x0, 2 * y + c), (x1, 2 * (1 - y) + c), (x2, 2 * y + 1 - c), (x3, 2 * (1 - y) + 1 - c)):
        rows = aligned(place * CHUNK)
        low = piece[...]
        x_all[rows, :] = low
        wide = low.astype(F32)
        normed = (wide * rows_norm(wide) * gain[...]).astype(LOW)
        normed_ref[rows, :] = normed
        q_ref[rows, :] = (dot_nn(normed, wq[...]).astype(LOW).astype(F32) * HEAD**-0.5).astype(LOW)
        k_ref[rows, :] = dot_nn(normed, wk[...]).astype(LOW)
        v_ref[rows, :] = dot_nn(normed, wv[...]).astype(LOW)
    keys, values = k_ref[...], v_ref[...]
    for a in range(window // CHUNK):
        rows = slice(a * CHUNK, (a + 1) * CHUNK)
        allowed = seg_col[rows, :] == seg_row[...]
        start = SPAN // 2 - a * CHUNK
        total, tops, sums = attend_chunk(
            q_ref[rows, :], keys, values, lambda h: bias[h, :, start : start + window], allowed
        )
        acc_ref[rows, :] = total
        stat_ref[rows, :] = pack_columns(sums, 8, pack_columns(tops))


def partner_kernel(
    info,
    x0,
    x1,
    x2,
    x3,
    gain,
    wq,
    wk,
    wv,
    bias,
    q_ref,
    acc_ref,
    stat_ref,
    mixed_low,
    mixed_ref,
    lse_ref,
    qp_ref,
    kp_ref,
    vp_ref,
):
    y, c, left, paired = info[0], info[1], info[2], info[3]
    width = wq.shape[1]
    heads = width // HEAD
    window = q_ref.shape[0]
    base = jnp.where(left == 1, SPAN // 2 - window, SPAN // 2 + window)

    @pl.when(paired == 1)
    def _():
        for piece, place in (
            (x0, 2 * y + c),
            (x1, 2 * (1 - y) + c),
            (x2, 2 * y + 1 - c),
            (x3, 2 * (1 - y) + 1 - c),
        ):
            rows = aligned(place * CHUNK)
            wide = piece[...].astype(F32)
            normed = (wide * rows_norm(wide) * gain[...]).astype(LOW)
            qp_ref[rows, :] = (dot_nn(normed, wq[...]).astype(LOW).astype(F32) * HEAD**-0.5).astype(LOW)
            kp_ref[rows, :] = dot_nn(normed, wk[...]).astype(LOW)
            vp_ref[rows, :] = dot_nn(normed, wv[...]).astype(LOW)
        keys, values = kp_ref[...], vp_ref[...]
        for a in range(window // CHUNK):
            rows = slice(a * CHUNK, (a + 1) * CHUNK)
            start = pl.multiple_of(base - a * CHUNK, CHUNK)
            total, tops, sums = attend_chunk(
                q_ref[rows, :], keys, values, lambda h: bias[h, :, pl.ds(start, window)], None
            )
            stat = stat_ref[rows, :]
            olds, news, logs, norms = [], [], [], []
            for h in range(heads):
                top_one, sum_one = stat[:, h : h + 1], stat[:, 8 + h : 9 + h]
                top = jnp.maximum(top_one, tops[h])
                one, two = jnp.exp(top_one - top), jnp.exp(tops[h] - top)
                whole = sum_one * one + sums[h] * two
                olds.append(one / whole)
                news.append(two / whole)
                logs.append(top + jnp.log(whole))
            mixed = acc_ref[rows, :] * by_head(olds, width) + total * by_head(news, width)
            mixed_ref[rows, :] = mixed
            mixed_low[rows, :] = mixed.astype(LOW)
            lse_ref[rows, :] = pack_columns(logs)

    @pl.when(paired == 0)
    def _():
        qp_ref[...] = jnp.zeros_like(qp_ref)
        kp_ref[...] = jnp.zeros_like(kp_ref)
        vp_ref[...] = jnp.zeros_like(vp_ref)
        for a in range(window // CHUNK):
            rows = slice(a * CHUNK, (a + 1) * CHUNK)
            stat = stat_ref[rows, :]
            sums = [stat[:, 8 + h : 9 + h] for h in range(heads)]
            logs = [stat[:, h : h + 1] + jnp.log(sums[h]) for h in range(heads)]
            mixed = acc_ref[rows, :] / by_head(sums, width)
            mixed_ref[rows, :] = mixed
            mixed_low[rows, :] = mixed.astype(LOW)
            lse_ref[rows, :] = pack_columns(logs)


def feed_kernel(
    info,
    x_all,
    m0,
    m1,
    m2,
    m3,
    o0,
    o1,
    o2,
    o3,
    g0,
    g1,
    g2,
    g3,
    gain,
    gate_w,
    up_w,
    down_w,
    second_ref,
    hidden_ref,
    act_ref,
    dgate_ref,
    dup_ref,
    cot_ref,
    send_ref,
    keep_ref,
    gain_ref,
):
    y, c = info[0], info[1]
    half = 2 * CHUNK
    gain_sum = jnp.zeros((1, gain.shape[1]), F32)
    for part, (core, first, second_piece) in enumerate(((1 - c, g2, g3), (c, g0, g1))):
        rows = slice(part * half, (part + 1) * half)
        spots = (aligned((2 * y + core) * CHUNK), aligned((2 * (1 - y) + core) * CHUNK))

        def pick(ref):
            return jnp.concatenate([ref[spots[0], :], ref[spots[1], :]], axis=0)

        hidden = pick(x_all).astype(F32)
        branch = dot_nn(pick(m0), o0[...])
        for m, o in ((m1, o1), (m2, o2), (m3, o3)):
            branch = branch + dot_nn(pick(m), o[...])
        hidden = hidden + branch
        if part == 1:
            hidden_ref[...] = hidden
        unit = hidden * rows_norm(hidden)
        second = (unit * gain[...]).astype(LOW)
        second_ref[rows, :] = second
        cot = jnp.concatenate([first[...], second_piece[...]], axis=0)
        cot_ref[rows, :] = cot
        gate = dot_nn(second, gate_w[...])
        up = dot_nn(second, up_w[...])
        d_act = dot_nt(cot, down_w[...])
        square = gate * gate
        tanh = jnp.tanh(ROOT * gate * (1.0 + CUBE * square))
        low_half = 0.5 * (1.0 + tanh)
        gelu = gate * low_half
        slope = low_half + 0.5 * gate * (1.0 - tanh * tanh) * (ROOT * (1.0 + 3.0 * CUBE * square))
        act_ref[rows, :] = (gelu * up).astype(LOW)
        d_gate = (d_act * up * slope).astype(LOW)
        d_up = (d_act * gelu).astype(LOW)
        dgate_ref[rows, :] = d_gate
        dup_ref[rows, :] = d_up
        d_second = dot_nt(d_gate, gate_w[...]) + dot_nt(d_up, up_w[...])
        gain_sum = gain_sum + jnp.sum(d_second * unit, axis=0, keepdims=True)
        if part == 0:
            send_ref[...] = d_second.astype(LOW)
        else:
            keep_ref[...] = d_second
    gain_ref[...] = gain_sum


def hidden_back_kernel(sum_ref, other_ref, hidden_ref, g0, g1, gain, dh_ref, low_ref):
    for part, cot in enumerate((g0, g1)):
        rows = slice(part * CHUNK, (part + 1) * CHUNK)
        flip = slice((1 - part) * CHUNK, (2 - part) * CHUNK)
        d_second = sum_ref[rows, :].astype(F32) + other_ref[flip, :].astype(F32)
        hidden = hidden_ref[rows, :]
        inverse = rows_norm(hidden)
        unit = hidden * inverse
        scaled = d_second * gain[...]
        dh = cot[...].astype(F32) + inverse * (scaled - unit * jnp.mean(unit * scaled, axis=-1, keepdims=True))
        low_ref[rows, :] = dh.astype(LOW)
        if part == 0:
            dh_ref[...] = dh


def mixed_back_kernel(info, pair_own, pair_other, out_w, mixed_ref, lse_ref, branch_ref, payload_ref, stat_ref):
    y, c = info[0], info[1]
    width = mixed_ref.shape[1]
    heads = width // HEAD
    for pair, core in ((pair_own, c), (pair_other, 1 - c)):
        for part, row in enumerate((y, 1 - y)):
            rows = aligned((2 * row + core) * CHUNK)
            branch = pair[part * CHUNK : (part + 1) * CHUNK, :]
            branch_ref[rows, :] = branch
            d_mixed = dot_nt(branch, out_w[...]).astype(LOW).astype(F32)
            product = d_mixed[:, :width] * mixed_ref[rows, :]
            deltas = [jnp.sum(keep_head(product, h), axis=-1, keepdims=True) for h in range(heads)]
            lse = lse_ref[rows, :]
            logs = [lse[:, h : h + 1] for h in range(heads)]
            high = [v.astype(LOW).astype(F32) for v in logs + deltas]
            rest = [v - u for v, u in zip(logs + deltas, high)]
            payload_ref[rows, :] = pack_columns(high + rest, width, d_mixed, d_mixed.shape[1]).astype(LOW)
            stat_ref[rows, :] = pack_columns(logs + deltas)


def own_back_kernel(
    info,
    q_ref,
    k_ref,
    v_ref,
    kp_ref,
    vp_ref,
    payload_ref,
    stat_ref,
    bias,
    bias_t,
    seg_col,
    seg_row,
    bucket_ref,
    flipped_ref,
    dq_ref,
    dk_ref,
    dv_ref,
    table_ref,
    ds_ref,
    dq_acc,
    near_ref,
    far_ref,
):
    left, paired = info[2], info[3]
    window, width = q_ref.shape
    heads = width // HEAD
    steps = window // CHUNK
    reach = near_ref.shape[1]
    scale = HEAD**-0.5
    q_all = q_ref[...]
    back = payload_ref[:, :width]
    stat_rows = stat_ref[...].T
    buckets = table_ref.shape[0]
    base = jnp.where(left == 1, SPAN // 2 - window, SPAN // 2 + window)
    dk_ref[...] = jnp.zeros_like(dk_ref)
    dv_ref[...] = jnp.zeros_like(dv_ref)
    dq_acc[...] = jnp.zeros_like(dq_acc)
    for h in range(heads):
        lse, delta = stat_rows[h : h + 1, :], stat_rows[heads + h : heads + h + 1, :]
        q_head = keep_head(q_all, h)
        back_head = keep_head(back, h)
        near_ref[...] = jnp.zeros_like(near_ref)
        for a in range(steps):
            rows = slice(a * CHUNK, (a + 1) * CHUNK)
            start = SPAN // 2 - a * CHUNK
            scores = dot_nt(keep_head(k_ref[rows, :], h), q_all) + bias_t[h, :, start : start + window]
            weights = jnp.exp(jnp.where(seg_col[rows, :] == seg_row[...], scores, NEG) - lse)
            products = dot_nt(keep_head(v_ref[rows, :], h), back)
            d_scores = weights * (products - delta)
            d_low = d_scores.astype(LOW)
            ds_ref[rows, :] = d_low
            spot = slice((steps - a) * CHUNK, (steps - a) * CHUNK + window)
            near_ref[:, spot] += d_low.astype(F32)
            dv_ref[rows, :] += dot_nn(weights.astype(LOW), back_head)
            dk_ref[rows, :] += dot_nn(d_low, q_head)
        dq_acc[...] += dot_tn(ds_ref[...], keep_head(k_ref[...], h))
        folded = fold_diagonals(near_ref[...])
        start = SPAN // 2 - steps * CHUNK
        which = lax.broadcasted_iota(jnp.int32, (buckets, reach), 0)
        onehot = flipped_ref[:, start : start + reach] == which
        table_ref[:, h : h + 1] = jnp.sum(jnp.where(onehot, folded, 0.0), axis=1, keepdims=True)

    @pl.when(paired == 1)
    def _():
        for h in range(heads):
            far_ref[...] = jnp.zeros_like(far_ref)
            for a in range(steps):
                rows = slice(a * CHUNK, (a + 1) * CHUNK)
                start = pl.multiple_of(base - a * CHUNK, CHUNK)
                stat = stat_ref[rows, :]
                lse, delta = stat[:, h : h + 1], stat[:, heads + h : heads + h + 1]
                scores = dot_nt(keep_head(q_ref[rows, :], h), kp_ref[...]) + bias[h, :, pl.ds(start, window)]
                weights = jnp.exp(scores - lse)
                products = dot_nt(keep_head(payload_ref[rows, :width], h), vp_ref[...])
                d_low = (weights * (products - delta)).astype(LOW)
                spot = slice((steps - a) * CHUNK, (steps - a) * CHUNK + window)
                far_ref[:, spot] += d_low.astype(F32)
                dq_acc[rows, :] += dot_nn(d_low, keep_head(kp_ref[...], h))
            folded = fold_diagonals(far_ref[...])
            start = pl.multiple_of(base - steps * CHUNK, CHUNK)
            which = lax.broadcasted_iota(jnp.int32, (buckets, reach), 0)
            onehot = bucket_ref[:, pl.ds(start, reach)] == which
            table_ref[:, h : h + 1] += jnp.sum(jnp.where(onehot, folded, 0.0), axis=1, keepdims=True)

    dq_ref[...] = (dq_acc[...] * scale).astype(LOW)


def partner_back_kernel(
    info,
    k_ref,
    v_ref,
    qp_ref,
    from_left,
    from_right,
    bias_t,
    dk_in,
    dv_in,
    dq_ref,
    normed_ref,
    x_all,
    gain,
    wq,
    wk,
    wv,
    joint_ref,
    send_ref,
    keep_ref,
    gain_ref,
    dk_acc,
    dv_acc,
    dk_low,
    dv_low,
):
    y, c, left, paired = info[0], info[1], info[2], info[3]
    window, width = k_ref.shape
    heads = width // HEAD
    steps = window // CHUNK
    base = jnp.where(left == 1, SPAN // 2 - window, SPAN // 2 + window)
    dk_acc[...] = dk_in[...]
    dv_acc[...] = dv_in[...]

    @pl.when(paired == 1)
    def _():
        payload = jnp.where(left == 1, from_left[...], from_right[...])
        back = payload[:, :width]
        columns = payload[:, payload.shape[1] - CHUNK :].astype(F32).T
        skip = width - (payload.shape[1] - CHUNK)
        queries = qp_ref[...]
        for h in range(heads):
            q_head = keep_head(queries, h)
            back_head = keep_head(back, h)
            at = skip + h
            lse = columns[at : at + 1, :] + columns[at + 2 * heads : at + 2 * heads + 1, :]
            at = at + heads
            delta = columns[at : at + 1, :] + columns[at + 2 * heads : at + 2 * heads + 1, :]
            for a in range(steps):
                rows = slice(a * CHUNK, (a + 1) * CHUNK)
                start = pl.multiple_of(base - a * CHUNK, CHUNK)
                scores = dot_nt(keep_head(k_ref[rows, :], h), queries) + bias_t[h, :, pl.ds(start, window)]
                weights = jnp.exp(scores - lse)
                products = dot_nt(keep_head(v_ref[rows, :], h), back)
                d_low = (weights * (products - delta)).astype(LOW)
                dv_acc[rows, :] += dot_nn(weights.astype(LOW), back_head)
                dk_acc[rows, :] += dot_nn(d_low, q_head)

    dk_low[...] = dk_acc[...].astype(LOW)
    dv_low[...] = dv_acc[...].astype(LOW)
    normed = normed_ref[...]
    joint_ref[:, :width] = dot_tn(normed, dq_ref[...]).astype(LOW)
    joint_ref[:, width : 2 * width] = dot_tn(normed, dk_low[...]).astype(LOW)
    joint_ref[:, 2 * width :] = dot_tn(normed, dv_low[...]).astype(LOW)
    gain_sum = jnp.zeros((1, gain.shape[1]), F32)
    for part, core in enumerate((1 - c, c)):
        for side, row in enumerate((y, 1 - y)):
            rows = aligned((2 * row + core) * CHUNK)
            d_normed = dot_nt(dq_ref[rows, :], wq[...])
            d_normed = d_normed + dot_nt(dk_low[rows, :], wk[...])
            d_normed = d_normed + dot_nt(dv_low[rows, :], wv[...])
            wide = x_all[rows, :].astype(F32)
            gain_sum = gain_sum + jnp.sum(d_normed * wide * rows_norm(wide), axis=0, keepdims=True)
            spot = slice(side * CHUNK, (side + 1) * CHUNK)
            if part == 0:
                send_ref[spot, :] = d_normed.astype(LOW)
            else:
                keep_ref[spot, :] = d_normed
    gain_ref[...] = gain_sum


def input_back_kernel(sum_ref, other_ref, x_ref, dh_ref, gain, out_ref):
    d_normed = sum_ref[...].astype(F32) + other_ref[...].astype(F32)
    wide = x_ref[...].astype(F32)
    inverse = rows_norm(wide)
    unit = wide * inverse
    scaled = d_normed * gain[...]
    back = inverse * (scaled - unit * jnp.mean(unit * scaled, axis=-1, keepdims=True))
    out_ref[...] = (dh_ref[...] + back).astype(LOW)


def swap(values, axis, bit):
    return lax.ppermute(values, axis, [(i, i ^ bit) for i in range(lax.axis_size(axis))])


def spread(own):
    across = swap(own, "mp", 2)
    return own, across, swap(own, "mp", 1), swap(across, "mp", 1)


def reduce_all(values, order, rank):
    for bit in order:
        half = values.shape[0] // 2
        side = (rank >> bit) & 1
        keep = lax.dynamic_slice_in_dim(values, side * half, half)
        send = lax.dynamic_slice_in_dim(values, (1 - side) * half, half)
        got = swap(send, "dp", 1 << bit)
        values = (keep.astype(F32) + got.astype(F32)).astype(LOW)
    for bit in reversed(order):
        side = (rank >> bit) & 1
        got = swap(values, "dp", 1 << bit)
        values = jnp.where(
            side == 0, jnp.concatenate([values, got], axis=0), jnp.concatenate([got, values], axis=0)
        )
    return values.astype(F32)


def per_device(
    inputs,
    attention_gain,
    query_weight,
    key_weight,
    value_weight,
    out_weight,
    bias_table,
    feedforward_gain,
    gate_weight,
    up_weight,
    down_weight,
    segment,
    bucket,
    cotangent,
):
    parts = lax.axis_size("mp")
    groups = lax.axis_size("dp")
    local, d = inputs.shape
    window = local * parts
    width = query_weight.shape[1]
    heads = width // HEAD
    hidden_units = gate_weight.shape[1]
    buckets = bias_table.shape[0]
    half = 2 * local
    rank = lax.axis_index("dp")
    member = lax.axis_index("mp")
    bits = list(range(groups.bit_length() - 1))
    order_one = bits
    order_two = [bits[1], bits[0]] + bits[2:]

    first = rank * window
    seg_own = lax.dynamic_slice_in_dim(segment, first, window)
    padded = jnp.concatenate([jnp.full((1,), -1, jnp.int32), segment, jnp.full((1,), -1, jnp.int32)])
    before = lax.dynamic_slice_in_dim(padded, first, 1)[0]
    after = lax.dynamic_slice_in_dim(padded, first + window + 1, 1)[0]
    left = before == seg_own[0]
    right = after == seg_own[window - 1]
    info = jnp.stack(
        [member // 2, member % 2, left.astype(jnp.int32), (left | right).astype(jnp.int32)]
    ).astype(jnp.int32)
    seg_col, seg_row = seg_own[:, None], seg_own[None, :]
    edge = jnp.full((1,), -1, jnp.int32)
    bucket_row = jnp.concatenate([edge, bucket])[None, :]
    flipped_row = jnp.concatenate([edge, bucket[::-1]])[None, :]
    gain_one, gain_two = attention_gain[None, :], feedforward_gain[None, :]

    x_pieces = spread(inputs)
    from_left = lax.ppermute(inputs, "dp", [(i, i + 1) for i in range(groups - 1)])
    from_right = lax.ppermute(inputs, "dp", [(i + 1, i) for i in range(groups - 1)])
    near = jnp.where(left, from_left, from_right)
    near_pieces = spread(near)
    cot_pieces = spread(cotangent)
    out_pieces = spread(out_weight)

    bias, bias_t = call(
        bias_kernel,
        [shape((heads, CHUNK, SPAN), F32)] * 2,
        [bucket_row, flipped_row, bias_table],
        smem=0,
    )
    low_rows = shape((window, width), LOW)
    wide_rows = shape((window, width), F32)
    x_all, normed, queries, keys, values, acc, stat = call(
        own_kernel,
        [shape((window, d), LOW)] * 2 + [low_rows] * 3 + [wide_rows, shape((window, CHUNK), F32)],
        [info, *x_pieces, gain_one, query_weight, key_weight, value_weight, bias, seg_col, seg_row],
    )
    mixed_low, mixed, lse, queries_near, keys_near, values_near = call(
        partner_kernel,
        [low_rows, wide_rows, shape((window, CHUNK), F32)] + [low_rows] * 3,
        [info, *near_pieces, gain_one, query_weight, key_weight, value_weight, bias, queries, acc, stat],
    )
    mixed_pieces = spread(mixed_low)
    second, hidden, act, d_gate, d_up, cot_all, second_send, second_keep, gain_two_part = call(
        feed_kernel,
        [shape((window, d), LOW), shape((half, d), F32)]
        + [shape((window, hidden_units), LOW)] * 3
        + [shape((window, d), LOW), shape((half, d), LOW), shape((half, d), F32), shape((1, d), F32)],
        [info, x_all, *mixed_pieces, *out_pieces, *cot_pieces, gain_two, gate_weight, up_weight, down_weight],
    )
    second_sum = (second_keep + swap(second_send, "mp", 1).astype(F32)).astype(LOW)
    second_other = swap(second_sum, "mp", 2)

    gate_grad = dot_tn(second, d_gate).astype(LOW)
    up_grad = dot_tn(second, d_up).astype(LOW)
    down_grad = dot_tn(act, cot_all).astype(LOW)
    feed = dot_nn(act, down_weight).astype(LOW)
    feed_sum = (feed[half:].astype(F32) + swap(feed[:half], "mp", 1).astype(F32)).astype(LOW)
    feed_own = feed_sum[:local].astype(F32) + swap(feed_sum[local:], "mp", 2).astype(F32)
    layer_out = (hidden[:local] + feed_own).astype(LOW)

    dh, branch_low = call(
        hidden_back_kernel,
        [shape((local, d), F32), shape((half, d), LOW)],
        [second_sum, second_other, hidden, cot_pieces[0], cot_pieces[1], gain_two],
        smem=0,
    )
    out_padded = jnp.pad(out_weight, ((0, 2 * CHUNK - width), (0, 0)))
    branch_all, payload, stat_back = call(
        mixed_back_kernel,
        [shape((window, d), LOW), shape((window, 2 * CHUNK), LOW), shape((window, CHUNK), F32)],
        [info, branch_low, swap(branch_low, "mp", 1), out_padded, mixed, lse],
    )
    payload_left = lax.ppermute(payload, "dp", [(i, i + 1) for i in range(groups - 1)])
    payload_right = lax.ppermute(payload, "dp", [(i + 1, i) for i in range(groups - 1)])
    out_grad = dot_tn(mixed_low, branch_all).astype(LOW)
    reach = 2 * window
    d_queries, d_keys, d_values, table_part = call(
        own_back_kernel,
        [low_rows, wide_rows, wide_rows, shape((buckets, heads), F32)],
        [
            info,
            queries,
            keys,
            values,
            keys_near,
            values_near,
            payload,
            stat_back,
            bias,
            bias_t,
            seg_col,
            seg_row,
            bucket_row,
            flipped_row,
        ],
        scratch=[
            pltpu.VMEM((window, window), LOW),
            pltpu.VMEM((window, width), F32),
            pltpu.VMEM((CHUNK, reach), F32),
            pltpu.VMEM((CHUNK, reach), F32),
        ],
    )
    joint, first_send, first_keep, gain_one_part = call(
        partner_back_kernel,
        [shape((d, 3 * width), LOW), shape((half, d), LOW), shape((half, d), F32), shape((1, d), F32)],
        [
            info,
            keys,
            values,
            queries_near,
            payload_left,
            payload_right,
            bias_t,
            d_keys,
            d_values,
            d_queries,
            normed,
            x_all,
            gain_one,
            query_weight,
            key_weight,
            value_weight,
        ],
        scratch=[pltpu.VMEM((window, width), F32)] * 2 + [pltpu.VMEM((window, width), LOW)] * 2,
    )
    first_sum = (first_keep + swap(first_send, "mp", 1).astype(F32)).astype(LOW)
    (input_grad,) = call(
        input_back_kernel,
        [shape((local, d), LOW)],
        [first_sum[:local], swap(first_sum[local:], "mp", 2), inputs, dh, gain_one],
        smem=0,
    )

    gains = jnp.concatenate([gain_one_part, gain_two_part], axis=0)
    gains = gains + swap(gains, "mp", 1)
    gains = gains + swap(gains, "mp", 2)
    small = jnp.concatenate([gains.reshape(-1), table_part.reshape(-1)])
    small = jnp.pad(small, (0, SPAN - small.shape[0])).reshape(-1, CHUNK)
    for bit in bits:
        small = small + swap(small, "dp", 1 << bit)
    small = small.reshape(-1)

    gate_total = reduce_all(gate_grad, order_one, rank)
    up_total = reduce_all(up_grad, order_one, rank)
    down_total = reduce_all(down_grad, order_two, rank)
    out_total = reduce_all(out_grad, order_two, rank)
    joint_total = reduce_all(joint, order_one, rank)
    return (
        layer_out,
        input_grad,
        small[:d],
        joint_total[:, :width],
        joint_total[:, width : 2 * width],
        joint_total[:, 2 * width :],
        out_total,
        small[2 * d : 2 * d + buckets * heads].reshape(buckets, heads),
        small[d : 2 * d],
        gate_total,
        up_total,
        down_total,
    )


def solution(mesh):
    rows = P(("dp", "mp"), None)
    in_specs = (
        rows,
        P(),
        P(None, "mp"),
        P(None, "mp"),
        P(None, "mp"),
        P("mp", None),
        P(None, "mp"),
        P(),
        P(None, "mp"),
        P(None, "mp"),
        P("mp", None),
        P(),
        P(),
        rows,
    )
    out_specs = (
        rows,
        rows,
        P(),
        P(None, "mp"),
        P(None, "mp"),
        P(None, "mp"),
        P("mp", None),
        P(None, "mp"),
        P(),
        P(None, "mp"),
        P(None, "mp"),
        P("mp", None),
    )
    return jax.shard_map(
        per_device, mesh=mesh, in_specs=in_specs, out_specs=out_specs, check_vma=False
    )
```

```python
import functools

import jax
import jax.numpy as jnp
from jax import lax
from jax.experimental import pallas as pl
from jax.experimental.pallas import tpu as pltpu
from jax.sharding import PartitionSpec as P

HEAD = 64
LOW = jnp.bfloat16
F32 = jnp.float32
CHUNK = 128
SPAN = 2048
EXTRA = 16
NEG = -1e30
ROOT = 0.7978845608
CUBE = 0.044715
VMEM = pl.BlockSpec(memory_space=pltpu.VMEM)
SMEM = pl.BlockSpec(memory_space=pltpu.SMEM)
HBM = pl.BlockSpec(memory_space=pltpu.HBM)


def dot_nn(a, b):
    return lax.dot_general(a, b, (((1,), (0,)), ((), ())), preferred_element_type=F32)


def dot_nt(a, b):
    return lax.dot_general(a, b, (((1,), (1,)), ((), ())), preferred_element_type=F32)


def dot_tn(a, b):
    return lax.dot_general(a, b, (((0,), (0,)), ((), ())), preferred_element_type=F32)


def call(kernel, outs, ins, scratch=(), smem=1, hbm=0, micros=2.0, out_smem=0, limit=20):
    return pl.pallas_call(
        kernel,
        out_shape=outs,
        in_specs=[SMEM] * smem + [VMEM] * (len(ins) - smem - hbm) + [HBM] * hbm,
        out_specs=[SMEM] * out_smem + [VMEM] * (len(outs) - out_smem),
        scratch_shapes=list(scratch),
        cost_estimate=pl.CostEstimate(flops=int(micros * 2e7), bytes_accessed=0, transcendentals=0),
        compiler_params=pltpu.CompilerParams(vmem_limit_bytes=limit * 1024 * 1024),
    )(*ins)


def in_hbm(values):
    return pltpu.with_memory_space_constraint(values, pltpu.HBM)


def shape(dims, dtype):
    return jax.ShapeDtypeStruct(dims, dtype)


def head_lanes(width, h):
    lane = lax.broadcasted_iota(jnp.int32, (1, width), 1)
    return (lane >= h * HEAD) & (lane < (h + 1) * HEAD)


def keep_head(values, h):
    return jnp.where(head_lanes(values.shape[-1], h), values, jnp.zeros_like(values))


def rows_norm(values):
    return lax.rsqrt(jnp.mean(values * values, axis=-1, keepdims=True) + 1e-06)


def aligned(start):
    return pl.ds(pl.multiple_of(start, CHUNK), CHUNK)


def lay_bias(row, table_ref, target):
    heads, buckets = table_ref.shape
    which = lax.broadcasted_iota(jnp.int32, (buckets, SPAN), 0)
    onehot = (row == which).astype(F32)
    table = table_ref[...].T
    for h in range(heads):
        rows = jnp.sum(onehot * table[:, h : h + 1], axis=0, keepdims=True)
        count = 1
        while count < 8:
            rows = jnp.concatenate([rows, pltpu.roll(rows, count, 1)], axis=0)
            count *= 2
        target[h, 0:8, :] = rows
        while count < CHUNK:
            target[h, count : 2 * count, :] = pltpu.roll(target[h, 0:count, :], count, 1)
            count *= 2


def setup_kernel(spot, segment_ref, bucket_ref, table_ref, info, row_ref, col_ref, bias_ref, *, groups, first_bits):
    rank, member = spot[0], spot[1]
    steps = row_ref.shape[1] // CHUNK
    rows = [segment_ref[pl.ds(rank * steps + k, 1), :] for k in range(steps)]
    lane = lax.broadcasted_iota(jnp.int32, (1, CHUNK), 1)

    def value(row, at):
        return jnp.max(jnp.where(lane == at, row, -1))

    before = segment_ref[pl.ds(jnp.maximum(rank * steps - 1, 0), 1), :]
    later = segment_ref[pl.ds(jnp.minimum((rank + 1) * steps, groups * steps - 1), 1), :]
    left = (value(before, CHUNK - 1) == value(rows[0], 0)) & (rank > 0)
    right = (value(later, 0) == value(rows[-1], CHUNK - 1)) & (rank < groups - 1)
    even = jnp.where(rank % 2 == 0, right.astype(jnp.int32), left.astype(jnp.int32))
    info[0] = member // 2
    info[1] = member % 2
    info[2] = left.astype(jnp.int32)
    info[3] = (left | right).astype(jnp.int32)
    info[4] = (rank >> first_bits[0]) & 1
    info[5] = (rank >> first_bits[1]) & 1
    info[6] = even
    info[7] = rank
    row = jnp.concatenate(rows, axis=1).astype(F32)
    row_ref[...] = row
    col_ref[...] = jnp.broadcast_to(row, (CHUNK, row.shape[1])).T
    lay_bias(row_of(bucket_ref, 0, bucket_ref.shape[0]), table_ref, bias_ref)


def row_of(ref, first, count):
    return jnp.concatenate([ref[pl.ds(first + k, 1), :] for k in range(count)], axis=1)


def flipped_kernel(bucket_ref, table_ref, bias_ref, flipped_ref):
    count = bucket_ref.shape[0]
    sub = lax.broadcasted_iota(jnp.int32, (CHUNK, CHUNK), 0)
    lane = lax.broadcasted_iota(jnp.int32, (CHUNK, CHUNK), 1)
    turned = dot_nn(bucket_ref[...].astype(F32).astype(LOW), (sub + lane == CHUNK - 1).astype(F32).astype(LOW))
    row = jnp.concatenate([turned[k : k + 1, :] for k in reversed(range(count))], axis=1)
    row = pltpu.roll(row, 1, 1).astype(jnp.int32)
    flipped_ref[...] = jnp.concatenate([row[:, k * CHUNK : (k + 1) * CHUNK] for k in range(count)], axis=0)
    lay_bias(row, table_ref, bias_ref)


def near_kernel(info, even_ref, odd_ref, out_ref):
    out_ref[...] = jnp.where(info[6] == 1, even_ref[...], odd_ref[...])


def fold_diagonals(tile):
    rows, cols = tile.shape
    while rows > 1:
        rows //= 2
        tile = tile[:rows] + pltpu.roll(tile[rows:], cols - rows, 1)
    return tile


def pack_columns(columns, offset=0, base=None, width=CHUNK):
    rows = columns[0].shape[0]
    lane = lax.broadcasted_iota(jnp.int32, (rows, width), 1)
    out = jnp.zeros((rows, width), F32) if base is None else base
    for k, column in enumerate(columns):
        out = jnp.where(lane == offset + k, column, out)
    return out


def by_head(packed, width):
    lane = lax.broadcasted_iota(jnp.int32, (packed.shape[0], width), 1)
    out = packed[:, 0:1]
    for h in range(1, width // HEAD):
        out = jnp.where(lane >= h * HEAD, packed[:, h : h + 1], out)
    return out


def place(y, c):
    return (2 * y + c, 2 * (1 - y) + c, 2 * y + 1 - c, 2 * (1 - y) + 1 - c)


def project(normed, rows, wq, wk, wv, q_ref, k_ref, v_ref):
    q_ref[rows, :] = (dot_nt(normed, wq[...]).astype(LOW).astype(F32) * HEAD**-0.5).astype(LOW)
    k_ref[rows, :] = dot_nt(normed, wk[...]).astype(LOW)
    v_ref[rows, :] = dot_nt(normed, wv[...]).astype(LOW)


def attend(q, keys, values, bias, first, seg_col, seg_row, scores_ref, probs_ref, acc_ref, top_ref, sum_ref):
    window, width = q.shape
    heads = width // HEAD
    for h in range(heads):
        scores_ref[h] = dot_nt(keep_head(q, h), keys)
    for h in range(heads):
        for a in range(window // CHUNK):
            rows = slice(a * CHUNK, (a + 1) * CHUNK)
            scores = scores_ref[h, rows, :] + bias[h, :, pl.ds(first - a * CHUNK, window)]
            if seg_col is not None:
                scores = jnp.where(seg_col[rows, 0:1] == seg_row[...], scores, NEG)
            top = jnp.max(scores, axis=-1, keepdims=True)
            weights = jnp.exp(scores - top)
            probs_ref[h, rows, :] = weights.astype(LOW)
            top_ref[rows, :] = pack_columns([top], h, top_ref[rows, :] if h else jnp.zeros((CHUNK, CHUNK), F32))
            total = jnp.sum(weights, axis=-1, keepdims=True)
            sum_ref[rows, :] = pack_columns([total], h, sum_ref[rows, :] if h else jnp.ones((CHUNK, CHUNK), F32))
    total = dot_nn(probs_ref[0], keep_head(values, 0))
    for h in range(1, heads):
        total = total + dot_nn(probs_ref[h], keep_head(values, h))
    acc_ref[...] = total


def own_kernel(
    info,
    x0,
    x1,
    x2,
    x3,
    gain,
    bias,
    seg_col,
    seg_row,
    wq_hbm,
    wk_hbm,
    wv_hbm,
    x_all,
    normed_ref,
    q_ref,
    k_ref,
    v_ref,
    acc_ref,
    top_ref,
    sum_ref,
    wq,
    wk,
    wv,
    scores_ref,
    probs_ref,
    sems,
):
    pairs = ((wq_hbm, wq), (wk_hbm, wk), (wv_hbm, wv))
    copies = [pltpu.make_async_copy(a, b, sems.at[k]) for k, (a, b) in enumerate(pairs)]
    for copy in copies:
        copy.start()
    for piece, spot in zip((x0, x1, x2, x3), place(info[0], info[1])):
        rows = aligned(spot * CHUNK)
        low = piece[...]
        x_all[rows, :] = low
        wide = low.astype(F32)
        normed_ref[rows, :] = (wide * rows_norm(wide) * gain[...]).astype(LOW)
    for copy in copies:
        copy.wait()
    project(normed_ref[...], slice(None), wq, wk, wv, q_ref, k_ref, v_ref)
    attend(
        q_ref[...],
        k_ref[...],
        v_ref[...],
        bias,
        SPAN // 2,
        seg_col,
        seg_row,
        scores_ref,
        probs_ref,
        acc_ref,
        top_ref,
        sum_ref,
    )


def far_start(info, window):
    return pl.multiple_of(jnp.where(info[2] == 1, SPAN // 2 - window, SPAN // 2 + window), CHUNK)


def partner_kernel(
    info,
    x0,
    x1,
    x2,
    x3,
    gain,
    wq,
    wk,
    wv,
    bias,
    q_ref,
    acc_ref,
    top_ref,
    sum_ref,
    mixed_low,
    mixed_ref,
    lse_ref,
    qp_ref,
    kp_ref,
    vp_ref,
    normed_ref,
    scores_ref,
    probs_ref,
    acc_two,
    top_two,
    sum_two,
):
    window, width = q_ref.shape
    paired = info[3]

    @pl.when(paired == 1)
    def _():
        for piece, spot in zip((x0, x1, x2, x3), place(info[0], info[1])):
            wide = piece[...].astype(F32)
            normed_ref[aligned(spot * CHUNK), :] = (wide * rows_norm(wide) * gain[...]).astype(LOW)
        project(normed_ref[...], slice(None), wq, wk, wv, qp_ref, kp_ref, vp_ref)
        attend(
            q_ref[...],
            kp_ref[...],
            vp_ref[...],
            bias,
            far_start(info, window),
            None,
            None,
            scores_ref,
            probs_ref,
            acc_two,
            top_two,
            sum_two,
        )
        for a in range(window // CHUNK):
            rows = slice(a * CHUNK, (a + 1) * CHUNK)
            top = jnp.maximum(top_ref[rows, :], top_two[rows, :])
            one, two = jnp.exp(top_ref[rows, :] - top), jnp.exp(top_two[rows, :] - top)
            whole = sum_ref[rows, :] * one + sum_two[rows, :] * two
            inverse = 1.0 / whole
            mixed = acc_ref[rows, :] * by_head(one * inverse, width)
            mixed = mixed + acc_two[rows, :] * by_head(two * inverse, width)
            mixed_ref[rows, :] = mixed
            mixed_low[rows, :] = mixed.astype(LOW)
            lse_ref[rows, :] = top + jnp.log(whole)

    @pl.when(paired == 0)
    def _():
        qp_ref[...] = jnp.zeros_like(qp_ref)
        kp_ref[...] = jnp.zeros_like(kp_ref)
        vp_ref[...] = jnp.zeros_like(vp_ref)
        for a in range(window // CHUNK):
            rows = slice(a * CHUNK, (a + 1) * CHUNK)
            whole = sum_ref[rows, :]
            mixed = acc_ref[rows, :] * by_head(1.0 / whole, width)
            mixed_ref[rows, :] = mixed
            mixed_low[rows, :] = mixed.astype(LOW)
            lse_ref[rows, :] = top_ref[rows, :] + jnp.log(whole)


def cotangent_kernel(g0, g1, g2, g3, down_w, cot_ref, d_act_ref):
    for part, piece in enumerate((g2, g3, g0, g1)):
        cot_ref[part * CHUNK : (part + 1) * CHUNK, :] = piece[...]
    d_act_ref[...] = dot_nt(cot_ref[...], down_w[...])


def feed_kernel(
    info,
    x_all,
    m0,
    m1,
    m2,
    m3,
    o0,
    o1,
    o2,
    o3,
    d_act_ref,
    gain,
    gate_w,
    up_w,
    second_ref,
    hidden_ref,
    act_ref,
    dgate_ref,
    dup_ref,
    send_ref,
    keep_ref,
    gain_ref,
):
    y, c = info[0], info[1]
    half = 2 * CHUNK
    gain_sum = jnp.zeros((1, gain.shape[1]), F32)
    for part, core in enumerate((1 - c, c)):
        rows = slice(part * half, (part + 1) * half)
        spots = (aligned((2 * y + core) * CHUNK), aligned((2 * (1 - y) + core) * CHUNK))

        def pick(ref):
            return jnp.concatenate([ref[spots[0], :], ref[spots[1], :]], axis=0)

        hidden = pick(x_all).astype(F32)
        branch = dot_nn(pick(m0), o0[...])
        for m, o in ((m1, o1), (m2, o2), (m3, o3)):
            branch = branch + dot_nn(pick(m), o[...])
        hidden = hidden + branch
        if part == 1:
            hidden_ref[...] = hidden
        unit = hidden * rows_norm(hidden)
        second = (unit * gain[...]).astype(LOW)
        second_ref[rows, :] = second
        gate = dot_nn(second, gate_w[...])
        up = dot_nn(second, up_w[...])
        d_act = d_act_ref[rows, :]
        square = gate * gate
        tanh = jnp.tanh(ROOT * gate * (1.0 + CUBE * square))
        low_half = 0.5 * (1.0 + tanh)
        gelu = gate * low_half
        slope = low_half + 0.5 * gate * (1.0 - tanh * tanh) * (ROOT * (1.0 + 3.0 * CUBE * square))
        act_ref[rows, :] = (gelu * up).astype(LOW)
        d_gate = (d_act * up * slope).astype(LOW)
        d_up = (d_act * gelu).astype(LOW)
        dgate_ref[rows, :] = d_gate
        dup_ref[rows, :] = d_up
        d_second = dot_nt(d_gate, gate_w[...]) + dot_nt(d_up, up_w[...])
        gain_sum = gain_sum + jnp.sum(d_second * unit, axis=0, keepdims=True)
        if part == 0:
            send_ref[...] = d_second.astype(LOW)
        else:
            keep_ref[...] = d_second
    gain_ref[...] = gain_sum


def feed_grad_kernel(
    info, second_ref, dgate_ref, dup_ref, act_ref, cot_ref, one_send, one_keep, two_send, two_keep, one_ref, two_ref
):
    d, units = second_ref.shape[1], dgate_ref.shape[1]
    one_ref[:d, :] = dot_tn(second_ref[...], dgate_ref[...]).astype(LOW)
    two_ref[:d, :] = dot_tn(second_ref[...], dup_ref[...]).astype(LOW)
    down = dot_tn(act_ref[...], cot_ref[...]).astype(LOW)
    half = units // 2
    quarter = half // 2
    for k, target in enumerate((one_ref, two_ref)):
        target[d : d + half, :] = down[k * half : (k + 1) * half, :units]
        for side in (0, 1):
            rows = slice(k * half + side * quarter, k * half + (side + 1) * quarter)
            target[d + half :, side * (units // 2) : (side + 1) * (units // 2)] = down[rows, units:]
    for source, side, send, keep in ((one_ref, info[4], one_send, one_keep), (two_ref, info[5], two_send, two_keep)):
        rows = send.shape[0]
        send[...] = source[pl.ds(pl.multiple_of((1 - side) * rows, 16), rows), :]
        keep[...] = source[pl.ds(pl.multiple_of(side * rows, 16), rows), :]


def feed_out_kernel(act_ref, down_w, send_ref, keep_ref):
    half = send_ref.shape[0]
    send_ref[...] = dot_nn(act_ref[:half, :], down_w[...]).astype(LOW)
    keep_ref[...] = dot_nn(act_ref[half:, :], down_w[...]).astype(LOW)


def feed_total_kernel(info, one, one_got, two, two_got, gate_ref, up_ref, down_ref, full_ref):
    d, units = gate_ref.shape
    half = units // 2
    quarter = half // 2
    parts = ((one, one_got, info[4], gate_ref), (two, two_got, info[5], up_ref))
    for k, (mine, got, side, target) in enumerate(parts):
        rows = mine.shape[0]
        full_ref[pl.ds(pl.multiple_of(side * rows, 16), rows), :] = mine[...]
        full_ref[pl.ds(pl.multiple_of((1 - side) * rows, 16), rows), :] = got[...]
        target[...] = full_ref[:d, :].astype(F32)
        down_ref[k * half : (k + 1) * half, :units] = full_ref[d : d + half, :].astype(F32)
        for part in (0, 1):
            rows = slice(k * half + part * quarter, k * half + (part + 1) * quarter)
            down_ref[rows, units:] = full_ref[d + half :, part * (units // 2) : (part + 1) * (units // 2)].astype(F32)


def feed_merge_kernel(keep_ref, got_ref, own_ref, send_ref):
    local = own_ref.shape[0]
    total = (keep_ref[...].astype(F32) + got_ref[...].astype(F32)).astype(LOW)
    own_ref[...] = total[:local, :]
    send_ref[...] = total[local:, :]


def layer_out_kernel(hidden_ref, own_ref, got_ref, out_ref):
    local = out_ref.shape[0]
    out_ref[...] = (hidden_ref[:local, :] + (own_ref[...].astype(F32) + got_ref[...].astype(F32))).astype(LOW)


def hidden_back_kernel(sum_ref, other_ref, hidden_ref, g0, g1, gain, dh_ref, low_ref):
    for part, cot in enumerate((g0, g1)):
        rows = slice(part * CHUNK, (part + 1) * CHUNK)
        flip = slice((1 - part) * CHUNK, (2 - part) * CHUNK)
        d_second = sum_ref[rows, :].astype(F32) + other_ref[flip, :].astype(F32)
        hidden = hidden_ref[rows, :]
        inverse = rows_norm(hidden)
        unit = hidden * inverse
        scaled = d_second * gain[...]
        dh = cot[...].astype(F32) + inverse * (scaled - unit * jnp.mean(unit * scaled, axis=-1, keepdims=True))
        low_ref[rows, :] = dh.astype(LOW)
        if part == 0:
            dh_ref[...] = dh


def mixed_back_kernel(
    info, pair_own, pair_other, out_w, mixed_ref, mixed_low, lse_ref, payload_ref, stat_ref, grad_ref, branch_ref, pad_ref
):
    width = mixed_ref.shape[1]
    heads = width // HEAD
    pieces = (pair_own[:CHUNK, :], pair_own[CHUNK:, :], pair_other[:CHUNK, :], pair_other[CHUNK:, :])
    for piece, spot in zip(pieces, place(info[0], info[1])):
        branch_ref[aligned(spot * CHUNK), :] = piece
    pad_ref[:width, :] = out_w[...]
    pad_ref[width:, :] = jnp.zeros((pad_ref.shape[0] - width, pad_ref.shape[1]), LOW)
    d_all = dot_nt(branch_ref[...], pad_ref[...]).astype(LOW).astype(F32)
    for a in range(d_all.shape[0] // CHUNK):
        rows = slice(a * CHUNK, (a + 1) * CHUNK)
        d_mixed = d_all[rows, :]
        product = d_mixed[:, :width] * mixed_ref[rows, :]
        deltas = [jnp.sum(keep_head(product, h), axis=-1, keepdims=True) for h in range(heads)]
        stat = pack_columns(deltas, heads, lse_ref[rows, :])
        stat_ref[rows, :] = stat
        high = stat.astype(LOW).astype(F32)
        rest = stat - high
        lane = lax.broadcasted_iota(jnp.int32, (CHUNK, CHUNK), 1)
        skip = width % CHUNK
        high = pltpu.roll(high, skip, 1)
        rest = pltpu.roll(rest, skip + 2 * heads, 1)
        tail = jnp.where(lane < skip, d_mixed[:, width - skip : width - skip + CHUNK], high)
        tail = jnp.where(lane >= skip + 2 * heads, rest, tail)
        tail = jnp.where(lane >= skip + 4 * heads, 0.0, tail)
        payload_ref[rows, : width - skip] = d_mixed[:, : width - skip].astype(LOW)
        payload_ref[rows, width - skip :] = tail.astype(LOW)
    grad_ref[...] = dot_tn(mixed_low[...], branch_ref[...]).astype(LOW)


def bend(scores_ref, products_ref, probs_ref, ds_ref, h, bias, first, lse_of, delta_of, seg_col, seg_row, fold_ref):
    window = scores_ref.shape[1]
    steps = window // CHUNK
    for a in range(steps):
        rows = slice(a * CHUNK, (a + 1) * CHUNK)
        scores = scores_ref[h, rows, :] + bias[h, :, pl.ds(first - a * CHUNK, window)]
        if seg_col is not None:
            scores = jnp.where(seg_col[rows, 0:1] == seg_row[...], scores, NEG)
        weights = jnp.exp(scores - lse_of(rows))
        d_scores = weights * (products_ref[h, rows, :] - delta_of(rows))
        ds_ref[h, rows, :] = d_scores.astype(LOW)
        if probs_ref is not None:
            probs_ref[h, rows, :] = weights.astype(LOW)
        if fold_ref is not None:
            at = (steps - a) * CHUNK
            if a == 0:
                fold_ref[h, :, :at] = jnp.zeros((CHUNK, at), F32)
                fold_ref[h, :, at:] = d_scores
            else:
                if a == steps - 1:
                    fold_ref[h, :, :CHUNK] = jnp.zeros((CHUNK, CHUNK), F32)
                fold_ref[h, :, at : at + window] += d_scores


def table_sums(fold_ref, bucket_ref, start, table_ref):
    heads, buckets = table_ref.shape
    reach = fold_ref.shape[2]
    row = row_of(bucket_ref, start // CHUNK, reach // CHUNK)
    onehot = row == lax.broadcasted_iota(jnp.int32, (buckets, reach), 0)
    columns = []
    for h in range(heads):
        folded = fold_diagonals(fold_ref[h])
        columns.append(jnp.sum(jnp.where(onehot, folded, 0.0), axis=1, keepdims=True))
    return pack_columns(columns).T[:heads, :]


def own_back_kernel(
    q_ref,
    k_ref,
    v_ref,
    payload_ref,
    stat_ref,
    bias_t,
    seg_col,
    seg_row,
    flipped_ref,
    dq_ref,
    dk_ref,
    dv_ref,
    table_ref,
    scores_ref,
    products_ref,
    probs_ref,
    ds_ref,
    fold_ref,
):
    window, width = q_ref.shape
    heads = width // HEAD
    queries, keys, values = q_ref[...], k_ref[...], v_ref[...]
    back = payload_ref[:, :width]
    stat = stat_ref[...].T
    for h in range(heads):
        scores_ref[h] = dot_nt(keep_head(keys, h), queries)
        products_ref[h] = dot_nt(keep_head(values, h), back)
    for h in range(heads):
        lse, delta = stat[h : h + 1, :], stat[heads + h : heads + h + 1, :]
        bend(
            scores_ref,
            products_ref,
            probs_ref,
            ds_ref,
            h,
            bias_t,
            SPAN // 2,
            lambda rows: lse,
            lambda rows: delta,
            seg_col,
            seg_row,
            fold_ref,
        )
    d_queries = dot_tn(ds_ref[0], keep_head(keys, 0))
    d_keys = dot_nn(ds_ref[0], keep_head(queries, 0))
    d_values = dot_nn(probs_ref[0], keep_head(back, 0))
    for h in range(1, heads):
        d_queries = d_queries + dot_tn(ds_ref[h], keep_head(keys, h))
        d_keys = d_keys + dot_nn(ds_ref[h], keep_head(queries, h))
        d_values = d_values + dot_nn(probs_ref[h], keep_head(back, h))
    dq_ref[...] = d_queries
    dk_ref[...] = d_keys
    dv_ref[...] = d_values
    table_ref[...] = table_sums(fold_ref, flipped_ref, SPAN // 2 - window, table_ref)


def far_back_kernel(
    info,
    q_ref,
    kp_ref,
    vp_ref,
    payload_ref,
    stat_ref,
    bias,
    bucket_ref,
    dq_in,
    table_in,
    dq_ref,
    table_ref,
    scores_ref,
    products_ref,
    ds_ref,
    fold_ref,
):
    window, width = q_ref.shape
    heads = width // HEAD

    @pl.when(info[3] == 1)
    def _():
        queries, keys, values = q_ref[...], kp_ref[...], vp_ref[...]
        back = payload_ref[:, :width]
        first = far_start(info, window)
        for h in range(heads):
            scores_ref[h] = dot_nt(keep_head(queries, h), keys)
            products_ref[h] = dot_nt(keep_head(back, h), values)
        for h in range(heads):
            bend(
                scores_ref,
                products_ref,
                None,
                ds_ref,
                h,
                bias,
                first,
                lambda rows: stat_ref[rows, h : h + 1],
                lambda rows: stat_ref[rows, heads + h : heads + h + 1],
                None,
                None,
                fold_ref,
            )
        d_queries = dq_in[...]
        for h in range(heads):
            d_queries = d_queries + dot_nn(ds_ref[h], keep_head(keys, h))
        dq_ref[...] = (d_queries * HEAD**-0.5).astype(LOW)
        table_ref[...] = table_in[...] + table_sums(fold_ref, bucket_ref, first - window, table_ref)

    @pl.when(info[3] == 0)
    def _():
        dq_ref[...] = (dq_in[...] * HEAD**-0.5).astype(LOW)
        table_ref[...] = table_in[...]


def partner_back_kernel(
    info,
    k_ref,
    v_ref,
    qp_ref,
    from_even,
    from_odd,
    bias_t,
    dk_in,
    dv_in,
    dq_ref,
    normed_ref,
    x_all,
    gain,
    wq,
    wk,
    wv,
    grad_in,
    gain_in,
    one_send,
    one_keep,
    two_send,
    two_keep,
    send_ref,
    keep_ref,
    small_ref,
    d_all,
    scores_ref,
    products_ref,
    probs_ref,
    ds_ref,
):
    window, width = k_ref.shape
    heads = width // HEAD
    y, c = info[0], info[1]
    d_all[:, :width] = dq_ref[...]

    @pl.when(info[3] == 1)
    def _():
        payload = jnp.where(info[6] == 1, from_even[...], from_odd[...])
        queries, keys, values = qp_ref[...], k_ref[...], v_ref[...]
        back = payload[:, :width]
        columns = payload[:, payload.shape[1] - CHUNK :].astype(F32).T
        skip = width % CHUNK
        first = far_start(info, window)
        for h in range(heads):
            scores_ref[h] = dot_nt(keep_head(keys, h), queries)
            products_ref[h] = dot_nt(keep_head(values, h), back)
        for h in range(heads):
            at = skip + h
            lse = columns[at : at + 1, :] + columns[at + 2 * heads : at + 2 * heads + 1, :]
            at = at + heads
            delta = columns[at : at + 1, :] + columns[at + 2 * heads : at + 2 * heads + 1, :]
            bend(
                scores_ref,
                products_ref,
                probs_ref,
                ds_ref,
                h,
                bias_t,
                first,
                lambda rows: lse,
                lambda rows: delta,
                None,
                None,
                None,
            )
        d_keys, d_values = dk_in[...], dv_in[...]
        for h in range(heads):
            d_keys = d_keys + dot_nn(ds_ref[h], keep_head(queries, h))
            d_values = d_values + dot_nn(probs_ref[h], keep_head(back, h))
        d_all[:, width : 2 * width] = d_keys.astype(LOW)
        d_all[:, 2 * width :] = d_values.astype(LOW)

    @pl.when(info[3] == 0)
    def _():
        d_all[:, width : 2 * width] = dk_in[...].astype(LOW)
        d_all[:, 2 * width :] = dv_in[...].astype(LOW)

    joint = dot_tn(d_all[...], normed_ref[...]).astype(LOW)
    halves = (joint[:width, :], joint[width : 2 * width, :])
    for side in (0, 1):

        @pl.when(info[4] == side)
        def _():
            one_keep[...] = halves[side]
            one_send[...] = halves[1 - side]

    halves_two = (joint[2 * width :, :], grad_in[...])
    for side in (0, 1):

        @pl.when(info[5] == side)
        def _():
            two_keep[...] = halves_two[side]
            two_send[...] = halves_two[1 - side]

    gain_sum = jnp.zeros((1, gain.shape[1]), F32)
    for part, core in enumerate((1 - c, c)):
        spots = (aligned((2 * y + core) * CHUNK), aligned((2 * (1 - y) + core) * CHUNK))
        mine = jnp.concatenate([d_all[spots[0], :], d_all[spots[1], :]], axis=0)
        d_normed = dot_nn(mine[:, :width], wq[...])
        d_normed = d_normed + dot_nn(mine[:, width : 2 * width], wk[...])
        d_normed = d_normed + dot_nn(mine[:, 2 * width :], wv[...])
        wide = jnp.concatenate([x_all[spots[0], :], x_all[spots[1], :]], axis=0).astype(F32)
        gain_sum = gain_sum + jnp.sum(d_normed * (wide * rows_norm(wide)), axis=0, keepdims=True)
        if part == 0:
            send_ref[: 2 * CHUNK, :] = d_normed.astype(LOW)
        else:
            keep_ref[...] = d_normed
    small = jnp.concatenate([gain_sum, gain_in[...], jnp.zeros((6, gain_sum.shape[1]), F32)], axis=0)
    small_ref[...] = small
    put_small(send_ref, 2 * CHUNK, small)


def put_small(target, start, small):
    high = small.astype(LOW).astype(F32)
    target[start : start + EXTRA, :] = jnp.concatenate([high, small - high], axis=0).astype(LOW)


def get_small(source, start):
    both = source[start : start + EXTRA, :].astype(F32)
    return both[: EXTRA // 2] + both[EXTRA // 2 :]


def first_merge_kernel(keep_ref, got_ref, small_in, send_ref, own_ref, small_ref):
    local = own_ref.shape[0]
    total = (keep_ref[...] + got_ref[: 2 * local, :].astype(F32)).astype(LOW)
    own_ref[...] = total[:local, :]
    send_ref[:local, :] = total[local:, :]
    small = small_in[...] + get_small(got_ref, 2 * local)
    small_ref[...] = small
    put_small(send_ref, local, small)


def input_back_kernel(own_ref, got_ref, x_ref, dh_ref, gain, small_in, table_ref, out_ref, small_ref):
    local = own_ref.shape[0]
    d_normed = own_ref[...].astype(F32) + got_ref[:local, :].astype(F32)
    wide = x_ref[...].astype(F32)
    inverse = rows_norm(wide)
    unit = wide * inverse
    scaled = d_normed * gain[...]
    back = inverse * (scaled - unit * jnp.mean(unit * scaled, axis=-1, keepdims=True))
    out_ref[...] = (dh_ref[...] + back).astype(LOW)
    small_ref[...] = small_in[...] + get_small(got_ref, local)
    heads, buckets = table_ref.shape
    small_ref[2 : 2 + heads, :buckets] = table_ref[...]


def halve_kernel(info, *refs, bits):
    count = len(bits)
    for k, bit in enumerate(bits):
        keep, got = refs[2 * k], refs[2 * k + 1]
        send_ref, keep_ref = refs[2 * count + 2 * k], refs[2 * count + 2 * k + 1]
        half = send_ref.shape[0]
        side = (info[7] >> bit) & 1
        for first, target in ((1 - side, send_ref), (side, keep_ref)):
            rows = pl.ds(pl.multiple_of(first * half, 16), half)
            target[...] = (keep[rows, :].astype(F32) + got[rows, :].astype(F32)).astype(LOW)


def sum_kernel(*refs, count, small):
    for k in range(count):
        keep, got = refs[2 * k], refs[2 * k + 1]
        target = refs[2 * count + small + k]
        rows = keep.shape[0]
        target[:rows, :] = (keep[...].astype(F32) + got[...].astype(F32)).astype(LOW)
        if small and k == 0:
            put_small(target, rows, refs[2 * count][...])


def double_kernel(info, *refs, bits, small):
    count = len(bits)
    for k, bit in enumerate(bits):
        mine, got, target = refs[2 * k], refs[2 * k + 1], refs[2 * count + k]
        extra = EXTRA if small and k == 0 else 0
        rows = mine.shape[0] - extra
        side = (info[7] >> bit) & 1
        target[pl.ds(pl.multiple_of(side * rows, 16), rows), :] = mine[:rows, :]
        target[pl.ds(pl.multiple_of((1 - side) * rows, 16), rows), :] = got[:rows, :]
        if extra:
            put_small(target, 2 * rows, get_small(mine, rows) + get_small(got, rows))


def attention_total_kernel(info, one, one_got, two, two_got, q_ref, k_ref, v_ref, out_ref, small_ref):
    rows = q_ref.shape[0]
    first = info[4] == 0
    mine, got = one[:rows, :], one_got[:rows, :]
    q_ref[...] = jnp.where(first, mine, got).astype(F32)
    k_ref[...] = jnp.where(first, got, mine).astype(F32)
    first = info[5] == 0
    v_ref[...] = jnp.where(first, two[...], two_got[...]).astype(F32)
    out_ref[...] = jnp.where(first, two_got[...], two[...]).astype(F32)
    if one.shape[0] > rows:
        small_ref[...] = get_small(one, rows) + get_small(one_got, rows)
    else:
        small_ref[...] = jnp.zeros_like(small_ref)


def swap(values, axis, bit):
    return lax.ppermute(values, axis, [(i, i ^ bit) for i in range(lax.axis_size(axis))])


def swap_odd(values):
    ends = range(1, lax.axis_size("dp") - 1, 2)
    return lax.ppermute(values, "dp", [(i, i + 1) for i in ends] + [(i + 1, i) for i in ends])


def after(values, *others):
    return lax.optimization_barrier((values, *others))[0]


def spread(own, across=None):
    across = swap(own, "mp", 2) if across is None else across
    return own, across, swap(own, "mp", 1), swap(across, "mp", 1)


def cut(values, first, count):
    return lax.dynamic_slice_in_dim(values, first, count)


class Sums:
    def __init__(self, info, rank, orders, sends, keeps):
        self.info, self.rank, self.orders, self.keeps = info, rank, orders, list(keeps)
        self.bits = len(orders[0])
        self.tiled = all((k.shape[0] >> (self.bits - 1)) % 16 == 0 for k in keeps)
        self.step, self.small = 0, None
        self.exchange(sends)

    def exchange(self, sends):
        done = self.step if self.step < self.bits else 2 * self.bits - 1 - self.step
        self.now = [order[done] for order in self.orders]
        self.gots = [swap(v, "dp", 1 << bit) for v, bit in zip(sends, self.now)]
        self.step += 1

    def pairs(self):
        return [v for pair in zip(self.keeps, self.gots) for v in pair]

    def advance(self, token, small=None):
        self.keeps[0] = after(self.keeps[0], token)
        count = len(self.keeps)
        if self.step < self.bits:
            bits = [order[self.step] for order in self.orders]
            halves = [v.shape[0] // 2 for v in self.keeps]
            if self.tiled:
                out = call(
                    functools.partial(halve_kernel, bits=bits),
                    [shape((h, v.shape[1]), LOW) for h, v in zip(halves, self.keeps) for _ in range(2)],
                    [self.info, *self.pairs()],
                    micros=1.0,
                )
                sends, self.keeps = out[0::2], list(out[1::2])
            else:
                sends, keeps = [], []
                for k, g, h, bit in zip(self.keeps, self.gots, halves, bits):
                    side = (self.rank >> bit) & 1
                    total = (k.astype(F32) + g.astype(F32)).astype(LOW)
                    sends.append(cut(total, (1 - side) * h, h))
                    keeps.append(cut(total, side * h, h))
                self.keeps = keeps
        elif self.step == self.bits:
            if self.tiled:
                self.small = small
                rows = [v.shape[0] for v in self.keeps]
                if small is not None:
                    rows[0] += EXTRA
                sends = call(
                    functools.partial(sum_kernel, count=count, small=int(small is not None)),
                    [shape((r, v.shape[1]), LOW) for r, v in zip(rows, self.keeps)],
                    self.pairs() + ([small] if small is not None else []),
                    smem=0,
                    micros=1.0,
                )
            else:
                sends = [(k.astype(F32) + g.astype(F32)).astype(LOW) for k, g in zip(self.keeps, self.gots)]
            self.keeps = list(sends)
        else:
            has = self.small is not None
            if self.tiled:
                rows = [2 * v.shape[0] for v in self.keeps]
                if has:
                    rows[0] -= EXTRA
                sends = call(
                    functools.partial(double_kernel, bits=self.now, small=has),
                    [shape((r, v.shape[1]), LOW) for r, v in zip(rows, self.keeps)],
                    [self.info, *self.pairs()],
                    micros=1.0,
                )
            else:
                sends = []
                for k, g, bit in zip(self.keeps, self.gots, self.now):
                    side = (self.rank >> bit) & 1
                    sends.append(
                        jnp.where(side == 0, jnp.concatenate([k, g], axis=0), jnp.concatenate([g, k], axis=0))
                    )
            self.keeps = list(sends)
        self.exchange(sends)
        return sends[0]


def per_device(
    inputs,
    attention_gain,
    query_weight,
    key_weight,
    value_weight,
    out_weight,
    bias_table,
    feedforward_gain,
    gate_weight,
    up_weight,
    down_weight,
    segment,
    bucket,
    cotangent,
):
    parts = lax.axis_size("mp")
    groups = lax.axis_size("dp")
    local, d = inputs.shape
    window = local * parts
    width = query_weight.shape[1]
    heads = width // HEAD
    units = gate_weight.shape[1]
    buckets = bias_table.shape[0]
    half = 2 * local
    rank = lax.axis_index("dp")
    member = lax.axis_index("mp")
    bits = list(range(groups.bit_length() - 1))
    order_one = bits
    order_two = [bits[1], bits[0]] + bits[2:]

    x_across = swap(inputs, "mp", 2)
    from_even = swap(inputs, "dp", 1)
    from_odd = swap_odd(inputs)

    spot = jnp.stack([rank, member]).astype(jnp.int32)
    edge = jnp.full((1,), -1, jnp.int32)
    bucket_rows = jnp.concatenate([edge, bucket]).reshape(-1, CHUNK)
    table = bias_table.T
    gain_one, gain_two = attention_gain[None, :], after(feedforward_gain[None, :], spot)
    band = shape((heads, CHUNK, SPAN), F32)
    info, seg_row, seg_col, bias = call(
        functools.partial(setup_kernel, groups=groups, first_bits=(order_one[0], order_two[0])),
        [shape((8,), jnp.int32), shape((1, window), F32), shape((window, CHUNK), F32), band],
        [spot, segment.reshape(-1, CHUNK), after(bucket_rows, gain_one, gain_two), table],
        out_smem=1,
        micros=3.0,
    )
    x_pieces = (inputs, x_across, swap(inputs, "mp", 1), swap(after(x_across, bias), "mp", 1))
    out_across = swap(out_weight, "mp", 2)
    (near,) = call(near_kernel, [shape((local, d), LOW)], [info, from_even, from_odd], micros=0.5)
    out_core = swap(after(out_across, near), "mp", 1)
    near_across = swap(near, "mp", 2)
    near_core = swap(near, "mp", 1)

    low_rows = shape((window, width), LOW)
    wide_rows = shape((window, width), F32)
    stats = shape((window, CHUNK), F32)
    square_wide = pltpu.VMEM((heads, window, window), F32)
    square_low = pltpu.VMEM((heads, window, window), LOW)
    weight = shape((width, d), LOW)
    x_all, normed, queries, keys, values, acc, top, total, wq, wk, wv = call(
        own_kernel,
        [shape((window, d), LOW)] * 2 + [low_rows] * 3 + [wide_rows, stats, stats] + [weight] * 3,
        [info, after(inputs, out_core), *x_pieces[1:], gain_one, bias, seg_col, seg_row, *[in_hbm(w.T) for w in (query_weight, key_weight, value_weight)]],
        scratch=[square_wide, square_low, pltpu.SemaphoreType.DMA((3,))],
        hbm=3,
        micros=5.0,
    )
    near_pieces = (near, near_across, near_core, swap(after(near_across, acc), "mp", 1))
    cot_across = swap(after(cotangent, near), "mp", 2)
    mixed_low, mixed, lse, queries_near, keys_near, values_near = call(
        partner_kernel,
        [low_rows, wide_rows, stats] + [low_rows] * 3,
        [info, *near_pieces, gain_one, wq, wk, wv, bias, queries, acc, top, total],
        scratch=[
            pltpu.VMEM((window, d), LOW),
            square_wide,
            square_low,
            pltpu.VMEM((window, width), F32),
            pltpu.VMEM((window, CHUNK), F32),
            pltpu.VMEM((window, CHUNK), F32),
        ],
        micros=5.0,
    )
    mixed_across = swap(mixed_low, "mp", 2)
    mixed_core = swap(mixed_low, "mp", 1)
    out_pieces = (out_weight, out_across, swap(after(out_weight, mixed_core), "mp", 1), out_core)
    cot_pieces = (
        cotangent,
        cot_across,
        swap(after(cotangent, mixed_core), "mp", 1),
        swap(after(cot_across, mixed_core), "mp", 1),
    )
    bias_t, flipped_rows = call(
        flipped_kernel,
        [band, shape(bucket_rows.shape, jnp.int32)],
        [after(bucket_rows, mixed_low), table],
        smem=0,
        micros=3.0,
    )
    cot_all, d_act = call(
        cotangent_kernel,
        [shape((window, d), LOW), shape((window, units), F32)],
        [*cot_pieces, after(down_weight, mixed_low)],
        smem=0,
        micros=1.0,
    )
    mixed_pieces = (mixed_low, mixed_across, mixed_core, swap(after(mixed_across, bias_t, d_act), "mp", 1))
    second, hidden, act, d_gate, d_up, second_send, second_keep, gain_two_part = call(
        feed_kernel,
        [shape((window, d), LOW), shape((half, d), F32)]
        + [shape((window, units), LOW)] * 3
        + [shape((half, d), LOW), shape((half, d), F32), shape((1, d), F32)],
        [info, x_all, *mixed_pieces, *out_pieces, d_act, gain_two, gate_weight, up_weight],
        micros=5.0,
    )
    (second_sum,) = call(
        functools.partial(sum_kernel, count=1, small=0),
        [shape((half, d), LOW)],
        [second_keep, swap(second_send, "mp", 1)],
        smem=0,
        micros=1.0,
    )
    second_other = swap(second_sum, "mp", 2)
    rows = d + units // 2 + units // 4
    gate_send, gate_keep, up_send, up_keep = call(
        feed_grad_kernel,
        [shape((rows // 2, units), LOW)] * 4,
        [info, after(second, second_sum), d_gate, d_up, act, cot_all],
        scratch=[pltpu.VMEM((rows, units), LOW)] * 2,
        micros=3.0,
    )
    feed_sums = Sums(info, rank, (order_one, order_two), (gate_send, up_send), (gate_keep, up_keep))
    feed_send, feed_keep = call(
        feed_out_kernel, [shape((half, d), LOW)] * 2, [after(act, gate_send), down_weight], smem=0
    )
    feed_own, feed_cross = call(
        feed_merge_kernel,
        [shape((local, d), LOW)] * 2,
        [feed_keep, swap(feed_send, "mp", 1)],
        smem=0,
        micros=1.0,
    )
    second_other = after(second_other, feed_cross)
    dh, branch_low = call(
        hidden_back_kernel,
        [shape((local, d), F32), shape((half, d), LOW)],
        [second_sum, second_other, hidden, cot_pieces[0], cot_pieces[1], gain_two],
        smem=0,
    )
    payload, stat_back, out_grad = call(
        mixed_back_kernel,
        [shape((window, 2 * CHUNK), LOW), stats, shape((width, d), LOW)],
        [info, branch_low, swap(branch_low, "mp", 1), out_weight, mixed, mixed_low, lse],
        scratch=[pltpu.VMEM((window, d), LOW), pltpu.VMEM((2 * CHUNK, d), LOW)],
    )
    payload_even = swap(payload, "dp", 1)
    payload_odd = swap_odd(payload)
    token = feed_sums.advance(payload)
    fold = pltpu.VMEM((heads, CHUNK, 2 * window), F32)
    d_queries, d_keys, d_values, table_part = call(
        own_back_kernel,
        [wide_rows, wide_rows, wide_rows, shape((heads, CHUNK), F32)],
        [after(queries, token), keys, values, payload, stat_back, bias_t, seg_col, seg_row, flipped_rows],
        scratch=[square_wide, square_wide, square_low, square_low, fold],
        smem=0,
        micros=200.0,
    )
    d_queries, table_part = call(
        far_back_kernel,
        [low_rows, shape((heads, CHUNK), F32)],
        [info, queries, keys_near, values_near, payload, stat_back, bias, bucket_rows, d_queries, table_part],
        scratch=[square_wide, square_wide, square_low, fold],
        micros=3.0,
    )
    one_send, one_keep, two_send, two_keep, first_send, first_keep, small = call(
        partner_back_kernel,
        [shape((width, d), LOW)] * 4
        + [shape((half + EXTRA, d), LOW), shape((half, d), F32), shape((EXTRA // 2, d), F32)],
        [
            info,
            keys,
            values,
            queries_near,
            payload_even,
            payload_odd,
            bias_t,
            d_keys,
            d_values,
            d_queries,
            normed,
            x_all,
            gain_one,
            wq,
            wk,
            wv,
            out_grad,
            gain_two_part,
        ],
        scratch=[pltpu.VMEM((window, 3 * width), LOW), square_wide, square_wide, square_low, square_low],
        micros=300.0,
    )
    joint_sums = Sums(info, rank, (order_one, order_two), (one_send, two_send), (one_keep, two_keep))
    token = feed_sums.advance(one_send)
    first_send, first_own, small = call(
        first_merge_kernel,
        [shape((local + EXTRA, d), LOW), shape((local, d), LOW), shape((EXTRA // 2, d), F32)],
        [after(first_keep, token), swap(first_send, "mp", 1), small],
        smem=0,
        micros=1.0,
    )
    first_got = swap(first_send, "mp", 2)
    token = joint_sums.advance(first_send)
    token = feed_sums.advance(token)
    feed_got = swap(after(feed_cross, token), "mp", 2)
    input_grad, small = call(
        input_back_kernel,
        [shape((local, d), LOW), shape((EXTRA // 2, d), F32)],
        [first_own, first_got, inputs, after(dh, token), gain_one, small, table_part],
        smem=0,
        micros=1.0,
    )
    last = 2 * len(bits)
    while joint_sums.step < last - 1 or feed_sums.step < last:
        if joint_sums.step < last - 1:
            token = joint_sums.advance(token, small)
        if feed_sums.step < last:
            token = feed_sums.advance(token)
    (layer_out,) = call(
        layer_out_kernel,
        [shape((local, d), LOW)],
        [after(hidden, small), feed_own, feed_got],
        smem=0,
        micros=1.0,
    )
    ready = feed_sums.pairs()
    gate_grad, up_grad, down_grad = call(
        feed_total_kernel,
        [shape((d, units), F32)] * 2 + [shape((units, d), F32)],
        [info, after(ready[0], token), *ready[1:]],
        scratch=[pltpu.VMEM((rows, units), LOW)],
        micros=2.0,
    )
    joint_sums.advance(down_grad)
    query_grad, key_grad, value_grad, out_total, small_total = call(
        attention_total_kernel,
        [shape((width, d), F32)] * 4 + [shape((EXTRA // 2, d), F32)],
        [info, *joint_sums.pairs()],
        micros=2.0,
    )
    if not joint_sums.tiled:
        small_total = lax.psum(small, "dp")
    return (
        layer_out,
        input_grad,
        small_total[0],
        query_grad.T,
        key_grad.T,
        value_grad.T,
        out_total,
        small_total[2 : 2 + heads, :buckets].T,
        small_total[1],
        gate_grad,
        up_grad,
        down_grad,
    )


def solution(mesh):
    rows = P(("dp", "mp"), None)
    in_specs = (
        rows,
        P(),
        P(None, "mp"),
        P(None, "mp"),
        P(None, "mp"),
        P("mp", None),
        P(None, "mp"),
        P(),
        P(None, "mp"),
        P(None, "mp"),
        P("mp", None),
        P(),
        P(),
        rows,
    )
    out_specs = (
        rows,
        rows,
        P(),
        P(None, "mp"),
        P(None, "mp"),
        P(None, "mp"),
        P("mp", None),
        P(None, "mp"),
        P(),
        P(None, "mp"),
        P(None, "mp"),
        P("mp", None),
    )
    return jax.shard_map(
        per_device, mesh=mesh, in_specs=in_specs, out_specs=out_specs, check_vma=False
    )
```

```python
import functools

import jax
import jax.numpy as jnp
from jax import lax
from jax.experimental import pallas as pl
from jax.experimental.pallas import tpu as pltpu
from jax.sharding import PartitionSpec as P

HEAD = 64
LOW = jnp.bfloat16
F32 = jnp.float32
CHUNK = 128
SPAN = 2048
EXTRA = 16
NEG = -1e30
ROOT = 0.7978845608
CUBE = 0.044715
VMEM = pl.BlockSpec(memory_space=pltpu.VMEM)
SMEM = pl.BlockSpec(memory_space=pltpu.SMEM)
HBM = pl.BlockSpec(memory_space=pltpu.HBM)


def dot_nn(a, b):
    return lax.dot_general(a, b, (((1,), (0,)), ((), ())), preferred_element_type=F32)


def dot_nt(a, b):
    return lax.dot_general(a, b, (((1,), (1,)), ((), ())), preferred_element_type=F32)


def dot_tn(a, b):
    return lax.dot_general(a, b, (((0,), (0,)), ((), ())), preferred_element_type=F32)


def call(kernel, outs, ins, scratch=(), smem=1, hbm=0, micros=2.0, out_smem=0, limit=20):
    return pl.pallas_call(
        kernel,
        out_shape=outs,
        in_specs=[SMEM] * smem + [VMEM] * (len(ins) - smem - hbm) + [HBM] * hbm,
        out_specs=[SMEM] * out_smem + [VMEM] * (len(outs) - out_smem),
        scratch_shapes=list(scratch),
        cost_estimate=pl.CostEstimate(flops=int(micros * 2e7), bytes_accessed=0, transcendentals=0),
        compiler_params=pltpu.CompilerParams(vmem_limit_bytes=limit * 1024 * 1024),
    )(*ins)


def in_hbm(values):
    return pltpu.with_memory_space_constraint(values, pltpu.HBM)


def shape(dims, dtype):
    return jax.ShapeDtypeStruct(dims, dtype)


def head_lanes(width, h):
    lane = lax.broadcasted_iota(jnp.int32, (1, width), 1)
    return (lane >= h * HEAD) & (lane < (h + 1) * HEAD)


def keep_head(values, h):
    return jnp.where(head_lanes(values.shape[-1], h), values, jnp.zeros_like(values))


def rows_norm(values):
    return lax.rsqrt(jnp.mean(values * values, axis=-1, keepdims=True) + 1e-06)


def as_row(ref):
    return jnp.concatenate([ref[k : k + 1, :] for k in range(ref.shape[0])], axis=1)


def aligned(start):
    return pl.ds(pl.multiple_of(start, CHUNK), CHUNK)


def lay_bias(row, table_ref, target):
    heads, buckets = table_ref.shape
    which = lax.broadcasted_iota(jnp.int32, (buckets, SPAN), 0)
    onehot = (row == which).astype(F32)
    table = table_ref[...].T
    for h in range(heads):
        rows = jnp.sum(onehot * table[:, h : h + 1], axis=0, keepdims=True)
        count = 1
        while count < 8:
            rows = jnp.concatenate([rows, pltpu.roll(rows, count, 1)], axis=0)
            count *= 2
        target[h, 0:8, :] = rows
        while count < CHUNK:
            target[h, count : 2 * count, :] = pltpu.roll(target[h, 0:count, :], count, 1)
            count *= 2


def setup_kernel(spot, segment_ref, bucket_ref, table_ref, info, row_ref, col_ref, bias_ref, *, groups, first_bits):
    rank, member = spot[0], spot[1]
    steps = row_ref.shape[1] // CHUNK
    rows = [segment_ref[pl.ds(rank * steps + k, 1), :] for k in range(steps)]
    lane = lax.broadcasted_iota(jnp.int32, (1, CHUNK), 1)

    def value(row, at):
        return jnp.max(jnp.where(lane == at, row, -1))

    before = segment_ref[pl.ds(jnp.maximum(rank * steps - 1, 0), 1), :]
    later = segment_ref[pl.ds(jnp.minimum((rank + 1) * steps, groups * steps - 1), 1), :]
    left = (value(before, CHUNK - 1) == value(rows[0], 0)) & (rank > 0)
    right = (value(later, 0) == value(rows[-1], CHUNK - 1)) & (rank < groups - 1)
    even = jnp.where(rank % 2 == 0, right.astype(jnp.int32), left.astype(jnp.int32))
    info[0] = member // 2
    info[1] = member % 2
    info[2] = left.astype(jnp.int32)
    info[3] = (left | right).astype(jnp.int32)
    info[4] = (rank >> first_bits[0]) & 1
    info[5] = (rank >> first_bits[1]) & 1
    info[6] = even
    info[7] = rank
    row = jnp.concatenate(rows, axis=1).astype(F32)
    row_ref[...] = row
    col_ref[...] = jnp.broadcast_to(row, (CHUNK, row.shape[1])).T
    lay_bias(row_of(bucket_ref, 0, bucket_ref.shape[0]), table_ref, bias_ref)


def row_of(ref, first, count):
    return jnp.concatenate([ref[pl.ds(first + k, 1), :] for k in range(count)], axis=1)


def flipped_kernel(bucket_ref, table_ref, bias_ref, flipped_ref):
    count = bucket_ref.shape[0]
    sub = lax.broadcasted_iota(jnp.int32, (CHUNK, CHUNK), 0)
    lane = lax.broadcasted_iota(jnp.int32, (CHUNK, CHUNK), 1)
    turned = dot_nn(bucket_ref[...].astype(F32).astype(LOW), (sub + lane == CHUNK - 1).astype(F32).astype(LOW))
    row = jnp.concatenate([turned[k : k + 1, :] for k in reversed(range(count))], axis=1)
    row = pltpu.roll(row, 1, 1).astype(jnp.int32)
    flipped_ref[...] = jnp.concatenate([row[:, k * CHUNK : (k + 1) * CHUNK] for k in range(count)], axis=0)
    lay_bias(row, table_ref, bias_ref)


def near_kernel(info, even_ref, odd_ref, out_ref):
    out_ref[...] = jnp.where(info[6] == 1, even_ref[...], odd_ref[...])


def fold_diagonals(tile):
    rows, cols = tile.shape
    while rows > 1:
        rows //= 2
        tile = tile[:rows] + pltpu.roll(tile[rows:], cols - rows, 1)
    return tile


def pack_columns(columns, offset=0, base=None, width=CHUNK):
    rows = columns[0].shape[0]
    lane = lax.broadcasted_iota(jnp.int32, (rows, width), 1)
    out = jnp.zeros((rows, width), F32) if base is None else base
    for k, column in enumerate(columns):
        out = jnp.where(lane == offset + k, column, out)
    return out


def by_head(packed, width):
    lane = lax.broadcasted_iota(jnp.int32, (packed.shape[0], width), 1)
    out = packed[:, 0:1]
    for h in range(1, width // HEAD):
        out = jnp.where(lane >= h * HEAD, packed[:, h : h + 1], out)
    return out


def place(y, c):
    return (2 * y + c, 2 * (1 - y) + c, 2 * y + 1 - c, 2 * (1 - y) + 1 - c)


def project(normed, rows, wq, wk, wv, q_ref, k_ref, v_ref):
    q_ref[rows, :] = (dot_nt(normed, wq[...]).astype(LOW).astype(F32) * HEAD**-0.5).astype(LOW)
    k_ref[rows, :] = dot_nt(normed, wk[...]).astype(LOW)
    v_ref[rows, :] = dot_nt(normed, wv[...]).astype(LOW)


def attend(q, keys, values, bias, first, seg_col, seg_row, scores_ref, probs_ref, acc_ref, top_ref, sum_ref):
    window, width = q.shape
    heads = width // HEAD
    for h in range(heads):
        scores_ref[h] = dot_nt(keep_head(q, h), keys)
    for h in range(heads):
        for a in range(window // CHUNK):
            rows = slice(a * CHUNK, (a + 1) * CHUNK)
            scores = scores_ref[h, rows, :] + bias[h, :, pl.ds(first - a * CHUNK, window)]
            if seg_col is not None:
                scores = jnp.where(seg_col[rows, 0:1] == seg_row[...], scores, NEG)
            top = jnp.max(scores, axis=-1, keepdims=True)
            weights = jnp.exp(scores - top)
            probs_ref[h, rows, :] = weights.astype(LOW)
            top_ref[rows, :] = pack_columns([top], h, top_ref[rows, :] if h else jnp.zeros((CHUNK, CHUNK), F32))
            total = jnp.sum(weights, axis=-1, keepdims=True)
            sum_ref[rows, :] = pack_columns([total], h, sum_ref[rows, :] if h else jnp.ones((CHUNK, CHUNK), F32))
    total = dot_nn(probs_ref[0], keep_head(values, 0))
    for h in range(1, heads):
        total = total + dot_nn(probs_ref[h], keep_head(values, h))
    acc_ref[...] = total


def own_kernel(
    info,
    x0,
    x1,
    x2,
    x3,
    gain,
    bias,
    seg_col,
    seg_row,
    wq_hbm,
    wk_hbm,
    wv_hbm,
    x_all,
    normed_ref,
    q_ref,
    k_ref,
    v_ref,
    acc_ref,
    top_ref,
    sum_ref,
    wq,
    wk,
    wv,
    scores_ref,
    probs_ref,
    sems,
):
    pairs = ((wq_hbm, wq), (wk_hbm, wk), (wv_hbm, wv))
    copies = [pltpu.make_async_copy(a, b, sems.at[k]) for k, (a, b) in enumerate(pairs)]
    for copy in copies:
        copy.start()
    for piece, spot in zip((x0, x1, x2, x3), place(info[0], info[1])):
        rows = aligned(spot * CHUNK)
        low = piece[...]
        x_all[rows, :] = low
        wide = low.astype(F32)
        normed_ref[rows, :] = (wide * rows_norm(wide) * as_row(gain)).astype(LOW)
    for copy in copies:
        copy.wait()
    project(normed_ref[...], slice(None), wq, wk, wv, q_ref, k_ref, v_ref)
    attend(
        q_ref[...],
        k_ref[...],
        v_ref[...],
        bias,
        SPAN // 2,
        seg_col,
        seg_row,
        scores_ref,
        probs_ref,
        acc_ref,
        top_ref,
        sum_ref,
    )


def far_start(info, window):
    return pl.multiple_of(jnp.where(info[2] == 1, SPAN // 2 - window, SPAN // 2 + window), CHUNK)


def partner_kernel(
    info,
    x0,
    x1,
    x2,
    x3,
    gain,
    wq,
    wk,
    wv,
    bias,
    q_ref,
    acc_ref,
    top_ref,
    sum_ref,
    mixed_low,
    mixed_ref,
    lse_ref,
    qp_ref,
    kp_ref,
    vp_ref,
    normed_ref,
    scores_ref,
    probs_ref,
    acc_two,
    top_two,
    sum_two,
):
    window, width = q_ref.shape
    paired = info[3]

    @pl.when(paired == 1)
    def _():
        for piece, spot in zip((x0, x1, x2, x3), place(info[0], info[1])):
            wide = piece[...].astype(F32)
            normed_ref[aligned(spot * CHUNK), :] = (wide * rows_norm(wide) * as_row(gain)).astype(LOW)
        project(normed_ref[...], slice(None), wq, wk, wv, qp_ref, kp_ref, vp_ref)
        attend(
            q_ref[...],
            kp_ref[...],
            vp_ref[...],
            bias,
            far_start(info, window),
            None,
            None,
            scores_ref,
            probs_ref,
            acc_two,
            top_two,
            sum_two,
        )
        for a in range(window // CHUNK):
            rows = slice(a * CHUNK, (a + 1) * CHUNK)
            top = jnp.maximum(top_ref[rows, :], top_two[rows, :])
            one, two = jnp.exp(top_ref[rows, :] - top), jnp.exp(top_two[rows, :] - top)
            whole = sum_ref[rows, :] * one + sum_two[rows, :] * two
            inverse = 1.0 / whole
            mixed = acc_ref[rows, :] * by_head(one * inverse, width)
            mixed = mixed + acc_two[rows, :] * by_head(two * inverse, width)
            mixed_ref[rows, :] = mixed
            mixed_low[rows, :] = mixed.astype(LOW)
            lse_ref[rows, :] = top + jnp.log(whole)

    @pl.when(paired == 0)
    def _():
        qp_ref[...] = jnp.zeros_like(qp_ref)
        kp_ref[...] = jnp.zeros_like(kp_ref)
        vp_ref[...] = jnp.zeros_like(vp_ref)
        for a in range(window // CHUNK):
            rows = slice(a * CHUNK, (a + 1) * CHUNK)
            whole = sum_ref[rows, :]
            mixed = acc_ref[rows, :] * by_head(1.0 / whole, width)
            mixed_ref[rows, :] = mixed
            mixed_low[rows, :] = mixed.astype(LOW)
            lse_ref[rows, :] = top_ref[rows, :] + jnp.log(whole)


def cotangent_kernel(g0, g1, g2, g3, down_w, cot_ref, d_act_ref):
    for part, piece in enumerate((g2, g3, g0, g1)):
        cot_ref[part * CHUNK : (part + 1) * CHUNK, :] = piece[...]
    d_act_ref[...] = dot_nt(cot_ref[...], down_w[...])


def feed_kernel(
    info,
    x_all,
    m0,
    m1,
    m2,
    m3,
    o0,
    o1,
    o2,
    o3,
    d_act_ref,
    gain,
    gate_w,
    up_w,
    second_ref,
    hidden_ref,
    act_ref,
    dgate_ref,
    dup_ref,
    send_ref,
    keep_ref,
    gain_ref,
):
    y, c = info[0], info[1]
    half = 2 * CHUNK
    gain_sum = jnp.zeros((1, x_all.shape[1]), F32)
    for part, core in enumerate((1 - c, c)):
        rows = slice(part * half, (part + 1) * half)
        spots = (aligned((2 * y + core) * CHUNK), aligned((2 * (1 - y) + core) * CHUNK))

        def pick(ref):
            return jnp.concatenate([ref[spots[0], :], ref[spots[1], :]], axis=0)

        hidden = pick(x_all).astype(F32)
        branch = dot_nn(pick(m0), o0[...])
        for m, o in ((m1, o1), (m2, o2), (m3, o3)):
            branch = branch + dot_nn(pick(m), o[...])
        hidden = hidden + branch
        if part == 1:
            hidden_ref[...] = hidden
        unit = hidden * rows_norm(hidden)
        second = (unit * as_row(gain)).astype(LOW)
        second_ref[rows, :] = second
        gate = dot_nn(second, gate_w[...])
        up = dot_nn(second, up_w[...])
        d_act = d_act_ref[rows, :]
        square = gate * gate
        tanh = jnp.tanh(ROOT * gate * (1.0 + CUBE * square))
        low_half = 0.5 * (1.0 + tanh)
        gelu = gate * low_half
        slope = low_half + 0.5 * gate * (1.0 - tanh * tanh) * (ROOT * (1.0 + 3.0 * CUBE * square))
        act_ref[rows, :] = (gelu * up).astype(LOW)
        d_gate = (d_act * up * slope).astype(LOW)
        d_up = (d_act * gelu).astype(LOW)
        dgate_ref[rows, :] = d_gate
        dup_ref[rows, :] = d_up
        d_second = dot_nt(d_gate, gate_w[...]) + dot_nt(d_up, up_w[...])
        gain_sum = gain_sum + jnp.sum(d_second * unit, axis=0, keepdims=True)
        if part == 0:
            send_ref[...] = d_second.astype(LOW)
        else:
            keep_ref[...] = d_second
    gain_ref[...] = gain_sum


def feed_grad_kernel(
    info, second_ref, dgate_ref, dup_ref, act_ref, cot_ref, one_send, one_keep, two_send, two_keep, one_ref, two_ref
):
    d, units = second_ref.shape[1], dgate_ref.shape[1]
    one_ref[:d, :] = dot_tn(second_ref[...], dgate_ref[...]).astype(LOW)
    two_ref[:d, :] = dot_tn(second_ref[...], dup_ref[...]).astype(LOW)
    down = dot_tn(act_ref[...], cot_ref[...]).astype(LOW)
    half = units // 2
    quarter = half // 2
    for k, target in enumerate((one_ref, two_ref)):
        target[d : d + half, :] = down[k * half : (k + 1) * half, :units]
        for side in (0, 1):
            rows = slice(k * half + side * quarter, k * half + (side + 1) * quarter)
            target[d + half :, side * (units // 2) : (side + 1) * (units // 2)] = down[rows, units:]
    for source, side, send, keep in ((one_ref, info[4], one_send, one_keep), (two_ref, info[5], two_send, two_keep)):
        rows = send.shape[0]
        send[...] = source[pl.ds(pl.multiple_of((1 - side) * rows, 16), rows), :]
        keep[...] = source[pl.ds(pl.multiple_of(side * rows, 16), rows), :]


def feed_out_kernel(act_ref, down_w, send_ref, keep_ref):
    half = send_ref.shape[0]
    send_ref[...] = dot_nn(act_ref[:half, :], down_w[...]).astype(LOW)
    keep_ref[...] = dot_nn(act_ref[half:, :], down_w[...]).astype(LOW)


def feed_total_kernel(info, one, one_got, two, two_got, gate_ref, up_ref, down_ref, full_ref):
    d, units = gate_ref.shape
    half = units // 2
    quarter = half // 2
    parts = ((one, one_got, info[4], gate_ref), (two, two_got, info[5], up_ref))
    for k, (mine, got, side, target) in enumerate(parts):
        rows = mine.shape[0]
        full_ref[pl.ds(pl.multiple_of(side * rows, 16), rows), :] = mine[...]
        full_ref[pl.ds(pl.multiple_of((1 - side) * rows, 16), rows), :] = got[...]
        target[...] = full_ref[:d, :].astype(F32)
        down_ref[k * half : (k + 1) * half, :units] = full_ref[d : d + half, :].astype(F32)
        for part in (0, 1):
            rows = slice(k * half + part * quarter, k * half + (part + 1) * quarter)
            down_ref[rows, units:] = full_ref[d + half :, part * (units // 2) : (part + 1) * (units // 2)].astype(F32)


def feed_merge_kernel(keep_ref, got_ref, own_ref, send_ref):
    local = own_ref.shape[0]
    total = (keep_ref[...].astype(F32) + got_ref[...].astype(F32)).astype(LOW)
    own_ref[...] = total[:local, :]
    send_ref[...] = total[local:, :]


def layer_out_kernel(hidden_ref, own_ref, got_ref, out_ref):
    local = out_ref.shape[0]
    out_ref[...] = (hidden_ref[:local, :] + (own_ref[...].astype(F32) + got_ref[...].astype(F32))).astype(LOW)


def hidden_back_kernel(sum_ref, other_ref, hidden_ref, g0, g1, gain, dh_ref, low_ref):
    for part, cot in enumerate((g0, g1)):
        rows = slice(part * CHUNK, (part + 1) * CHUNK)
        flip = slice((1 - part) * CHUNK, (2 - part) * CHUNK)
        d_second = sum_ref[rows, :].astype(F32) + other_ref[flip, :].astype(F32)
        hidden = hidden_ref[rows, :]
        inverse = rows_norm(hidden)
        unit = hidden * inverse
        scaled = d_second * as_row(gain)
        dh = cot[...].astype(F32) + inverse * (scaled - unit * jnp.mean(unit * scaled, axis=-1, keepdims=True))
        low_ref[rows, :] = dh.astype(LOW)
        if part == 0:
            dh_ref[...] = dh


def mixed_back_kernel(
    info, pair_own, pair_other, out_w, mixed_ref, mixed_low, lse_ref, payload_ref, stat_ref, grad_ref, branch_ref, pad_ref
):
    width = mixed_ref.shape[1]
    heads = width // HEAD
    pieces = (pair_own[:CHUNK, :], pair_own[CHUNK:, :], pair_other[:CHUNK, :], pair_other[CHUNK:, :])
    for piece, spot in zip(pieces, place(info[0], info[1])):
        branch_ref[aligned(spot * CHUNK), :] = piece
    pad_ref[:width, :] = out_w[...]
    pad_ref[width:, :] = jnp.zeros((pad_ref.shape[0] - width, pad_ref.shape[1]), LOW)
    d_all = dot_nt(branch_ref[...], pad_ref[...]).astype(LOW).astype(F32)
    for a in range(d_all.shape[0] // CHUNK):
        rows = slice(a * CHUNK, (a + 1) * CHUNK)
        d_mixed = d_all[rows, :]
        product = d_mixed[:, :width] * mixed_ref[rows, :]
        deltas = [jnp.sum(keep_head(product, h), axis=-1, keepdims=True) for h in range(heads)]
        stat = pack_columns(deltas, heads, lse_ref[rows, :])
        stat_ref[rows, :] = stat
        high = stat.astype(LOW).astype(F32)
        rest = stat - high
        lane = lax.broadcasted_iota(jnp.int32, (CHUNK, CHUNK), 1)
        skip = width % CHUNK
        high = pltpu.roll(high, skip, 1)
        rest = pltpu.roll(rest, skip + 2 * heads, 1)
        tail = jnp.where(lane < skip, d_mixed[:, width - skip : width - skip + CHUNK], high)
        tail = jnp.where(lane >= skip + 2 * heads, rest, tail)
        tail = jnp.where(lane >= skip + 4 * heads, 0.0, tail)
        payload_ref[rows, : width - skip] = d_mixed[:, : width - skip].astype(LOW)
        payload_ref[rows, width - skip :] = tail.astype(LOW)
    grad_ref[...] = dot_tn(mixed_low[...], branch_ref[...]).astype(LOW)


def bend(scores_ref, products_ref, probs_ref, ds_ref, h, bias, first, lse_of, delta_of, seg_col, seg_row, fold_ref):
    window = scores_ref.shape[1]
    steps = window // CHUNK
    for a in range(steps):
        rows = slice(a * CHUNK, (a + 1) * CHUNK)
        scores = scores_ref[h, rows, :] + bias[h, :, pl.ds(first - a * CHUNK, window)]
        if seg_col is not None:
            scores = jnp.where(seg_col[rows, 0:1] == seg_row[...], scores, NEG)
        weights = jnp.exp(scores - lse_of(rows))
        d_scores = weights * (products_ref[h, rows, :] - delta_of(rows))
        ds_ref[h, rows, :] = d_scores.astype(LOW)
        if probs_ref is not None:
            probs_ref[h, rows, :] = weights.astype(LOW)
        if fold_ref is not None:
            at = (steps - a) * CHUNK
            if a == 0:
                fold_ref[h, :, :at] = jnp.zeros((CHUNK, at), F32)
                fold_ref[h, :, at:] = d_scores
            else:
                if a == steps - 1:
                    fold_ref[h, :, :CHUNK] = jnp.zeros((CHUNK, CHUNK), F32)
                fold_ref[h, :, at : at + window] += d_scores


def table_sums(fold_ref, bucket_ref, start, table_ref):
    heads, buckets = table_ref.shape
    reach = fold_ref.shape[2]
    row = row_of(bucket_ref, start // CHUNK, reach // CHUNK)
    onehot = row == lax.broadcasted_iota(jnp.int32, (buckets, reach), 0)
    columns = []
    for h in range(heads):
        folded = fold_diagonals(fold_ref[h])
        columns.append(jnp.sum(jnp.where(onehot, folded, 0.0), axis=1, keepdims=True))
    return pack_columns(columns).T[:heads, :]


def own_back_kernel(
    q_ref,
    k_ref,
    v_ref,
    payload_ref,
    stat_ref,
    bias_t,
    seg_col,
    seg_row,
    flipped_ref,
    dq_ref,
    dk_ref,
    dv_ref,
    table_ref,
    scores_ref,
    products_ref,
    probs_ref,
    ds_ref,
    fold_ref,
):
    window, width = q_ref.shape
    heads = width // HEAD
    queries, keys, values = q_ref[...], k_ref[...], v_ref[...]
    back = payload_ref[:, :width]
    stat = stat_ref[...].T
    for h in range(heads):
        scores_ref[h] = dot_nt(keep_head(keys, h), queries)
        products_ref[h] = dot_nt(keep_head(values, h), back)
    for h in range(heads):
        lse, delta = stat[h : h + 1, :], stat[heads + h : heads + h + 1, :]
        bend(
            scores_ref,
            products_ref,
            probs_ref,
            ds_ref,
            h,
            bias_t,
            SPAN // 2,
            lambda rows: lse,
            lambda rows: delta,
            seg_col,
            seg_row,
            fold_ref,
        )
    d_queries = dot_tn(ds_ref[0], keep_head(keys, 0))
    d_keys = dot_nn(ds_ref[0], keep_head(queries, 0))
    d_values = dot_nn(probs_ref[0], keep_head(back, 0))
    for h in range(1, heads):
        d_queries = d_queries + dot_tn(ds_ref[h], keep_head(keys, h))
        d_keys = d_keys + dot_nn(ds_ref[h], keep_head(queries, h))
        d_values = d_values + dot_nn(probs_ref[h], keep_head(back, h))
    dq_ref[...] = d_queries
    dk_ref[...] = d_keys
    dv_ref[...] = d_values
    table_ref[...] = table_sums(fold_ref, flipped_ref, SPAN // 2 - window, table_ref)


def far_back_kernel(
    info,
    q_ref,
    kp_ref,
    vp_ref,
    payload_ref,
    stat_ref,
    bias,
    bucket_ref,
    dq_in,
    table_in,
    dq_ref,
    table_ref,
    scores_ref,
    products_ref,
    ds_ref,
    fold_ref,
):
    window, width = q_ref.shape
    heads = width // HEAD

    @pl.when(info[3] == 1)
    def _():
        queries, keys, values = q_ref[...], kp_ref[...], vp_ref[...]
        back = payload_ref[:, :width]
        first = far_start(info, window)
        for h in range(heads):
            scores_ref[h] = dot_nt(keep_head(queries, h), keys)
            products_ref[h] = dot_nt(keep_head(back, h), values)
        for h in range(heads):
            bend(
                scores_ref,
                products_ref,
                None,
                ds_ref,
                h,
                bias,
                first,
                lambda rows: stat_ref[rows, h : h + 1],
                lambda rows: stat_ref[rows, heads + h : heads + h + 1],
                None,
                None,
                fold_ref,
            )
        d_queries = dq_in[...]
        for h in range(heads):
            d_queries = d_queries + dot_nn(ds_ref[h], keep_head(keys, h))
        dq_ref[...] = (d_queries * HEAD**-0.5).astype(LOW)
        table_ref[...] = table_in[...] + table_sums(fold_ref, bucket_ref, first - window, table_ref)

    @pl.when(info[3] == 0)
    def _():
        dq_ref[...] = (dq_in[...] * HEAD**-0.5).astype(LOW)
        table_ref[...] = table_in[...]


def partner_back_kernel(
    info,
    k_ref,
    v_ref,
    qp_ref,
    from_even,
    from_odd,
    bias_t,
    dk_in,
    dv_in,
    dq_ref,
    normed_ref,
    x_all,
    gain,
    wq,
    wk,
    wv,
    grad_in,
    gain_in,
    one_send,
    one_keep,
    two_send,
    two_keep,
    send_ref,
    keep_ref,
    small_ref,
    d_all,
    scores_ref,
    products_ref,
    probs_ref,
    ds_ref,
):
    window, width = k_ref.shape
    heads = width // HEAD
    y, c = info[0], info[1]
    d_all[:, :width] = dq_ref[...]

    @pl.when(info[3] == 1)
    def _():
        payload = jnp.where(info[6] == 1, from_even[...], from_odd[...])
        queries, keys, values = qp_ref[...], k_ref[...], v_ref[...]
        back = payload[:, :width]
        columns = payload[:, payload.shape[1] - CHUNK :].astype(F32).T
        skip = width % CHUNK
        first = far_start(info, window)
        for h in range(heads):
            scores_ref[h] = dot_nt(keep_head(keys, h), queries)
            products_ref[h] = dot_nt(keep_head(values, h), back)
        for h in range(heads):
            at = skip + h
            lse = columns[at : at + 1, :] + columns[at + 2 * heads : at + 2 * heads + 1, :]
            at = at + heads
            delta = columns[at : at + 1, :] + columns[at + 2 * heads : at + 2 * heads + 1, :]
            bend(
                scores_ref,
                products_ref,
                probs_ref,
                ds_ref,
                h,
                bias_t,
                first,
                lambda rows: lse,
                lambda rows: delta,
                None,
                None,
                None,
            )
        d_keys, d_values = dk_in[...], dv_in[...]
        for h in range(heads):
            d_keys = d_keys + dot_nn(ds_ref[h], keep_head(queries, h))
            d_values = d_values + dot_nn(probs_ref[h], keep_head(back, h))
        d_all[:, width : 2 * width] = d_keys.astype(LOW)
        d_all[:, 2 * width :] = d_values.astype(LOW)

    @pl.when(info[3] == 0)
    def _():
        d_all[:, width : 2 * width] = dk_in[...].astype(LOW)
        d_all[:, 2 * width :] = dv_in[...].astype(LOW)

    joint = dot_tn(d_all[...], normed_ref[...]).astype(LOW)
    halves = (joint[:width, :], joint[width : 2 * width, :])
    for side in (0, 1):

        @pl.when(info[4] == side)
        def _():
            one_keep[...] = halves[side]
            one_send[...] = halves[1 - side]

    halves_two = (joint[2 * width :, :], grad_in[...])
    for side in (0, 1):

        @pl.when(info[5] == side)
        def _():
            two_keep[...] = halves_two[side]
            two_send[...] = halves_two[1 - side]

    gain_sum = jnp.zeros((1, x_all.shape[1]), F32)
    for part, core in enumerate((1 - c, c)):
        spots = (aligned((2 * y + core) * CHUNK), aligned((2 * (1 - y) + core) * CHUNK))
        mine = jnp.concatenate([d_all[spots[0], :], d_all[spots[1], :]], axis=0)
        d_normed = dot_nn(mine[:, :width], wq[...])
        d_normed = d_normed + dot_nn(mine[:, width : 2 * width], wk[...])
        d_normed = d_normed + dot_nn(mine[:, 2 * width :], wv[...])
        wide = jnp.concatenate([x_all[spots[0], :], x_all[spots[1], :]], axis=0).astype(F32)
        gain_sum = gain_sum + jnp.sum(d_normed * (wide * rows_norm(wide)), axis=0, keepdims=True)
        if part == 0:
            send_ref[: 2 * CHUNK, :] = d_normed.astype(LOW)
        else:
            keep_ref[...] = d_normed
    small = jnp.concatenate([gain_sum, gain_in[...], jnp.zeros((6, gain_sum.shape[1]), F32)], axis=0)
    small_ref[...] = small
    put_small(send_ref, 2 * CHUNK, small)


def put_small(target, start, small):
    high = small.astype(LOW).astype(F32)
    target[start : start + EXTRA, :] = jnp.concatenate([high, small - high], axis=0).astype(LOW)


def get_small(source, start):
    both = source[start : start + EXTRA, :].astype(F32)
    return both[: EXTRA // 2] + both[EXTRA // 2 :]


def first_merge_kernel(keep_ref, got_ref, small_in, send_ref, own_ref, small_ref):
    local = own_ref.shape[0]
    total = (keep_ref[...] + got_ref[: 2 * local, :].astype(F32)).astype(LOW)
    own_ref[...] = total[:local, :]
    send_ref[:local, :] = total[local:, :]
    small = small_in[...] + get_small(got_ref, 2 * local)
    small_ref[...] = small
    put_small(send_ref, local, small)


def input_back_kernel(own_ref, got_ref, x_ref, dh_ref, gain, small_in, table_ref, out_ref, small_ref):
    local = own_ref.shape[0]
    d_normed = own_ref[...].astype(F32) + got_ref[:local, :].astype(F32)
    wide = x_ref[...].astype(F32)
    inverse = rows_norm(wide)
    unit = wide * inverse
    scaled = d_normed * as_row(gain)
    back = inverse * (scaled - unit * jnp.mean(unit * scaled, axis=-1, keepdims=True))
    out_ref[...] = (dh_ref[...] + back).astype(LOW)
    small_ref[...] = small_in[...] + get_small(got_ref, local)
    heads, buckets = table_ref.shape
    small_ref[2 : 2 + heads, :buckets] = table_ref[...]


def halve_kernel(info, *refs, bits):
    count = len(bits)
    for k, bit in enumerate(bits):
        keep, got = refs[2 * k], refs[2 * k + 1]
        send_ref, keep_ref = refs[2 * count + 2 * k], refs[2 * count + 2 * k + 1]
        half = send_ref.shape[0]
        side = (info[7] >> bit) & 1
        for first, target in ((1 - side, send_ref), (side, keep_ref)):
            rows = pl.ds(pl.multiple_of(first * half, 16), half)
            target[...] = (keep[rows, :].astype(F32) + got[rows, :].astype(F32)).astype(LOW)


def sum_kernel(*refs, count, small):
    for k in range(count):
        keep, got = refs[2 * k], refs[2 * k + 1]
        target = refs[2 * count + small + k]
        rows = keep.shape[0]
        target[:rows, :] = (keep[...].astype(F32) + got[...].astype(F32)).astype(LOW)
        if small and k == 0:
            put_small(target, rows, refs[2 * count][...])


def pair_kernel(*refs, count, small):
    for k in range(count):
        mine, got, target = refs[2 * k], refs[2 * k + 1], refs[2 * count + k]
        extra = EXTRA if small and k == 0 else 0
        rows = mine.shape[0] - extra
        target[:rows, :] = (mine[:rows, :].astype(F32) + got[:rows, :].astype(F32)).astype(LOW)
        if extra:
            put_small(target, rows, get_small(mine, rows) + get_small(got, rows))


def double_kernel(info, *refs, bits, small):
    count = len(bits)
    for k, bit in enumerate(bits):
        mine, got, target = refs[2 * k], refs[2 * k + 1], refs[2 * count + k]
        extra = EXTRA if small and k == 0 else 0
        rows = mine.shape[0] - extra
        side = (info[7] >> bit) & 1
        target[pl.ds(pl.multiple_of(side * rows, 16), rows), :] = mine[:rows, :]
        target[pl.ds(pl.multiple_of((1 - side) * rows, 16), rows), :] = got[:rows, :]
        if extra:
            put_small(target, 2 * rows, get_small(mine, rows) + get_small(got, rows))


def attention_total_kernel(info, one, one_got, two, two_got, q_ref, k_ref, v_ref, out_ref, small_ref):
    rows = q_ref.shape[0]
    first = info[4] == 0
    mine, got = one[:rows, :], one_got[:rows, :]
    q_ref[...] = jnp.where(first, mine, got).astype(F32)
    k_ref[...] = jnp.where(first, got, mine).astype(F32)
    first = info[5] == 0
    v_ref[...] = jnp.where(first, two[...], two_got[...]).astype(F32)
    out_ref[...] = jnp.where(first, two_got[...], two[...]).astype(F32)
    if one.shape[0] > rows:
        small_ref[...] = get_small(one, rows) + get_small(one_got, rows)
    else:
        small_ref[...] = jnp.zeros_like(small_ref)


def swap(values, axis, bit):
    return lax.ppermute(values, axis, [(i, i ^ bit) for i in range(lax.axis_size(axis))])


def swap_odd(values):
    ends = range(1, lax.axis_size("dp") - 1, 2)
    return lax.ppermute(values, "dp", [(i, i + 1) for i in ends] + [(i + 1, i) for i in ends])


def after(values, *others):
    return lax.optimization_barrier((values, *others))[0]


def spread(own, across=None):
    across = swap(own, "mp", 2) if across is None else across
    return own, across, swap(own, "mp", 1), swap(across, "mp", 1)


def cut(values, first, count):
    return lax.dynamic_slice_in_dim(values, first, count)


class Sums:
    def __init__(self, info, rank, orders, sends, keeps):
        self.info, self.rank, self.orders, self.keeps = info, rank, orders, list(keeps)
        self.bits = len(orders[0])
        self.tiled = all((k.shape[0] >> (self.bits - 2)) % 16 == 0 for k in keeps)
        self.step, self.small = 0, None
        self.exchange(sends)

    def exchange(self, sends):
        done = self.step if self.step < self.bits else 2 * self.bits - 2 - self.step
        self.now = [order[done] for order in self.orders]
        self.gots = [swap(v, "dp", 1 << bit) for v, bit in zip(sends, self.now)]
        self.step += 1

    def pairs(self):
        return [v for pair in zip(self.keeps, self.gots) for v in pair]

    def advance(self, token, small=None, micros=1):
        self.keeps[0] = after(self.keeps[0], token)
        count = len(self.keeps)
        if self.step < self.bits - 1:
            bits = [order[self.step] for order in self.orders]
            halves = [v.shape[0] // 2 for v in self.keeps]
            if self.tiled:
                out = call(
                    functools.partial(halve_kernel, bits=bits),
                    [shape((h, v.shape[1]), LOW) for h, v in zip(halves, self.keeps) for _ in range(2)],
                    [self.info, *self.pairs()],
                    micros=micros,
                )
                sends, self.keeps = out[0::2], list(out[1::2])
            else:
                sends, keeps = [], []
                for k, g, h, bit in zip(self.keeps, self.gots, halves, bits):
                    side = (self.rank >> bit) & 1
                    total = (k.astype(F32) + g.astype(F32)).astype(LOW)
                    sends.append(cut(total, (1 - side) * h, h))
                    keeps.append(cut(total, side * h, h))
                self.keeps = keeps
        elif self.step == self.bits - 1:
            if self.tiled:
                self.small = small
                rows = [v.shape[0] for v in self.keeps]
                if small is not None:
                    rows[0] += EXTRA
                sends = call(
                    functools.partial(sum_kernel, count=count, small=int(small is not None)),
                    [shape((r, v.shape[1]), LOW) for r, v in zip(rows, self.keeps)],
                    self.pairs() + ([small] if small is not None else []),
                    smem=0,
                    micros=micros,
                )
            else:
                sends = [(k.astype(F32) + g.astype(F32)).astype(LOW) for k, g in zip(self.keeps, self.gots)]
            self.keeps = list(sends)
        elif self.step == self.bits:
            if self.tiled:
                sends = call(
                    functools.partial(pair_kernel, count=count, small=self.small is not None),
                    [shape(v.shape, LOW) for v in self.keeps],
                    self.pairs(),
                    smem=0,
                    micros=micros,
                )
            else:
                sends = [(k.astype(F32) + g.astype(F32)).astype(LOW) for k, g in zip(self.keeps, self.gots)]
            self.keeps = list(sends)
        else:
            has = self.small is not None
            if self.tiled:
                rows = [2 * v.shape[0] for v in self.keeps]
                if has:
                    rows[0] -= EXTRA
                sends = call(
                    functools.partial(double_kernel, bits=self.now, small=has),
                    [shape((r, v.shape[1]), LOW) for r, v in zip(rows, self.keeps)],
                    [self.info, *self.pairs()],
                    micros=micros,
                )
            else:
                sends = []
                for k, g, bit in zip(self.keeps, self.gots, self.now):
                    side = (self.rank >> bit) & 1
                    sends.append(
                        jnp.where(side == 0, jnp.concatenate([k, g], axis=0), jnp.concatenate([g, k], axis=0))
                    )
            self.keeps = list(sends)
        self.exchange(sends)
        return sends[0]


def per_device(
    inputs,
    attention_gain,
    query_weight,
    key_weight,
    value_weight,
    out_weight,
    bias_table,
    feedforward_gain,
    gate_weight,
    up_weight,
    down_weight,
    segment,
    bucket,
    cotangent,
):
    parts = lax.axis_size("mp")
    groups = lax.axis_size("dp")
    local, d = inputs.shape
    window = local * parts
    width = query_weight.shape[1]
    heads = width // HEAD
    units = gate_weight.shape[1]
    buckets = bias_table.shape[0]
    half = 2 * local
    rank = lax.axis_index("dp")
    member = lax.axis_index("mp")
    bits = list(range(groups.bit_length() - 1))
    order_one = bits
    order_two = [bits[1], bits[0]] + bits[2:]

    x_across = swap(inputs, "mp", 2)
    from_even = swap(inputs, "dp", 1)
    from_odd = swap_odd(inputs)

    spot = jnp.stack([rank, member]).astype(jnp.int32)
    edge = jnp.full((1,), -1, jnp.int32)
    bucket_rows = jnp.concatenate([edge, bucket]).reshape(-1, CHUNK)
    table = bias_table.T
    gain_one, gain_two = attention_gain.reshape(-1, CHUNK), feedforward_gain.reshape(-1, CHUNK)
    band = shape((heads, CHUNK, SPAN), F32)
    info, seg_row, seg_col, bias = call(
        functools.partial(setup_kernel, groups=groups, first_bits=(order_one[0], order_two[0])),
        [shape((8,), jnp.int32), shape((1, window), F32), shape((window, CHUNK), F32), band],
        [spot, segment.reshape(-1, CHUNK), bucket_rows, table],
        out_smem=1,
        micros=3.0,
    )
    x_pieces = (inputs, x_across, swap(inputs, "mp", 1), swap(after(x_across, bias), "mp", 1))
    out_across = swap(out_weight, "mp", 2)
    cot_across = swap(cotangent, "mp", 2)
    (near,) = call(near_kernel, [shape((local, d), LOW)], [info, from_even, from_odd], micros=0.5)
    out_core = swap(after(out_across, near), "mp", 1)
    near_across = swap(near, "mp", 2)
    near_core = swap(near, "mp", 1)

    low_rows = shape((window, width), LOW)
    wide_rows = shape((window, width), F32)
    stats = shape((window, CHUNK), F32)
    square_wide = pltpu.VMEM((heads, window, window), F32)
    square_low = pltpu.VMEM((heads, window, window), LOW)
    weight = shape((width, d), LOW)
    x_all, normed, queries, keys, values, acc, top, total, wq, wk, wv = call(
        own_kernel,
        [shape((window, d), LOW)] * 2 + [low_rows] * 3 + [wide_rows, stats, stats] + [weight] * 3,
        [info, after(inputs, out_core), *x_pieces[1:], gain_one, bias, seg_col, seg_row, *[in_hbm(w.T) for w in (query_weight, key_weight, value_weight)]],
        scratch=[square_wide, square_low, pltpu.SemaphoreType.DMA((3,))],
        hbm=3,
        micros=5.0,
    )
    near_pieces = (near, near_across, near_core, swap(after(near_across, acc), "mp", 1))
    cot_pieces = (cotangent, cot_across, swap(after(cotangent, near), "mp", 1), swap(after(cot_across, acc), "mp", 1))
    mixed_low, mixed, lse, queries_near, keys_near, values_near = call(
        partner_kernel,
        [low_rows, wide_rows, stats] + [low_rows] * 3,
        [info, *near_pieces, gain_one, wq, wk, wv, bias, queries, after(acc, cot_pieces[3]), top, total],
        scratch=[
            pltpu.VMEM((window, d), LOW),
            square_wide,
            square_low,
            pltpu.VMEM((window, width), F32),
            pltpu.VMEM((window, CHUNK), F32),
            pltpu.VMEM((window, CHUNK), F32),
        ],
        micros=5.0,
    )
    mixed_across = swap(mixed_low, "mp", 2)
    mixed_core = swap(mixed_low, "mp", 1)
    out_pieces = (out_weight, out_across, swap(after(out_weight, mixed_core), "mp", 1), out_core)
    bias_t, flipped_rows = call(
        flipped_kernel,
        [band, shape(bucket_rows.shape, jnp.int32)],
        [after(bucket_rows, mixed_low), table],
        smem=0,
        micros=3.0,
    )
    cot_all, d_act = call(
        cotangent_kernel,
        [shape((window, d), LOW), shape((window, units), F32)],
        [*cot_pieces, after(down_weight, mixed_low)],
        smem=0,
        micros=1.0,
    )
    mixed_pieces = (mixed_low, mixed_across, mixed_core, swap(after(mixed_across, bias_t, d_act), "mp", 1))
    second, hidden, act, d_gate, d_up, second_send, second_keep, gain_two_part = call(
        feed_kernel,
        [shape((window, d), LOW), shape((half, d), F32)]
        + [shape((window, units), LOW)] * 3
        + [shape((half, d), LOW), shape((half, d), F32), shape((1, d), F32)],
        [info, x_all, *mixed_pieces, *out_pieces, d_act, gain_two, gate_weight, up_weight],
        micros=5.0,
    )
    (second_sum,) = call(
        functools.partial(sum_kernel, count=1, small=0),
        [shape((half, d), LOW)],
        [second_keep, swap(second_send, "mp", 1)],
        smem=0,
        micros=1.0,
    )
    second_other = swap(second_sum, "mp", 2)
    rows = d + units // 2 + units // 4
    gate_send, gate_keep, up_send, up_keep = call(
        feed_grad_kernel,
        [shape((rows // 2, units), LOW)] * 4,
        [info, after(second, second_sum), d_gate, d_up, act, cot_all],
        scratch=[pltpu.VMEM((rows, units), LOW)] * 2,
        micros=3.0,
    )
    feed_sums = Sums(info, rank, (order_one, order_two), (gate_send, up_send), (gate_keep, up_keep))
    feed_send, feed_keep = call(
        feed_out_kernel, [shape((half, d), LOW)] * 2, [after(act, gate_send), down_weight], smem=0, micros=30
    )
    feed_got = swap(feed_send, "mp", 1)
    second_other = after(second_other, feed_send)
    dh, branch_low = call(
        hidden_back_kernel,
        [shape((local, d), F32), shape((half, d), LOW)],
        [second_sum, second_other, hidden, cot_pieces[0], cot_pieces[1], gain_two],
        smem=0,
    )
    feed_own, feed_cross = call(
        feed_merge_kernel,
        [shape((local, d), LOW)] * 2,
        [after(feed_keep, branch_low), feed_got],
        smem=0,
        micros=100,
    )
    payload, stat_back, out_grad = call(
        mixed_back_kernel,
        [shape((window, 2 * CHUNK), LOW), stats, shape((width, d), LOW)],
        [info, after(branch_low, feed_cross), swap(branch_low, "mp", 1), out_weight, mixed, mixed_low, lse],
        scratch=[pltpu.VMEM((window, d), LOW), pltpu.VMEM((2 * CHUNK, d), LOW)],
    )
    payload_even = swap(payload, "dp", 1)
    payload_odd = swap_odd(payload)
    token = feed_sums.advance(payload)
    fold = pltpu.VMEM((heads, CHUNK, 2 * window), F32)
    d_queries, d_keys, d_values, table_part = call(
        own_back_kernel,
        [wide_rows, wide_rows, wide_rows, shape((heads, CHUNK), F32)],
        [after(queries, token), keys, values, payload, stat_back, bias_t, seg_col, seg_row, flipped_rows],
        scratch=[square_wide, square_wide, square_low, square_low, fold],
        smem=0,
        micros=200,
    )
    d_queries, table_part = call(
        far_back_kernel,
        [low_rows, shape((heads, CHUNK), F32)],
        [info, queries, keys_near, values_near, payload, stat_back, bias, bucket_rows, d_queries, table_part],
        scratch=[square_wide, square_wide, square_low, fold],
        micros=3.0,
    )
    one_send, one_keep, two_send, two_keep, first_send, first_keep, small = call(
        partner_back_kernel,
        [shape((width, d), LOW)] * 4
        + [shape((half + EXTRA, d), LOW), shape((half, d), F32), shape((EXTRA // 2, d), F32)],
        [
            info,
            keys,
            values,
            queries_near,
            payload_even,
            payload_odd,
            bias_t,
            d_keys,
            d_values,
            d_queries,
            normed,
            x_all,
            gain_one,
            wq,
            wk,
            wv,
            out_grad,
            gain_two_part,
        ],
        scratch=[pltpu.VMEM((window, 3 * width), LOW), square_wide, square_wide, square_low, square_low],
        micros=300,
    )
    joint_sums = Sums(info, rank, (order_one, order_two), (one_send, two_send), (one_keep, two_keep))
    token = feed_sums.advance(one_send, micros=300)
    first_send, first_own, small = call(
        first_merge_kernel,
        [shape((local + EXTRA, d), LOW), shape((local, d), LOW), shape((EXTRA // 2, d), F32)],
        [after(first_keep, token), swap(first_send, "mp", 1), small],
        smem=0,
        micros=1,
    )
    first_got = swap(first_send, "mp", 2)
    token = joint_sums.advance(first_send)
    input_grad, small = call(
        input_back_kernel,
        [shape((local, d), LOW), shape((EXTRA // 2, d), F32)],
        [first_own, first_got, inputs, after(dh, token), gain_one, small, table_part],
        smem=0,
        micros=1,
    )
    token = joint_sums.advance(small, small)
    token = feed_sums.advance(token)
    feed_got = swap(after(feed_cross, token), "mp", 2)
    token = joint_sums.advance(token, small, micros=1)
    token = feed_sums.advance(token)
    last = 2 * len(bits) - 1
    while joint_sums.step < last or feed_sums.step < last:
        if joint_sums.step < last:
            token = joint_sums.advance(token, small, micros=300)
        if feed_sums.step < last:
            token = feed_sums.advance(token)
    (layer_out,) = call(
        layer_out_kernel,
        [shape((local, d), LOW)],
        [after(hidden, token), feed_own, feed_got],
        smem=0,
        micros=40,
    )
    ready = feed_sums.pairs()
    gate_grad, up_grad, down_grad = call(
        feed_total_kernel,
        [shape((d, units), F32)] * 2 + [shape((units, d), F32)],
        [info, after(ready[0], layer_out), *ready[1:]],
        scratch=[pltpu.VMEM((rows, units), LOW)],
        micros=2.0,
    )
    ready = joint_sums.pairs()
    query_grad, key_grad, value_grad, out_total, small_total = call(
        attention_total_kernel,
        [shape((width, d), F32)] * 4 + [shape((EXTRA // 2, d), F32)],
        [info, after(ready[0], down_grad), *ready[1:]],
        micros=2.0,
    )
    if not joint_sums.tiled:
        small_total = lax.psum(small, "dp")
    return (
        layer_out,
        input_grad,
        small_total[0],
        query_grad.T,
        key_grad.T,
        value_grad.T,
        out_total,
        small_total[2 : 2 + heads, :buckets].T,
        small_total[1],
        gate_grad,
        up_grad,
        down_grad,
    )


def solution(mesh):
    rows = P(("dp", "mp"), None)
    in_specs = (
        rows,
        P(),
        P(None, "mp"),
        P(None, "mp"),
        P(None, "mp"),
        P("mp", None),
        P(None, "mp"),
        P(),
        P(None, "mp"),
        P(None, "mp"),
        P("mp", None),
        P(),
        P(),
        rows,
    )
    out_specs = (
        rows,
        rows,
        P(),
        P(None, "mp"),
        P(None, "mp"),
        P(None, "mp"),
        P("mp", None),
        P(None, "mp"),
        P(),
        P(None, "mp"),
        P(None, "mp"),
        P("mp", None),
    )
    return jax.shard_map(
        per_device, mesh=mesh, in_specs=in_specs, out_specs=out_specs, check_vma=False
    )
```

```python
import functools

import jax
import jax.numpy as jnp
from jax import lax
from jax.experimental import pallas as pl
from jax.experimental.pallas import tpu as pltpu
from jax.sharding import PartitionSpec as P

HEAD = 64
LOW = jnp.bfloat16
F32 = jnp.float32
CHUNK = 128
SPAN = 2048
EXTRA = 16
NEG = -1e30
ROOT = 0.7978845608
CUBE = 0.044715
VMEM = pl.BlockSpec(memory_space=pltpu.VMEM)
SMEM = pl.BlockSpec(memory_space=pltpu.SMEM)
HBM = pl.BlockSpec(memory_space=pltpu.HBM)


def dot_nn(a, b):
    return lax.dot_general(a, b, (((1,), (0,)), ((), ())), preferred_element_type=F32)


def dot_nt(a, b):
    return lax.dot_general(a, b, (((1,), (1,)), ((), ())), preferred_element_type=F32)


def dot_tn(a, b):
    return lax.dot_general(a, b, (((0,), (0,)), ((), ())), preferred_element_type=F32)


def call(kernel, outs, ins, scratch=(), smem=1, hbm=0, micros=2.0, out_smem=0, limit=20):
    return pl.pallas_call(
        kernel,
        out_shape=outs,
        in_specs=[SMEM] * smem + [VMEM] * (len(ins) - smem - hbm) + [HBM] * hbm,
        out_specs=[SMEM] * out_smem + [VMEM] * (len(outs) - out_smem),
        scratch_shapes=list(scratch),
        cost_estimate=pl.CostEstimate(flops=int(micros * 2e7), bytes_accessed=0, transcendentals=0),
        compiler_params=pltpu.CompilerParams(vmem_limit_bytes=limit * 1024 * 1024),
    )(*ins)


def in_hbm(values):
    return pltpu.with_memory_space_constraint(values, pltpu.HBM)


def shape(dims, dtype):
    return jax.ShapeDtypeStruct(dims, dtype)


def head_lanes(width, h):
    lane = lax.broadcasted_iota(jnp.int32, (1, width), 1)
    return (lane >= h * HEAD) & (lane < (h + 1) * HEAD)


def keep_head(values, h):
    return jnp.where(head_lanes(values.shape[-1], h), values, jnp.zeros_like(values))


def rows_norm(values):
    return lax.rsqrt(jnp.mean(values * values, axis=-1, keepdims=True) + 1e-06)


def as_row(ref):
    return jnp.concatenate([ref[k : k + 1, :] for k in range(ref.shape[0])], axis=1)


def aligned(start):
    return pl.ds(pl.multiple_of(start, CHUNK), CHUNK)


def lay_bias(row, table_ref, target):
    heads, buckets = table_ref.shape
    which = lax.broadcasted_iota(jnp.int32, (buckets, SPAN), 0)
    onehot = (row == which).astype(F32)
    table = table_ref[...].T
    for h in range(heads):
        rows = jnp.sum(onehot * table[:, h : h + 1], axis=0, keepdims=True)
        count = 1
        while count < 8:
            rows = jnp.concatenate([rows, pltpu.roll(rows, count, 1)], axis=0)
            count *= 2
        target[h, 0:8, :] = rows
        while count < CHUNK:
            target[h, count : 2 * count, :] = pltpu.roll(target[h, 0:count, :], count, 1)
            count *= 2


def setup_kernel(
    spot,
    bucket_ref,
    segment_hbm,
    table_hbm,
    one_hbm,
    two_hbm,
    info,
    row_ref,
    col_ref,
    bias_ref,
    table_ref,
    one_ref,
    two_ref,
    segment_ref,
    sems,
    *,
    groups,
    first_bits,
):
    pairs = ((segment_hbm, segment_ref), (table_hbm, table_ref), (one_hbm, one_ref), (two_hbm, two_ref))
    copies = [pltpu.make_async_copy(a, b, sems.at[k]) for k, (a, b) in enumerate(pairs)]
    for copy in copies:
        copy.start()
    for copy in copies:
        copy.wait()
    rank, member = spot[0], spot[1]
    steps = row_ref.shape[1] // CHUNK
    rows = [segment_ref[pl.ds(rank * steps + k, 1), :] for k in range(steps)]
    lane = lax.broadcasted_iota(jnp.int32, (1, CHUNK), 1)

    def value(row, at):
        return jnp.max(jnp.where(lane == at, row, -1))

    before = segment_ref[pl.ds(jnp.maximum(rank * steps - 1, 0), 1), :]
    later = segment_ref[pl.ds(jnp.minimum((rank + 1) * steps, groups * steps - 1), 1), :]
    left = (value(before, CHUNK - 1) == value(rows[0], 0)) & (rank > 0)
    right = (value(later, 0) == value(rows[-1], CHUNK - 1)) & (rank < groups - 1)
    even = jnp.where(rank % 2 == 0, right.astype(jnp.int32), left.astype(jnp.int32))
    info[0] = member // 2
    info[1] = member % 2
    info[2] = left.astype(jnp.int32)
    info[3] = (left | right).astype(jnp.int32)
    info[4] = (rank >> first_bits[0]) & 1
    info[5] = (rank >> first_bits[1]) & 1
    info[6] = even
    info[7] = rank
    row = jnp.concatenate(rows, axis=1).astype(F32)
    row_ref[...] = row
    col_ref[...] = jnp.broadcast_to(row, (CHUNK, row.shape[1])).T
    lay_bias(row_of(bucket_ref, 0, bucket_ref.shape[0]), table_ref, bias_ref)


def row_of(ref, first, count):
    return jnp.concatenate([ref[pl.ds(first + k, 1), :] for k in range(count)], axis=1)


def flipped_kernel(bucket_ref, table_ref, bias_ref, flipped_ref):
    count = bucket_ref.shape[0]
    sub = lax.broadcasted_iota(jnp.int32, (CHUNK, CHUNK), 0)
    lane = lax.broadcasted_iota(jnp.int32, (CHUNK, CHUNK), 1)
    turned = dot_nn(bucket_ref[...].astype(F32).astype(LOW), (sub + lane == CHUNK - 1).astype(F32).astype(LOW))
    row = jnp.concatenate([turned[k : k + 1, :] for k in reversed(range(count))], axis=1)
    row = pltpu.roll(row, 1, 1).astype(jnp.int32)
    flipped_ref[...] = jnp.concatenate([row[:, k * CHUNK : (k + 1) * CHUNK] for k in range(count)], axis=0)
    lay_bias(row, table_ref, bias_ref)


def near_kernel(info, even_ref, odd_ref, out_ref):
    out_ref[...] = jnp.where(info[6] == 1, even_ref[...], odd_ref[...])


def fold_diagonals(tile):
    rows, cols = tile.shape
    while rows > 1:
        rows //= 2
        tile = tile[:rows] + pltpu.roll(tile[rows:], cols - rows, 1)
    return tile


def pack_columns(columns, offset=0, base=None, width=CHUNK):
    rows = columns[0].shape[0]
    lane = lax.broadcasted_iota(jnp.int32, (rows, width), 1)
    out = jnp.zeros((rows, width), F32) if base is None else base
    for k, column in enumerate(columns):
        out = jnp.where(lane == offset + k, column, out)
    return out


def by_head(packed, width):
    lane = lax.broadcasted_iota(jnp.int32, (packed.shape[0], width), 1)
    out = packed[:, 0:1]
    for h in range(1, width // HEAD):
        out = jnp.where(lane >= h * HEAD, packed[:, h : h + 1], out)
    return out


def place(y, c):
    return (2 * y + c, 2 * (1 - y) + c, 2 * y + 1 - c, 2 * (1 - y) + 1 - c)


def project(normed, rows, wq, wk, wv, q_ref, k_ref, v_ref):
    q_ref[rows, :] = (dot_nt(normed, wq[...]).astype(LOW).astype(F32) * HEAD**-0.5).astype(LOW)
    k_ref[rows, :] = dot_nt(normed, wk[...]).astype(LOW)
    v_ref[rows, :] = dot_nt(normed, wv[...]).astype(LOW)


def attend(q, keys, values, bias, first, seg_col, seg_row, scores_ref, probs_ref, acc_ref, top_ref, sum_ref):
    window, width = q.shape
    heads = width // HEAD
    for h in range(heads):
        scores_ref[h] = dot_nt(keep_head(q, h), keys)
    for h in range(heads):
        for a in range(window // CHUNK):
            rows = slice(a * CHUNK, (a + 1) * CHUNK)
            scores = scores_ref[h, rows, :] + bias[h, :, pl.ds(first - a * CHUNK, window)]
            if seg_col is not None:
                scores = jnp.where(seg_col[rows, 0:1] == seg_row[...], scores, NEG)
            top = jnp.max(scores, axis=-1, keepdims=True)
            weights = jnp.exp(scores - top)
            probs_ref[h, rows, :] = weights.astype(LOW)
            top_ref[rows, :] = pack_columns([top], h, top_ref[rows, :] if h else jnp.zeros((CHUNK, CHUNK), F32))
            total = jnp.sum(weights, axis=-1, keepdims=True)
            sum_ref[rows, :] = pack_columns([total], h, sum_ref[rows, :] if h else jnp.ones((CHUNK, CHUNK), F32))
    total = dot_nn(probs_ref[0], keep_head(values, 0))
    for h in range(1, heads):
        total = total + dot_nn(probs_ref[h], keep_head(values, h))
    acc_ref[...] = total


def own_kernel(
    info,
    x1,
    x2,
    x3,
    gain,
    bias,
    seg_col,
    seg_row,
    x_hbm,
    wq_hbm,
    wk_hbm,
    wv_hbm,
    x_all,
    normed_ref,
    q_ref,
    k_ref,
    v_ref,
    acc_ref,
    top_ref,
    sum_ref,
    wq,
    wk,
    wv,
    scores_ref,
    probs_ref,
    x0,
    sems,
):
    pairs = ((x_hbm, x0), (wq_hbm, wq), (wk_hbm, wk), (wv_hbm, wv))
    copies = [pltpu.make_async_copy(a, b, sems.at[k]) for k, (a, b) in enumerate(pairs)]
    for copy in copies:
        copy.start()
    spots = place(info[0], info[1])
    for piece, spot in zip((x1, x2, x3, x0), spots[1:] + spots[:1]):
        if piece is x0:
            copies[0].wait()
        rows = aligned(spot * CHUNK)
        low = piece[...]
        x_all[rows, :] = low
        wide = low.astype(F32)
        normed_ref[rows, :] = (wide * rows_norm(wide) * as_row(gain)).astype(LOW)
    for copy in copies[1:]:
        copy.wait()
    project(normed_ref[...], slice(None), wq, wk, wv, q_ref, k_ref, v_ref)
    attend(
        q_ref[...],
        k_ref[...],
        v_ref[...],
        bias,
        SPAN // 2,
        seg_col,
        seg_row,
        scores_ref,
        probs_ref,
        acc_ref,
        top_ref,
        sum_ref,
    )


def far_start(info, window):
    return pl.multiple_of(jnp.where(info[2] == 1, SPAN // 2 - window, SPAN // 2 + window), CHUNK)


def partner_kernel(
    info,
    x0,
    x1,
    x2,
    x3,
    gain,
    wq,
    wk,
    wv,
    bias,
    q_ref,
    acc_ref,
    top_ref,
    sum_ref,
    mixed_low,
    mixed_ref,
    lse_ref,
    qp_ref,
    kp_ref,
    vp_ref,
    normed_ref,
    scores_ref,
    probs_ref,
    acc_two,
    top_two,
    sum_two,
):
    window, width = q_ref.shape
    paired = info[3]

    @pl.when(paired == 1)
    def _():
        for piece, spot in zip((x0, x1, x2, x3), place(info[0], info[1])):
            wide = piece[...].astype(F32)
            normed_ref[aligned(spot * CHUNK), :] = (wide * rows_norm(wide) * as_row(gain)).astype(LOW)
        project(normed_ref[...], slice(None), wq, wk, wv, qp_ref, kp_ref, vp_ref)
        attend(
            q_ref[...],
            kp_ref[...],
            vp_ref[...],
            bias,
            far_start(info, window),
            None,
            None,
            scores_ref,
            probs_ref,
            acc_two,
            top_two,
            sum_two,
        )
        for a in range(window // CHUNK):
            rows = slice(a * CHUNK, (a + 1) * CHUNK)
            top = jnp.maximum(top_ref[rows, :], top_two[rows, :])
            one, two = jnp.exp(top_ref[rows, :] - top), jnp.exp(top_two[rows, :] - top)
            whole = sum_ref[rows, :] * one + sum_two[rows, :] * two
            inverse = 1.0 / whole
            mixed = acc_ref[rows, :] * by_head(one * inverse, width)
            mixed = mixed + acc_two[rows, :] * by_head(two * inverse, width)
            mixed_ref[rows, :] = mixed
            mixed_low[rows, :] = mixed.astype(LOW)
            lse_ref[rows, :] = top + jnp.log(whole)

    @pl.when(paired == 0)
    def _():
        qp_ref[...] = jnp.zeros_like(qp_ref)
        kp_ref[...] = jnp.zeros_like(kp_ref)
        vp_ref[...] = jnp.zeros_like(vp_ref)
        for a in range(window // CHUNK):
            rows = slice(a * CHUNK, (a + 1) * CHUNK)
            whole = sum_ref[rows, :]
            mixed = acc_ref[rows, :] * by_head(1.0 / whole, width)
            mixed_ref[rows, :] = mixed
            mixed_low[rows, :] = mixed.astype(LOW)
            lse_ref[rows, :] = top_ref[rows, :] + jnp.log(whole)


def cotangent_kernel(g0, g1, g2, g3, down_w, cot_ref, d_act_ref):
    for part, piece in enumerate((g2, g3, g0, g1)):
        cot_ref[part * CHUNK : (part + 1) * CHUNK, :] = piece[...]
    d_act_ref[...] = dot_nt(cot_ref[...], down_w[...])


def feed_kernel(
    info,
    x_all,
    m0,
    m1,
    m2,
    m3,
    o0,
    o1,
    o2,
    o3,
    d_act_ref,
    gain,
    gate_w,
    up_w,
    second_ref,
    hidden_ref,
    act_ref,
    dgate_ref,
    dup_ref,
    send_ref,
    keep_ref,
    gain_ref,
):
    y, c = info[0], info[1]
    half = 2 * CHUNK
    gain_sum = jnp.zeros((1, x_all.shape[1]), F32)
    for part, core in enumerate((1 - c, c)):
        rows = slice(part * half, (part + 1) * half)
        spots = (aligned((2 * y + core) * CHUNK), aligned((2 * (1 - y) + core) * CHUNK))

        def pick(ref):
            return jnp.concatenate([ref[spots[0], :], ref[spots[1], :]], axis=0)

        hidden = pick(x_all).astype(F32)
        branch = dot_nn(pick(m0), o0[...])
        for m, o in ((m1, o1), (m2, o2), (m3, o3)):
            branch = branch + dot_nn(pick(m), o[...])
        hidden = hidden + branch
        if part == 1:
            hidden_ref[...] = hidden
        unit = hidden * rows_norm(hidden)
        second = (unit * as_row(gain)).astype(LOW)
        second_ref[rows, :] = second
        gate = dot_nn(second, gate_w[...])
        up = dot_nn(second, up_w[...])
        d_act = d_act_ref[rows, :]
        square = gate * gate
        tanh = jnp.tanh(ROOT * gate * (1.0 + CUBE * square))
        low_half = 0.5 * (1.0 + tanh)
        gelu = gate * low_half
        slope = low_half + 0.5 * gate * (1.0 - tanh * tanh) * (ROOT * (1.0 + 3.0 * CUBE * square))
        act_ref[rows, :] = (gelu * up).astype(LOW)
        d_gate = (d_act * up * slope).astype(LOW)
        d_up = (d_act * gelu).astype(LOW)
        dgate_ref[rows, :] = d_gate
        dup_ref[rows, :] = d_up
        d_second = dot_nt(d_gate, gate_w[...]) + dot_nt(d_up, up_w[...])
        gain_sum = gain_sum + jnp.sum(d_second * unit, axis=0, keepdims=True)
        if part == 0:
            send_ref[...] = d_second.astype(LOW)
        else:
            keep_ref[...] = d_second
    gain_ref[...] = gain_sum


def feed_grad_kernel(
    info, second_ref, dgate_ref, dup_ref, act_ref, cot_ref, one_send, one_keep, two_send, two_keep, one_ref, two_ref
):
    d, units = second_ref.shape[1], dgate_ref.shape[1]
    one_ref[:d, :] = dot_tn(second_ref[...], dgate_ref[...]).astype(LOW)
    two_ref[:d, :] = dot_tn(second_ref[...], dup_ref[...]).astype(LOW)
    down = dot_tn(act_ref[...], cot_ref[...]).astype(LOW)
    half = units // 2
    quarter = half // 2
    for k, target in enumerate((one_ref, two_ref)):
        target[d : d + half, :] = down[k * half : (k + 1) * half, :units]
        for side in (0, 1):
            rows = slice(k * half + side * quarter, k * half + (side + 1) * quarter)
            target[d + half :, side * (units // 2) : (side + 1) * (units // 2)] = down[rows, units:]
    for source, side, send, keep in ((one_ref, info[4], one_send, one_keep), (two_ref, info[5], two_send, two_keep)):
        rows = send.shape[0]
        send[...] = source[pl.ds(pl.multiple_of((1 - side) * rows, 16), rows), :]
        keep[...] = source[pl.ds(pl.multiple_of(side * rows, 16), rows), :]


def feed_out_kernel(act_ref, down_w, send_ref, keep_ref):
    half = send_ref.shape[0]
    send_ref[...] = dot_nn(act_ref[:half, :], down_w[...]).astype(LOW)
    keep_ref[...] = dot_nn(act_ref[half:, :], down_w[...]).astype(LOW)


def feed_total_kernel(info, one, one_got, two, two_got, gate_ref, up_ref, down_ref, full_ref):
    d, units = gate_ref.shape
    half = units // 2
    quarter = half // 2
    parts = ((one, one_got, info[4], gate_ref), (two, two_got, info[5], up_ref))
    for k, (mine, got, side, target) in enumerate(parts):
        rows = mine.shape[0]
        full_ref[pl.ds(pl.multiple_of(side * rows, 16), rows), :] = mine[...]
        full_ref[pl.ds(pl.multiple_of((1 - side) * rows, 16), rows), :] = got[...]
        target[...] = full_ref[:d, :].astype(F32)
        down_ref[k * half : (k + 1) * half, :units] = full_ref[d : d + half, :].astype(F32)
        for part in (0, 1):
            rows = slice(k * half + part * quarter, k * half + (part + 1) * quarter)
            down_ref[rows, units:] = full_ref[d + half :, part * (units // 2) : (part + 1) * (units // 2)].astype(F32)


def feed_merge_kernel(keep_ref, got_ref, own_ref, send_ref):
    local = own_ref.shape[0]
    total = (keep_ref[...].astype(F32) + got_ref[...].astype(F32)).astype(LOW)
    own_ref[...] = total[:local, :]
    send_ref[...] = total[local:, :]


def layer_out_kernel(hidden_ref, own_ref, got_ref, out_ref):
    local = out_ref.shape[0]
    out_ref[...] = (hidden_ref[:local, :] + (own_ref[...].astype(F32) + got_ref[...].astype(F32))).astype(LOW)


def hidden_back_kernel(sum_ref, other_ref, hidden_ref, g0, g1, gain, dh_ref, low_ref):
    for part, cot in enumerate((g0, g1)):
        rows = slice(part * CHUNK, (part + 1) * CHUNK)
        flip = slice((1 - part) * CHUNK, (2 - part) * CHUNK)
        d_second = sum_ref[rows, :].astype(F32) + other_ref[flip, :].astype(F32)
        hidden = hidden_ref[rows, :]
        inverse = rows_norm(hidden)
        unit = hidden * inverse
        scaled = d_second * as_row(gain)
        dh = cot[...].astype(F32) + inverse * (scaled - unit * jnp.mean(unit * scaled, axis=-1, keepdims=True))
        low_ref[rows, :] = dh.astype(LOW)
        if part == 0:
            dh_ref[...] = dh


def mixed_back_kernel(
    info, pair_own, pair_other, out_w, mixed_ref, mixed_low, lse_ref, payload_ref, stat_ref, grad_ref, branch_ref, pad_ref
):
    width = mixed_ref.shape[1]
    heads = width // HEAD
    pieces = (pair_own[:CHUNK, :], pair_own[CHUNK:, :], pair_other[:CHUNK, :], pair_other[CHUNK:, :])
    for piece, spot in zip(pieces, place(info[0], info[1])):
        branch_ref[aligned(spot * CHUNK), :] = piece
    pad_ref[:width, :] = out_w[...]
    pad_ref[width:, :] = jnp.zeros((pad_ref.shape[0] - width, pad_ref.shape[1]), LOW)
    d_all = dot_nt(branch_ref[...], pad_ref[...]).astype(LOW).astype(F32)
    for a in range(d_all.shape[0] // CHUNK):
        rows = slice(a * CHUNK, (a + 1) * CHUNK)
        d_mixed = d_all[rows, :]
        product = d_mixed[:, :width] * mixed_ref[rows, :]
        deltas = [jnp.sum(keep_head(product, h), axis=-1, keepdims=True) for h in range(heads)]
        stat = pack_columns(deltas, heads, lse_ref[rows, :])
        stat_ref[rows, :] = stat
        high = stat.astype(LOW).astype(F32)
        rest = stat - high
        lane = lax.broadcasted_iota(jnp.int32, (CHUNK, CHUNK), 1)
        skip = width % CHUNK
        high = pltpu.roll(high, skip, 1)
        rest = pltpu.roll(rest, skip + 2 * heads, 1)
        tail = jnp.where(lane < skip, d_mixed[:, width - skip : width - skip + CHUNK], high)
        tail = jnp.where(lane >= skip + 2 * heads, rest, tail)
        tail = jnp.where(lane >= skip + 4 * heads, 0.0, tail)
        payload_ref[rows, : width - skip] = d_mixed[:, : width - skip].astype(LOW)
        payload_ref[rows, width - skip :] = tail.astype(LOW)
    grad_ref[...] = dot_tn(mixed_low[...], branch_ref[...]).astype(LOW)


def bend(scores_ref, products_ref, probs_ref, ds_ref, h, bias, first, lse_of, delta_of, seg_col, seg_row, fold_ref):
    window = scores_ref.shape[1]
    steps = window // CHUNK
    for a in range(steps):
        rows = slice(a * CHUNK, (a + 1) * CHUNK)
        scores = scores_ref[h, rows, :] + bias[h, :, pl.ds(first - a * CHUNK, window)]
        if seg_col is not None:
            scores = jnp.where(seg_col[rows, 0:1] == seg_row[...], scores, NEG)
        weights = jnp.exp(scores - lse_of(rows))
        d_scores = weights * (products_ref[h, rows, :] - delta_of(rows))
        ds_ref[h, rows, :] = d_scores.astype(LOW)
        if probs_ref is not None:
            probs_ref[h, rows, :] = weights.astype(LOW)
        if fold_ref is not None:
            at = (steps - a) * CHUNK
            if a == 0:
                fold_ref[h, :, :at] = jnp.zeros((CHUNK, at), F32)
                fold_ref[h, :, at:] = d_scores
            else:
                if a == steps - 1:
                    fold_ref[h, :, :CHUNK] = jnp.zeros((CHUNK, CHUNK), F32)
                fold_ref[h, :, at : at + window] += d_scores


def table_sums(fold_ref, bucket_ref, start, table_ref):
    heads, buckets = table_ref.shape
    reach = fold_ref.shape[2]
    row = row_of(bucket_ref, start // CHUNK, reach // CHUNK)
    onehot = row == lax.broadcasted_iota(jnp.int32, (buckets, reach), 0)
    columns = []
    for h in range(heads):
        folded = fold_diagonals(fold_ref[h])
        columns.append(jnp.sum(jnp.where(onehot, folded, 0.0), axis=1, keepdims=True))
    return pack_columns(columns).T[:heads, :]


def own_back_kernel(
    q_ref,
    k_ref,
    v_ref,
    payload_ref,
    stat_ref,
    bias_t,
    seg_col,
    seg_row,
    flipped_ref,
    dq_ref,
    dk_ref,
    dv_ref,
    table_ref,
    scores_ref,
    products_ref,
    probs_ref,
    ds_ref,
    fold_ref,
):
    window, width = q_ref.shape
    heads = width // HEAD
    queries, keys, values = q_ref[...], k_ref[...], v_ref[...]
    back = payload_ref[:, :width]
    stat = stat_ref[...].T
    for h in range(heads):
        scores_ref[h] = dot_nt(keep_head(keys, h), queries)
        products_ref[h] = dot_nt(keep_head(values, h), back)
    for h in range(heads):
        lse, delta = stat[h : h + 1, :], stat[heads + h : heads + h + 1, :]
        bend(
            scores_ref,
            products_ref,
            probs_ref,
            ds_ref,
            h,
            bias_t,
            SPAN // 2,
            lambda rows: lse,
            lambda rows: delta,
            seg_col,
            seg_row,
            fold_ref,
        )
    d_queries = dot_tn(ds_ref[0], keep_head(keys, 0))
    d_keys = dot_nn(ds_ref[0], keep_head(queries, 0))
    d_values = dot_nn(probs_ref[0], keep_head(back, 0))
    for h in range(1, heads):
        d_queries = d_queries + dot_tn(ds_ref[h], keep_head(keys, h))
        d_keys = d_keys + dot_nn(ds_ref[h], keep_head(queries, h))
        d_values = d_values + dot_nn(probs_ref[h], keep_head(back, h))
    dq_ref[...] = d_queries
    dk_ref[...] = d_keys
    dv_ref[...] = d_values
    table_ref[...] = table_sums(fold_ref, flipped_ref, SPAN // 2 - window, table_ref)


def far_back_kernel(
    info,
    q_ref,
    kp_ref,
    vp_ref,
    payload_ref,
    stat_ref,
    bias,
    bucket_ref,
    dq_in,
    table_in,
    dq_ref,
    table_ref,
    scores_ref,
    products_ref,
    ds_ref,
    fold_ref,
):
    window, width = q_ref.shape
    heads = width // HEAD

    @pl.when(info[3] == 1)
    def _():
        queries, keys, values = q_ref[...], kp_ref[...], vp_ref[...]
        back = payload_ref[:, :width]
        first = far_start(info, window)
        for h in range(heads):
            scores_ref[h] = dot_nt(keep_head(queries, h), keys)
            products_ref[h] = dot_nt(keep_head(back, h), values)
        for h in range(heads):
            bend(
                scores_ref,
                products_ref,
                None,
                ds_ref,
                h,
                bias,
                first,
                lambda rows: stat_ref[rows, h : h + 1],
                lambda rows: stat_ref[rows, heads + h : heads + h + 1],
                None,
                None,
                fold_ref,
            )
        d_queries = dq_in[...]
        for h in range(heads):
            d_queries = d_queries + dot_nn(ds_ref[h], keep_head(keys, h))
        dq_ref[...] = (d_queries * HEAD**-0.5).astype(LOW)
        table_ref[...] = table_in[...] + table_sums(fold_ref, bucket_ref, first - window, table_ref)

    @pl.when(info[3] == 0)
    def _():
        dq_ref[...] = (dq_in[...] * HEAD**-0.5).astype(LOW)
        table_ref[...] = table_in[...]


def partner_back_kernel(
    info,
    k_ref,
    v_ref,
    qp_ref,
    from_even,
    from_odd,
    bias_t,
    dk_in,
    dv_in,
    dq_ref,
    normed_ref,
    x_all,
    gain,
    wq,
    wk,
    wv,
    grad_in,
    gain_in,
    one_send,
    one_keep,
    two_send,
    two_keep,
    send_ref,
    keep_ref,
    small_ref,
    d_all,
    scores_ref,
    products_ref,
    probs_ref,
    ds_ref,
):
    window, width = k_ref.shape
    heads = width // HEAD
    y, c = info[0], info[1]
    d_all[:, :width] = dq_ref[...]

    @pl.when(info[3] == 1)
    def _():
        payload = jnp.where(info[6] == 1, from_even[...], from_odd[...])
        queries, keys, values = qp_ref[...], k_ref[...], v_ref[...]
        back = payload[:, :width]
        columns = payload[:, payload.shape[1] - CHUNK :].astype(F32).T
        skip = width % CHUNK
        first = far_start(info, window)
        for h in range(heads):
            scores_ref[h] = dot_nt(keep_head(keys, h), queries)
            products_ref[h] = dot_nt(keep_head(values, h), back)
        for h in range(heads):
            at = skip + h
            lse = columns[at : at + 1, :] + columns[at + 2 * heads : at + 2 * heads + 1, :]
            at = at + heads
            delta = columns[at : at + 1, :] + columns[at + 2 * heads : at + 2 * heads + 1, :]
            bend(
                scores_ref,
                products_ref,
                probs_ref,
                ds_ref,
                h,
                bias_t,
                first,
                lambda rows: lse,
                lambda rows: delta,
                None,
                None,
                None,
            )
        d_keys, d_values = dk_in[...], dv_in[...]
        for h in range(heads):
            d_keys = d_keys + dot_nn(ds_ref[h], keep_head(queries, h))
            d_values = d_values + dot_nn(probs_ref[h], keep_head(back, h))
        d_all[:, width : 2 * width] = d_keys.astype(LOW)
        d_all[:, 2 * width :] = d_values.astype(LOW)

    @pl.when(info[3] == 0)
    def _():
        d_all[:, width : 2 * width] = dk_in[...].astype(LOW)
        d_all[:, 2 * width :] = dv_in[...].astype(LOW)

    joint = dot_tn(d_all[...], normed_ref[...]).astype(LOW)
    halves = (joint[:width, :], joint[width : 2 * width, :])
    for side in (0, 1):

        @pl.when(info[4] == side)
        def _():
            one_keep[...] = halves[side]
            one_send[...] = halves[1 - side]

    halves_two = (joint[2 * width :, :], grad_in[...])
    for side in (0, 1):

        @pl.when(info[5] == side)
        def _():
            two_keep[...] = halves_two[side]
            two_send[...] = halves_two[1 - side]

    gain_sum = jnp.zeros((1, x_all.shape[1]), F32)
    for part, core in enumerate((1 - c, c)):
        spots = (aligned((2 * y + core) * CHUNK), aligned((2 * (1 - y) + core) * CHUNK))
        mine = jnp.concatenate([d_all[spots[0], :], d_all[spots[1], :]], axis=0)
        d_normed = dot_nn(mine[:, :width], wq[...])
        d_normed = d_normed + dot_nn(mine[:, width : 2 * width], wk[...])
        d_normed = d_normed + dot_nn(mine[:, 2 * width :], wv[...])
        wide = jnp.concatenate([x_all[spots[0], :], x_all[spots[1], :]], axis=0).astype(F32)
        gain_sum = gain_sum + jnp.sum(d_normed * (wide * rows_norm(wide)), axis=0, keepdims=True)
        if part == 0:
            send_ref[: 2 * CHUNK, :] = d_normed.astype(LOW)
        else:
            keep_ref[...] = d_normed
    small = jnp.concatenate([gain_sum, gain_in[...], jnp.zeros((6, gain_sum.shape[1]), F32)], axis=0)
    small_ref[...] = small
    put_small(send_ref, 2 * CHUNK, small)


def put_small(target, start, small):
    high = small.astype(LOW).astype(F32)
    target[start : start + EXTRA, :] = jnp.concatenate([high, small - high], axis=0).astype(LOW)


def get_small(source, start):
    both = source[start : start + EXTRA, :].astype(F32)
    return both[: EXTRA // 2] + both[EXTRA // 2 :]


def first_merge_kernel(keep_ref, got_ref, small_in, send_ref, own_ref, small_ref):
    local = own_ref.shape[0]
    total = (keep_ref[...] + got_ref[: 2 * local, :].astype(F32)).astype(LOW)
    own_ref[...] = total[:local, :]
    send_ref[:local, :] = total[local:, :]
    small = small_in[...] + get_small(got_ref, 2 * local)
    small_ref[...] = small
    put_small(send_ref, local, small)


def input_back_kernel(own_ref, got_ref, x_ref, dh_ref, gain, small_in, table_ref, out_ref, small_ref):
    local = own_ref.shape[0]
    d_normed = own_ref[...].astype(F32) + got_ref[:local, :].astype(F32)
    wide = x_ref[...].astype(F32)
    inverse = rows_norm(wide)
    unit = wide * inverse
    scaled = d_normed * as_row(gain)
    back = inverse * (scaled - unit * jnp.mean(unit * scaled, axis=-1, keepdims=True))
    out_ref[...] = (dh_ref[...] + back).astype(LOW)
    small_ref[...] = small_in[...] + get_small(got_ref, local)
    heads, buckets = table_ref.shape
    small_ref[2 : 2 + heads, :buckets] = table_ref[...]


def halve_kernel(info, *refs, bits):
    count = len(bits)
    for k, bit in enumerate(bits):
        keep, got = refs[2 * k], refs[2 * k + 1]
        send_ref, keep_ref = refs[2 * count + 2 * k], refs[2 * count + 2 * k + 1]
        half = send_ref.shape[0]
        side = (info[7] >> bit) & 1
        for first, target in ((1 - side, send_ref), (side, keep_ref)):
            rows = pl.ds(pl.multiple_of(first * half, 16), half)
            target[...] = (keep[rows, :].astype(F32) + got[rows, :].astype(F32)).astype(LOW)


def sum_kernel(*refs, count, small):
    for k in range(count):
        keep, got = refs[2 * k], refs[2 * k + 1]
        target = refs[2 * count + small + k]
        rows = keep.shape[0]
        target[:rows, :] = (keep[...].astype(F32) + got[...].astype(F32)).astype(LOW)
        if small and k == 0:
            put_small(target, rows, refs[2 * count][...])


def pair_kernel(*refs, count, small):
    for k in range(count):
        mine, got, target = refs[2 * k], refs[2 * k + 1], refs[2 * count + k]
        extra = EXTRA if small and k == 0 else 0
        rows = mine.shape[0] - extra
        target[:rows, :] = (mine[:rows, :].astype(F32) + got[:rows, :].astype(F32)).astype(LOW)
        if extra:
            put_small(target, rows, get_small(mine, rows) + get_small(got, rows))


def double_kernel(info, *refs, bits, small):
    count = len(bits)
    for k, bit in enumerate(bits):
        mine, got, target = refs[2 * k], refs[2 * k + 1], refs[2 * count + k]
        extra = EXTRA if small and k == 0 else 0
        rows = mine.shape[0] - extra
        side = (info[7] >> bit) & 1
        target[pl.ds(pl.multiple_of(side * rows, 16), rows), :] = mine[:rows, :]
        target[pl.ds(pl.multiple_of((1 - side) * rows, 16), rows), :] = got[:rows, :]
        if extra:
            put_small(target, 2 * rows, get_small(mine, rows) + get_small(got, rows))


def attention_total_kernel(
    info, one, one_got, two, two_got, q_ref, k_ref, v_ref, out_ref, gain_one_ref, gain_two_ref, table_ref
):
    rows = q_ref.shape[0]
    first = info[4] == 0
    mine, got = one[:rows, :], one_got[:rows, :]
    q_ref[...] = jnp.where(first, mine, got).astype(F32)
    k_ref[...] = jnp.where(first, got, mine).astype(F32)
    first = info[5] == 0
    v_ref[...] = jnp.where(first, two[...], two_got[...]).astype(F32)
    out_ref[...] = jnp.where(first, two_got[...], two[...]).astype(F32)
    if one.shape[0] > rows:
        small = get_small(one, rows) + get_small(one_got, rows)
        for k in range(gain_one_ref.shape[0]):
            columns = slice(k * CHUNK, (k + 1) * CHUNK)
            gain_one_ref[k : k + 1, :] = small[0:1, columns]
            gain_two_ref[k : k + 1, :] = small[1:2, columns]
        heads, buckets = table_ref.shape
        table_ref[...] = small[2 : 2 + heads, :buckets]
    else:
        gain_one_ref[...] = jnp.zeros_like(gain_one_ref)
        gain_two_ref[...] = jnp.zeros_like(gain_two_ref)
        table_ref[...] = jnp.zeros_like(table_ref)


def swap(values, axis, bit):
    return lax.ppermute(values, axis, [(i, i ^ bit) for i in range(lax.axis_size(axis))])


def swap_odd(values):
    ends = range(1, lax.axis_size("dp") - 1, 2)
    return lax.ppermute(values, "dp", [(i, i + 1) for i in ends] + [(i + 1, i) for i in ends])


def after(values, *others):
    return lax.optimization_barrier((values, *others))[0]


def spread(own, across=None):
    across = swap(own, "mp", 2) if across is None else across
    return own, across, swap(own, "mp", 1), swap(across, "mp", 1)


def cut(values, first, count):
    return lax.dynamic_slice_in_dim(values, first, count)


class Sums:
    def __init__(self, info, rank, orders, sends, keeps):
        self.info, self.rank, self.orders, self.keeps = info, rank, orders, list(keeps)
        self.bits = len(orders[0])
        self.tiled = all((k.shape[0] >> (self.bits - 2)) % 16 == 0 for k in keeps)
        self.step, self.small = 0, None
        self.exchange(sends)

    def exchange(self, sends):
        done = self.step if self.step < self.bits else 2 * self.bits - 2 - self.step
        self.now = [order[done] for order in self.orders]
        self.gots = [swap(v, "dp", 1 << bit) for v, bit in zip(sends, self.now)]
        self.step += 1

    def pairs(self):
        return [v for pair in zip(self.keeps, self.gots) for v in pair]

    def advance(self, token, small=None, micros=1):
        self.keeps[0] = after(self.keeps[0], token)
        count = len(self.keeps)
        if self.step < self.bits - 1:
            bits = [order[self.step] for order in self.orders]
            halves = [v.shape[0] // 2 for v in self.keeps]
            if self.tiled:
                out = call(
                    functools.partial(halve_kernel, bits=bits),
                    [shape((h, v.shape[1]), LOW) for h, v in zip(halves, self.keeps) for _ in range(2)],
                    [self.info, *self.pairs()],
                    micros=micros,
                )
                sends, self.keeps = out[0::2], list(out[1::2])
            else:
                sends, keeps = [], []
                for k, g, h, bit in zip(self.keeps, self.gots, halves, bits):
                    side = (self.rank >> bit) & 1
                    total = (k.astype(F32) + g.astype(F32)).astype(LOW)
                    sends.append(cut(total, (1 - side) * h, h))
                    keeps.append(cut(total, side * h, h))
                self.keeps = keeps
        elif self.step == self.bits - 1:
            if self.tiled:
                self.small = small
                rows = [v.shape[0] for v in self.keeps]
                if small is not None:
                    rows[0] += EXTRA
                sends = call(
                    functools.partial(sum_kernel, count=count, small=int(small is not None)),
                    [shape((r, v.shape[1]), LOW) for r, v in zip(rows, self.keeps)],
                    self.pairs() + ([small] if small is not None else []),
                    smem=0,
                    micros=micros,
                )
            else:
                sends = [(k.astype(F32) + g.astype(F32)).astype(LOW) for k, g in zip(self.keeps, self.gots)]
            self.keeps = list(sends)
        elif self.step == self.bits:
            if self.tiled:
                sends = call(
                    functools.partial(pair_kernel, count=count, small=self.small is not None),
                    [shape(v.shape, LOW) for v in self.keeps],
                    self.pairs(),
                    smem=0,
                    micros=micros,
                )
            else:
                sends = [(k.astype(F32) + g.astype(F32)).astype(LOW) for k, g in zip(self.keeps, self.gots)]
            self.keeps = list(sends)
        else:
            has = self.small is not None
            if self.tiled:
                rows = [2 * v.shape[0] for v in self.keeps]
                if has:
                    rows[0] -= EXTRA
                sends = call(
                    functools.partial(double_kernel, bits=self.now, small=has),
                    [shape((r, v.shape[1]), LOW) for r, v in zip(rows, self.keeps)],
                    [self.info, *self.pairs()],
                    micros=micros,
                )
            else:
                sends = []
                for k, g, bit in zip(self.keeps, self.gots, self.now):
                    side = (self.rank >> bit) & 1
                    sends.append(
                        jnp.where(side == 0, jnp.concatenate([k, g], axis=0), jnp.concatenate([g, k], axis=0))
                    )
            self.keeps = list(sends)
        self.exchange(sends)
        return sends[0]


def per_device(
    inputs,
    attention_gain,
    query_weight,
    key_weight,
    value_weight,
    out_weight,
    bias_table,
    feedforward_gain,
    gate_weight,
    up_weight,
    down_weight,
    segment,
    bucket,
    cotangent,
):
    parts = lax.axis_size("mp")
    groups = lax.axis_size("dp")
    local, d = inputs.shape
    window = local * parts
    width = query_weight.shape[1]
    heads = width // HEAD
    units = gate_weight.shape[1]
    buckets = bias_table.shape[0]
    half = 2 * local
    rank = lax.axis_index("dp")
    member = lax.axis_index("mp")
    bits = list(range(groups.bit_length() - 1))
    order_one = bits
    order_two = [bits[1], bits[0]] + bits[2:]

    x_across = swap(inputs, "mp", 2)
    from_even = swap(inputs, "dp", 1)
    from_odd = swap_odd(inputs)

    spot = jnp.stack([rank, member]).astype(jnp.int32)
    edge = jnp.full((1,), -1, jnp.int32)
    bucket_rows = jnp.concatenate([edge, bucket]).reshape(-1, CHUNK)
    table = bias_table.T
    gain_one, gain_two = attention_gain.reshape(-1, CHUNK), feedforward_gain.reshape(-1, CHUNK)
    band = shape((heads, CHUNK, SPAN), F32)
    segments = segment.reshape(-1, CHUNK)
    info, seg_row, seg_col, bias, table, gain_one, gain_two = call(
        functools.partial(setup_kernel, groups=groups, first_bits=(order_one[0], order_two[0])),
        [shape((8,), jnp.int32), shape((1, window), F32), shape((window, CHUNK), F32), band]
        + [shape(v.shape, F32) for v in (table, gain_one, gain_two)],
        [spot, bucket_rows] + [in_hbm(v) for v in (segments, table, gain_one, gain_two)],
        scratch=[pltpu.VMEM(segments.shape, jnp.int32), pltpu.SemaphoreType.DMA((4,))],
        hbm=4,
        out_smem=1,
        micros=3.0,
    )
    cot_across = swap(cotangent, "mp", 2)
    (near,) = call(near_kernel, [shape((local, d), LOW)], [info, after(from_even, x_across, cot_across), from_odd], micros=0.5)
    near_across = swap(near, "mp", 2)
    near_core = swap(near, "mp", 1)
    x_pieces = (inputs, x_across, swap(inputs, "mp", 1), swap(after(x_across, near_core), "mp", 1))

    low_rows = shape((window, width), LOW)
    wide_rows = shape((window, width), F32)
    stats = shape((window, CHUNK), F32)
    square_wide = pltpu.VMEM((heads, window, window), F32)
    square_low = pltpu.VMEM((heads, window, window), LOW)
    weight = shape((width, d), LOW)
    x_all, normed, queries, keys, values, acc, top, total, wq, wk, wv = call(
        own_kernel,
        [shape((window, d), LOW)] * 2 + [low_rows] * 3 + [wide_rows, stats, stats] + [weight] * 3,
        [info, x_across, *x_pieces[2:], gain_one, bias, seg_col, seg_row]
        + [in_hbm(v) for v in (inputs, query_weight.T, key_weight.T, value_weight.T)],
        scratch=[square_wide, square_low, pltpu.VMEM((local, d), LOW), pltpu.SemaphoreType.DMA((4,))],
        hbm=4,
        micros=5.0,
    )
    near_pieces = (near, near_across, near_core, swap(after(near_across, acc), "mp", 1))
    mixed_low, mixed, lse, queries_near, keys_near, values_near = call(
        partner_kernel,
        [low_rows, wide_rows, stats] + [low_rows] * 3,
        [info, *near_pieces, gain_one, wq, wk, wv, bias, queries, acc, top, total],
        scratch=[
            pltpu.VMEM((window, d), LOW),
            square_wide,
            square_low,
            pltpu.VMEM((window, width), F32),
            pltpu.VMEM((window, CHUNK), F32),
            pltpu.VMEM((window, CHUNK), F32),
        ],
        micros=300,
    )
    mixed_across = swap(mixed_low, "mp", 2)
    mixed_core = swap(mixed_low, "mp", 1)
    cot_pieces = (
        cotangent,
        cot_across,
        swap(after(cotangent, mixed_core), "mp", 1),
        swap(after(cot_across, mixed_core), "mp", 1),
    )
    out_across = swap(after(out_weight, near), "mp", 2)
    out_pieces = (
        out_weight,
        out_across,
        swap(after(out_weight, mixed_core), "mp", 1),
        swap(after(out_across, mixed_core), "mp", 1),
    )
    bias_t, flipped_rows = call(
        flipped_kernel,
        [band, shape(bucket_rows.shape, jnp.int32)],
        [after(bucket_rows, mixed_low), table],
        smem=0,
        micros=3.0,
    )
    cot_all, d_act = call(
        cotangent_kernel,
        [shape((window, d), LOW), shape((window, units), F32)],
        [*cot_pieces, after(down_weight, mixed_across)],
        smem=0,
        micros=1.0,
    )
    mixed_pieces = (mixed_low, mixed_across, mixed_core, swap(after(mixed_across, bias_t), "mp", 1))
    second, hidden, act, d_gate, d_up, second_send, second_keep, gain_two_part = call(
        feed_kernel,
        [shape((window, d), LOW), shape((half, d), F32)]
        + [shape((window, units), LOW)] * 3
        + [shape((half, d), LOW), shape((half, d), F32), shape((1, d), F32)],
        [info, x_all, *mixed_pieces, *out_pieces, d_act, gain_two, gate_weight, up_weight],
        micros=5.0,
    )
    (second_sum,) = call(
        functools.partial(sum_kernel, count=1, small=0),
        [shape((half, d), LOW)],
        [second_keep, swap(second_send, "mp", 1)],
        smem=0,
        micros=1.0,
    )
    second_other = swap(second_sum, "mp", 2)
    rows = d + units // 2 + units // 4
    gate_send, gate_keep, up_send, up_keep = call(
        feed_grad_kernel,
        [shape((rows // 2, units), LOW)] * 4,
        [info, after(second, second_sum), d_gate, d_up, act, cot_all],
        scratch=[pltpu.VMEM((rows, units), LOW)] * 2,
        micros=3.0,
    )
    feed_sums = Sums(info, rank, (order_one, order_two), (gate_send, up_send), (gate_keep, up_keep))
    feed_send, feed_keep = call(
        feed_out_kernel, [shape((half, d), LOW)] * 2, [after(act, gate_send), down_weight], smem=0, micros=30
    )
    feed_got = swap(feed_send, "mp", 1)
    second_other = after(second_other, feed_send)
    dh, branch_low = call(
        hidden_back_kernel,
        [shape((local, d), F32), shape((half, d), LOW)],
        [second_sum, second_other, hidden, cot_pieces[0], cot_pieces[1], gain_two],
        smem=0,
    )
    feed_own, feed_cross = call(
        feed_merge_kernel,
        [shape((local, d), LOW)] * 2,
        [after(feed_keep, branch_low), feed_got],
        smem=0,
        micros=100,
    )
    payload, stat_back, out_grad = call(
        mixed_back_kernel,
        [shape((window, 2 * CHUNK), LOW), stats, shape((width, d), LOW)],
        [info, after(branch_low, feed_cross), swap(branch_low, "mp", 1), out_weight, mixed, mixed_low, lse],
        scratch=[pltpu.VMEM((window, d), LOW), pltpu.VMEM((2 * CHUNK, d), LOW)],
    )
    payload_even = swap(payload, "dp", 1)
    payload_odd = swap_odd(payload)
    token = feed_sums.advance(payload)
    fold = pltpu.VMEM((heads, CHUNK, 2 * window), F32)
    d_queries, d_keys, d_values, table_part = call(
        own_back_kernel,
        [wide_rows, wide_rows, wide_rows, shape((heads, CHUNK), F32)],
        [after(queries, token), keys, values, payload, stat_back, bias_t, seg_col, seg_row, flipped_rows],
        scratch=[square_wide, square_wide, square_low, square_low, fold],
        smem=0,
        micros=200,
    )
    d_queries, table_part = call(
        far_back_kernel,
        [low_rows, shape((heads, CHUNK), F32)],
        [info, queries, keys_near, values_near, payload, stat_back, bias, bucket_rows, d_queries, table_part],
        scratch=[square_wide, square_wide, square_low, fold],
        micros=3.0,
    )
    one_send, one_keep, two_send, two_keep, first_send, first_keep, small = call(
        partner_back_kernel,
        [shape((width, d), LOW)] * 4
        + [shape((half + EXTRA, d), LOW), shape((half, d), F32), shape((EXTRA // 2, d), F32)],
        [
            info,
            keys,
            values,
            queries_near,
            payload_even,
            payload_odd,
            bias_t,
            d_keys,
            d_values,
            d_queries,
            normed,
            x_all,
            gain_one,
            wq,
            wk,
            wv,
            out_grad,
            gain_two_part,
        ],
        scratch=[pltpu.VMEM((window, 3 * width), LOW), square_wide, square_wide, square_low, square_low],
        micros=300,
    )
    token = feed_sums.advance(one_send, micros=300)
    joint_sums = Sums(info, rank, (order_one, order_two), (after(one_send, token), two_send), (one_keep, two_keep))
    first_send, first_own, small = call(
        first_merge_kernel,
        [shape((local + EXTRA, d), LOW), shape((local, d), LOW), shape((EXTRA // 2, d), F32)],
        [after(first_keep, token), swap(first_send, "mp", 1), small],
        smem=0,
        micros=1,
    )
    first_got = swap(first_send, "mp", 2)
    token = joint_sums.advance(first_send)
    input_grad, small = call(
        input_back_kernel,
        [shape((local, d), LOW), shape((EXTRA // 2, d), F32)],
        [first_own, first_got, inputs, after(dh, token), gain_one, small, table_part],
        smem=0,
        micros=1,
    )
    token = joint_sums.advance(small, small)
    token = feed_sums.advance(token)
    feed_got = swap(after(feed_cross, token), "mp", 2)
    token = joint_sums.advance(token, small, micros=1)
    token = feed_sums.advance(token)
    last = 2 * len(bits) - 1
    while joint_sums.step < last or feed_sums.step < last:
        if joint_sums.step < last:
            token = joint_sums.advance(token, small, micros=300)
        if feed_sums.step < last:
            token = feed_sums.advance(token)
    (layer_out,) = call(
        layer_out_kernel,
        [shape((local, d), LOW)],
        [after(hidden, token), feed_own, feed_got],
        smem=0,
        micros=40,
    )
    ready = feed_sums.pairs()
    gate_grad, up_grad, down_grad = call(
        feed_total_kernel,
        [shape((d, units), F32)] * 2 + [shape((units, d), F32)],
        [info, after(ready[0], layer_out), *ready[1:]],
        scratch=[pltpu.VMEM((rows, units), LOW)],
        micros=2.0,
    )
    ready = joint_sums.pairs()
    query_grad, key_grad, value_grad, out_total, gain_one_total, gain_two_total, table_total = call(
        attention_total_kernel,
        [shape((width, d), F32)] * 4 + [shape((d // CHUNK, CHUNK), F32)] * 2 + [shape((heads, buckets), F32)],
        [info, after(ready[0], down_grad), *ready[1:]],
        micros=2.0,
    )
    if not joint_sums.tiled:
        small = lax.psum(small, "dp")
        gain_one_total, gain_two_total = small[0].reshape(-1, CHUNK), small[1].reshape(-1, CHUNK)
        table_total = small[2 : 2 + heads, :buckets]
    return (
        layer_out,
        input_grad,
        gain_one_total.reshape(-1),
        query_grad.T,
        key_grad.T,
        value_grad.T,
        out_total,
        table_total.T,
        gain_two_total.reshape(-1),
        gate_grad,
        up_grad,
        down_grad,
    )


def solution(mesh):
    rows = P(("dp", "mp"), None)
    in_specs = (
        rows,
        P(),
        P(None, "mp"),
        P(None, "mp"),
        P(None, "mp"),
        P("mp", None),
        P(None, "mp"),
        P(),
        P(None, "mp"),
        P(None, "mp"),
        P("mp", None),
        P(),
        P(),
        rows,
    )
    out_specs = (
        rows,
        rows,
        P(),
        P(None, "mp"),
        P(None, "mp"),
        P(None, "mp"),
        P("mp", None),
        P(None, "mp"),
        P(),
        P(None, "mp"),
        P(None, "mp"),
        P("mp", None),
    )
    return jax.shard_map(
        per_device, mesh=mesh, in_specs=in_specs, out_specs=out_specs, check_vma=False
    )
```

```python
import functools

import jax
import jax.numpy as jnp
from jax import lax
from jax.experimental import pallas as pl
from jax.experimental.pallas import tpu as pltpu
from jax.sharding import PartitionSpec as P

HEAD = 64
LOW = jnp.bfloat16
F32 = jnp.float32
CHUNK = 128
SPAN = 2048
EXTRA = 16
NEG = -1e30
ROOT = 0.7978845608
CUBE = 0.044715
VMEM = pl.BlockSpec(memory_space=pltpu.VMEM)
SMEM = pl.BlockSpec(memory_space=pltpu.SMEM)
HBM = pl.BlockSpec(memory_space=pltpu.HBM)


def dot_nn(a, b):
    return lax.dot_general(a, b, (((1,), (0,)), ((), ())), preferred_element_type=F32)


def dot_nt(a, b):
    return lax.dot_general(a, b, (((1,), (1,)), ((), ())), preferred_element_type=F32)


def dot_tn(a, b):
    return lax.dot_general(a, b, (((0,), (0,)), ((), ())), preferred_element_type=F32)


def call(kernel, outs, ins, scratch=(), smem=1, hbm=0, micros=2.0, out_smem=0, limit=20):
    return pl.pallas_call(
        kernel,
        out_shape=outs,
        in_specs=[SMEM] * smem + [VMEM] * (len(ins) - smem - hbm) + [HBM] * hbm,
        out_specs=[SMEM] * out_smem + [VMEM] * (len(outs) - out_smem),
        scratch_shapes=list(scratch),
        cost_estimate=pl.CostEstimate(flops=int(micros * 2e7), bytes_accessed=0, transcendentals=0),
        compiler_params=pltpu.CompilerParams(vmem_limit_bytes=limit * 1024 * 1024),
    )(*ins)


def in_hbm(values):
    return pltpu.with_memory_space_constraint(values, pltpu.HBM)


def shape(dims, dtype):
    return jax.ShapeDtypeStruct(dims, dtype)


def head_lanes(width, h):
    lane = lax.broadcasted_iota(jnp.int32, (1, width), 1)
    return (lane >= h * HEAD) & (lane < (h + 1) * HEAD)


def keep_head(values, h):
    return jnp.where(head_lanes(values.shape[-1], h), values, jnp.zeros_like(values))


def rows_norm(values):
    return lax.rsqrt(jnp.mean(values * values, axis=-1, keepdims=True) + 1e-06)


def as_row(ref):
    return jnp.concatenate([ref[k : k + 1, :] for k in range(ref.shape[0])], axis=1)


def aligned(start):
    return pl.ds(pl.multiple_of(start, CHUNK), CHUNK)


def lay_bias(row, table_ref, target):
    heads, buckets = table_ref.shape
    which = lax.broadcasted_iota(jnp.int32, (buckets, SPAN), 0)
    onehot = (row == which).astype(F32)
    table = table_ref[...].T
    for h in range(heads):
        rows = jnp.sum(onehot * table[:, h : h + 1], axis=0, keepdims=True)
        count = 1
        while count < 8:
            rows = jnp.concatenate([rows, pltpu.roll(rows, count, 1)], axis=0)
            count *= 2
        target[h, 0:8, :] = rows
        while count < CHUNK:
            target[h, count : 2 * count, :] = pltpu.roll(target[h, 0:count, :], count, 1)
            count *= 2


def setup_kernel(
    spot,
    bucket_ref,
    segment_hbm,
    table_hbm,
    one_hbm,
    two_hbm,
    info,
    row_ref,
    col_ref,
    bias_ref,
    table_ref,
    one_ref,
    two_ref,
    segment_ref,
    sems,
    *,
    groups,
    first_bits,
):
    pairs = ((segment_hbm, segment_ref), (table_hbm, table_ref), (one_hbm, one_ref), (two_hbm, two_ref))
    copies = [pltpu.make_async_copy(a, b, sems.at[k]) for k, (a, b) in enumerate(pairs)]
    for copy in copies:
        copy.start()
    for copy in copies:
        copy.wait()
    rank, member = spot[0], spot[1]
    steps = row_ref.shape[1] // CHUNK
    rows = [segment_ref[pl.ds(rank * steps + k, 1), :] for k in range(steps)]
    lane = lax.broadcasted_iota(jnp.int32, (1, CHUNK), 1)

    def value(row, at):
        return jnp.max(jnp.where(lane == at, row, -1))

    before = segment_ref[pl.ds(jnp.maximum(rank * steps - 1, 0), 1), :]
    later = segment_ref[pl.ds(jnp.minimum((rank + 1) * steps, groups * steps - 1), 1), :]
    left = (value(before, CHUNK - 1) == value(rows[0], 0)) & (rank > 0)
    right = (value(later, 0) == value(rows[-1], CHUNK - 1)) & (rank < groups - 1)
    even = jnp.where(rank % 2 == 0, right.astype(jnp.int32), left.astype(jnp.int32))
    info[0] = member // 2
    info[1] = member % 2
    info[2] = left.astype(jnp.int32)
    info[3] = (left | right).astype(jnp.int32)
    info[4] = (rank >> first_bits[0]) & 1
    info[5] = (rank >> first_bits[1]) & 1
    info[6] = even
    info[7] = rank
    row = jnp.concatenate(rows, axis=1).astype(F32)
    row_ref[...] = row
    col_ref[...] = jnp.broadcast_to(row, (CHUNK, row.shape[1])).T
    lay_bias(row_of(bucket_ref, 0, bucket_ref.shape[0]), table_ref, bias_ref)


def row_of(ref, first, count):
    return jnp.concatenate([ref[pl.ds(first + k, 1), :] for k in range(count)], axis=1)


def flipped_kernel(bucket_ref, table_ref, bias_ref, flipped_ref):
    count = bucket_ref.shape[0]
    sub = lax.broadcasted_iota(jnp.int32, (CHUNK, CHUNK), 0)
    lane = lax.broadcasted_iota(jnp.int32, (CHUNK, CHUNK), 1)
    turned = dot_nn(bucket_ref[...].astype(F32).astype(LOW), (sub + lane == CHUNK - 1).astype(F32).astype(LOW))
    row = jnp.concatenate([turned[k : k + 1, :] for k in reversed(range(count))], axis=1)
    row = pltpu.roll(row, 1, 1).astype(jnp.int32)
    flipped_ref[...] = jnp.concatenate([row[:, k * CHUNK : (k + 1) * CHUNK] for k in range(count)], axis=0)
    lay_bias(row, table_ref, bias_ref)


def near_kernel(info, even_ref, odd_ref, out_ref):
    out_ref[...] = jnp.where(info[6] == 1, even_ref[...], odd_ref[...])


def fold_diagonals(tile):
    rows, cols = tile.shape
    while rows > 1:
        rows //= 2
        tile = tile[:rows] + pltpu.roll(tile[rows:], cols - rows, 1)
    return tile


def pack_columns(columns, offset=0, base=None, width=CHUNK):
    rows = columns[0].shape[0]
    lane = lax.broadcasted_iota(jnp.int32, (rows, width), 1)
    out = jnp.zeros((rows, width), F32) if base is None else base
    for k, column in enumerate(columns):
        out = jnp.where(lane == offset + k, column, out)
    return out


def by_head(packed, width):
    lane = lax.broadcasted_iota(jnp.int32, (packed.shape[0], width), 1)
    out = packed[:, 0:1]
    for h in range(1, width // HEAD):
        out = jnp.where(lane >= h * HEAD, packed[:, h : h + 1], out)
    return out


def place(y, c):
    return (2 * y + c, 2 * (1 - y) + c, 2 * y + 1 - c, 2 * (1 - y) + 1 - c)


def project(normed, rows, wq, wk, wv, q_ref, k_ref, v_ref):
    q_ref[rows, :] = (dot_nt(normed, wq[...]).astype(LOW).astype(F32) * HEAD**-0.5).astype(LOW)
    k_ref[rows, :] = dot_nt(normed, wk[...]).astype(LOW)
    v_ref[rows, :] = dot_nt(normed, wv[...]).astype(LOW)


def attend(q, keys, values, bias, first, seg_col, seg_row, scores_ref, probs_ref, acc_ref, top_ref, sum_ref):
    window, width = q.shape
    heads = width // HEAD
    for h in range(heads):
        scores_ref[h] = dot_nt(keep_head(q, h), keys)
    for h in range(heads):
        for a in range(window // CHUNK):
            rows = slice(a * CHUNK, (a + 1) * CHUNK)
            scores = scores_ref[h, rows, :] + bias[h, :, pl.ds(first - a * CHUNK, window)]
            if seg_col is not None:
                scores = jnp.where(seg_col[rows, 0:1] == seg_row[...], scores, NEG)
            top = jnp.max(scores, axis=-1, keepdims=True)
            weights = jnp.exp(scores - top)
            probs_ref[h, rows, :] = weights.astype(LOW)
            top_ref[rows, :] = pack_columns([top], h, top_ref[rows, :] if h else jnp.zeros((CHUNK, CHUNK), F32))
            total = jnp.sum(weights, axis=-1, keepdims=True)
            sum_ref[rows, :] = pack_columns([total], h, sum_ref[rows, :] if h else jnp.ones((CHUNK, CHUNK), F32))
    total = dot_nn(probs_ref[0], keep_head(values, 0))
    for h in range(1, heads):
        total = total + dot_nn(probs_ref[h], keep_head(values, h))
    acc_ref[...] = total


def own_kernel(
    info,
    x1,
    x2,
    x3,
    gain,
    bias,
    seg_col,
    seg_row,
    x_hbm,
    wq_hbm,
    wk_hbm,
    wv_hbm,
    x_all,
    normed_ref,
    q_ref,
    k_ref,
    v_ref,
    acc_ref,
    top_ref,
    sum_ref,
    wq,
    wk,
    wv,
    scores_ref,
    probs_ref,
    x0,
    sems,
):
    pairs = ((x_hbm, x0), (wq_hbm, wq), (wk_hbm, wk), (wv_hbm, wv))
    copies = [pltpu.make_async_copy(a, b, sems.at[k]) for k, (a, b) in enumerate(pairs)]
    for copy in copies:
        copy.start()
    spots = place(info[0], info[1])
    for piece, spot in zip((x1, x2, x3, x0), spots[1:] + spots[:1]):
        if piece is x0:
            copies[0].wait()
        rows = aligned(spot * CHUNK)
        low = piece[...]
        x_all[rows, :] = low
        wide = low.astype(F32)
        normed_ref[rows, :] = (wide * rows_norm(wide) * as_row(gain)).astype(LOW)
    for copy in copies[1:]:
        copy.wait()
    project(normed_ref[...], slice(None), wq, wk, wv, q_ref, k_ref, v_ref)
    attend(
        q_ref[...],
        k_ref[...],
        v_ref[...],
        bias,
        SPAN // 2,
        seg_col,
        seg_row,
        scores_ref,
        probs_ref,
        acc_ref,
        top_ref,
        sum_ref,
    )


def far_start(info, window):
    return pl.multiple_of(jnp.where(info[2] == 1, SPAN // 2 - window, SPAN // 2 + window), CHUNK)


def partner_kernel(
    info,
    x0,
    x1,
    x2,
    x3,
    gain,
    wq,
    wk,
    wv,
    bias,
    q_ref,
    acc_ref,
    top_ref,
    sum_ref,
    mixed_low,
    mixed_ref,
    lse_ref,
    qp_ref,
    kp_ref,
    vp_ref,
    normed_ref,
    scores_ref,
    probs_ref,
    acc_two,
    top_two,
    sum_two,
):
    window, width = q_ref.shape
    paired = info[3]

    @pl.when(paired == 1)
    def _():
        for piece, spot in zip((x0, x1, x2, x3), place(info[0], info[1])):
            wide = piece[...].astype(F32)
            normed_ref[aligned(spot * CHUNK), :] = (wide * rows_norm(wide) * as_row(gain)).astype(LOW)
        project(normed_ref[...], slice(None), wq, wk, wv, qp_ref, kp_ref, vp_ref)
        attend(
            q_ref[...],
            kp_ref[...],
            vp_ref[...],
            bias,
            far_start(info, window),
            None,
            None,
            scores_ref,
            probs_ref,
            acc_two,
            top_two,
            sum_two,
        )
        for a in range(window // CHUNK):
            rows = slice(a * CHUNK, (a + 1) * CHUNK)
            top = jnp.maximum(top_ref[rows, :], top_two[rows, :])
            one, two = jnp.exp(top_ref[rows, :] - top), jnp.exp(top_two[rows, :] - top)
            whole = sum_ref[rows, :] * one + sum_two[rows, :] * two
            inverse = 1.0 / whole
            mixed = acc_ref[rows, :] * by_head(one * inverse, width)
            mixed = mixed + acc_two[rows, :] * by_head(two * inverse, width)
            mixed_ref[rows, :] = mixed
            mixed_low[rows, :] = mixed.astype(LOW)
            lse_ref[rows, :] = top + jnp.log(whole)

    @pl.when(paired == 0)
    def _():
        qp_ref[...] = jnp.zeros_like(qp_ref)
        kp_ref[...] = jnp.zeros_like(kp_ref)
        vp_ref[...] = jnp.zeros_like(vp_ref)
        for a in range(window // CHUNK):
            rows = slice(a * CHUNK, (a + 1) * CHUNK)
            whole = sum_ref[rows, :]
            mixed = acc_ref[rows, :] * by_head(1.0 / whole, width)
            mixed_ref[rows, :] = mixed
            mixed_low[rows, :] = mixed.astype(LOW)
            lse_ref[rows, :] = top_ref[rows, :] + jnp.log(whole)


def cotangent_kernel(g0, g1, g2, g3, down_w, cot_ref, d_act_ref):
    for part, piece in enumerate((g2, g3, g0, g1)):
        cot_ref[part * CHUNK : (part + 1) * CHUNK, :] = piece[...]
    d_act_ref[...] = dot_nt(cot_ref[...], down_w[...])


def feed_kernel(
    info,
    x_all,
    m0,
    m1,
    m2,
    m3,
    o0,
    o1,
    o2,
    o3,
    d_act_ref,
    gain,
    gate_w,
    up_w,
    second_ref,
    hidden_ref,
    act_ref,
    dgate_ref,
    dup_ref,
    send_ref,
    keep_ref,
    gain_ref,
):
    y, c = info[0], info[1]
    half = 2 * CHUNK
    gain_sum = jnp.zeros((1, x_all.shape[1]), F32)
    for part, core in enumerate((1 - c, c)):
        rows = slice(part * half, (part + 1) * half)
        spots = (aligned((2 * y + core) * CHUNK), aligned((2 * (1 - y) + core) * CHUNK))

        def pick(ref):
            return jnp.concatenate([ref[spots[0], :], ref[spots[1], :]], axis=0)

        hidden = pick(x_all).astype(F32)
        branch = dot_nn(pick(m0), o0[...])
        for m, o in ((m1, o1), (m2, o2), (m3, o3)):
            branch = branch + dot_nn(pick(m), o[...])
        hidden = hidden + branch
        if part == 1:
            hidden_ref[...] = hidden
        unit = hidden * rows_norm(hidden)
        second = (unit * as_row(gain)).astype(LOW)
        second_ref[rows, :] = second
        gate = dot_nn(second, gate_w[...])
        up = dot_nn(second, up_w[...])
        d_act = d_act_ref[rows, :]
        square = gate * gate
        tanh = jnp.tanh(ROOT * gate * (1.0 + CUBE * square))
        low_half = 0.5 * (1.0 + tanh)
        gelu = gate * low_half
        slope = low_half + 0.5 * gate * (1.0 - tanh * tanh) * (ROOT * (1.0 + 3.0 * CUBE * square))
        act_ref[rows, :] = (gelu * up).astype(LOW)
        d_gate = (d_act * up * slope).astype(LOW)
        d_up = (d_act * gelu).astype(LOW)
        dgate_ref[rows, :] = d_gate
        dup_ref[rows, :] = d_up
        d_second = dot_nt(d_gate, gate_w[...]) + dot_nt(d_up, up_w[...])
        gain_sum = gain_sum + jnp.sum(d_second * unit, axis=0, keepdims=True)
        if part == 0:
            send_ref[...] = d_second.astype(LOW)
        else:
            keep_ref[...] = d_second
    gain_ref[...] = gain_sum


def feed_grad_kernel(
    info, second_ref, dgate_ref, dup_ref, act_ref, cot_ref, one_send, one_keep, two_send, two_keep, one_ref, two_ref
):
    d, units = second_ref.shape[1], dgate_ref.shape[1]
    one_ref[:d, :] = dot_tn(second_ref[...], dgate_ref[...]).astype(LOW)
    two_ref[:d, :] = dot_tn(second_ref[...], dup_ref[...]).astype(LOW)
    down = dot_tn(act_ref[...], cot_ref[...]).astype(LOW)
    half = units // 2
    quarter = half // 2
    for k, target in enumerate((one_ref, two_ref)):
        target[d : d + half, :] = down[k * half : (k + 1) * half, :units]
        for side in (0, 1):
            rows = slice(k * half + side * quarter, k * half + (side + 1) * quarter)
            target[d + half :, side * (units // 2) : (side + 1) * (units // 2)] = down[rows, units:]
    for source, side, send, keep in ((one_ref, info[4], one_send, one_keep), (two_ref, info[5], two_send, two_keep)):
        rows = send.shape[0]
        send[...] = source[pl.ds(pl.multiple_of((1 - side) * rows, 16), rows), :]
        keep[...] = source[pl.ds(pl.multiple_of(side * rows, 16), rows), :]


def feed_out_kernel(act_ref, down_w, send_ref, keep_ref):
    half = send_ref.shape[0]
    send_ref[...] = dot_nn(act_ref[:half, :], down_w[...]).astype(LOW)
    keep_ref[...] = dot_nn(act_ref[half:, :], down_w[...]).astype(LOW)


def feed_total_kernel(info, one, one_got, two, two_got, gate_ref, up_ref, down_ref, full_ref):
    d, units = gate_ref.shape
    half = units // 2
    quarter = half // 2
    parts = ((one, one_got, info[4], gate_ref), (two, two_got, info[5], up_ref))
    for k, (mine, got, side, target) in enumerate(parts):
        rows = mine.shape[0]
        full_ref[pl.ds(pl.multiple_of(side * rows, 16), rows), :] = mine[...]
        full_ref[pl.ds(pl.multiple_of((1 - side) * rows, 16), rows), :] = got[...]
        target[...] = full_ref[:d, :].astype(F32)
        down_ref[k * half : (k + 1) * half, :units] = full_ref[d : d + half, :].astype(F32)
        for part in (0, 1):
            rows = slice(k * half + part * quarter, k * half + (part + 1) * quarter)
            down_ref[rows, units:] = full_ref[d + half :, part * (units // 2) : (part + 1) * (units // 2)].astype(F32)


def feed_merge_kernel(keep_ref, got_ref, own_ref, send_ref):
    local = own_ref.shape[0]
    total = (keep_ref[...].astype(F32) + got_ref[...].astype(F32)).astype(LOW)
    own_ref[...] = total[:local, :]
    send_ref[...] = total[local:, :]


def layer_out_kernel(hidden_ref, own_ref, got_ref, out_ref):
    local = out_ref.shape[0]
    out_ref[...] = (hidden_ref[:local, :] + (own_ref[...].astype(F32) + got_ref[...].astype(F32))).astype(LOW)


def hidden_back_kernel(sum_ref, other_ref, hidden_ref, g0, g1, gain, dh_ref, low_ref):
    for part, cot in enumerate((g0, g1)):
        rows = slice(part * CHUNK, (part + 1) * CHUNK)
        flip = slice((1 - part) * CHUNK, (2 - part) * CHUNK)
        d_second = sum_ref[rows, :].astype(F32) + other_ref[flip, :].astype(F32)
        hidden = hidden_ref[rows, :]
        inverse = rows_norm(hidden)
        unit = hidden * inverse
        scaled = d_second * as_row(gain)
        dh = cot[...].astype(F32) + inverse * (scaled - unit * jnp.mean(unit * scaled, axis=-1, keepdims=True))
        low_ref[rows, :] = dh.astype(LOW)
        if part == 0:
            dh_ref[...] = dh


def mixed_back_kernel(
    info, pair_own, pair_other, out_w, mixed_ref, mixed_low, lse_ref, payload_ref, stat_ref, grad_ref, branch_ref, pad_ref
):
    width = mixed_ref.shape[1]
    heads = width // HEAD
    pieces = (pair_own[:CHUNK, :], pair_own[CHUNK:, :], pair_other[:CHUNK, :], pair_other[CHUNK:, :])
    for piece, spot in zip(pieces, place(info[0], info[1])):
        branch_ref[aligned(spot * CHUNK), :] = piece
    pad_ref[:width, :] = out_w[...]
    pad_ref[width:, :] = jnp.zeros((pad_ref.shape[0] - width, pad_ref.shape[1]), LOW)
    d_all = dot_nt(branch_ref[...], pad_ref[...]).astype(LOW).astype(F32)
    for a in range(d_all.shape[0] // CHUNK):
        rows = slice(a * CHUNK, (a + 1) * CHUNK)
        d_mixed = d_all[rows, :]
        product = d_mixed[:, :width] * mixed_ref[rows, :]
        deltas = [jnp.sum(keep_head(product, h), axis=-1, keepdims=True) for h in range(heads)]
        stat = pack_columns(deltas, heads, lse_ref[rows, :])
        stat_ref[rows, :] = stat
        high = stat.astype(LOW).astype(F32)
        rest = stat - high
        lane = lax.broadcasted_iota(jnp.int32, (CHUNK, CHUNK), 1)
        skip = width % CHUNK
        high = pltpu.roll(high, skip, 1)
        rest = pltpu.roll(rest, skip + 2 * heads, 1)
        tail = jnp.where(lane < skip, d_mixed[:, width - skip : width - skip + CHUNK], high)
        tail = jnp.where(lane >= skip + 2 * heads, rest, tail)
        tail = jnp.where(lane >= skip + 4 * heads, 0.0, tail)
        payload_ref[rows, : width - skip] = d_mixed[:, : width - skip].astype(LOW)
        payload_ref[rows, width - skip :] = tail.astype(LOW)
    grad_ref[...] = dot_tn(mixed_low[...], branch_ref[...]).astype(LOW)


def recall_kernel(
    info, q_ref, k_ref, qp_ref, kp_ref, lse_ref, bias, bias_t, seg_col, seg_row, own_ref, far_ref, near_ref
):
    window, width = q_ref.shape
    heads = width // HEAD
    queries, keys = q_ref[...], k_ref[...]
    for h in range(heads):
        own_ref[h] = dot_nt(keep_head(keys, h), queries)
    lse = lse_ref[...].T
    for h in range(heads):
        for a in range(window // CHUNK):
            rows = slice(a * CHUNK, (a + 1) * CHUNK)
            start = SPAN // 2 - a * CHUNK
            scores = own_ref[h, rows, :] + bias_t[h, :, start : start + window]
            scores = jnp.where(seg_col[rows, 0:1] == seg_row[...], scores, NEG)
            own_ref[h, rows, :] = jnp.exp(scores - lse[h : h + 1, :])

    @pl.when(info[3] == 1)
    def _():
        first = far_start(info, window)
        for h in range(heads):
            far_ref[h] = dot_nt(keep_head(queries, h), kp_ref[...])
            near_ref[h] = dot_nt(keep_head(keys, h), qp_ref[...])
        for h in range(heads):
            for a in range(window // CHUNK):
                rows = slice(a * CHUNK, (a + 1) * CHUNK)
                spot = pl.ds(pl.multiple_of(first - a * CHUNK, CHUNK), window)
                far_ref[h, rows, :] = jnp.exp(far_ref[h, rows, :] + bias[h, :, spot] - lse_ref[rows, h : h + 1])
                near_ref[h, rows, :] += bias_t[h, :, spot]


def bend(weights_of, products_ref, probs_ref, ds_ref, h, delta_of, fold_ref):
    window = products_ref.shape[1]
    steps = window // CHUNK
    for a in range(steps):
        rows = slice(a * CHUNK, (a + 1) * CHUNK)
        weights = weights_of(rows)
        d_scores = weights * (products_ref[h, rows, :] - delta_of(rows))
        ds_ref[h, rows, :] = d_scores.astype(LOW)
        if probs_ref is not None:
            probs_ref[h, rows, :] = weights.astype(LOW)
        if fold_ref is not None:
            at = (steps - a) * CHUNK
            if a == 0:
                fold_ref[h, :, :at] = jnp.zeros((CHUNK, at), F32)
                fold_ref[h, :, at:] = d_scores
            else:
                if a == steps - 1:
                    fold_ref[h, :, :CHUNK] = jnp.zeros((CHUNK, CHUNK), F32)
                fold_ref[h, :, at : at + window] += d_scores


def table_kernel(info, near_fold, far_fold, flipped_ref, bucket_ref, table_ref):
    window = near_fold.shape[2] // 2
    table_ref[...] = table_sums(near_fold, flipped_ref, SPAN // 2 - window, table_ref)

    @pl.when(info[3] == 1)
    def _():
        table_ref[...] += table_sums(far_fold, bucket_ref, far_start(info, window) - window, table_ref)


def table_sums(fold_ref, bucket_ref, start, table_ref):
    heads, buckets = table_ref.shape
    reach = fold_ref.shape[2]
    row = row_of(bucket_ref, start // CHUNK, reach // CHUNK)
    onehot = row == lax.broadcasted_iota(jnp.int32, (buckets, reach), 0)
    columns = []
    for h in range(heads):
        folded = fold_diagonals(fold_ref[h])
        columns.append(jnp.sum(jnp.where(onehot, folded, 0.0), axis=1, keepdims=True))
    return pack_columns(columns).T[:heads, :]


def own_back_kernel(
    own_ref,
    q_ref,
    k_ref,
    v_ref,
    payload_ref,
    stat_ref,
    dq_ref,
    dk_ref,
    dv_ref,
    fold_ref,
    products_ref,
    probs_ref,
    ds_ref,
):
    window, width = q_ref.shape
    heads = width // HEAD
    queries, keys, values = q_ref[...], k_ref[...], v_ref[...]
    back = payload_ref[:, :width]
    stat = stat_ref[...].T
    for h in range(heads):
        products_ref[h] = dot_nt(keep_head(values, h), back)
    for h in range(heads):
        delta = stat[heads + h : heads + h + 1, :]
        bend(lambda rows: own_ref[h, rows, :], products_ref, probs_ref, ds_ref, h, lambda rows: delta, fold_ref)
    d_queries = dot_tn(ds_ref[0], keep_head(keys, 0))
    d_keys = dot_nn(ds_ref[0], keep_head(queries, 0))
    d_values = dot_nn(probs_ref[0], keep_head(back, 0))
    for h in range(1, heads):
        d_queries = d_queries + dot_tn(ds_ref[h], keep_head(keys, h))
        d_keys = d_keys + dot_nn(ds_ref[h], keep_head(queries, h))
        d_values = d_values + dot_nn(probs_ref[h], keep_head(back, h))
    dq_ref[...] = d_queries
    dk_ref[...] = d_keys
    dv_ref[...] = d_values


def far_back_kernel(
    info, far_ref, kp_ref, vp_ref, payload_ref, stat_ref, dq_in, dq_ref, fold_ref, products_ref, ds_ref
):
    width = kp_ref.shape[1]
    heads = width // HEAD

    @pl.when(info[3] == 1)
    def _():
        keys, values = kp_ref[...], vp_ref[...]
        back = payload_ref[:, :width]
        for h in range(heads):
            products_ref[h] = dot_nt(keep_head(back, h), values)
        for h in range(heads):
            bend(
                lambda rows: far_ref[h, rows, :],
                products_ref,
                None,
                ds_ref,
                h,
                lambda rows: stat_ref[rows, heads + h : heads + h + 1],
                fold_ref,
            )
        d_queries = dq_in[...]
        for h in range(heads):
            d_queries = d_queries + dot_nn(ds_ref[h], keep_head(keys, h))
        dq_ref[...] = (d_queries * HEAD**-0.5).astype(LOW)

    @pl.when(info[3] == 0)
    def _():
        dq_ref[...] = (dq_in[...] * HEAD**-0.5).astype(LOW)


def partner_back_kernel(
    info,
    near_ref,
    v_ref,
    qp_ref,
    from_even,
    from_odd,
    dk_in,
    dv_in,
    dq_ref,
    normed_ref,
    x_all,
    gain,
    wq,
    wk,
    wv,
    grad_in,
    gain_in,
    one_send,
    one_keep,
    two_send,
    two_keep,
    send_ref,
    keep_ref,
    small_ref,
    d_all,
    products_ref,
    probs_ref,
    ds_ref,
):
    window, width = v_ref.shape
    heads = width // HEAD
    y, c = info[0], info[1]
    d_all[:, :width] = dq_ref[...]

    @pl.when(info[3] == 1)
    def _():
        payload = jnp.where(info[6] == 1, from_even[...], from_odd[...])
        queries, values = qp_ref[...], v_ref[...]
        back = payload[:, :width]
        columns = payload[:, payload.shape[1] - CHUNK :].astype(F32).T
        skip = width % CHUNK
        for h in range(heads):
            products_ref[h] = dot_nt(keep_head(values, h), back)
        for h in range(heads):
            at = skip + h
            lse = columns[at : at + 1, :] + columns[at + 2 * heads : at + 2 * heads + 1, :]
            at = at + heads
            delta = columns[at : at + 1, :] + columns[at + 2 * heads : at + 2 * heads + 1, :]
            bend(
                lambda rows: jnp.exp(near_ref[h, rows, :] - lse),
                products_ref,
                probs_ref,
                ds_ref,
                h,
                lambda rows: delta,
                None,
            )
        d_keys, d_values = dk_in[...], dv_in[...]
        for h in range(heads):
            d_keys = d_keys + dot_nn(ds_ref[h], keep_head(queries, h))
            d_values = d_values + dot_nn(probs_ref[h], keep_head(back, h))
        d_all[:, width : 2 * width] = d_keys.astype(LOW)
        d_all[:, 2 * width :] = d_values.astype(LOW)

    @pl.when(info[3] == 0)
    def _():
        d_all[:, width : 2 * width] = dk_in[...].astype(LOW)
        d_all[:, 2 * width :] = dv_in[...].astype(LOW)

    joint = dot_tn(d_all[...], normed_ref[...]).astype(LOW)
    halves = (joint[:width, :], joint[width : 2 * width, :])
    for side in (0, 1):

        @pl.when(info[4] == side)
        def _():
            one_keep[...] = halves[side]
            one_send[...] = halves[1 - side]

    halves_two = (joint[2 * width :, :], grad_in[...])
    for side in (0, 1):

        @pl.when(info[5] == side)
        def _():
            two_keep[...] = halves_two[side]
            two_send[...] = halves_two[1 - side]

    gain_sum = jnp.zeros((1, x_all.shape[1]), F32)
    for part, core in enumerate((1 - c, c)):
        spots = (aligned((2 * y + core) * CHUNK), aligned((2 * (1 - y) + core) * CHUNK))
        mine = jnp.concatenate([d_all[spots[0], :], d_all[spots[1], :]], axis=0)
        d_normed = dot_nn(mine[:, :width], wq[...])
        d_normed = d_normed + dot_nn(mine[:, width : 2 * width], wk[...])
        d_normed = d_normed + dot_nn(mine[:, 2 * width :], wv[...])
        wide = jnp.concatenate([x_all[spots[0], :], x_all[spots[1], :]], axis=0).astype(F32)
        gain_sum = gain_sum + jnp.sum(d_normed * (wide * rows_norm(wide)), axis=0, keepdims=True)
        if part == 0:
            send_ref[: 2 * CHUNK, :] = d_normed.astype(LOW)
        else:
            keep_ref[...] = d_normed
    small = jnp.concatenate([gain_sum, gain_in[...], jnp.zeros((6, gain_sum.shape[1]), F32)], axis=0)
    small_ref[...] = small
    put_small(send_ref, 2 * CHUNK, small)


def put_small(target, start, small):
    high = small.astype(LOW).astype(F32)
    target[start : start + EXTRA, :] = jnp.concatenate([high, small - high], axis=0).astype(LOW)


def get_small(source, start):
    both = source[start : start + EXTRA, :].astype(F32)
    return both[: EXTRA // 2] + both[EXTRA // 2 :]


def first_merge_kernel(keep_ref, got_ref, small_in, send_ref, own_ref, small_ref):
    local = own_ref.shape[0]
    total = (keep_ref[...] + got_ref[: 2 * local, :].astype(F32)).astype(LOW)
    own_ref[...] = total[:local, :]
    send_ref[:local, :] = total[local:, :]
    small = small_in[...] + get_small(got_ref, 2 * local)
    small_ref[...] = small
    put_small(send_ref, local, small)


def input_back_kernel(own_ref, got_ref, x_ref, dh_ref, gain, small_in, table_ref, out_ref, small_ref):
    local = own_ref.shape[0]
    d_normed = own_ref[...].astype(F32) + got_ref[:local, :].astype(F32)
    wide = x_ref[...].astype(F32)
    inverse = rows_norm(wide)
    unit = wide * inverse
    scaled = d_normed * as_row(gain)
    back = inverse * (scaled - unit * jnp.mean(unit * scaled, axis=-1, keepdims=True))
    out_ref[...] = (dh_ref[...] + back).astype(LOW)
    small_ref[...] = small_in[...] + get_small(got_ref, local)
    heads, buckets = table_ref.shape
    small_ref[2 : 2 + heads, :buckets] = table_ref[...]


def halve_kernel(info, *refs, bits):
    count = len(bits)
    for k, bit in enumerate(bits):
        keep, got = refs[2 * k], refs[2 * k + 1]
        send_ref, keep_ref = refs[2 * count + 2 * k], refs[2 * count + 2 * k + 1]
        half = send_ref.shape[0]
        side = (info[7] >> bit) & 1
        for first, target in ((1 - side, send_ref), (side, keep_ref)):
            rows = pl.ds(pl.multiple_of(first * half, 16), half)
            target[...] = (keep[rows, :].astype(F32) + got[rows, :].astype(F32)).astype(LOW)


def sum_kernel(*refs, count, small):
    for k in range(count):
        keep, got = refs[2 * k], refs[2 * k + 1]
        target = refs[2 * count + small + k]
        rows = keep.shape[0]
        target[:rows, :] = (keep[...].astype(F32) + got[...].astype(F32)).astype(LOW)
        if small and k == 0:
            put_small(target, rows, refs[2 * count][...])


def pair_kernel(*refs, count, small):
    for k in range(count):
        mine, got, target = refs[2 * k], refs[2 * k + 1], refs[2 * count + k]
        extra = EXTRA if small and k == 0 else 0
        rows = mine.shape[0] - extra
        target[:rows, :] = (mine[:rows, :].astype(F32) + got[:rows, :].astype(F32)).astype(LOW)
        if extra:
            put_small(target, rows, get_small(mine, rows) + get_small(got, rows))


def double_kernel(info, *refs, bits, small):
    count = len(bits)
    for k, bit in enumerate(bits):
        mine, got, target = refs[2 * k], refs[2 * k + 1], refs[2 * count + k]
        extra = EXTRA if small and k == 0 else 0
        rows = mine.shape[0] - extra
        side = (info[7] >> bit) & 1
        target[pl.ds(pl.multiple_of(side * rows, 16), rows), :] = mine[:rows, :]
        target[pl.ds(pl.multiple_of((1 - side) * rows, 16), rows), :] = got[:rows, :]
        if extra:
            put_small(target, 2 * rows, get_small(mine, rows) + get_small(got, rows))


def attention_total_kernel(
    info, one, one_got, two, two_got, q_ref, k_ref, v_ref, out_ref, gain_one_ref, gain_two_ref, table_ref
):
    rows = q_ref.shape[0]
    first = info[4] == 0
    mine, got = one[:rows, :], one_got[:rows, :]
    q_ref[...] = jnp.where(first, mine, got).astype(F32)
    k_ref[...] = jnp.where(first, got, mine).astype(F32)
    first = info[5] == 0
    v_ref[...] = jnp.where(first, two[...], two_got[...]).astype(F32)
    out_ref[...] = jnp.where(first, two_got[...], two[...]).astype(F32)
    if one.shape[0] > rows:
        small = get_small(one, rows) + get_small(one_got, rows)
        for k in range(gain_one_ref.shape[0]):
            columns = slice(k * CHUNK, (k + 1) * CHUNK)
            gain_one_ref[k : k + 1, :] = small[0:1, columns]
            gain_two_ref[k : k + 1, :] = small[1:2, columns]
        heads, buckets = table_ref.shape
        table_ref[...] = small[2 : 2 + heads, :buckets]
    else:
        gain_one_ref[...] = jnp.zeros_like(gain_one_ref)
        gain_two_ref[...] = jnp.zeros_like(gain_two_ref)
        table_ref[...] = jnp.zeros_like(table_ref)


def swap(values, axis, bit):
    return lax.ppermute(values, axis, [(i, i ^ bit) for i in range(lax.axis_size(axis))])


def swap_odd(values):
    ends = range(1, lax.axis_size("dp") - 1, 2)
    return lax.ppermute(values, "dp", [(i, i + 1) for i in ends] + [(i + 1, i) for i in ends])


def after(values, *others):
    return lax.optimization_barrier((values, *others))[0]


def spread(own, across=None):
    across = swap(own, "mp", 2) if across is None else across
    return own, across, swap(own, "mp", 1), swap(across, "mp", 1)


def cut(values, first, count):
    return lax.dynamic_slice_in_dim(values, first, count)


class Sums:
    def __init__(self, info, rank, orders, sends, keeps):
        self.info, self.rank, self.orders, self.keeps = info, rank, orders, list(keeps)
        self.bits = len(orders[0])
        self.tiled = all((k.shape[0] >> (self.bits - 2)) % 16 == 0 for k in keeps)
        self.step, self.small = 0, None
        self.exchange(sends)

    def exchange(self, sends):
        done = self.step if self.step < self.bits else 2 * self.bits - 2 - self.step
        self.now = [order[done] for order in self.orders]
        self.gots = [swap(v, "dp", 1 << bit) for v, bit in zip(sends, self.now)]
        self.step += 1

    def pairs(self):
        return [v for pair in zip(self.keeps, self.gots) for v in pair]

    def advance(self, token, small=None, micros=1):
        self.keeps[0] = after(self.keeps[0], token)
        count = len(self.keeps)
        if self.step < self.bits - 1:
            bits = [order[self.step] for order in self.orders]
            halves = [v.shape[0] // 2 for v in self.keeps]
            if self.tiled:
                out = call(
                    functools.partial(halve_kernel, bits=bits),
                    [shape((h, v.shape[1]), LOW) for h, v in zip(halves, self.keeps) for _ in range(2)],
                    [self.info, *self.pairs()],
                    micros=micros,
                )
                sends, self.keeps = out[0::2], list(out[1::2])
            else:
                sends, keeps = [], []
                for k, g, h, bit in zip(self.keeps, self.gots, halves, bits):
                    side = (self.rank >> bit) & 1
                    total = (k.astype(F32) + g.astype(F32)).astype(LOW)
                    sends.append(cut(total, (1 - side) * h, h))
                    keeps.append(cut(total, side * h, h))
                self.keeps = keeps
        elif self.step == self.bits - 1:
            if self.tiled:
                self.small = small
                rows = [v.shape[0] for v in self.keeps]
                if small is not None:
                    rows[0] += EXTRA
                sends = call(
                    functools.partial(sum_kernel, count=count, small=int(small is not None)),
                    [shape((r, v.shape[1]), LOW) for r, v in zip(rows, self.keeps)],
                    self.pairs() + ([small] if small is not None else []),
                    smem=0,
                    micros=micros,
                )
            else:
                sends = [(k.astype(F32) + g.astype(F32)).astype(LOW) for k, g in zip(self.keeps, self.gots)]
            self.keeps = list(sends)
        elif self.step == self.bits:
            if self.tiled:
                sends = call(
                    functools.partial(pair_kernel, count=count, small=self.small is not None),
                    [shape(v.shape, LOW) for v in self.keeps],
                    self.pairs(),
                    smem=0,
                    micros=micros,
                )
            else:
                sends = [(k.astype(F32) + g.astype(F32)).astype(LOW) for k, g in zip(self.keeps, self.gots)]
            self.keeps = list(sends)
        else:
            has = self.small is not None
            if self.tiled:
                rows = [2 * v.shape[0] for v in self.keeps]
                if has:
                    rows[0] -= EXTRA
                sends = call(
                    functools.partial(double_kernel, bits=self.now, small=has),
                    [shape((r, v.shape[1]), LOW) for r, v in zip(rows, self.keeps)],
                    [self.info, *self.pairs()],
                    micros=micros,
                )
            else:
                sends = []
                for k, g, bit in zip(self.keeps, self.gots, self.now):
                    side = (self.rank >> bit) & 1
                    sends.append(
                        jnp.where(side == 0, jnp.concatenate([k, g], axis=0), jnp.concatenate([g, k], axis=0))
                    )
            self.keeps = list(sends)
        self.exchange(sends)
        return sends[0]


def per_device(
    inputs,
    attention_gain,
    query_weight,
    key_weight,
    value_weight,
    out_weight,
    bias_table,
    feedforward_gain,
    gate_weight,
    up_weight,
    down_weight,
    segment,
    bucket,
    cotangent,
):
    parts = lax.axis_size("mp")
    groups = lax.axis_size("dp")
    local, d = inputs.shape
    window = local * parts
    width = query_weight.shape[1]
    heads = width // HEAD
    units = gate_weight.shape[1]
    buckets = bias_table.shape[0]
    half = 2 * local
    rank = lax.axis_index("dp")
    member = lax.axis_index("mp")
    bits = list(range(groups.bit_length() - 1))
    order_one = bits
    order_two = [bits[1], bits[0]] + bits[2:]

    x_across = swap(inputs, "mp", 2)
    from_even = swap(inputs, "dp", 1)
    from_odd = swap_odd(inputs)

    spot = jnp.stack([rank, member]).astype(jnp.int32)
    edge = jnp.full((1,), -1, jnp.int32)
    bucket_rows = jnp.concatenate([edge, bucket]).reshape(-1, CHUNK)
    table = bias_table.T
    gain_one, gain_two = attention_gain.reshape(-1, CHUNK), feedforward_gain.reshape(-1, CHUNK)
    band = shape((heads, CHUNK, SPAN), F32)
    segments = segment.reshape(-1, CHUNK)
    info, seg_row, seg_col, bias, table, gain_one, gain_two = call(
        functools.partial(setup_kernel, groups=groups, first_bits=(order_one[0], order_two[0])),
        [shape((8,), jnp.int32), shape((1, window), F32), shape((window, CHUNK), F32), band]
        + [shape(v.shape, F32) for v in (table, gain_one, gain_two)],
        [spot, bucket_rows] + [in_hbm(v) for v in (segments, table, gain_one, gain_two)],
        scratch=[pltpu.VMEM(segments.shape, jnp.int32), pltpu.SemaphoreType.DMA((4,))],
        hbm=4,
        out_smem=1,
        micros=3.0,
    )
    cot_across = swap(cotangent, "mp", 2)
    (near,) = call(near_kernel, [shape((local, d), LOW)], [info, after(from_even, x_across, cot_across), from_odd], micros=0.5)
    near_across = swap(near, "mp", 2)
    near_core = swap(near, "mp", 1)
    x_pieces = (inputs, x_across, swap(inputs, "mp", 1), swap(after(x_across, near_core), "mp", 1))

    low_rows = shape((window, width), LOW)
    wide_rows = shape((window, width), F32)
    stats = shape((window, CHUNK), F32)
    square_wide = pltpu.VMEM((heads, window, window), F32)
    square_low = pltpu.VMEM((heads, window, window), LOW)
    weight = shape((width, d), LOW)
    x_all, normed, queries, keys, values, acc, top, total, wq, wk, wv = call(
        own_kernel,
        [shape((window, d), LOW)] * 2 + [low_rows] * 3 + [wide_rows, stats, stats] + [weight] * 3,
        [info, x_across, *x_pieces[2:], gain_one, bias, seg_col, seg_row]
        + [in_hbm(v) for v in (inputs, query_weight.T, key_weight.T, value_weight.T)],
        scratch=[square_wide, square_low, pltpu.VMEM((local, d), LOW), pltpu.SemaphoreType.DMA((4,))],
        hbm=4,
        micros=5.0,
    )
    near_pieces = (near, near_across, near_core, swap(after(near_across, acc), "mp", 1))
    mixed_low, mixed, lse, queries_near, keys_near, values_near = call(
        partner_kernel,
        [low_rows, wide_rows, stats] + [low_rows] * 3,
        [info, *near_pieces, gain_one, wq, wk, wv, bias, queries, acc, top, total],
        scratch=[
            pltpu.VMEM((window, d), LOW),
            square_wide,
            square_low,
            pltpu.VMEM((window, width), F32),
            pltpu.VMEM((window, CHUNK), F32),
            pltpu.VMEM((window, CHUNK), F32),
        ],
        micros=300,
    )
    mixed_across = swap(mixed_low, "mp", 2)
    mixed_core = swap(mixed_low, "mp", 1)
    cot_pieces = (
        cotangent,
        cot_across,
        swap(after(cotangent, mixed_core), "mp", 1),
        swap(after(cot_across, mixed_core), "mp", 1),
    )
    out_across = swap(after(out_weight, near), "mp", 2)
    out_pieces = (
        out_weight,
        out_across,
        swap(after(out_weight, mixed_core), "mp", 1),
        swap(after(out_across, mixed_core), "mp", 1),
    )
    bias_t, flipped_rows = call(
        flipped_kernel,
        [band, shape(bucket_rows.shape, jnp.int32)],
        [after(bucket_rows, mixed_low), table],
        smem=0,
        micros=3.0,
    )
    cot_all, d_act = call(
        cotangent_kernel,
        [shape((window, d), LOW), shape((window, units), F32)],
        [*cot_pieces, after(down_weight, mixed_across)],
        smem=0,
        micros=1.0,
    )
    mixed_pieces = (mixed_low, mixed_across, mixed_core, swap(after(mixed_across, bias_t), "mp", 1))
    second, hidden, act, d_gate, d_up, second_send, second_keep, gain_two_part = call(
        feed_kernel,
        [shape((window, d), LOW), shape((half, d), F32)]
        + [shape((window, units), LOW)] * 3
        + [shape((half, d), LOW), shape((half, d), F32), shape((1, d), F32)],
        [info, x_all, *mixed_pieces, *out_pieces, d_act, gain_two, gate_weight, up_weight],
        micros=5.0,
    )
    (second_sum,) = call(
        functools.partial(sum_kernel, count=1, small=0),
        [shape((half, d), LOW)],
        [second_keep, swap(second_send, "mp", 1)],
        smem=0,
        micros=1.0,
    )
    second_other = swap(second_sum, "mp", 2)
    rows = d + units // 2 + units // 4
    gate_send, gate_keep, up_send, up_keep = call(
        feed_grad_kernel,
        [shape((rows // 2, units), LOW)] * 4,
        [info, after(second, second_sum), d_gate, d_up, act, cot_all],
        scratch=[pltpu.VMEM((rows, units), LOW)] * 2,
        micros=3.0,
    )
    feed_sums = Sums(info, rank, (order_one, order_two), (gate_send, up_send), (gate_keep, up_keep))
    feed_send, feed_keep = call(
        feed_out_kernel, [shape((half, d), LOW)] * 2, [after(act, gate_send), down_weight], smem=0, micros=30
    )
    feed_got = swap(feed_send, "mp", 1)
    block = shape((heads, window, window), F32)
    own_probs, far_probs, near_scores = call(
        recall_kernel,
        [block] * 3,
        [
            info,
            after(queries, feed_send),
            keys,
            queries_near,
            keys_near,
            lse,
            bias,
            bias_t,
            seg_col,
            seg_row,
        ],
        micros=1.0,
    )
    second_other = after(second_other, own_probs)
    dh, branch_low = call(
        hidden_back_kernel,
        [shape((local, d), F32), shape((half, d), LOW)],
        [second_sum, second_other, hidden, cot_pieces[0], cot_pieces[1], gain_two],
        smem=0,
    )
    feed_own, feed_cross = call(
        feed_merge_kernel,
        [shape((local, d), LOW)] * 2,
        [after(feed_keep, branch_low), feed_got],
        smem=0,
        micros=100,
    )
    payload, stat_back, out_grad = call(
        mixed_back_kernel,
        [shape((window, 2 * CHUNK), LOW), stats, shape((width, d), LOW)],
        [info, after(branch_low, feed_cross), swap(branch_low, "mp", 1), out_weight, mixed, mixed_low, lse],
        scratch=[pltpu.VMEM((window, d), LOW), pltpu.VMEM((2 * CHUNK, d), LOW)],
    )
    payload_even = swap(payload, "dp", 1)
    payload_odd = swap_odd(payload)
    token = feed_sums.advance(payload)
    fold = shape((heads, CHUNK, 2 * window), F32)
    d_queries, d_keys, d_values, near_fold = call(
        own_back_kernel,
        [wide_rows, wide_rows, wide_rows, fold],
        [own_probs, after(queries, token), keys, values, payload, stat_back],
        scratch=[square_wide, square_low, square_low],
        smem=0,
        micros=200,
    )
    d_queries, far_fold = call(
        far_back_kernel,
        [low_rows, fold],
        [info, far_probs, keys_near, values_near, payload, stat_back, d_queries],
        scratch=[square_wide, square_low],
        micros=3.0,
    )
    one_send, one_keep, two_send, two_keep, first_send, first_keep, small = call(
        partner_back_kernel,
        [shape((width, d), LOW)] * 4
        + [shape((half + EXTRA, d), LOW), shape((half, d), F32), shape((EXTRA // 2, d), F32)],
        [
            info,
            near_scores,
            values,
            queries_near,
            payload_even,
            payload_odd,
            d_keys,
            d_values,
            d_queries,
            normed,
            x_all,
            gain_one,
            wq,
            wk,
            wv,
            out_grad,
            gain_two_part,
        ],
        scratch=[pltpu.VMEM((window, 3 * width), LOW), square_wide, square_low, square_low],
        micros=300,
    )
    token = feed_sums.advance(one_send, micros=300)
    joint_sums = Sums(info, rank, (order_one, order_two), (after(one_send, token), two_send), (one_keep, two_keep))
    first_send, first_own, small = call(
        first_merge_kernel,
        [shape((local + EXTRA, d), LOW), shape((local, d), LOW), shape((EXTRA // 2, d), F32)],
        [after(first_keep, token), swap(first_send, "mp", 1), small],
        smem=0,
        micros=1,
    )
    first_got = swap(first_send, "mp", 2)
    token = joint_sums.advance(first_send)
    (table_part,) = call(
        table_kernel,
        [shape((heads, CHUNK), F32)],
        [info, after(near_fold, token), far_fold, flipped_rows, bucket_rows],
        micros=1.0,
    )
    input_grad, small = call(
        input_back_kernel,
        [shape((local, d), LOW), shape((EXTRA // 2, d), F32)],
        [first_own, first_got, inputs, after(dh, token), gain_one, small, table_part],
        smem=0,
        micros=1,
    )
    token = joint_sums.advance(small, small)
    token = feed_sums.advance(token)
    feed_got = swap(after(feed_cross, token), "mp", 2)
    token = joint_sums.advance(token, small, micros=1)
    token = feed_sums.advance(token)
    last = 2 * len(bits) - 1
    while joint_sums.step < last or feed_sums.step < last:
        if joint_sums.step < last:
            token = joint_sums.advance(token, small, micros=300)
        if feed_sums.step < last:
            token = feed_sums.advance(token)
    (layer_out,) = call(
        layer_out_kernel,
        [shape((local, d), LOW)],
        [after(hidden, token), feed_own, feed_got],
        smem=0,
        micros=40,
    )
    ready = feed_sums.pairs()
    gate_grad, up_grad, down_grad = call(
        feed_total_kernel,
        [shape((d, units), F32)] * 2 + [shape((units, d), F32)],
        [info, after(ready[0], layer_out), *ready[1:]],
        scratch=[pltpu.VMEM((rows, units), LOW)],
        micros=2.0,
    )
    ready = joint_sums.pairs()
    query_grad, key_grad, value_grad, out_total, gain_one_total, gain_two_total, table_total = call(
        attention_total_kernel,
        [shape((width, d), F32)] * 4 + [shape((d // CHUNK, CHUNK), F32)] * 2 + [shape((heads, buckets), F32)],
        [info, after(ready[0], down_grad), *ready[1:]],
        micros=2.0,
    )
    if not joint_sums.tiled:
        small = lax.psum(small, "dp")
        gain_one_total, gain_two_total = small[0].reshape(-1, CHUNK), small[1].reshape(-1, CHUNK)
        table_total = small[2 : 2 + heads, :buckets]
    return (
        layer_out,
        input_grad,
        gain_one_total.reshape(-1),
        query_grad.T,
        key_grad.T,
        value_grad.T,
        out_total,
        table_total.T,
        gain_two_total.reshape(-1),
        gate_grad,
        up_grad,
        down_grad,
    )


def solution(mesh):
    rows = P(("dp", "mp"), None)
    in_specs = (
        rows,
        P(),
        P(None, "mp"),
        P(None, "mp"),
        P(None, "mp"),
        P("mp", None),
        P(None, "mp"),
        P(),
        P(None, "mp"),
        P(None, "mp"),
        P("mp", None),
        P(),
        P(),
        rows,
    )
    out_specs = (
        rows,
        rows,
        P(),
        P(None, "mp"),
        P(None, "mp"),
        P(None, "mp"),
        P("mp", None),
        P(None, "mp"),
        P(),
        P(None, "mp"),
        P(None, "mp"),
        P("mp", None),
    )
    return jax.shard_map(
        per_device, mesh=mesh, in_specs=in_specs, out_specs=out_specs, check_vma=False
    )
```

```python
import functools

import jax
import jax.numpy as jnp
from jax import lax
from jax.experimental import pallas as pl
from jax.experimental.pallas import tpu as pltpu
from jax.sharding import PartitionSpec as P

HEAD = 64
LOW = jnp.bfloat16
F32 = jnp.float32
CHUNK = 128
SPAN = 2048
EXTRA = 16
NEG = -1e30
ROOT = 0.7978845608
CUBE = 0.044715
VMEM = pl.BlockSpec(memory_space=pltpu.VMEM)
SMEM = pl.BlockSpec(memory_space=pltpu.SMEM)
HBM = pl.BlockSpec(memory_space=pltpu.HBM)


def dot_nn(a, b):
    return lax.dot_general(a, b, (((1,), (0,)), ((), ())), preferred_element_type=F32)


def dot_nt(a, b):
    return lax.dot_general(a, b, (((1,), (1,)), ((), ())), preferred_element_type=F32)


def dot_tn(a, b):
    return lax.dot_general(a, b, (((0,), (0,)), ((), ())), preferred_element_type=F32)


def call(kernel, outs, ins, scratch=(), smem=1, hbm=0, micros=2.0, out_smem=0, limit=20):
    return pl.pallas_call(
        kernel,
        out_shape=outs,
        in_specs=[SMEM] * smem + [VMEM] * (len(ins) - smem - hbm) + [HBM] * hbm,
        out_specs=[SMEM] * out_smem + [VMEM] * (len(outs) - out_smem),
        scratch_shapes=list(scratch),
        cost_estimate=pl.CostEstimate(flops=int(micros * 2e7), bytes_accessed=0, transcendentals=0),
        compiler_params=pltpu.CompilerParams(vmem_limit_bytes=limit * 1024 * 1024),
    )(*ins)


def in_hbm(values):
    return pltpu.with_memory_space_constraint(values, pltpu.HBM)


def shape(dims, dtype):
    return jax.ShapeDtypeStruct(dims, dtype)


def head_lanes(width, h):
    lane = lax.broadcasted_iota(jnp.int32, (1, width), 1)
    return (lane >= h * HEAD) & (lane < (h + 1) * HEAD)


def keep_head(values, h):
    return jnp.where(head_lanes(values.shape[-1], h), values, jnp.zeros_like(values))


def rows_norm(values):
    return lax.rsqrt(jnp.mean(values * values, axis=-1, keepdims=True) + 1e-06)


def as_row(ref):
    return jnp.concatenate([ref[k : k + 1, :] for k in range(ref.shape[0])], axis=1)


def aligned(start):
    return pl.ds(pl.multiple_of(start, CHUNK), CHUNK)


def lay_bias(row, table_ref, target):
    heads, buckets = table_ref.shape
    which = lax.broadcasted_iota(jnp.int32, (buckets, SPAN), 0)
    onehot = (row == which).astype(F32)
    table = table_ref[...].T
    for h in range(heads):
        rows = jnp.sum(onehot * table[:, h : h + 1], axis=0, keepdims=True)
        count = 1
        while count < 8:
            rows = jnp.concatenate([rows, pltpu.roll(rows, count, 1)], axis=0)
            count *= 2
        target[h, 0:8, :] = rows
        while count < CHUNK:
            target[h, count : 2 * count, :] = pltpu.roll(target[h, 0:count, :], count, 1)
            count *= 2


def setup_kernel(
    spot,
    bucket_ref,
    segment_hbm,
    table_hbm,
    one_hbm,
    two_hbm,
    info,
    row_ref,
    col_ref,
    bias_ref,
    table_ref,
    one_ref,
    two_ref,
    segment_ref,
    sems,
    *,
    groups,
    first_bits,
):
    pairs = ((segment_hbm, segment_ref), (table_hbm, table_ref), (one_hbm, one_ref), (two_hbm, two_ref))
    copies = [pltpu.make_async_copy(a, b, sems.at[k]) for k, (a, b) in enumerate(pairs)]
    for copy in copies:
        copy.start()
    for copy in copies:
        copy.wait()
    rank, member = spot[0], spot[1]
    steps = row_ref.shape[1] // CHUNK
    rows = [segment_ref[pl.ds(rank * steps + k, 1), :] for k in range(steps)]
    lane = lax.broadcasted_iota(jnp.int32, (1, CHUNK), 1)

    def value(row, at):
        return jnp.max(jnp.where(lane == at, row, -1))

    before = segment_ref[pl.ds(jnp.maximum(rank * steps - 1, 0), 1), :]
    later = segment_ref[pl.ds(jnp.minimum((rank + 1) * steps, groups * steps - 1), 1), :]
    left = (value(before, CHUNK - 1) == value(rows[0], 0)) & (rank > 0)
    right = (value(later, 0) == value(rows[-1], CHUNK - 1)) & (rank < groups - 1)
    even = jnp.where(rank % 2 == 0, right.astype(jnp.int32), left.astype(jnp.int32))
    info[0] = member // 2
    info[1] = member % 2
    info[2] = left.astype(jnp.int32)
    info[3] = (left | right).astype(jnp.int32)
    info[4] = (rank >> first_bits[0]) & 1
    info[5] = (rank >> first_bits[1]) & 1
    info[6] = even
    info[7] = rank
    row = jnp.concatenate(rows, axis=1).astype(F32)
    row_ref[...] = row
    col_ref[...] = jnp.broadcast_to(row, (CHUNK, row.shape[1])).T
    lay_bias(row_of(bucket_ref, 0, bucket_ref.shape[0]), table_ref, bias_ref)


def row_of(ref, first, count):
    return jnp.concatenate([ref[pl.ds(first + k, 1), :] for k in range(count)], axis=1)


def flipped_kernel(bucket_ref, table_ref, bias_ref, flipped_ref):
    count = bucket_ref.shape[0]
    sub = lax.broadcasted_iota(jnp.int32, (CHUNK, CHUNK), 0)
    lane = lax.broadcasted_iota(jnp.int32, (CHUNK, CHUNK), 1)
    turned = dot_nn(bucket_ref[...].astype(F32).astype(LOW), (sub + lane == CHUNK - 1).astype(F32).astype(LOW))
    row = jnp.concatenate([turned[k : k + 1, :] for k in reversed(range(count))], axis=1)
    row = pltpu.roll(row, 1, 1).astype(jnp.int32)
    flipped_ref[...] = jnp.concatenate([row[:, k * CHUNK : (k + 1) * CHUNK] for k in range(count)], axis=0)
    lay_bias(row, table_ref, bias_ref)


def near_kernel(info, even_ref, odd_ref, out_ref):
    out_ref[...] = jnp.where(info[6] == 1, even_ref[...], odd_ref[...])


def fold_diagonals(tile):
    rows, cols = tile.shape
    while rows > 1:
        rows //= 2
        tile = tile[:rows] + pltpu.roll(tile[rows:], cols - rows, 1)
    return tile


def pack_columns(columns, offset=0, base=None, width=CHUNK):
    rows = columns[0].shape[0]
    lane = lax.broadcasted_iota(jnp.int32, (rows, width), 1)
    out = jnp.zeros((rows, width), F32) if base is None else base
    for k, column in enumerate(columns):
        out = jnp.where(lane == offset + k, column, out)
    return out


def by_head(packed, width):
    lane = lax.broadcasted_iota(jnp.int32, (packed.shape[0], width), 1)
    out = packed[:, 0:1]
    for h in range(1, width // HEAD):
        out = jnp.where(lane >= h * HEAD, packed[:, h : h + 1], out)
    return out


def pack_lanes(values, target):
    rows = values.shape[0]
    target[:rows, :] = values[:, :CHUNK]
    rest = values[:, CHUNK:]
    target[rows : rows + rows // 2, :] = jnp.concatenate([rest[: rows // 2], rest[rows // 2 :]], axis=1)


def unpack_lanes(packed, rows):
    rest = packed[rows : rows + rows // 2, :]
    half = CHUNK // 2
    return jnp.concatenate(
        [packed[:rows, :], jnp.concatenate([rest[:, :half], rest[:, half:]], axis=0)], axis=1
    )


def place(y, c):
    return (2 * y + c, 2 * (1 - y) + c, 2 * y + 1 - c, 2 * (1 - y) + 1 - c)


def project(normed, rows, wq, wk, wv, q_ref, k_ref, v_ref):
    q_ref[rows, :] = (dot_nt(normed, wq[...]).astype(LOW).astype(F32) * HEAD**-0.5).astype(LOW)
    k_ref[rows, :] = dot_nt(normed, wk[...]).astype(LOW)
    v_ref[rows, :] = dot_nt(normed, wv[...]).astype(LOW)


def attend(q, keys, values, bias, first, seg_col, seg_row, scores_ref, probs_ref, acc_ref, top_ref, sum_ref):
    window, width = q.shape
    heads = width // HEAD
    for h in range(heads):
        scores_ref[h] = dot_nt(keep_head(q, h), keys)
    for h in range(heads):
        for a in range(window // CHUNK):
            rows = slice(a * CHUNK, (a + 1) * CHUNK)
            scores = scores_ref[h, rows, :] + bias[h, :, pl.ds(first - a * CHUNK, window)]
            if seg_col is not None:
                scores = jnp.where(seg_col[rows, 0:1] == seg_row[...], scores, NEG)
            top = jnp.max(scores, axis=-1, keepdims=True)
            weights = jnp.exp(scores - top)
            probs_ref[h, rows, :] = weights.astype(LOW)
            top_ref[rows, :] = pack_columns([top], h, top_ref[rows, :] if h else jnp.zeros((CHUNK, CHUNK), F32))
            total = jnp.sum(weights, axis=-1, keepdims=True)
            sum_ref[rows, :] = pack_columns([total], h, sum_ref[rows, :] if h else jnp.ones((CHUNK, CHUNK), F32))
    total = dot_nn(probs_ref[0], keep_head(values, 0))
    for h in range(1, heads):
        total = total + dot_nn(probs_ref[h], keep_head(values, h))
    acc_ref[...] = total


def own_kernel(
    info,
    x1,
    x2,
    x3,
    gain,
    bias,
    seg_col,
    seg_row,
    x_hbm,
    wq_hbm,
    wk_hbm,
    wv_hbm,
    x_all,
    normed_ref,
    q_ref,
    k_ref,
    v_ref,
    acc_ref,
    top_ref,
    sum_ref,
    wq,
    wk,
    wv,
    scores_ref,
    probs_ref,
    x0,
    sems,
):
    pairs = ((x_hbm, x0), (wq_hbm, wq), (wk_hbm, wk), (wv_hbm, wv))
    copies = [pltpu.make_async_copy(a, b, sems.at[k]) for k, (a, b) in enumerate(pairs)]
    for copy in copies:
        copy.start()
    spots = place(info[0], info[1])
    for piece, spot in zip((x1, x2, x3, x0), spots[1:] + spots[:1]):
        if piece is x0:
            copies[0].wait()
        rows = aligned(spot * CHUNK)
        low = piece[...]
        x_all[rows, :] = low
        wide = low.astype(F32)
        normed_ref[rows, :] = (wide * rows_norm(wide) * as_row(gain)).astype(LOW)
    for copy in copies[1:]:
        copy.wait()
    project(normed_ref[...], slice(None), wq, wk, wv, q_ref, k_ref, v_ref)
    attend(
        q_ref[...],
        k_ref[...],
        v_ref[...],
        bias,
        SPAN // 2,
        seg_col,
        seg_row,
        scores_ref,
        probs_ref,
        acc_ref,
        top_ref,
        sum_ref,
    )


def far_start(info, window):
    return pl.multiple_of(jnp.where(info[2] == 1, SPAN // 2 - window, SPAN // 2 + window), CHUNK)


def partner_kernel(
    info,
    x0,
    x1,
    x2,
    x3,
    gain,
    wq,
    wk,
    wv,
    bias,
    q_ref,
    acc_ref,
    top_ref,
    sum_ref,
    mixed_low,
    packed_ref,
    mixed_ref,
    lse_ref,
    qp_ref,
    kp_ref,
    vp_ref,
    normed_ref,
    scores_ref,
    probs_ref,
    acc_two,
    top_two,
    sum_two,
):
    window, width = q_ref.shape
    paired = info[3]

    @pl.when(paired == 1)
    def _():
        for piece, spot in zip((x0, x1, x2, x3), place(info[0], info[1])):
            wide = piece[...].astype(F32)
            normed_ref[aligned(spot * CHUNK), :] = (wide * rows_norm(wide) * as_row(gain)).astype(LOW)
        project(normed_ref[...], slice(None), wq, wk, wv, qp_ref, kp_ref, vp_ref)
        attend(
            q_ref[...],
            kp_ref[...],
            vp_ref[...],
            bias,
            far_start(info, window),
            None,
            None,
            scores_ref,
            probs_ref,
            acc_two,
            top_two,
            sum_two,
        )
        for a in range(window // CHUNK):
            rows = slice(a * CHUNK, (a + 1) * CHUNK)
            top = jnp.maximum(top_ref[rows, :], top_two[rows, :])
            one, two = jnp.exp(top_ref[rows, :] - top), jnp.exp(top_two[rows, :] - top)
            whole = sum_ref[rows, :] * one + sum_two[rows, :] * two
            inverse = 1.0 / whole
            mixed = acc_ref[rows, :] * by_head(one * inverse, width)
            mixed = mixed + acc_two[rows, :] * by_head(two * inverse, width)
            mixed_ref[rows, :] = mixed
            mixed_low[rows, :] = mixed.astype(LOW)
            lse_ref[rows, :] = top + jnp.log(whole)

    @pl.when(paired == 0)
    def _():
        qp_ref[...] = jnp.zeros_like(qp_ref)
        kp_ref[...] = jnp.zeros_like(kp_ref)
        vp_ref[...] = jnp.zeros_like(vp_ref)
        for a in range(window // CHUNK):
            rows = slice(a * CHUNK, (a + 1) * CHUNK)
            whole = sum_ref[rows, :]
            mixed = acc_ref[rows, :] * by_head(1.0 / whole, width)
            mixed_ref[rows, :] = mixed
            mixed_low[rows, :] = mixed.astype(LOW)
            lse_ref[rows, :] = top_ref[rows, :] + jnp.log(whole)

    pack_lanes(mixed_low[...], packed_ref)


def cotangent_kernel(g0, g1, g2, g3, down_w, cot_ref, d_act_ref):
    for part, piece in enumerate((g2, g3, g0, g1)):
        cot_ref[part * CHUNK : (part + 1) * CHUNK, :] = piece[...]
    d_act_ref[...] = dot_nt(cot_ref[...], down_w[...])


def base_kernel(x_all, m0, o0, base_ref):
    base_ref[...] = x_all[...].astype(F32) + dot_nn(m0[...], o0[...])


def feed_kernel(
    info,
    base_ref,
    m1,
    m2,
    m3,
    o1,
    o2,
    o3,
    d_act_ref,
    gain,
    gate_w,
    up_w,
    second_ref,
    hidden_ref,
    act_ref,
    dgate_ref,
    dup_ref,
    send_ref,
    keep_ref,
    gain_ref,
):
    y, c = info[0], info[1]
    half = 2 * CHUNK
    gain_sum = jnp.zeros((1, base_ref.shape[1]), F32)
    for part, core in enumerate((1 - c, c)):
        rows = slice(part * half, (part + 1) * half)
        spots = (aligned((2 * y + core) * CHUNK), aligned((2 * (1 - y) + core) * CHUNK))

        def pick(ref):
            return jnp.concatenate([ref[spots[0], :], ref[spots[1], :]], axis=0)

        hidden = pick(base_ref)
        window = base_ref.shape[0]
        for m, o in ((m2, o2), (m1, o1), (m3, o3)):
            parts = []
            for row in (y, 1 - y):
                block = m[aligned(window + core * CHUNK), :]
                lane = lax.broadcasted_iota(jnp.int32, block.shape, 1)
                parts.append(jnp.where(lane // HEAD == row, block, jnp.zeros_like(block)))
            both = jnp.concatenate([pick(m), jnp.concatenate(parts, axis=0)], axis=1)
            hidden = hidden + dot_nn(both, jnp.concatenate([o[...], o[CHUNK:, :]], axis=0))
        if part == 1:
            hidden_ref[...] = hidden
        unit = hidden * rows_norm(hidden)
        second = (unit * as_row(gain)).astype(LOW)
        second_ref[rows, :] = second
        gate = dot_nn(second, gate_w[...])
        up = dot_nn(second, up_w[...])
        d_act = d_act_ref[rows, :]
        square = gate * gate
        tanh = jnp.tanh(ROOT * gate * (1.0 + CUBE * square))
        low_half = 0.5 * (1.0 + tanh)
        gelu = gate * low_half
        slope = low_half + 0.5 * gate * (1.0 - tanh * tanh) * (ROOT * (1.0 + 3.0 * CUBE * square))
        act_ref[rows, :] = (gelu * up).astype(LOW)
        d_gate = (d_act * up * slope).astype(LOW)
        d_up = (d_act * gelu).astype(LOW)
        dgate_ref[rows, :] = d_gate
        dup_ref[rows, :] = d_up
        d_second = dot_nt(d_gate, gate_w[...]) + dot_nt(d_up, up_w[...])
        gain_sum = gain_sum + jnp.sum(d_second * unit, axis=0, keepdims=True)
        if part == 0:
            send_ref[...] = d_second.astype(LOW)
        else:
            keep_ref[...] = d_second
    gain_ref[...] = gain_sum


def feed_grad_kernel(
    info, second_ref, dgate_ref, dup_ref, act_ref, cot_ref, one_send, one_keep, two_send, two_keep, one_ref, two_ref
):
    d, units = second_ref.shape[1], dgate_ref.shape[1]
    one_ref[:d, :] = dot_tn(second_ref[...], dgate_ref[...]).astype(LOW)
    two_ref[:d, :] = dot_tn(second_ref[...], dup_ref[...]).astype(LOW)
    down = dot_tn(act_ref[...], cot_ref[...]).astype(LOW)
    half = units // 2
    quarter = half // 2
    for k, target in enumerate((one_ref, two_ref)):
        target[d : d + half, :] = down[k * half : (k + 1) * half, :units]
        for side in (0, 1):
            rows = slice(k * half + side * quarter, k * half + (side + 1) * quarter)
            target[d + half :, side * (units // 2) : (side + 1) * (units // 2)] = down[rows, units:]
    for source, side, send, keep in ((one_ref, info[4], one_send, one_keep), (two_ref, info[5], two_send, two_keep)):
        rows = send.shape[0]
        send[...] = source[pl.ds(pl.multiple_of((1 - side) * rows, 16), rows), :]
        keep[...] = source[pl.ds(pl.multiple_of(side * rows, 16), rows), :]


def feed_out_kernel(act_ref, down_w, send_ref, keep_ref):
    half = send_ref.shape[0]
    send_ref[...] = dot_nn(act_ref[:half, :], down_w[...]).astype(LOW)
    keep_ref[...] = dot_nn(act_ref[half:, :], down_w[...]).astype(LOW)


def feed_total_kernel(info, one, one_got, two, two_got, gate_ref, up_ref, down_ref, full_ref):
    d, units = gate_ref.shape
    half = units // 2
    quarter = half // 2
    parts = ((one, one_got, info[4], gate_ref), (two, two_got, info[5], up_ref))
    for k, (mine, got, side, target) in enumerate(parts):
        rows = mine.shape[0]
        full_ref[pl.ds(pl.multiple_of(side * rows, 16), rows), :] = mine[...]
        full_ref[pl.ds(pl.multiple_of((1 - side) * rows, 16), rows), :] = got[...]
        target[...] = full_ref[:d, :].astype(F32)
        down_ref[k * half : (k + 1) * half, :units] = full_ref[d : d + half, :].astype(F32)
        for part in (0, 1):
            rows = slice(k * half + part * quarter, k * half + (part + 1) * quarter)
            down_ref[rows, units:] = full_ref[d + half :, part * (units // 2) : (part + 1) * (units // 2)].astype(F32)


def feed_merge_kernel(keep_ref, got_ref, own_ref, send_ref):
    local = own_ref.shape[0]
    total = (keep_ref[...].astype(F32) + got_ref[...].astype(F32)).astype(LOW)
    own_ref[...] = total[:local, :]
    send_ref[...] = total[local:, :]


def layer_out_kernel(hidden_ref, own_ref, got_ref, out_ref):
    local = out_ref.shape[0]
    out_ref[...] = (hidden_ref[:local, :] + (own_ref[...].astype(F32) + got_ref[...].astype(F32))).astype(LOW)


def hidden_back_kernel(sum_ref, other_ref, hidden_ref, g0, g1, gain, dh_ref, low_ref):
    for part, cot in enumerate((g0, g1)):
        rows = slice(part * CHUNK, (part + 1) * CHUNK)
        flip = slice((1 - part) * CHUNK, (2 - part) * CHUNK)
        d_second = sum_ref[rows, :].astype(F32) + other_ref[flip, :].astype(F32)
        hidden = hidden_ref[rows, :]
        inverse = rows_norm(hidden)
        unit = hidden * inverse
        scaled = d_second * as_row(gain)
        dh = cot[...].astype(F32) + inverse * (scaled - unit * jnp.mean(unit * scaled, axis=-1, keepdims=True))
        low_ref[rows, :] = dh.astype(LOW)
        if part == 0:
            dh_ref[...] = dh


def mixed_back_kernel(
    info, pair_own, pair_other, out_w, mixed_ref, lse_ref, payload_ref, back_ref, stat_ref, branch_ref
):
    window, width = mixed_ref.shape
    heads = width // HEAD
    pieces = (pair_own[:CHUNK, :], pair_own[CHUNK:, :], pair_other[:CHUNK, :], pair_other[CHUNK:, :])
    for piece, spot in zip(pieces, place(info[0], info[1])):
        branch_ref[aligned(spot * CHUNK), :] = piece
    d_all = dot_nt(branch_ref[...], out_w[...]).astype(LOW)
    back_ref[...] = d_all
    pack_lanes(d_all, payload_ref)
    first = window + window // 2
    for a in range(window // CHUNK):
        rows = slice(a * CHUNK, (a + 1) * CHUNK)
        product = d_all[rows, :].astype(F32) * mixed_ref[rows, :]
        deltas = [jnp.sum(keep_head(product, h), axis=-1, keepdims=True) for h in range(heads)]
        stat = pack_columns(deltas, heads, lse_ref[rows, :])
        stat_ref[rows, :] = stat
        turned = stat.T[: 2 * heads, :]
        high = turned.astype(LOW).astype(F32)
        blank = jnp.zeros((EXTRA - 4 * heads, CHUNK), F32)
        block = jnp.concatenate([high, turned - high, blank], axis=0)
        payload_ref[first + a * EXTRA : first + (a + 1) * EXTRA, :] = block.astype(LOW)


def recall_kernel(
    info, q_ref, k_ref, qp_ref, kp_ref, lse_ref, bias, bias_t, seg_col, seg_row, own_ref, far_ref, near_ref
):
    window, width = q_ref.shape
    heads = width // HEAD
    queries, keys = q_ref[...], k_ref[...]
    for h in range(heads):
        own_ref[h] = dot_nt(keep_head(keys, h), queries)
    lse = lse_ref[...].T
    for h in range(heads):
        for a in range(window // CHUNK):
            rows = slice(a * CHUNK, (a + 1) * CHUNK)
            start = SPAN // 2 - a * CHUNK
            scores = own_ref[h, rows, :] + bias_t[h, :, start : start + window]
            scores = jnp.where(seg_col[rows, 0:1] == seg_row[...], scores, NEG)
            own_ref[h, rows, :] = jnp.exp(scores - lse[h : h + 1, :])

    @pl.when(info[3] == 1)
    def _():
        first = far_start(info, window)
        for h in range(heads):
            far_ref[h] = dot_nt(keep_head(queries, h), kp_ref[...])
            near_ref[h] = dot_nt(keep_head(keys, h), qp_ref[...])
        for h in range(heads):
            for a in range(window // CHUNK):
                rows = slice(a * CHUNK, (a + 1) * CHUNK)
                spot = pl.ds(pl.multiple_of(first - a * CHUNK, CHUNK), window)
                far_ref[h, rows, :] = jnp.exp(far_ref[h, rows, :] + bias[h, :, spot] - lse_ref[rows, h : h + 1])
                near_ref[h, rows, :] += bias_t[h, :, spot]


def bend(weights_of, products_ref, probs_ref, ds_ref, h, delta_of, fold_ref):
    window = products_ref.shape[1]
    steps = window // CHUNK
    for a in range(steps):
        rows = slice(a * CHUNK, (a + 1) * CHUNK)
        weights = weights_of(rows)
        d_scores = weights * (products_ref[h, rows, :] - delta_of(rows))
        ds_ref[h, rows, :] = d_scores.astype(LOW)
        if probs_ref is not None:
            probs_ref[h, rows, :] = weights.astype(LOW)
        if fold_ref is not None:
            at = (steps - a) * CHUNK
            if a == 0:
                fold_ref[h, :, :at] = jnp.zeros((CHUNK, at), F32)
                fold_ref[h, :, at:] = d_scores
            else:
                if a == steps - 1:
                    fold_ref[h, :, :CHUNK] = jnp.zeros((CHUNK, CHUNK), F32)
                fold_ref[h, :, at : at + window] += d_scores


def table_kernel(info, near_fold, far_fold, flipped_ref, bucket_ref, table_ref):
    window = near_fold.shape[2] // 2
    table_ref[...] = table_sums(near_fold, flipped_ref, SPAN // 2 - window, table_ref)

    @pl.when(info[3] == 1)
    def _():
        table_ref[...] += table_sums(far_fold, bucket_ref, far_start(info, window) - window, table_ref)


def table_sums(fold_ref, bucket_ref, start, table_ref):
    heads, buckets = table_ref.shape
    reach = fold_ref.shape[2]
    row = row_of(bucket_ref, start // CHUNK, reach // CHUNK)
    onehot = row == lax.broadcasted_iota(jnp.int32, (buckets, reach), 0)
    columns = []
    for h in range(heads):
        folded = fold_diagonals(fold_ref[h])
        columns.append(jnp.sum(jnp.where(onehot, folded, 0.0), axis=1, keepdims=True))
    return pack_columns(columns).T[:heads, :]


def own_back_kernel(
    own_ref,
    q_ref,
    k_ref,
    v_ref,
    back_ref,
    stat_ref,
    dq_ref,
    dk_ref,
    dv_ref,
    fold_ref,
    products_ref,
    probs_ref,
    ds_ref,
):
    window, width = q_ref.shape
    heads = width // HEAD
    queries, keys, values = q_ref[...], k_ref[...], v_ref[...]
    back = back_ref[...]
    stat = stat_ref[...].T
    for h in range(heads):
        products_ref[h] = dot_nt(keep_head(values, h), back)
    for h in range(heads):
        delta = stat[heads + h : heads + h + 1, :]
        bend(lambda rows: own_ref[h, rows, :], products_ref, probs_ref, ds_ref, h, lambda rows: delta, fold_ref)
    d_queries = dot_tn(ds_ref[0], keep_head(keys, 0))
    d_keys = dot_nn(ds_ref[0], keep_head(queries, 0))
    d_values = dot_nn(probs_ref[0], keep_head(back, 0))
    for h in range(1, heads):
        d_queries = d_queries + dot_tn(ds_ref[h], keep_head(keys, h))
        d_keys = d_keys + dot_nn(ds_ref[h], keep_head(queries, h))
        d_values = d_values + dot_nn(probs_ref[h], keep_head(back, h))
    dq_ref[...] = d_queries
    dk_ref[...] = d_keys
    dv_ref[...] = d_values


def far_back_kernel(
    info,
    far_ref,
    kp_ref,
    vp_ref,
    back_ref,
    stat_ref,
    dq_in,
    mixed_low,
    branch_ref,
    dq_ref,
    fold_ref,
    grad_ref,
    products_ref,
    ds_ref,
):
    grad_ref[...] = dot_tn(mixed_low[...], branch_ref[...]).astype(LOW)
    width = kp_ref.shape[1]
    heads = width // HEAD

    @pl.when(info[3] == 1)
    def _():
        keys, values = kp_ref[...], vp_ref[...]
        back = back_ref[...]
        for h in range(heads):
            products_ref[h] = dot_nt(keep_head(back, h), values)
        for h in range(heads):
            bend(
                lambda rows: far_ref[h, rows, :],
                products_ref,
                None,
                ds_ref,
                h,
                lambda rows: stat_ref[rows, heads + h : heads + h + 1],
                fold_ref,
            )
        d_queries = dq_in[...]
        for h in range(heads):
            d_queries = d_queries + dot_nn(ds_ref[h], keep_head(keys, h))
        dq_ref[...] = (d_queries * HEAD**-0.5).astype(LOW)

    @pl.when(info[3] == 0)
    def _():
        dq_ref[...] = (dq_in[...] * HEAD**-0.5).astype(LOW)


def partner_back_kernel(
    info,
    near_ref,
    v_ref,
    qp_ref,
    from_even,
    from_odd,
    dk_in,
    dv_in,
    dq_ref,
    normed_ref,
    x_all,
    gain,
    wq,
    wk,
    wv,
    grad_in,
    gain_in,
    one_send,
    one_keep,
    two_send,
    two_keep,
    send_ref,
    keep_ref,
    small_ref,
    d_all,
    products_ref,
    probs_ref,
    ds_ref,
):
    window, width = v_ref.shape
    heads = width // HEAD
    y, c = info[0], info[1]
    d_all[:, :width] = dq_ref[...]

    @pl.when(info[3] == 1)
    def _():
        payload = jnp.where(info[6] == 1, from_even[...], from_odd[...])
        queries, values = qp_ref[...], v_ref[...]
        back = unpack_lanes(payload, window)
        at = window + window // 2
        blocks = [payload[at + a * EXTRA : at + (a + 1) * EXTRA, :] for a in range(window // CHUNK)]
        columns = jnp.concatenate(blocks, axis=1).astype(F32)
        for h in range(heads):
            products_ref[h] = dot_nt(keep_head(values, h), back)
        for h in range(heads):
            at = h
            lse = columns[at : at + 1, :] + columns[at + 2 * heads : at + 2 * heads + 1, :]
            at = at + heads
            delta = columns[at : at + 1, :] + columns[at + 2 * heads : at + 2 * heads + 1, :]
            bend(
                lambda rows: jnp.exp(near_ref[h, rows, :] - lse),
                products_ref,
                probs_ref,
                ds_ref,
                h,
                lambda rows: delta,
                None,
            )
        d_keys, d_values = dk_in[...], dv_in[...]
        for h in range(heads):
            d_keys = d_keys + dot_nn(ds_ref[h], keep_head(queries, h))
            d_values = d_values + dot_nn(probs_ref[h], keep_head(back, h))
        d_all[:, width : 2 * width] = d_keys.astype(LOW)
        d_all[:, 2 * width :] = d_values.astype(LOW)

    @pl.when(info[3] == 0)
    def _():
        d_all[:, width : 2 * width] = dk_in[...].astype(LOW)
        d_all[:, 2 * width :] = dv_in[...].astype(LOW)

    joint = dot_tn(d_all[...], normed_ref[...]).astype(LOW)
    halves = (joint[:width, :], joint[width : 2 * width, :])
    for side in (0, 1):

        @pl.when(info[4] == side)
        def _():
            one_keep[...] = halves[side]
            one_send[...] = halves[1 - side]

    halves_two = (joint[2 * width :, :], grad_in[...])
    for side in (0, 1):

        @pl.when(info[5] == side)
        def _():
            two_keep[...] = halves_two[side]
            two_send[...] = halves_two[1 - side]

    gain_sum = jnp.zeros((1, x_all.shape[1]), F32)
    for part, core in enumerate((1 - c, c)):
        spots = (aligned((2 * y + core) * CHUNK), aligned((2 * (1 - y) + core) * CHUNK))
        mine = jnp.concatenate([d_all[spots[0], :], d_all[spots[1], :]], axis=0)
        d_normed = dot_nn(mine[:, :width], wq[...])
        d_normed = d_normed + dot_nn(mine[:, width : 2 * width], wk[...])
        d_normed = d_normed + dot_nn(mine[:, 2 * width :], wv[...])
        wide = jnp.concatenate([x_all[spots[0], :], x_all[spots[1], :]], axis=0).astype(F32)
        gain_sum = gain_sum + jnp.sum(d_normed * (wide * rows_norm(wide)), axis=0, keepdims=True)
        if part == 0:
            send_ref[: 2 * CHUNK, :] = d_normed.astype(LOW)
        else:
            keep_ref[...] = d_normed
    small = jnp.concatenate([gain_sum, gain_in[...], jnp.zeros((6, gain_sum.shape[1]), F32)], axis=0)
    small_ref[...] = small
    put_small(send_ref, 2 * CHUNK, small)


def put_small(target, start, small):
    high = small.astype(LOW).astype(F32)
    target[start : start + EXTRA, :] = jnp.concatenate([high, small - high], axis=0).astype(LOW)


def get_small(source, start):
    both = source[start : start + EXTRA, :].astype(F32)
    return both[: EXTRA // 2] + both[EXTRA // 2 :]


def first_merge_kernel(keep_ref, got_ref, small_in, send_ref, own_ref, small_ref):
    local = own_ref.shape[0]
    total = (keep_ref[...] + got_ref[: 2 * local, :].astype(F32)).astype(LOW)
    own_ref[...] = total[:local, :]
    send_ref[:local, :] = total[local:, :]
    small = small_in[...] + get_small(got_ref, 2 * local)
    small_ref[...] = small
    put_small(send_ref, local, small)


def input_back_kernel(own_ref, got_ref, x_ref, dh_ref, gain, small_in, table_ref, out_ref, small_ref):
    local = own_ref.shape[0]
    d_normed = own_ref[...].astype(F32) + got_ref[:local, :].astype(F32)
    wide = x_ref[...].astype(F32)
    inverse = rows_norm(wide)
    unit = wide * inverse
    scaled = d_normed * as_row(gain)
    back = inverse * (scaled - unit * jnp.mean(unit * scaled, axis=-1, keepdims=True))
    out_ref[...] = (dh_ref[...] + back).astype(LOW)
    small_ref[...] = small_in[...] + get_small(got_ref, local)
    heads, buckets = table_ref.shape
    small_ref[2 : 2 + heads, :buckets] = table_ref[...]


def halve_kernel(info, *refs, bits):
    count = len(bits)
    for k, bit in enumerate(bits):
        keep, got = refs[2 * k], refs[2 * k + 1]
        send_ref, keep_ref = refs[2 * count + 2 * k], refs[2 * count + 2 * k + 1]
        half = send_ref.shape[0]
        side = (info[7] >> bit) & 1
        for first, target in ((1 - side, send_ref), (side, keep_ref)):
            rows = pl.ds(pl.multiple_of(first * half, 16), half)
            target[...] = (keep[rows, :].astype(F32) + got[rows, :].astype(F32)).astype(LOW)


def sum_kernel(*refs, count, small):
    for k in range(count):
        keep, got = refs[2 * k], refs[2 * k + 1]
        target = refs[2 * count + small + k]
        rows = keep.shape[0]
        target[:rows, :] = (keep[...].astype(F32) + got[...].astype(F32)).astype(LOW)
        if small and k == 0:
            put_small(target, rows, refs[2 * count][...])


def pair_kernel(*refs, count, small):
    for k in range(count):
        mine, got, target = refs[2 * k], refs[2 * k + 1], refs[2 * count + k]
        extra = EXTRA if small and k == 0 else 0
        rows = mine.shape[0] - extra
        target[:rows, :] = (mine[:rows, :].astype(F32) + got[:rows, :].astype(F32)).astype(LOW)
        if extra:
            put_small(target, rows, get_small(mine, rows) + get_small(got, rows))


def double_kernel(info, *refs, bits, small):
    count = len(bits)
    for k, bit in enumerate(bits):
        mine, got, target = refs[2 * k], refs[2 * k + 1], refs[2 * count + k]
        extra = EXTRA if small and k == 0 else 0
        rows = mine.shape[0] - extra
        side = (info[7] >> bit) & 1
        target[pl.ds(pl.multiple_of(side * rows, 16), rows), :] = mine[:rows, :]
        target[pl.ds(pl.multiple_of((1 - side) * rows, 16), rows), :] = got[:rows, :]
        if extra:
            put_small(target, 2 * rows, get_small(mine, rows) + get_small(got, rows))


def attention_total_kernel(
    info, one, one_got, two, two_got, q_ref, k_ref, v_ref, out_ref, gain_one_ref, gain_two_ref, table_ref
):
    rows = q_ref.shape[0]
    first = info[4] == 0
    mine, got = one[:rows, :], one_got[:rows, :]
    q_ref[...] = jnp.where(first, mine, got).astype(F32)
    k_ref[...] = jnp.where(first, got, mine).astype(F32)
    first = info[5] == 0
    v_ref[...] = jnp.where(first, two[...], two_got[...]).astype(F32)
    out_ref[...] = jnp.where(first, two_got[...], two[...]).astype(F32)
    if one.shape[0] > rows:
        small = get_small(one, rows) + get_small(one_got, rows)
        for k in range(gain_one_ref.shape[0]):
            columns = slice(k * CHUNK, (k + 1) * CHUNK)
            gain_one_ref[k : k + 1, :] = small[0:1, columns]
            gain_two_ref[k : k + 1, :] = small[1:2, columns]
        heads, buckets = table_ref.shape
        table_ref[...] = small[2 : 2 + heads, :buckets]
    else:
        gain_one_ref[...] = jnp.zeros_like(gain_one_ref)
        gain_two_ref[...] = jnp.zeros_like(gain_two_ref)
        table_ref[...] = jnp.zeros_like(table_ref)


def swap(values, axis, bit):
    return lax.ppermute(values, axis, [(i, i ^ bit) for i in range(lax.axis_size(axis))])


def swap_odd(values):
    ends = range(1, lax.axis_size("dp") - 1, 2)
    return lax.ppermute(values, "dp", [(i, i + 1) for i in ends] + [(i + 1, i) for i in ends])


def after(values, *others):
    return lax.optimization_barrier((values, *others))[0]


def spread(own, across=None):
    across = swap(own, "mp", 2) if across is None else across
    return own, across, swap(own, "mp", 1), swap(across, "mp", 1)


def cut(values, first, count):
    return lax.dynamic_slice_in_dim(values, first, count)


class Sums:
    def __init__(self, info, rank, orders, sends, keeps):
        self.info, self.rank, self.orders, self.keeps = info, rank, orders, list(keeps)
        self.bits = len(orders[0])
        self.tiled = all((k.shape[0] >> (self.bits - 2)) % 16 == 0 for k in keeps)
        self.step, self.small = 0, None
        self.exchange(sends)

    def exchange(self, sends):
        done = self.step if self.step < self.bits else 2 * self.bits - 2 - self.step
        self.now = [order[done] for order in self.orders]
        self.gots = [swap(v, "dp", 1 << bit) for v, bit in zip(sends, self.now)]
        self.step += 1

    def pairs(self):
        return [v for pair in zip(self.keeps, self.gots) for v in pair]

    def advance(self, token, small=None, micros=1):
        self.keeps[0] = after(self.keeps[0], token)
        count = len(self.keeps)
        if self.step < self.bits - 1:
            bits = [order[self.step] for order in self.orders]
            halves = [v.shape[0] // 2 for v in self.keeps]
            if self.tiled:
                out = call(
                    functools.partial(halve_kernel, bits=bits),
                    [shape((h, v.shape[1]), LOW) for h, v in zip(halves, self.keeps) for _ in range(2)],
                    [self.info, *self.pairs()],
                    micros=micros,
                )
                sends, self.keeps = out[0::2], list(out[1::2])
            else:
                sends, keeps = [], []
                for k, g, h, bit in zip(self.keeps, self.gots, halves, bits):
                    side = (self.rank >> bit) & 1
                    total = (k.astype(F32) + g.astype(F32)).astype(LOW)
                    sends.append(cut(total, (1 - side) * h, h))
                    keeps.append(cut(total, side * h, h))
                self.keeps = keeps
        elif self.step == self.bits - 1:
            if self.tiled:
                self.small = small
                rows = [v.shape[0] for v in self.keeps]
                if small is not None:
                    rows[0] += EXTRA
                sends = call(
                    functools.partial(sum_kernel, count=count, small=int(small is not None)),
                    [shape((r, v.shape[1]), LOW) for r, v in zip(rows, self.keeps)],
                    self.pairs() + ([small] if small is not None else []),
                    smem=0,
                    micros=micros,
                )
            else:
                sends = [(k.astype(F32) + g.astype(F32)).astype(LOW) for k, g in zip(self.keeps, self.gots)]
            self.keeps = list(sends)
        elif self.step == self.bits:
            if self.tiled:
                sends = call(
                    functools.partial(pair_kernel, count=count, small=self.small is not None),
                    [shape(v.shape, LOW) for v in self.keeps],
                    self.pairs(),
                    smem=0,
                    micros=micros,
                )
            else:
                sends = [(k.astype(F32) + g.astype(F32)).astype(LOW) for k, g in zip(self.keeps, self.gots)]
            self.keeps = list(sends)
        else:
            has = self.small is not None
            if self.tiled:
                rows = [2 * v.shape[0] for v in self.keeps]
                if has:
                    rows[0] -= EXTRA
                sends = call(
                    functools.partial(double_kernel, bits=self.now, small=has),
                    [shape((r, v.shape[1]), LOW) for r, v in zip(rows, self.keeps)],
                    [self.info, *self.pairs()],
                    micros=micros,
                )
            else:
                sends = []
                for k, g, bit in zip(self.keeps, self.gots, self.now):
                    side = (self.rank >> bit) & 1
                    sends.append(
                        jnp.where(side == 0, jnp.concatenate([k, g], axis=0), jnp.concatenate([g, k], axis=0))
                    )
            self.keeps = list(sends)
        self.exchange(sends)
        return sends[0]


def per_device(
    inputs,
    attention_gain,
    query_weight,
    key_weight,
    value_weight,
    out_weight,
    bias_table,
    feedforward_gain,
    gate_weight,
    up_weight,
    down_weight,
    segment,
    bucket,
    cotangent,
):
    parts = lax.axis_size("mp")
    groups = lax.axis_size("dp")
    local, d = inputs.shape
    window = local * parts
    width = query_weight.shape[1]
    heads = width // HEAD
    units = gate_weight.shape[1]
    buckets = bias_table.shape[0]
    half = 2 * local
    rank = lax.axis_index("dp")
    member = lax.axis_index("mp")
    bits = list(range(groups.bit_length() - 1))
    order_one = bits
    order_two = [bits[1], bits[0]] + bits[2:]

    x_across = swap(inputs, "mp", 2)
    from_even = swap(inputs, "dp", 1)
    from_odd = swap_odd(inputs)

    spot = jnp.stack([rank, member]).astype(jnp.int32)
    edge = jnp.full((1,), -1, jnp.int32)
    bucket_rows = jnp.concatenate([edge, bucket]).reshape(-1, CHUNK)
    table = bias_table.T
    gain_one, gain_two = attention_gain.reshape(-1, CHUNK), feedforward_gain.reshape(-1, CHUNK)
    band = shape((heads, CHUNK, SPAN), F32)
    segments = segment.reshape(-1, CHUNK)
    info, seg_row, seg_col, bias, table, gain_one, gain_two = call(
        functools.partial(setup_kernel, groups=groups, first_bits=(order_one[0], order_two[0])),
        [shape((8,), jnp.int32), shape((1, window), F32), shape((window, CHUNK), F32), band]
        + [shape(v.shape, F32) for v in (table, gain_one, gain_two)],
        [spot, bucket_rows] + [in_hbm(v) for v in (segments, table, gain_one, gain_two)],
        scratch=[pltpu.VMEM(segments.shape, jnp.int32), pltpu.SemaphoreType.DMA((4,))],
        hbm=4,
        out_smem=1,
        micros=3.0,
    )
    cot_across = swap(cotangent, "mp", 2)
    (near,) = call(near_kernel, [shape((local, d), LOW)], [info, after(from_even, x_across, cot_across), from_odd], micros=0.5)
    near_across = swap(near, "mp", 2)
    near_core = swap(near, "mp", 1)
    x_pieces = (inputs, x_across, swap(inputs, "mp", 1), swap(after(x_across, near_core), "mp", 1))

    low_rows = shape((window, width), LOW)
    wide_rows = shape((window, width), F32)
    stats = shape((window, CHUNK), F32)
    square_wide = pltpu.VMEM((heads, window, window), F32)
    square_low = pltpu.VMEM((heads, window, window), LOW)
    weight = shape((width, d), LOW)
    x_all, normed, queries, keys, values, acc, top, total, wq, wk, wv = call(
        own_kernel,
        [shape((window, d), LOW)] * 2 + [low_rows] * 3 + [wide_rows, stats, stats] + [weight] * 3,
        [info, x_across, *x_pieces[2:], gain_one, bias, seg_col, seg_row]
        + [in_hbm(v) for v in (inputs, query_weight.T, key_weight.T, value_weight.T)],
        scratch=[square_wide, square_low, pltpu.VMEM((local, d), LOW), pltpu.SemaphoreType.DMA((4,))],
        hbm=4,
        micros=5.0,
    )
    near_pieces = (near, near_across, near_core, swap(after(near_across, acc), "mp", 1))
    mixed_low, packed, mixed, lse, queries_near, keys_near, values_near = call(
        partner_kernel,
        [low_rows, shape((window + window // 2, CHUNK), LOW), wide_rows, stats] + [low_rows] * 3,
        [info, *near_pieces, gain_one, wq, wk, wv, bias, queries, acc, top, total],
        scratch=[
            pltpu.VMEM((window, d), LOW),
            square_wide,
            square_low,
            pltpu.VMEM((window, width), F32),
            pltpu.VMEM((window, CHUNK), F32),
            pltpu.VMEM((window, CHUNK), F32),
        ],
        micros=300,
    )
    mixed_across = swap(packed, "mp", 2)
    mixed_core = swap(packed, "mp", 1)
    cot_pieces = (
        cotangent,
        cot_across,
        swap(after(cotangent, mixed_core), "mp", 1),
        swap(after(cot_across, mixed_core), "mp", 1),
    )
    out_across = swap(after(out_weight, near), "mp", 2)
    out_pieces = (
        out_weight,
        out_across,
        swap(after(out_weight, mixed_core), "mp", 1),
        swap(after(out_across, mixed_core), "mp", 1),
    )
    bias_t, flipped_rows = call(
        flipped_kernel,
        [band, shape(bucket_rows.shape, jnp.int32)],
        [after(bucket_rows, mixed_low), table],
        smem=0,
        micros=3.0,
    )
    cot_all, d_act = call(
        cotangent_kernel,
        [shape((window, d), LOW), shape((window, units), F32)],
        [*cot_pieces, after(down_weight, mixed_across)],
        smem=0,
        micros=1.0,
    )
    (base,) = call(
        base_kernel,
        [shape((window, d), F32)],
        [x_all, after(mixed_low, bias_t), out_weight],
        smem=0,
        micros=1.0,
    )
    mixed_pieces = (mixed_low, mixed_across, mixed_core, swap(after(mixed_across, bias_t, base), "mp", 1))
    second, hidden, act, d_gate, d_up, second_send, second_keep, gain_two_part = call(
        feed_kernel,
        [shape((window, d), LOW), shape((half, d), F32)]
        + [shape((window, units), LOW)] * 3
        + [shape((half, d), LOW), shape((half, d), F32), shape((1, d), F32)],
        [info, base, *mixed_pieces[1:], *out_pieces[1:], d_act, gain_two, gate_weight, up_weight],
        micros=5.0,
    )
    (second_sum,) = call(
        functools.partial(sum_kernel, count=1, small=0),
        [shape((half, d), LOW)],
        [second_keep, swap(second_send, "mp", 1)],
        smem=0,
        micros=1.0,
    )
    second_other = swap(second_sum, "mp", 2)
    rows = d + units // 2 + units // 4
    gate_send, gate_keep, up_send, up_keep = call(
        feed_grad_kernel,
        [shape((rows // 2, units), LOW)] * 4,
        [info, after(second, second_sum), d_gate, d_up, act, cot_all],
        scratch=[pltpu.VMEM((rows, units), LOW)] * 2,
        micros=3.0,
    )
    feed_sums = Sums(info, rank, (order_one, order_two), (gate_send, up_send), (gate_keep, up_keep))
    feed_send, feed_keep = call(
        feed_out_kernel, [shape((half, d), LOW)] * 2, [after(act, gate_send), down_weight], smem=0, micros=30
    )
    feed_got = swap(feed_send, "mp", 1)
    block = shape((heads, window, window), F32)
    own_probs, far_probs, near_scores = call(
        recall_kernel,
        [block] * 3,
        [
            info,
            after(queries, feed_send),
            keys,
            queries_near,
            keys_near,
            lse,
            bias,
            bias_t,
            seg_col,
            seg_row,
        ],
        micros=1.0,
    )
    second_other = after(second_other, own_probs)
    dh, branch_low = call(
        hidden_back_kernel,
        [shape((local, d), F32), shape((half, d), LOW)],
        [second_sum, second_other, hidden, cot_pieces[0], cot_pieces[1], gain_two],
        smem=0,
    )
    feed_own, feed_cross = call(
        feed_merge_kernel,
        [shape((local, d), LOW)] * 2,
        [after(feed_keep, branch_low), feed_got],
        smem=0,
        micros=100,
    )
    payload, back, stat_back, branch_all = call(
        mixed_back_kernel,
        [shape((window + window // 2 + window // CHUNK * EXTRA, CHUNK), LOW), low_rows, stats, shape((window, d), LOW)],
        [info, after(branch_low, feed_cross), swap(branch_low, "mp", 1), out_weight, mixed, lse],
    )
    payload_even = swap(payload, "dp", 1)
    payload_odd = swap_odd(payload)
    token = feed_sums.advance(payload)
    fold = shape((heads, CHUNK, 2 * window), F32)
    d_queries, d_keys, d_values, near_fold = call(
        own_back_kernel,
        [wide_rows, wide_rows, wide_rows, fold],
        [own_probs, after(queries, token), keys, values, back, stat_back],
        scratch=[square_wide, square_low, square_low],
        smem=0,
        micros=200,
    )
    d_queries, far_fold, out_grad = call(
        far_back_kernel,
        [low_rows, fold, shape((width, d), LOW)],
        [info, far_probs, keys_near, values_near, back, stat_back, d_queries, mixed_low, branch_all],
        scratch=[square_wide, square_low],
        micros=3.0,
    )
    one_send, one_keep, two_send, two_keep, first_send, first_keep, small = call(
        partner_back_kernel,
        [shape((width, d), LOW)] * 4
        + [shape((half + EXTRA, d), LOW), shape((half, d), F32), shape((EXTRA // 2, d), F32)],
        [
            info,
            near_scores,
            values,
            queries_near,
            payload_even,
            payload_odd,
            d_keys,
            d_values,
            d_queries,
            normed,
            x_all,
            gain_one,
            wq,
            wk,
            wv,
            out_grad,
            gain_two_part,
        ],
        scratch=[pltpu.VMEM((window, 3 * width), LOW), square_wide, square_low, square_low],
        micros=300,
    )
    token = feed_sums.advance(one_send, micros=300)
    joint_sums = Sums(info, rank, (order_one, order_two), (after(one_send, token), two_send), (one_keep, two_keep))
    first_send, first_own, small = call(
        first_merge_kernel,
        [shape((local + EXTRA, d), LOW), shape((local, d), LOW), shape((EXTRA // 2, d), F32)],
        [after(first_keep, token), swap(first_send, "mp", 1), small],
        smem=0,
        micros=1,
    )
    first_got = swap(first_send, "mp", 2)
    token = joint_sums.advance(first_send)
    (table_part,) = call(
        table_kernel,
        [shape((heads, CHUNK), F32)],
        [info, after(near_fold, token), far_fold, flipped_rows, bucket_rows],
        micros=1.0,
    )
    input_grad, small = call(
        input_back_kernel,
        [shape((local, d), LOW), shape((EXTRA // 2, d), F32)],
        [first_own, first_got, inputs, after(dh, token), gain_one, small, table_part],
        smem=0,
        micros=1,
    )
    token = joint_sums.advance(small, small)
    token = feed_sums.advance(token)
    feed_got = swap(after(feed_cross, token), "mp", 2)
    token = joint_sums.advance(token, small, micros=1)
    token = feed_sums.advance(token)
    last = 2 * len(bits) - 1
    while joint_sums.step < last or feed_sums.step < last:
        if joint_sums.step < last:
            token = joint_sums.advance(token, small, micros=300)
        if feed_sums.step < last:
            token = feed_sums.advance(token)
    (layer_out,) = call(
        layer_out_kernel,
        [shape((local, d), LOW)],
        [after(hidden, token), feed_own, feed_got],
        smem=0,
        micros=40,
    )
    ready = feed_sums.pairs()
    gate_grad, up_grad, down_grad = call(
        feed_total_kernel,
        [shape((d, units), F32)] * 2 + [shape((units, d), F32)],
        [info, after(ready[0], layer_out), *ready[1:]],
        scratch=[pltpu.VMEM((rows, units), LOW)],
        micros=2.0,
    )
    ready = joint_sums.pairs()
    query_grad, key_grad, value_grad, out_total, gain_one_total, gain_two_total, table_total = call(
        attention_total_kernel,
        [shape((width, d), F32)] * 4 + [shape((d // CHUNK, CHUNK), F32)] * 2 + [shape((heads, buckets), F32)],
        [info, after(ready[0], down_grad), *ready[1:]],
        micros=2.0,
    )
    if not joint_sums.tiled:
        small = lax.psum(small, "dp")
        gain_one_total, gain_two_total = small[0].reshape(-1, CHUNK), small[1].reshape(-1, CHUNK)
        table_total = small[2 : 2 + heads, :buckets]
    return (
        layer_out,
        input_grad,
        gain_one_total.reshape(-1),
        query_grad.T,
        key_grad.T,
        value_grad.T,
        out_total,
        table_total.T,
        gain_two_total.reshape(-1),
        gate_grad,
        up_grad,
        down_grad,
    )


def solution(mesh):
    rows = P(("dp", "mp"), None)
    in_specs = (
        rows,
        P(),
        P(None, "mp"),
        P(None, "mp"),
        P(None, "mp"),
        P("mp", None),
        P(None, "mp"),
        P(),
        P(None, "mp"),
        P(None, "mp"),
        P("mp", None),
        P(),
        P(),
        rows,
    )
    out_specs = (
        rows,
        rows,
        P(),
        P(None, "mp"),
        P(None, "mp"),
        P(None, "mp"),
        P("mp", None),
        P(None, "mp"),
        P(),
        P(None, "mp"),
        P(None, "mp"),
        P("mp", None),
    )
    return jax.shard_map(
        per_device, mesh=mesh, in_specs=in_specs, out_specs=out_specs, check_vma=False
    )
```

```python
import functools

import jax
import jax.numpy as jnp
from jax import lax
from jax.experimental import pallas as pl
from jax.experimental.pallas import tpu as pltpu
from jax.sharding import PartitionSpec as P

HEAD = 64
LOW = jnp.bfloat16
F32 = jnp.float32
CHUNK = 128
SPAN = 2048
EXTRA = 16
NEG = -1e30
ROOT = 0.7978845608
CUBE = 0.044715
VMEM = pl.BlockSpec(memory_space=pltpu.VMEM)
SMEM = pl.BlockSpec(memory_space=pltpu.SMEM)
HBM = pl.BlockSpec(memory_space=pltpu.HBM)


def dot_nn(a, b):
    return lax.dot_general(a, b, (((1,), (0,)), ((), ())), preferred_element_type=F32)


def dot_nt(a, b):
    return lax.dot_general(a, b, (((1,), (1,)), ((), ())), preferred_element_type=F32)


def dot_tn(a, b):
    return lax.dot_general(a, b, (((0,), (0,)), ((), ())), preferred_element_type=F32)


def call(kernel, outs, ins, scratch=(), smem=1, hbm=0, micros=2.0, out_smem=0, limit=20):
    return pl.pallas_call(
        kernel,
        out_shape=outs,
        in_specs=[SMEM] * smem + [VMEM] * (len(ins) - smem - hbm) + [HBM] * hbm,
        out_specs=[SMEM] * out_smem + [VMEM] * (len(outs) - out_smem),
        scratch_shapes=list(scratch),
        cost_estimate=pl.CostEstimate(flops=int(micros * 2e7), bytes_accessed=0, transcendentals=0),
        compiler_params=pltpu.CompilerParams(vmem_limit_bytes=limit * 1024 * 1024),
    )(*ins)


def in_hbm(values):
    return pltpu.with_memory_space_constraint(values, pltpu.HBM)


def shape(dims, dtype):
    return jax.ShapeDtypeStruct(dims, dtype)


def head_lanes(width, h):
    lane = lax.broadcasted_iota(jnp.int32, (1, width), 1)
    return (lane >= h * HEAD) & (lane < (h + 1) * HEAD)


def keep_head(values, h):
    return jnp.where(head_lanes(values.shape[-1], h), values, jnp.zeros_like(values))


def rows_norm(values):
    return lax.rsqrt(jnp.mean(values * values, axis=-1, keepdims=True) + 1e-06)


def as_row(ref):
    return jnp.concatenate([ref[k : k + 1, :] for k in range(ref.shape[0])], axis=1)


def aligned(start):
    return pl.ds(pl.multiple_of(start, CHUNK), CHUNK)


def lay_bias(row, table_ref, target):
    heads, buckets = table_ref.shape
    which = lax.broadcasted_iota(jnp.int32, (buckets, SPAN), 0)
    onehot = (row == which).astype(F32)
    table = table_ref[...].T
    for h in range(heads):
        rows = jnp.sum(onehot * table[:, h : h + 1], axis=0, keepdims=True)
        count = 1
        while count < 8:
            rows = jnp.concatenate([rows, pltpu.roll(rows, count, 1)], axis=0)
            count *= 2
        target[h, 0:8, :] = rows
        while count < CHUNK:
            target[h, count : 2 * count, :] = pltpu.roll(target[h, 0:count, :], count, 1)
            count *= 2


def setup_kernel(
    spot,
    bucket_ref,
    segment_hbm,
    table_hbm,
    one_hbm,
    two_hbm,
    info,
    row_ref,
    col_ref,
    bias_ref,
    table_ref,
    one_ref,
    two_ref,
    segment_ref,
    sems,
    *,
    groups,
    first_bits,
):
    pairs = ((segment_hbm, segment_ref), (table_hbm, table_ref), (one_hbm, one_ref), (two_hbm, two_ref))
    copies = [pltpu.make_async_copy(a, b, sems.at[k]) for k, (a, b) in enumerate(pairs)]
    for copy in copies:
        copy.start()
    for copy in copies:
        copy.wait()
    rank, member = spot[0], spot[1]
    steps = row_ref.shape[1] // CHUNK
    rows = [segment_ref[pl.ds(rank * steps + k, 1), :] for k in range(steps)]
    lane = lax.broadcasted_iota(jnp.int32, (1, CHUNK), 1)

    def value(row, at):
        return jnp.max(jnp.where(lane == at, row, -1))

    before = segment_ref[pl.ds(jnp.maximum(rank * steps - 1, 0), 1), :]
    later = segment_ref[pl.ds(jnp.minimum((rank + 1) * steps, groups * steps - 1), 1), :]
    left = (value(before, CHUNK - 1) == value(rows[0], 0)) & (rank > 0)
    right = (value(later, 0) == value(rows[-1], CHUNK - 1)) & (rank < groups - 1)
    even = jnp.where(rank % 2 == 0, right.astype(jnp.int32), left.astype(jnp.int32))
    info[0] = member // 2
    info[1] = member % 2
    info[2] = left.astype(jnp.int32)
    info[3] = (left | right).astype(jnp.int32)
    info[4] = (rank >> first_bits[0]) & 1
    info[5] = (rank >> first_bits[1]) & 1
    info[6] = even
    info[7] = rank
    row = jnp.concatenate(rows, axis=1).astype(F32)
    row_ref[...] = row
    col_ref[...] = jnp.broadcast_to(row, (CHUNK, row.shape[1])).T
    lay_bias(row_of(bucket_ref, 0, bucket_ref.shape[0]), table_ref, bias_ref)


def row_of(ref, first, count):
    return jnp.concatenate([ref[pl.ds(first + k, 1), :] for k in range(count)], axis=1)


def flipped_kernel(bucket_ref, table_ref, bias_ref, flipped_ref):
    count = bucket_ref.shape[0]
    sub = lax.broadcasted_iota(jnp.int32, (CHUNK, CHUNK), 0)
    lane = lax.broadcasted_iota(jnp.int32, (CHUNK, CHUNK), 1)
    turned = dot_nn(bucket_ref[...].astype(F32).astype(LOW), (sub + lane == CHUNK - 1).astype(F32).astype(LOW))
    row = jnp.concatenate([turned[k : k + 1, :] for k in reversed(range(count))], axis=1)
    row = pltpu.roll(row, 1, 1).astype(jnp.int32)
    flipped_ref[...] = jnp.concatenate([row[:, k * CHUNK : (k + 1) * CHUNK] for k in range(count)], axis=0)
    lay_bias(row, table_ref, bias_ref)


def near_kernel(info, even_ref, odd_ref, out_ref):
    out_ref[...] = jnp.where(info[6] == 1, even_ref[...], odd_ref[...])


def fold_diagonals(tile):
    rows, cols = tile.shape
    while rows > 1:
        rows //= 2
        tile = tile[:rows] + pltpu.roll(tile[rows:], cols - rows, 1)
    return tile


def pack_columns(columns, offset=0, base=None, width=CHUNK):
    rows = columns[0].shape[0]
    lane = lax.broadcasted_iota(jnp.int32, (rows, width), 1)
    out = jnp.zeros((rows, width), F32) if base is None else base
    for k, column in enumerate(columns):
        out = jnp.where(lane == offset + k, column, out)
    return out


def by_head(packed, width):
    lane = lax.broadcasted_iota(jnp.int32, (packed.shape[0], width), 1)
    out = packed[:, 0:1]
    for h in range(1, width // HEAD):
        out = jnp.where(lane >= h * HEAD, packed[:, h : h + 1], out)
    return out


def pack_lanes(values, target):
    rows = values.shape[0]
    target[:rows, :] = values[:, :CHUNK]
    rest = values[:, CHUNK:]
    target[rows : rows + rows // 2, :] = jnp.concatenate([rest[: rows // 2], rest[rows // 2 :]], axis=1)


def unpack_lanes(packed, rows):
    rest = packed[rows : rows + rows // 2, :]
    half = CHUNK // 2
    return jnp.concatenate(
        [packed[:rows, :], jnp.concatenate([rest[:, :half], rest[:, half:]], axis=0)], axis=1
    )


def place(y, c):
    return (2 * y + c, 2 * (1 - y) + c, 2 * y + 1 - c, 2 * (1 - y) + 1 - c)


def project(normed, rows, wq, wk, wv, q_ref, k_ref, v_ref):
    q_ref[rows, :] = (dot_nt(normed, wq[...]).astype(LOW).astype(F32) * HEAD**-0.5).astype(LOW)
    k_ref[rows, :] = dot_nt(normed, wk[...]).astype(LOW)
    v_ref[rows, :] = dot_nt(normed, wv[...]).astype(LOW)


def attend(q, keys, values, bias, first, seg_col, seg_row, scores_ref, probs_ref, acc_ref, top_ref, sum_ref):
    window, width = q.shape
    heads = width // HEAD
    for h in range(heads):
        scores_ref[h] = dot_nt(keep_head(q, h), keys)
    for h in range(heads):
        for a in range(window // CHUNK):
            rows = slice(a * CHUNK, (a + 1) * CHUNK)
            scores = scores_ref[h, rows, :] + bias[h, :, pl.ds(first - a * CHUNK, window)]
            if seg_col is not None:
                scores = jnp.where(seg_col[rows, 0:1] == seg_row[...], scores, NEG)
            top = jnp.max(scores, axis=-1, keepdims=True)
            weights = jnp.exp(scores - top)
            probs_ref[h, rows, :] = weights.astype(LOW)
            top_ref[rows, :] = pack_columns([top], h, top_ref[rows, :] if h else jnp.zeros((CHUNK, CHUNK), F32))
            total = jnp.sum(weights, axis=-1, keepdims=True)
            sum_ref[rows, :] = pack_columns([total], h, sum_ref[rows, :] if h else jnp.ones((CHUNK, CHUNK), F32))
    total = dot_nn(probs_ref[0], keep_head(values, 0))
    for h in range(1, heads):
        total = total + dot_nn(probs_ref[h], keep_head(values, h))
    acc_ref[...] = total


def own_kernel(
    info,
    x1,
    x2,
    x3,
    gain,
    bias,
    seg_col,
    seg_row,
    x_hbm,
    wq_hbm,
    wk_hbm,
    wv_hbm,
    x_all,
    normed_ref,
    q_ref,
    k_ref,
    v_ref,
    acc_ref,
    top_ref,
    sum_ref,
    wq,
    wk,
    wv,
    scores_ref,
    probs_ref,
    x0,
    sems,
):
    pairs = ((x_hbm, x0), (wq_hbm, wq), (wk_hbm, wk), (wv_hbm, wv))
    copies = [pltpu.make_async_copy(a, b, sems.at[k]) for k, (a, b) in enumerate(pairs)]
    for copy in copies:
        copy.start()
    spots = place(info[0], info[1])
    for piece, spot in zip((x1, x2, x3, x0), spots[1:] + spots[:1]):
        if piece is x0:
            copies[0].wait()
        rows = aligned(spot * CHUNK)
        low = piece[...]
        x_all[rows, :] = low
        wide = low.astype(F32)
        normed_ref[rows, :] = (wide * rows_norm(wide) * as_row(gain)).astype(LOW)
    for copy in copies[1:]:
        copy.wait()
    project(normed_ref[...], slice(None), wq, wk, wv, q_ref, k_ref, v_ref)
    attend(
        q_ref[...],
        k_ref[...],
        v_ref[...],
        bias,
        SPAN // 2,
        seg_col,
        seg_row,
        scores_ref,
        probs_ref,
        acc_ref,
        top_ref,
        sum_ref,
    )


def far_start(info, window):
    return pl.multiple_of(jnp.where(info[2] == 1, SPAN // 2 - window, SPAN // 2 + window), CHUNK)


def partner_kernel(
    info,
    x0,
    x1,
    x2,
    x3,
    gain,
    wq,
    wk,
    wv,
    bias,
    q_ref,
    acc_ref,
    top_ref,
    sum_ref,
    mixed_low,
    packed_ref,
    mixed_ref,
    lse_ref,
    qp_ref,
    kp_ref,
    vp_ref,
    normed_ref,
    scores_ref,
    probs_ref,
    acc_two,
    top_two,
    sum_two,
):
    window, width = q_ref.shape
    paired = info[3]

    @pl.when(paired == 1)
    def _():
        for piece, spot in zip((x0, x1, x2, x3), place(info[0], info[1])):
            wide = piece[...].astype(F32)
            normed_ref[aligned(spot * CHUNK), :] = (wide * rows_norm(wide) * as_row(gain)).astype(LOW)
        project(normed_ref[...], slice(None), wq, wk, wv, qp_ref, kp_ref, vp_ref)
        attend(
            q_ref[...],
            kp_ref[...],
            vp_ref[...],
            bias,
            far_start(info, window),
            None,
            None,
            scores_ref,
            probs_ref,
            acc_two,
            top_two,
            sum_two,
        )
        for a in range(window // CHUNK):
            rows = slice(a * CHUNK, (a + 1) * CHUNK)
            top = jnp.maximum(top_ref[rows, :], top_two[rows, :])
            one, two = jnp.exp(top_ref[rows, :] - top), jnp.exp(top_two[rows, :] - top)
            whole = sum_ref[rows, :] * one + sum_two[rows, :] * two
            inverse = 1.0 / whole
            mixed = acc_ref[rows, :] * by_head(one * inverse, width)
            mixed = mixed + acc_two[rows, :] * by_head(two * inverse, width)
            mixed_ref[rows, :] = mixed
            mixed_low[rows, :] = mixed.astype(LOW)
            lse_ref[rows, :] = top + jnp.log(whole)

    @pl.when(paired == 0)
    def _():
        qp_ref[...] = jnp.zeros_like(qp_ref)
        kp_ref[...] = jnp.zeros_like(kp_ref)
        vp_ref[...] = jnp.zeros_like(vp_ref)
        for a in range(window // CHUNK):
            rows = slice(a * CHUNK, (a + 1) * CHUNK)
            whole = sum_ref[rows, :]
            mixed = acc_ref[rows, :] * by_head(1.0 / whole, width)
            mixed_ref[rows, :] = mixed
            mixed_low[rows, :] = mixed.astype(LOW)
            lse_ref[rows, :] = top_ref[rows, :] + jnp.log(whole)

    pack_lanes(mixed_low[...], packed_ref)


def cotangent_kernel(g0, g1, g2, g3, down_w, cot_ref, d_act_ref):
    for part, piece in enumerate((g2, g3, g0, g1)):
        cot_ref[part * CHUNK : (part + 1) * CHUNK, :] = piece[...]
    d_act_ref[...] = dot_nt(cot_ref[...], down_w[...])


def base_kernel(x_all, m0, o0, base_ref):
    base_ref[...] = x_all[...].astype(F32) + dot_nn(m0[...], o0[...])


def feed_kernel(
    info,
    base_ref,
    m1,
    m2,
    m3,
    o1,
    o2,
    o3,
    d_act_ref,
    gain,
    gate_w,
    up_w,
    second_ref,
    hidden_ref,
    act_ref,
    dgate_ref,
    dup_ref,
    send_ref,
    keep_ref,
    gain_ref,
):
    y, c = info[0], info[1]
    half = 2 * CHUNK
    gain_sum = jnp.zeros((1, base_ref.shape[1]), F32)
    for part, core in enumerate((1 - c, c)):
        rows = slice(part * half, (part + 1) * half)
        spots = (aligned((2 * y + core) * CHUNK), aligned((2 * (1 - y) + core) * CHUNK))

        def pick(ref):
            return jnp.concatenate([ref[spots[0], :], ref[spots[1], :]], axis=0)

        hidden = pick(base_ref)
        window = base_ref.shape[0]
        for m, o in ((m2, o2), (m1, o1), (m3, o3)):
            parts = []
            for row in (y, 1 - y):
                block = m[aligned(window + core * CHUNK), :]
                lane = lax.broadcasted_iota(jnp.int32, block.shape, 1)
                parts.append(jnp.where(lane // HEAD == row, block, jnp.zeros_like(block)))
            both = jnp.concatenate([pick(m), jnp.concatenate(parts, axis=0)], axis=1)
            hidden = hidden + dot_nn(both, jnp.concatenate([o[...], o[CHUNK:, :]], axis=0))
        if part == 1:
            hidden_ref[...] = hidden
        unit = hidden * rows_norm(hidden)
        second = (unit * as_row(gain)).astype(LOW)
        second_ref[rows, :] = second
        gate = dot_nn(second, gate_w[...])
        up = dot_nn(second, up_w[...])
        d_act = d_act_ref[rows, :]
        square = gate * gate
        tanh = jnp.tanh(ROOT * gate * (1.0 + CUBE * square))
        low_half = 0.5 * (1.0 + tanh)
        gelu = gate * low_half
        slope = low_half + 0.5 * gate * (1.0 - tanh * tanh) * (ROOT * (1.0 + 3.0 * CUBE * square))
        act_ref[rows, :] = (gelu * up).astype(LOW)
        d_gate = (d_act * up * slope).astype(LOW)
        d_up = (d_act * gelu).astype(LOW)
        dgate_ref[rows, :] = d_gate
        dup_ref[rows, :] = d_up
        d_second = dot_nt(d_gate, gate_w[...]) + dot_nt(d_up, up_w[...])
        gain_sum = gain_sum + jnp.sum(d_second * unit, axis=0, keepdims=True)
        if part == 0:
            send_ref[...] = d_second.astype(LOW)
        else:
            keep_ref[...] = d_second
    gain_ref[...] = gain_sum


def feed_grad_kernel(
    info, second_ref, dgate_ref, dup_ref, act_ref, cot_ref, one_send, one_keep, two_send, two_keep, one_ref, two_ref
):
    d, units = second_ref.shape[1], dgate_ref.shape[1]
    one_ref[:d, :] = dot_tn(second_ref[...], dgate_ref[...]).astype(LOW)
    two_ref[:d, :] = dot_tn(second_ref[...], dup_ref[...]).astype(LOW)
    down = dot_tn(act_ref[...], cot_ref[...]).astype(LOW)
    half = units // 2
    quarter = half // 2
    for k, target in enumerate((one_ref, two_ref)):
        target[d : d + half, :] = down[k * half : (k + 1) * half, :units]
        for side in (0, 1):
            rows = slice(k * half + side * quarter, k * half + (side + 1) * quarter)
            target[d + half :, side * (units // 2) : (side + 1) * (units // 2)] = down[rows, units:]
    for source, side, send, keep in ((one_ref, info[4], one_send, one_keep), (two_ref, info[5], two_send, two_keep)):
        rows = send.shape[0]
        send[...] = source[pl.ds(pl.multiple_of((1 - side) * rows, 16), rows), :]
        keep[...] = source[pl.ds(pl.multiple_of(side * rows, 16), rows), :]


def feed_out_kernel(act_ref, down_w, send_ref, keep_ref):
    half = send_ref.shape[0]
    send_ref[...] = dot_nn(act_ref[:half, :], down_w[...]).astype(LOW)
    keep_ref[...] = dot_nn(act_ref[half:, :], down_w[...]).astype(LOW)


def feed_total_kernel(info, one, one_got, two, two_got, gate_ref, up_ref, down_ref, full_ref):
    d, units = gate_ref.shape
    half = units // 2
    quarter = half // 2
    parts = ((one, one_got, info[4], gate_ref), (two, two_got, info[5], up_ref))
    for k, (mine, got, side, target) in enumerate(parts):
        rows = mine.shape[0]
        full_ref[pl.ds(pl.multiple_of(side * rows, 16), rows), :] = mine[...]
        full_ref[pl.ds(pl.multiple_of((1 - side) * rows, 16), rows), :] = got[...]
        target[...] = full_ref[:d, :].astype(F32)
        down_ref[k * half : (k + 1) * half, :units] = full_ref[d : d + half, :].astype(F32)
        for part in (0, 1):
            rows = slice(k * half + part * quarter, k * half + (part + 1) * quarter)
            down_ref[rows, units:] = full_ref[d + half :, part * (units // 2) : (part + 1) * (units // 2)].astype(F32)


def feed_merge_kernel(keep_ref, got_ref, own_ref, send_ref):
    local = own_ref.shape[0]
    total = (keep_ref[...].astype(F32) + got_ref[...].astype(F32)).astype(LOW)
    own_ref[...] = total[:local, :]
    send_ref[...] = total[local:, :]


def layer_out_kernel(hidden_ref, own_ref, got_ref, out_ref):
    local = out_ref.shape[0]
    out_ref[...] = (hidden_ref[:local, :] + (own_ref[...].astype(F32) + got_ref[...].astype(F32))).astype(LOW)


def hidden_back_kernel(sum_ref, other_ref, hidden_ref, g0, g1, gain, dh_ref, low_ref):
    for part, cot in enumerate((g0, g1)):
        rows = slice(part * CHUNK, (part + 1) * CHUNK)
        flip = slice((1 - part) * CHUNK, (2 - part) * CHUNK)
        d_second = sum_ref[rows, :].astype(F32) + other_ref[flip, :].astype(F32)
        hidden = hidden_ref[rows, :]
        inverse = rows_norm(hidden)
        unit = hidden * inverse
        scaled = d_second * as_row(gain)
        dh = cot[...].astype(F32) + inverse * (scaled - unit * jnp.mean(unit * scaled, axis=-1, keepdims=True))
        low_ref[rows, :] = dh.astype(LOW)
        if part == 0:
            dh_ref[...] = dh


def mixed_back_kernel(
    info, pair_own, pair_other, out_w, mixed_ref, lse_ref, payload_ref, back_ref, stat_ref, branch_ref
):
    window, width = mixed_ref.shape
    heads = width // HEAD
    pieces = (pair_own[:CHUNK, :], pair_own[CHUNK:, :], pair_other[:CHUNK, :], pair_other[CHUNK:, :])
    for piece, spot in zip(pieces, place(info[0], info[1])):
        branch_ref[aligned(spot * CHUNK), :] = piece
    d_all = dot_nt(branch_ref[...], out_w[...]).astype(LOW)
    back_ref[...] = d_all
    pack_lanes(d_all, payload_ref)
    first = window + window // 2
    for a in range(window // CHUNK):
        rows = slice(a * CHUNK, (a + 1) * CHUNK)
        product = d_all[rows, :].astype(F32) * mixed_ref[rows, :]
        deltas = [jnp.sum(keep_head(product, h), axis=-1, keepdims=True) for h in range(heads)]
        stat = pack_columns(deltas, heads, lse_ref[rows, :])
        stat_ref[rows, :] = stat
        turned = stat.T[: 2 * heads, :]
        high = turned.astype(LOW).astype(F32)
        blank = jnp.zeros((EXTRA - 4 * heads, CHUNK), F32)
        block = jnp.concatenate([high, turned - high, blank], axis=0)
        payload_ref[first + a * EXTRA : first + (a + 1) * EXTRA, :] = block.astype(LOW)


def recall_kernel(
    info, q_ref, k_ref, qp_ref, kp_ref, lse_ref, bias, bias_t, seg_col, seg_row, own_ref, far_ref, near_ref
):
    window, width = q_ref.shape
    heads = width // HEAD
    queries, keys = q_ref[...], k_ref[...]
    for h in range(heads):
        own_ref[h] = dot_nt(keep_head(keys, h), queries)
    lse = lse_ref[...].T
    for h in range(heads):
        for a in range(window // CHUNK):
            rows = slice(a * CHUNK, (a + 1) * CHUNK)
            start = SPAN // 2 - a * CHUNK
            scores = own_ref[h, rows, :] + bias_t[h, :, start : start + window]
            scores = jnp.where(seg_col[rows, 0:1] == seg_row[...], scores, NEG)
            own_ref[h, rows, :] = jnp.exp(scores - lse[h : h + 1, :])

    @pl.when(info[3] == 1)
    def _():
        first = far_start(info, window)
        for h in range(heads):
            far_ref[h] = dot_nt(keep_head(queries, h), kp_ref[...])
            near_ref[h] = dot_nt(keep_head(keys, h), qp_ref[...])
        for h in range(heads):
            for a in range(window // CHUNK):
                rows = slice(a * CHUNK, (a + 1) * CHUNK)
                spot = pl.ds(pl.multiple_of(first - a * CHUNK, CHUNK), window)
                far_ref[h, rows, :] = jnp.exp(far_ref[h, rows, :] + bias[h, :, spot] - lse_ref[rows, h : h + 1])
                near_ref[h, rows, :] += bias_t[h, :, spot]


def bend(weights_of, products_ref, probs_ref, ds_ref, h, delta_of, fold_ref):
    window = products_ref.shape[1]
    steps = window // CHUNK
    for a in range(steps):
        rows = slice(a * CHUNK, (a + 1) * CHUNK)
        weights = weights_of(rows)
        d_scores = weights * (products_ref[h, rows, :] - delta_of(rows))
        ds_ref[h, rows, :] = d_scores.astype(LOW)
        if probs_ref is not None:
            probs_ref[h, rows, :] = weights.astype(LOW)
        if fold_ref is not None:
            at = (steps - a) * CHUNK
            if a == 0:
                fold_ref[h, :, :at] = jnp.zeros((CHUNK, at), F32)
                fold_ref[h, :, at:] = d_scores
            else:
                if a == steps - 1:
                    fold_ref[h, :, :CHUNK] = jnp.zeros((CHUNK, CHUNK), F32)
                fold_ref[h, :, at : at + window] += d_scores


def table_kernel(info, near_fold, far_fold, flipped_ref, bucket_ref, table_ref):
    window = near_fold.shape[2] // 2
    table_ref[...] = table_sums(near_fold, flipped_ref, SPAN // 2 - window, table_ref)

    @pl.when(info[3] == 1)
    def _():
        table_ref[...] += table_sums(far_fold, bucket_ref, far_start(info, window) - window, table_ref)


def table_sums(fold_ref, bucket_ref, start, table_ref):
    heads, buckets = table_ref.shape
    reach = fold_ref.shape[2]
    row = row_of(bucket_ref, start // CHUNK, reach // CHUNK)
    onehot = row == lax.broadcasted_iota(jnp.int32, (buckets, reach), 0)
    columns = []
    for h in range(heads):
        folded = fold_diagonals(fold_ref[h])
        columns.append(jnp.sum(jnp.where(onehot, folded, 0.0), axis=1, keepdims=True))
    return pack_columns(columns).T[:heads, :]


def own_back_kernel(
    own_ref,
    q_ref,
    k_ref,
    v_ref,
    back_ref,
    stat_ref,
    dq_ref,
    dk_ref,
    dv_ref,
    fold_ref,
    products_ref,
    probs_ref,
    ds_ref,
):
    window, width = q_ref.shape
    heads = width // HEAD
    queries, keys, values = q_ref[...], k_ref[...], v_ref[...]
    back = back_ref[...]
    stat = stat_ref[...].T
    for h in range(heads):
        products_ref[h] = dot_nt(keep_head(values, h), back)
    for h in range(heads):
        delta = stat[heads + h : heads + h + 1, :]
        bend(lambda rows: own_ref[h, rows, :], products_ref, probs_ref, ds_ref, h, lambda rows: delta, fold_ref)
    d_queries = dot_tn(ds_ref[0], keep_head(keys, 0))
    d_keys = dot_nn(ds_ref[0], keep_head(queries, 0))
    d_values = dot_nn(probs_ref[0], keep_head(back, 0))
    for h in range(1, heads):
        d_queries = d_queries + dot_tn(ds_ref[h], keep_head(keys, h))
        d_keys = d_keys + dot_nn(ds_ref[h], keep_head(queries, h))
        d_values = d_values + dot_nn(probs_ref[h], keep_head(back, h))
    dq_ref[...] = d_queries
    dk_ref[...] = d_keys
    dv_ref[...] = d_values


def far_back_kernel(
    info,
    far_ref,
    kp_ref,
    vp_ref,
    back_ref,
    stat_ref,
    dq_in,
    mixed_low,
    branch_ref,
    dq_ref,
    fold_ref,
    grad_ref,
    products_ref,
    ds_ref,
):
    grad_ref[...] = dot_tn(mixed_low[...], branch_ref[...]).astype(LOW)
    width = kp_ref.shape[1]
    heads = width // HEAD

    @pl.when(info[3] == 1)
    def _():
        keys, values = kp_ref[...], vp_ref[...]
        back = back_ref[...]
        for h in range(heads):
            products_ref[h] = dot_nt(keep_head(back, h), values)
        for h in range(heads):
            bend(
                lambda rows: far_ref[h, rows, :],
                products_ref,
                None,
                ds_ref,
                h,
                lambda rows: stat_ref[rows, heads + h : heads + h + 1],
                fold_ref,
            )
        d_queries = dq_in[...]
        for h in range(heads):
            d_queries = d_queries + dot_nn(ds_ref[h], keep_head(keys, h))
        dq_ref[...] = (d_queries * HEAD**-0.5).astype(LOW)

    @pl.when(info[3] == 0)
    def _():
        dq_ref[...] = (dq_in[...] * HEAD**-0.5).astype(LOW)


def partner_back_kernel(
    info,
    near_ref,
    v_ref,
    qp_ref,
    from_even,
    from_odd,
    dk_in,
    dv_in,
    dq_ref,
    normed_ref,
    x_all,
    gain,
    wq,
    wk,
    wv,
    grad_in,
    gain_in,
    one_send,
    one_keep,
    two_send,
    two_keep,
    send_ref,
    keep_ref,
    small_ref,
    d_all,
    products_ref,
    probs_ref,
    ds_ref,
):
    window, width = v_ref.shape
    heads = width // HEAD
    y, c = info[0], info[1]
    d_all[:, :width] = dq_ref[...]

    @pl.when(info[3] == 1)
    def _():
        payload = jnp.where(info[6] == 1, from_even[...], from_odd[...])
        queries, values = qp_ref[...], v_ref[...]
        back = unpack_lanes(payload, window)
        at = window + window // 2
        blocks = [payload[at + a * EXTRA : at + (a + 1) * EXTRA, :] for a in range(window // CHUNK)]
        columns = jnp.concatenate(blocks, axis=1).astype(F32)
        for h in range(heads):
            products_ref[h] = dot_nt(keep_head(values, h), back)
        for h in range(heads):
            at = h
            lse = columns[at : at + 1, :] + columns[at + 2 * heads : at + 2 * heads + 1, :]
            at = at + heads
            delta = columns[at : at + 1, :] + columns[at + 2 * heads : at + 2 * heads + 1, :]
            bend(
                lambda rows: jnp.exp(near_ref[h, rows, :] - lse),
                products_ref,
                probs_ref,
                ds_ref,
                h,
                lambda rows: delta,
                None,
            )
        d_keys, d_values = dk_in[...], dv_in[...]
        for h in range(heads):
            d_keys = d_keys + dot_nn(ds_ref[h], keep_head(queries, h))
            d_values = d_values + dot_nn(probs_ref[h], keep_head(back, h))
        d_all[:, width : 2 * width] = d_keys.astype(LOW)
        d_all[:, 2 * width :] = d_values.astype(LOW)

    @pl.when(info[3] == 0)
    def _():
        d_all[:, width : 2 * width] = dk_in[...].astype(LOW)
        d_all[:, 2 * width :] = dv_in[...].astype(LOW)

    joint = dot_tn(d_all[...], normed_ref[...]).astype(LOW)
    halves = (joint[:width, :], joint[width : 2 * width, :])
    for side in (0, 1):

        @pl.when(info[4] == side)
        def _():
            one_keep[...] = halves[side]
            one_send[...] = halves[1 - side]

    halves_two = (joint[2 * width :, :], grad_in[...])
    for side in (0, 1):

        @pl.when(info[5] == side)
        def _():
            two_keep[...] = halves_two[side]
            two_send[...] = halves_two[1 - side]

    gain_sum = jnp.zeros((1, x_all.shape[1]), F32)
    for part, core in enumerate((1 - c, c)):
        spots = (aligned((2 * y + core) * CHUNK), aligned((2 * (1 - y) + core) * CHUNK))
        mine = jnp.concatenate([d_all[spots[0], :], d_all[spots[1], :]], axis=0)
        d_normed = dot_nn(mine[:, :width], wq[...])
        d_normed = d_normed + dot_nn(mine[:, width : 2 * width], wk[...])
        d_normed = d_normed + dot_nn(mine[:, 2 * width :], wv[...])
        wide = jnp.concatenate([x_all[spots[0], :], x_all[spots[1], :]], axis=0).astype(F32)
        gain_sum = gain_sum + jnp.sum(d_normed * (wide * rows_norm(wide)), axis=0, keepdims=True)
        if part == 0:
            send_ref[: 2 * CHUNK, :] = d_normed.astype(LOW)
        else:
            keep_ref[...] = d_normed
    small = jnp.concatenate([gain_sum, gain_in[...], jnp.zeros((6, gain_sum.shape[1]), F32)], axis=0)
    small_ref[...] = small
    put_small(send_ref, 2 * CHUNK, small)


def put_small(target, start, small):
    high = small.astype(LOW).astype(F32)
    target[start : start + EXTRA, :] = jnp.concatenate([high, small - high], axis=0).astype(LOW)


def get_small(source, start):
    both = source[start : start + EXTRA, :].astype(F32)
    return both[: EXTRA // 2] + both[EXTRA // 2 :]


def first_merge_kernel(keep_ref, got_ref, small_in, send_ref, own_ref, small_ref):
    local = own_ref.shape[0]
    total = (keep_ref[...] + got_ref[: 2 * local, :].astype(F32)).astype(LOW)
    own_ref[...] = total[:local, :]
    send_ref[:local, :] = total[local:, :]
    small = small_in[...] + get_small(got_ref, 2 * local)
    small_ref[...] = small
    put_small(send_ref, local, small)


def input_back_kernel(own_ref, got_ref, x_ref, dh_ref, gain, small_in, table_ref, out_ref, small_ref):
    local = own_ref.shape[0]
    d_normed = own_ref[...].astype(F32) + got_ref[:local, :].astype(F32)
    wide = x_ref[...].astype(F32)
    inverse = rows_norm(wide)
    unit = wide * inverse
    scaled = d_normed * as_row(gain)
    back = inverse * (scaled - unit * jnp.mean(unit * scaled, axis=-1, keepdims=True))
    out_ref[...] = (dh_ref[...] + back).astype(LOW)
    small_ref[...] = small_in[...] + get_small(got_ref, local)
    heads, buckets = table_ref.shape
    small_ref[2 : 2 + heads, :buckets] = table_ref[...]


def halve_kernel(info, *refs, bits):
    count = len(bits)
    for k, bit in enumerate(bits):
        keep, got = refs[2 * k], refs[2 * k + 1]
        send_ref, keep_ref = refs[2 * count + 2 * k], refs[2 * count + 2 * k + 1]
        half = send_ref.shape[0]
        side = (info[7] >> bit) & 1
        for first, target in ((1 - side, send_ref), (side, keep_ref)):
            rows = pl.ds(pl.multiple_of(first * half, 16), half)
            target[...] = (keep[rows, :].astype(F32) + got[rows, :].astype(F32)).astype(LOW)


def sum_kernel(*refs, count, small):
    for k in range(count):
        keep, got = refs[2 * k], refs[2 * k + 1]
        target = refs[2 * count + small + k]
        rows = keep.shape[0]
        target[:rows, :] = (keep[...].astype(F32) + got[...].astype(F32)).astype(LOW)
        if small and k == 0:
            put_small(target, rows, refs[2 * count][...])


def pair_kernel(*refs, count, small):
    for k in range(count):
        mine, got, target = refs[2 * k], refs[2 * k + 1], refs[2 * count + k]
        extra = EXTRA if small and k == 0 else 0
        rows = mine.shape[0] - extra
        target[:rows, :] = (mine[:rows, :].astype(F32) + got[:rows, :].astype(F32)).astype(LOW)
        if extra:
            put_small(target, rows, get_small(mine, rows) + get_small(got, rows))


def double_kernel(info, *refs, bits, small):
    count = len(bits)
    for k, bit in enumerate(bits):
        mine, got, target = refs[2 * k], refs[2 * k + 1], refs[2 * count + k]
        extra = EXTRA if small and k == 0 else 0
        rows = mine.shape[0] - extra
        side = (info[7] >> bit) & 1
        target[pl.ds(pl.multiple_of(side * rows, 16), rows), :] = mine[:rows, :]
        target[pl.ds(pl.multiple_of((1 - side) * rows, 16), rows), :] = got[:rows, :]
        if extra:
            put_small(target, 2 * rows, get_small(mine, rows) + get_small(got, rows))


def attention_total_kernel(
    info, one, one_got, two, two_got, q_ref, k_ref, v_ref, out_ref, gain_one_ref, gain_two_ref, table_ref
):
    rows = q_ref.shape[0]
    first = info[4] == 0
    mine, got = one[:rows, :], one_got[:rows, :]
    q_ref[...] = jnp.where(first, mine, got).astype(F32)
    k_ref[...] = jnp.where(first, got, mine).astype(F32)
    first = info[5] == 0
    v_ref[...] = jnp.where(first, two[...], two_got[...]).astype(F32)
    out_ref[...] = jnp.where(first, two_got[...], two[...]).astype(F32)
    if one.shape[0] > rows:
        small = get_small(one, rows) + get_small(one_got, rows)
        for k in range(gain_one_ref.shape[0]):
            columns = slice(k * CHUNK, (k + 1) * CHUNK)
            gain_one_ref[k : k + 1, :] = small[0:1, columns]
            gain_two_ref[k : k + 1, :] = small[1:2, columns]
        heads, buckets = table_ref.shape
        table_ref[...] = small[2 : 2 + heads, :buckets]
    else:
        gain_one_ref[...] = jnp.zeros_like(gain_one_ref)
        gain_two_ref[...] = jnp.zeros_like(gain_two_ref)
        table_ref[...] = jnp.zeros_like(table_ref)


def swap(values, axis, bit):
    return lax.ppermute(values, axis, [(i, i ^ bit) for i in range(lax.axis_size(axis))])


def swap_odd(values):
    ends = range(1, lax.axis_size("dp") - 1, 2)
    return lax.ppermute(values, "dp", [(i, i + 1) for i in ends] + [(i + 1, i) for i in ends])


def after(values, *others):
    return lax.optimization_barrier((values, *others))[0]


def spread(own, across=None):
    across = swap(own, "mp", 2) if across is None else across
    return own, across, swap(own, "mp", 1), swap(across, "mp", 1)


def cut(values, first, count):
    return lax.dynamic_slice_in_dim(values, first, count)


class Sums:
    def __init__(self, info, rank, orders, sends, keeps):
        self.info, self.rank, self.orders, self.keeps = info, rank, orders, list(keeps)
        self.bits = len(orders[0])
        self.tiled = all((k.shape[0] >> (self.bits - 2)) % 16 == 0 for k in keeps)
        self.step, self.small = 0, None
        self.exchange(sends)

    def exchange(self, sends):
        done = self.step if self.step < self.bits else 2 * self.bits - 2 - self.step
        self.now = [order[done] for order in self.orders]
        self.gots = [swap(v, "dp", 1 << bit) for v, bit in zip(sends, self.now)]
        self.step += 1

    def pairs(self):
        return [v for pair in zip(self.keeps, self.gots) for v in pair]

    def advance(self, token, small=None, micros=1):
        self.keeps[0] = after(self.keeps[0], token)
        count = len(self.keeps)
        if self.step < self.bits - 1:
            bits = [order[self.step] for order in self.orders]
            halves = [v.shape[0] // 2 for v in self.keeps]
            if self.tiled:
                out = call(
                    functools.partial(halve_kernel, bits=bits),
                    [shape((h, v.shape[1]), LOW) for h, v in zip(halves, self.keeps) for _ in range(2)],
                    [self.info, *self.pairs()],
                    micros=micros,
                )
                sends, self.keeps = out[0::2], list(out[1::2])
            else:
                sends, keeps = [], []
                for k, g, h, bit in zip(self.keeps, self.gots, halves, bits):
                    side = (self.rank >> bit) & 1
                    total = (k.astype(F32) + g.astype(F32)).astype(LOW)
                    sends.append(cut(total, (1 - side) * h, h))
                    keeps.append(cut(total, side * h, h))
                self.keeps = keeps
        elif self.step == self.bits - 1:
            if self.tiled:
                self.small = small
                rows = [v.shape[0] for v in self.keeps]
                if small is not None:
                    rows[0] += EXTRA
                sends = call(
                    functools.partial(sum_kernel, count=count, small=int(small is not None)),
                    [shape((r, v.shape[1]), LOW) for r, v in zip(rows, self.keeps)],
                    self.pairs() + ([small] if small is not None else []),
                    smem=0,
                    micros=micros,
                )
            else:
                sends = [(k.astype(F32) + g.astype(F32)).astype(LOW) for k, g in zip(self.keeps, self.gots)]
            self.keeps = list(sends)
        elif self.step == self.bits:
            if self.tiled:
                sends = call(
                    functools.partial(pair_kernel, count=count, small=self.small is not None),
                    [shape(v.shape, LOW) for v in self.keeps],
                    self.pairs(),
                    smem=0,
                    micros=micros,
                )
            else:
                sends = [(k.astype(F32) + g.astype(F32)).astype(LOW) for k, g in zip(self.keeps, self.gots)]
            self.keeps = list(sends)
        else:
            has = self.small is not None
            if self.tiled:
                rows = [2 * v.shape[0] for v in self.keeps]
                if has:
                    rows[0] -= EXTRA
                sends = call(
                    functools.partial(double_kernel, bits=self.now, small=has),
                    [shape((r, v.shape[1]), LOW) for r, v in zip(rows, self.keeps)],
                    [self.info, *self.pairs()],
                    micros=micros,
                )
            else:
                sends = []
                for k, g, bit in zip(self.keeps, self.gots, self.now):
                    side = (self.rank >> bit) & 1
                    sends.append(
                        jnp.where(side == 0, jnp.concatenate([k, g], axis=0), jnp.concatenate([g, k], axis=0))
                    )
            self.keeps = list(sends)
        self.exchange(sends)
        return sends[0]


def per_device(
    inputs,
    attention_gain,
    query_weight,
    key_weight,
    value_weight,
    out_weight,
    bias_table,
    feedforward_gain,
    gate_weight,
    up_weight,
    down_weight,
    segment,
    bucket,
    cotangent,
):
    parts = lax.axis_size("mp")
    groups = lax.axis_size("dp")
    local, d = inputs.shape
    window = local * parts
    width = query_weight.shape[1]
    heads = width // HEAD
    units = gate_weight.shape[1]
    buckets = bias_table.shape[0]
    half = 2 * local
    rank = lax.axis_index("dp")
    member = lax.axis_index("mp")
    bits = list(range(groups.bit_length() - 1))
    order_one = bits
    order_two = [bits[1], bits[0]] + bits[2:]

    x_across = swap(inputs, "mp", 2)
    from_even = swap(inputs, "dp", 1)
    from_odd = swap_odd(inputs)

    spot = jnp.stack([rank, member]).astype(jnp.int32)
    edge = jnp.full((1,), -1, jnp.int32)
    bucket_rows = jnp.concatenate([edge, bucket]).reshape(-1, CHUNK)
    table = bias_table.T
    gain_one, gain_two = attention_gain.reshape(-1, CHUNK), feedforward_gain.reshape(-1, CHUNK)
    band = shape((heads, CHUNK, SPAN), F32)
    segments = segment.reshape(-1, CHUNK)
    info, seg_row, seg_col, bias, table, gain_one, gain_two = call(
        functools.partial(setup_kernel, groups=groups, first_bits=(order_one[0], order_two[0])),
        [shape((8,), jnp.int32), shape((1, window), F32), shape((window, CHUNK), F32), band]
        + [shape(v.shape, F32) for v in (table, gain_one, gain_two)],
        [spot, bucket_rows] + [in_hbm(v) for v in (segments, table, gain_one, gain_two)],
        scratch=[pltpu.VMEM(segments.shape, jnp.int32), pltpu.SemaphoreType.DMA((4,))],
        hbm=4,
        out_smem=1,
        micros=3.0,
    )
    cot_across = swap(cotangent, "mp", 2)
    (near,) = call(near_kernel, [shape((local, d), LOW)], [info, after(from_even, x_across, cot_across), from_odd], micros=0.5)
    near_across = swap(near, "mp", 2)
    near_core = swap(near, "mp", 1)
    x_pieces = (inputs, x_across, swap(inputs, "mp", 1), swap(after(x_across, bias), "mp", 1))

    low_rows = shape((window, width), LOW)
    wide_rows = shape((window, width), F32)
    stats = shape((window, CHUNK), F32)
    square_wide = pltpu.VMEM((heads, window, window), F32)
    square_low = pltpu.VMEM((heads, window, window), LOW)
    weight = shape((width, d), LOW)
    x_all, normed, queries, keys, values, acc, top, total, wq, wk, wv = call(
        own_kernel,
        [shape((window, d), LOW)] * 2 + [low_rows] * 3 + [wide_rows, stats, stats] + [weight] * 3,
        [info, x_across, *x_pieces[2:], gain_one, bias, seg_col, seg_row]
        + [in_hbm(v) for v in (inputs, query_weight.T, key_weight.T, value_weight.T)],
        scratch=[square_wide, square_low, pltpu.VMEM((local, d), LOW), pltpu.SemaphoreType.DMA((4,))],
        hbm=4,
        micros=5.0,
    )
    near_pieces = (near, near_across, near_core, swap(after(near_across, acc), "mp", 1))
    mixed_low, packed, mixed, lse, queries_near, keys_near, values_near = call(
        partner_kernel,
        [low_rows, shape((window + window // 2, CHUNK), LOW), wide_rows, stats] + [low_rows] * 3,
        [info, *near_pieces, gain_one, wq, wk, wv, bias, queries, acc, top, total],
        scratch=[
            pltpu.VMEM((window, d), LOW),
            square_wide,
            square_low,
            pltpu.VMEM((window, width), F32),
            pltpu.VMEM((window, CHUNK), F32),
            pltpu.VMEM((window, CHUNK), F32),
        ],
        micros=300,
    )
    mixed_across = swap(packed, "mp", 2)
    mixed_core = swap(packed, "mp", 1)
    cot_pieces = (
        cotangent,
        cot_across,
        swap(after(cotangent, mixed_core), "mp", 1),
        swap(after(cot_across, mixed_core), "mp", 1),
    )
    out_across = swap(after(out_weight, near), "mp", 2)
    out_pieces = (
        out_weight,
        out_across,
        swap(after(out_weight, mixed_core), "mp", 1),
        swap(after(out_across, mixed_core), "mp", 1),
    )
    bias_t, flipped_rows = call(
        flipped_kernel,
        [band, shape(bucket_rows.shape, jnp.int32)],
        [after(bucket_rows, mixed_low), table],
        smem=0,
        micros=3.0,
    )
    cot_all, d_act = call(
        cotangent_kernel,
        [shape((window, d), LOW), shape((window, units), F32)],
        [*cot_pieces, after(down_weight, mixed_across)],
        smem=0,
        micros=1.0,
    )
    (base,) = call(
        base_kernel,
        [shape((window, d), F32)],
        [x_all, after(mixed_low, bias_t), out_weight],
        smem=0,
        micros=1.0,
    )
    mixed_pieces = (mixed_low, mixed_across, mixed_core, swap(after(mixed_across, bias_t, base), "mp", 1))
    second, hidden, act, d_gate, d_up, second_send, second_keep, gain_two_part = call(
        feed_kernel,
        [shape((window, d), LOW), shape((half, d), F32)]
        + [shape((window, units), LOW)] * 3
        + [shape((half, d), LOW), shape((half, d), F32), shape((1, d), F32)],
        [info, base, *mixed_pieces[1:], *out_pieces[1:], d_act, gain_two, gate_weight, up_weight],
        micros=5.0,
    )
    (second_sum,) = call(
        functools.partial(sum_kernel, count=1, small=0),
        [shape((half, d), LOW)],
        [second_keep, swap(second_send, "mp", 1)],
        smem=0,
        micros=1.0,
    )
    second_other = swap(second_sum, "mp", 2)
    rows = d + units // 2 + units // 4
    gate_send, gate_keep, up_send, up_keep = call(
        feed_grad_kernel,
        [shape((rows // 2, units), LOW)] * 4,
        [info, after(second, second_sum), d_gate, d_up, act, cot_all],
        scratch=[pltpu.VMEM((rows, units), LOW)] * 2,
        micros=3.0,
    )
    feed_sums = Sums(info, rank, (order_one, order_two), (gate_send, up_send), (gate_keep, up_keep))
    feed_send, feed_keep = call(
        feed_out_kernel, [shape((half, d), LOW)] * 2, [after(act, gate_send), down_weight], smem=0, micros=30
    )
    feed_got = swap(feed_send, "mp", 1)
    block = shape((heads, window, window), F32)
    own_probs, far_probs, near_scores = call(
        recall_kernel,
        [block] * 3,
        [
            info,
            after(queries, feed_send),
            keys,
            queries_near,
            keys_near,
            lse,
            bias,
            bias_t,
            seg_col,
            seg_row,
        ],
        micros=1.0,
    )
    second_other = after(second_other, own_probs)
    dh, branch_low = call(
        hidden_back_kernel,
        [shape((local, d), F32), shape((half, d), LOW)],
        [second_sum, second_other, hidden, cot_pieces[0], cot_pieces[1], gain_two],
        smem=0,
    )
    feed_own, feed_cross = call(
        feed_merge_kernel,
        [shape((local, d), LOW)] * 2,
        [after(feed_keep, branch_low), feed_got],
        smem=0,
        micros=100,
    )
    payload, back, stat_back, branch_all = call(
        mixed_back_kernel,
        [shape((window + window // 2 + window // CHUNK * EXTRA, CHUNK), LOW), low_rows, stats, shape((window, d), LOW)],
        [info, after(branch_low, feed_cross), swap(branch_low, "mp", 1), out_weight, mixed, lse],
    )
    payload_even = swap(payload, "dp", 1)
    payload_odd = swap_odd(payload)
    token = feed_sums.advance(payload)
    fold = shape((heads, CHUNK, 2 * window), F32)
    d_queries, d_keys, d_values, near_fold = call(
        own_back_kernel,
        [wide_rows, wide_rows, wide_rows, fold],
        [own_probs, after(queries, token), keys, values, back, stat_back],
        scratch=[square_wide, square_low, square_low],
        smem=0,
        micros=200,
    )
    d_queries, far_fold, out_grad = call(
        far_back_kernel,
        [low_rows, fold, shape((width, d), LOW)],
        [info, far_probs, keys_near, values_near, back, stat_back, d_queries, mixed_low, branch_all],
        scratch=[square_wide, square_low],
        micros=3.0,
    )
    one_send, one_keep, two_send, two_keep, first_send, first_keep, small = call(
        partner_back_kernel,
        [shape((width, d), LOW)] * 4
        + [shape((half + EXTRA, d), LOW), shape((half, d), F32), shape((EXTRA // 2, d), F32)],
        [
            info,
            near_scores,
            values,
            queries_near,
            payload_even,
            payload_odd,
            d_keys,
            d_values,
            d_queries,
            normed,
            x_all,
            gain_one,
            wq,
            wk,
            wv,
            out_grad,
            gain_two_part,
        ],
        scratch=[pltpu.VMEM((window, 3 * width), LOW), square_wide, square_low, square_low],
        micros=300,
    )
    token = feed_sums.advance(one_send, micros=300)
    joint_sums = Sums(info, rank, (order_one, order_two), (after(one_send, token), two_send), (one_keep, two_keep))
    first_send, first_own, small = call(
        first_merge_kernel,
        [shape((local + EXTRA, d), LOW), shape((local, d), LOW), shape((EXTRA // 2, d), F32)],
        [after(first_keep, token), swap(first_send, "mp", 1), small],
        smem=0,
        micros=1,
    )
    first_got = swap(first_send, "mp", 2)
    token = joint_sums.advance(first_send)
    (table_part,) = call(
        table_kernel,
        [shape((heads, CHUNK), F32)],
        [info, after(near_fold, token), far_fold, flipped_rows, bucket_rows],
        micros=1.0,
    )
    input_grad, small = call(
        input_back_kernel,
        [shape((local, d), LOW), shape((EXTRA // 2, d), F32)],
        [first_own, first_got, inputs, after(dh, token), gain_one, small, table_part],
        smem=0,
        micros=1,
    )
    token = joint_sums.advance(small, small)
    token = feed_sums.advance(token)
    feed_got = swap(after(feed_cross, token), "mp", 2)
    token = joint_sums.advance(token, small, micros=1)
    token = feed_sums.advance(token)
    last = 2 * len(bits) - 1
    while joint_sums.step < last or feed_sums.step < last:
        if joint_sums.step < last:
            token = joint_sums.advance(token, small, micros=300)
        if feed_sums.step < last:
            token = feed_sums.advance(token)
    (layer_out,) = call(
        layer_out_kernel,
        [shape((local, d), LOW)],
        [after(hidden, token), feed_own, feed_got],
        smem=0,
        micros=40,
    )
    ready = feed_sums.pairs()
    gate_grad, up_grad, down_grad = call(
        feed_total_kernel,
        [shape((d, units), F32)] * 2 + [shape((units, d), F32)],
        [info, after(ready[0], layer_out), *ready[1:]],
        scratch=[pltpu.VMEM((rows, units), LOW)],
        micros=2.0,
    )
    ready = joint_sums.pairs()
    query_grad, key_grad, value_grad, out_total, gain_one_total, gain_two_total, table_total = call(
        attention_total_kernel,
        [shape((width, d), F32)] * 4 + [shape((d // CHUNK, CHUNK), F32)] * 2 + [shape((heads, buckets), F32)],
        [info, after(ready[0], down_grad), *ready[1:]],
        micros=2.0,
    )
    if not joint_sums.tiled:
        small = lax.psum(small, "dp")
        gain_one_total, gain_two_total = small[0].reshape(-1, CHUNK), small[1].reshape(-1, CHUNK)
        table_total = small[2 : 2 + heads, :buckets]
    return (
        layer_out,
        input_grad,
        gain_one_total.reshape(-1),
        query_grad.T,
        key_grad.T,
        value_grad.T,
        out_total,
        table_total.T,
        gain_two_total.reshape(-1),
        gate_grad,
        up_grad,
        down_grad,
    )


def solution(mesh):
    rows = P(("dp", "mp"), None)
    in_specs = (
        rows,
        P(),
        P(None, "mp"),
        P(None, "mp"),
        P(None, "mp"),
        P("mp", None),
        P(None, "mp"),
        P(),
        P(None, "mp"),
        P(None, "mp"),
        P("mp", None),
        P(),
        P(),
        rows,
    )
    out_specs = (
        rows,
        rows,
        P(),
        P(None, "mp"),
        P(None, "mp"),
        P(None, "mp"),
        P("mp", None),
        P(None, "mp"),
        P(),
        P(None, "mp"),
        P(None, "mp"),
        P("mp", None),
    )
    return jax.shard_map(
        per_device, mesh=mesh, in_specs=in_specs, out_specs=out_specs, check_vma=False
    )
```

```python
import functools

import jax
import jax.numpy as jnp
from jax import lax
from jax.experimental import pallas as pl
from jax.experimental.pallas import tpu as pltpu
from jax.sharding import PartitionSpec as P

HEAD = 64
LOW = jnp.bfloat16
F32 = jnp.float32
CHUNK = 128
SPAN = 2048
EXTRA = 16
NEG = -1e30
ROOT = 0.7978845608
CUBE = 0.044715
VMEM = pl.BlockSpec(memory_space=pltpu.VMEM)
SMEM = pl.BlockSpec(memory_space=pltpu.SMEM)
HBM = pl.BlockSpec(memory_space=pltpu.HBM)


def dot_nn(a, b):
    return lax.dot_general(a, b, (((1,), (0,)), ((), ())), preferred_element_type=F32)


def dot_nt(a, b):
    return lax.dot_general(a, b, (((1,), (1,)), ((), ())), preferred_element_type=F32)


def dot_tn(a, b):
    return lax.dot_general(a, b, (((0,), (0,)), ((), ())), preferred_element_type=F32)


def call(kernel, outs, ins, scratch=(), smem=1, hbm=0, micros=2.0, out_smem=0, out_hbm=0, limit=20):
    return pl.pallas_call(
        kernel,
        out_shape=outs,
        in_specs=[SMEM] * smem + [VMEM] * (len(ins) - smem - hbm) + [HBM] * hbm,
        out_specs=[SMEM] * out_smem + [HBM] * out_hbm + [VMEM] * (len(outs) - out_smem - out_hbm),
        scratch_shapes=list(scratch),
        cost_estimate=pl.CostEstimate(flops=int(micros * 2e7), bytes_accessed=0, transcendentals=0),
        compiler_params=pltpu.CompilerParams(vmem_limit_bytes=limit * 1024 * 1024),
    )(*ins)


def in_hbm(values):
    return pltpu.with_memory_space_constraint(values, pltpu.HBM)


def shape(dims, dtype):
    return jax.ShapeDtypeStruct(dims, dtype)


def head_lanes(width, h):
    lane = lax.broadcasted_iota(jnp.int32, (1, width), 1)
    return (lane >= h * HEAD) & (lane < (h + 1) * HEAD)


def keep_head(values, h):
    return jnp.where(head_lanes(values.shape[-1], h), values, jnp.zeros_like(values))


def rows_norm(values):
    return lax.rsqrt(jnp.mean(values * values, axis=-1, keepdims=True) + 1e-06)


def as_row(ref):
    return jnp.concatenate([ref[k : k + 1, :] for k in range(ref.shape[0])], axis=1)


def aligned(start):
    return pl.ds(pl.multiple_of(start, CHUNK), CHUNK)


def lay_bias(row, table_ref, target):
    heads, buckets = table_ref.shape
    which = lax.broadcasted_iota(jnp.int32, (buckets, SPAN), 0)
    onehot = (row == which).astype(F32)
    table = table_ref[...].T
    for h in range(heads):
        rows = jnp.sum(onehot * table[:, h : h + 1], axis=0, keepdims=True)
        count = 1
        while count < 8:
            rows = jnp.concatenate([rows, pltpu.roll(rows, count, 1)], axis=0)
            count *= 2
        target[h, 0:8, :] = rows
        while count < CHUNK:
            target[h, count : 2 * count, :] = pltpu.roll(target[h, 0:count, :], count, 1)
            count *= 2


def setup_kernel(
    spot,
    bucket_ref,
    segment_hbm,
    table_hbm,
    one_hbm,
    two_hbm,
    info,
    row_ref,
    col_ref,
    bias_ref,
    table_ref,
    one_ref,
    two_ref,
    segment_ref,
    sems,
    *,
    groups,
    first_bits,
):
    pairs = ((segment_hbm, segment_ref), (table_hbm, table_ref), (one_hbm, one_ref), (two_hbm, two_ref))
    copies = [pltpu.make_async_copy(a, b, sems.at[k]) for k, (a, b) in enumerate(pairs)]
    for copy in copies:
        copy.start()
    for copy in copies:
        copy.wait()
    rank, member = spot[0], spot[1]
    steps = row_ref.shape[1] // CHUNK
    rows = [segment_ref[pl.ds(rank * steps + k, 1), :] for k in range(steps)]
    lane = lax.broadcasted_iota(jnp.int32, (1, CHUNK), 1)

    def value(row, at):
        return jnp.max(jnp.where(lane == at, row, -1))

    before = segment_ref[pl.ds(jnp.maximum(rank * steps - 1, 0), 1), :]
    later = segment_ref[pl.ds(jnp.minimum((rank + 1) * steps, groups * steps - 1), 1), :]
    left = (value(before, CHUNK - 1) == value(rows[0], 0)) & (rank > 0)
    right = (value(later, 0) == value(rows[-1], CHUNK - 1)) & (rank < groups - 1)
    even = jnp.where(rank % 2 == 0, right.astype(jnp.int32), left.astype(jnp.int32))
    info[0] = member // 2
    info[1] = member % 2
    info[2] = left.astype(jnp.int32)
    info[3] = (left | right).astype(jnp.int32)
    info[4] = (rank >> first_bits[0]) & 1
    info[5] = (rank >> first_bits[1]) & 1
    info[6] = even
    info[7] = rank
    row = jnp.concatenate(rows, axis=1).astype(F32)
    row_ref[...] = row
    col_ref[...] = jnp.broadcast_to(row, (CHUNK, row.shape[1])).T
    lay_bias(row_of(bucket_ref, 0, bucket_ref.shape[0]), table_ref, bias_ref)


def row_of(ref, first, count):
    return jnp.concatenate([ref[pl.ds(first + k, 1), :] for k in range(count)], axis=1)


def flipped_kernel(bucket_ref, table_ref, bias_ref, flipped_ref):
    count = bucket_ref.shape[0]
    sub = lax.broadcasted_iota(jnp.int32, (CHUNK, CHUNK), 0)
    lane = lax.broadcasted_iota(jnp.int32, (CHUNK, CHUNK), 1)
    turned = dot_nn(bucket_ref[...].astype(F32).astype(LOW), (sub + lane == CHUNK - 1).astype(F32).astype(LOW))
    row = jnp.concatenate([turned[k : k + 1, :] for k in reversed(range(count))], axis=1)
    row = pltpu.roll(row, 1, 1).astype(jnp.int32)
    flipped_ref[...] = jnp.concatenate([row[:, k * CHUNK : (k + 1) * CHUNK] for k in range(count)], axis=0)
    lay_bias(row, table_ref, bias_ref)


def near_kernel(info, even_ref, odd_ref, out_ref):
    out_ref[...] = jnp.where(info[6] == 1, even_ref[...], odd_ref[...])


def fold_diagonals(tile):
    rows, cols = tile.shape
    while rows > 1:
        rows //= 2
        tile = tile[:rows] + pltpu.roll(tile[rows:], cols - rows, 1)
    return tile


def pack_columns(columns, offset=0, base=None, width=CHUNK):
    rows = columns[0].shape[0]
    lane = lax.broadcasted_iota(jnp.int32, (rows, width), 1)
    out = jnp.zeros((rows, width), F32) if base is None else base
    for k, column in enumerate(columns):
        out = jnp.where(lane == offset + k, column, out)
    return out


def by_head(packed, width):
    lane = lax.broadcasted_iota(jnp.int32, (packed.shape[0], width), 1)
    out = packed[:, 0:1]
    for h in range(1, width // HEAD):
        out = jnp.where(lane >= h * HEAD, packed[:, h : h + 1], out)
    return out


def pack_lanes(values, target):
    rows = values.shape[0]
    target[:rows, :] = values[:, :CHUNK]
    rest = values[:, CHUNK:]
    target[rows : rows + rows // 2, :] = jnp.concatenate([rest[: rows // 2], rest[rows // 2 :]], axis=1)


def unpack_lanes(packed, rows):
    rest = packed[rows : rows + rows // 2, :]
    half = CHUNK // 2
    return jnp.concatenate(
        [packed[:rows, :], jnp.concatenate([rest[:, :half], rest[:, half:]], axis=0)], axis=1
    )


def place(y, c):
    return (2 * y + c, 2 * (1 - y) + c, 2 * y + 1 - c, 2 * (1 - y) + 1 - c)


def project(normed, rows, wq, wk, wv, q_ref, k_ref, v_ref):
    q_ref[rows, :] = (dot_nt(normed, wq[...]).astype(LOW).astype(F32) * HEAD**-0.5).astype(LOW)
    k_ref[rows, :] = dot_nt(normed, wk[...]).astype(LOW)
    v_ref[rows, :] = dot_nt(normed, wv[...]).astype(LOW)


def attend(q, keys, values, bias, first, seg_col, seg_row, scores_ref, probs_ref, acc_ref, top_ref, sum_ref):
    window, width = q.shape
    heads = width // HEAD
    for h in range(heads):
        scores_ref[h] = dot_nt(keep_head(q, h), keys)
    for h in range(heads):
        for a in range(window // CHUNK):
            rows = slice(a * CHUNK, (a + 1) * CHUNK)
            scores = scores_ref[h, rows, :] + bias[h, :, pl.ds(first - a * CHUNK, window)]
            if seg_col is not None:
                scores = jnp.where(seg_col[rows, 0:1] == seg_row[...], scores, NEG)
            top = jnp.max(scores, axis=-1, keepdims=True)
            weights = jnp.exp(scores - top)
            probs_ref[h, rows, :] = weights.astype(LOW)
            top_ref[rows, :] = pack_columns([top], h, top_ref[rows, :] if h else jnp.zeros((CHUNK, CHUNK), F32))
            total = jnp.sum(weights, axis=-1, keepdims=True)
            sum_ref[rows, :] = pack_columns([total], h, sum_ref[rows, :] if h else jnp.ones((CHUNK, CHUNK), F32))
    total = dot_nn(probs_ref[0], keep_head(values, 0))
    for h in range(1, heads):
        total = total + dot_nn(probs_ref[h], keep_head(values, h))
    acc_ref[...] = total


def own_kernel(
    info,
    x1,
    x2,
    x3,
    gain,
    bias,
    seg_col,
    seg_row,
    x_hbm,
    wq_hbm,
    wk_hbm,
    wv_hbm,
    x_all,
    normed_ref,
    q_ref,
    k_ref,
    v_ref,
    acc_ref,
    top_ref,
    sum_ref,
    wq,
    wk,
    wv,
    scores_ref,
    probs_ref,
    x0,
    sems,
):
    pairs = ((x_hbm, x0), (wq_hbm, wq), (wk_hbm, wk), (wv_hbm, wv))
    copies = [pltpu.make_async_copy(a, b, sems.at[k]) for k, (a, b) in enumerate(pairs)]
    for copy in copies:
        copy.start()
    spots = place(info[0], info[1])
    for piece, spot in zip((x1, x2, x3, x0), spots[1:] + spots[:1]):
        if piece is x0:
            copies[0].wait()
        rows = aligned(spot * CHUNK)
        low = piece[...]
        x_all[rows, :] = low
        wide = low.astype(F32)
        normed_ref[rows, :] = (wide * rows_norm(wide) * as_row(gain)).astype(LOW)
    for copy in copies[1:]:
        copy.wait()
    project(normed_ref[...], slice(None), wq, wk, wv, q_ref, k_ref, v_ref)
    attend(
        q_ref[...],
        k_ref[...],
        v_ref[...],
        bias,
        SPAN // 2,
        seg_col,
        seg_row,
        scores_ref,
        probs_ref,
        acc_ref,
        top_ref,
        sum_ref,
    )


def far_start(info, window):
    return pl.multiple_of(jnp.where(info[2] == 1, SPAN // 2 - window, SPAN // 2 + window), CHUNK)


def partner_kernel(
    info,
    x0,
    x1,
    x2,
    x3,
    gain,
    wq,
    wk,
    wv,
    bias,
    q_ref,
    acc_ref,
    top_ref,
    sum_ref,
    mixed_low,
    packed_ref,
    mixed_ref,
    lse_ref,
    qp_ref,
    kp_ref,
    vp_ref,
    normed_ref,
    scores_ref,
    probs_ref,
    acc_two,
    top_two,
    sum_two,
):
    window, width = q_ref.shape
    paired = info[3]

    @pl.when(paired == 1)
    def _():
        for piece, spot in zip((x0, x1, x2, x3), place(info[0], info[1])):
            wide = piece[...].astype(F32)
            normed_ref[aligned(spot * CHUNK), :] = (wide * rows_norm(wide) * as_row(gain)).astype(LOW)
        project(normed_ref[...], slice(None), wq, wk, wv, qp_ref, kp_ref, vp_ref)
        attend(
            q_ref[...],
            kp_ref[...],
            vp_ref[...],
            bias,
            far_start(info, window),
            None,
            None,
            scores_ref,
            probs_ref,
            acc_two,
            top_two,
            sum_two,
        )
        for a in range(window // CHUNK):
            rows = slice(a * CHUNK, (a + 1) * CHUNK)
            top = jnp.maximum(top_ref[rows, :], top_two[rows, :])
            one, two = jnp.exp(top_ref[rows, :] - top), jnp.exp(top_two[rows, :] - top)
            whole = sum_ref[rows, :] * one + sum_two[rows, :] * two
            inverse = 1.0 / whole
            mixed = acc_ref[rows, :] * by_head(one * inverse, width)
            mixed = mixed + acc_two[rows, :] * by_head(two * inverse, width)
            mixed_ref[rows, :] = mixed
            mixed_low[rows, :] = mixed.astype(LOW)
            lse_ref[rows, :] = top + jnp.log(whole)

    @pl.when(paired == 0)
    def _():
        qp_ref[...] = jnp.zeros_like(qp_ref)
        kp_ref[...] = jnp.zeros_like(kp_ref)
        vp_ref[...] = jnp.zeros_like(vp_ref)
        for a in range(window // CHUNK):
            rows = slice(a * CHUNK, (a + 1) * CHUNK)
            whole = sum_ref[rows, :]
            mixed = acc_ref[rows, :] * by_head(1.0 / whole, width)
            mixed_ref[rows, :] = mixed
            mixed_low[rows, :] = mixed.astype(LOW)
            lse_ref[rows, :] = top_ref[rows, :] + jnp.log(whole)

    pack_lanes(mixed_low[...], packed_ref)


def cotangent_kernel(g0, g1, g2, g3, down_w, cot_ref, d_act_ref):
    for part, piece in enumerate((g2, g3, g0, g1)):
        cot_ref[part * CHUNK : (part + 1) * CHUNK, :] = piece[...]
    d_act_ref[...] = dot_nt(cot_ref[...], down_w[...])


def base_kernel(x_all, m0, o0, base_ref):
    base_ref[...] = x_all[...].astype(F32) + dot_nn(m0[...], o0[...])


def feed_kernel(
    info,
    base_ref,
    m1,
    m2,
    m3,
    o1,
    o2,
    o3,
    d_act_ref,
    gain,
    gate_w,
    up_w,
    second_ref,
    hidden_ref,
    act_ref,
    dgate_ref,
    dup_ref,
    send_ref,
    keep_ref,
    gain_ref,
):
    y, c = info[0], info[1]
    half = 2 * CHUNK
    gain_sum = jnp.zeros((1, base_ref.shape[1]), F32)
    for part, core in enumerate((1 - c, c)):
        rows = slice(part * half, (part + 1) * half)
        spots = (aligned((2 * y + core) * CHUNK), aligned((2 * (1 - y) + core) * CHUNK))

        def pick(ref):
            return jnp.concatenate([ref[spots[0], :], ref[spots[1], :]], axis=0)

        hidden = pick(base_ref)
        window = base_ref.shape[0]
        for m, o in ((m2, o2), (m1, o1), (m3, o3)):
            parts = []
            for row in (y, 1 - y):
                block = m[aligned(window + core * CHUNK), :]
                lane = lax.broadcasted_iota(jnp.int32, block.shape, 1)
                parts.append(jnp.where(lane // HEAD == row, block, jnp.zeros_like(block)))
            both = jnp.concatenate([pick(m), jnp.concatenate(parts, axis=0)], axis=1)
            hidden = hidden + dot_nn(both, jnp.concatenate([o[...], o[CHUNK:, :]], axis=0))
        if part == 1:
            hidden_ref[...] = hidden
        unit = hidden * rows_norm(hidden)
        second = (unit * as_row(gain)).astype(LOW)
        second_ref[rows, :] = second
        gate = dot_nn(second, gate_w[...])
        up = dot_nn(second, up_w[...])
        d_act = d_act_ref[rows, :]
        square = gate * gate
        tanh = jnp.tanh(ROOT * gate * (1.0 + CUBE * square))
        low_half = 0.5 * (1.0 + tanh)
        gelu = gate * low_half
        slope = low_half + 0.5 * gate * (1.0 - tanh * tanh) * (ROOT * (1.0 + 3.0 * CUBE * square))
        act_ref[rows, :] = (gelu * up).astype(LOW)
        d_gate = (d_act * up * slope).astype(LOW)
        d_up = (d_act * gelu).astype(LOW)
        dgate_ref[rows, :] = d_gate
        dup_ref[rows, :] = d_up
        d_second = dot_nt(d_gate, gate_w[...]) + dot_nt(d_up, up_w[...])
        gain_sum = gain_sum + jnp.sum(d_second * unit, axis=0, keepdims=True)
        if part == 0:
            send_ref[...] = d_second.astype(LOW)
        else:
            keep_ref[...] = d_second
    gain_ref[...] = gain_sum


def feed_grad_kernel(
    info, second_ref, dgate_ref, dup_ref, act_ref, cot_ref, one_send, one_keep, two_send, two_keep, one_ref, two_ref
):
    d, units = second_ref.shape[1], dgate_ref.shape[1]
    one_ref[:d, :] = dot_tn(second_ref[...], dgate_ref[...]).astype(LOW)
    two_ref[:d, :] = dot_tn(second_ref[...], dup_ref[...]).astype(LOW)
    down = dot_tn(act_ref[...], cot_ref[...]).astype(LOW)
    half = units // 2
    quarter = half // 2
    for k, target in enumerate((one_ref, two_ref)):
        target[d : d + half, :] = down[k * half : (k + 1) * half, :units]
        for side in (0, 1):
            rows = slice(k * half + side * quarter, k * half + (side + 1) * quarter)
            target[d + half :, side * (units // 2) : (side + 1) * (units // 2)] = down[rows, units:]
    for source, side, send, keep in ((one_ref, info[4], one_send, one_keep), (two_ref, info[5], two_send, two_keep)):
        rows = send.shape[0]
        send[...] = source[pl.ds(pl.multiple_of((1 - side) * rows, 16), rows), :]
        keep[...] = source[pl.ds(pl.multiple_of(side * rows, 16), rows), :]


def feed_out_kernel(act_ref, down_w, send_ref, keep_ref):
    half = send_ref.shape[0]
    send_ref[...] = dot_nn(act_ref[:half, :], down_w[...]).astype(LOW)
    keep_ref[...] = dot_nn(act_ref[half:, :], down_w[...]).astype(LOW)


def feed_total_kernel(info, one, one_got, two, two_got, gate_ref, up_ref, down_ref, full_ref):
    d, units = gate_ref.shape
    half = units // 2
    quarter = half // 2
    parts = ((one, one_got, info[4], gate_ref), (two, two_got, info[5], up_ref))
    for k, (mine, got, side, target) in enumerate(parts):
        rows = mine.shape[0]
        full_ref[pl.ds(pl.multiple_of(side * rows, 16), rows), :] = mine[...]
        full_ref[pl.ds(pl.multiple_of((1 - side) * rows, 16), rows), :] = got[...]
        target[...] = full_ref[:d, :].astype(F32)
        down_ref[k * half : (k + 1) * half, :units] = full_ref[d : d + half, :].astype(F32)
        for part in (0, 1):
            rows = slice(k * half + part * quarter, k * half + (part + 1) * quarter)
            down_ref[rows, units:] = full_ref[d + half :, part * (units // 2) : (part + 1) * (units // 2)].astype(F32)


def feed_merge_kernel(keep_ref, got_ref, own_ref, send_ref):
    local = own_ref.shape[0]
    total = (keep_ref[...].astype(F32) + got_ref[...].astype(F32)).astype(LOW)
    own_ref[...] = total[:local, :]
    send_ref[...] = total[local:, :]


def layer_out_kernel(hidden_ref, own_ref, got_ref, out_ref):
    local = out_ref.shape[0]
    out_ref[...] = (hidden_ref[:local, :] + (own_ref[...].astype(F32) + got_ref[...].astype(F32))).astype(LOW)


def hidden_back_kernel(sum_ref, other_ref, hidden_ref, g0, g1, gain, dh_ref, low_ref):
    for part, cot in enumerate((g0, g1)):
        rows = slice(part * CHUNK, (part + 1) * CHUNK)
        flip = slice((1 - part) * CHUNK, (2 - part) * CHUNK)
        d_second = sum_ref[rows, :].astype(F32) + other_ref[flip, :].astype(F32)
        hidden = hidden_ref[rows, :]
        inverse = rows_norm(hidden)
        unit = hidden * inverse
        scaled = d_second * as_row(gain)
        dh = cot[...].astype(F32) + inverse * (scaled - unit * jnp.mean(unit * scaled, axis=-1, keepdims=True))
        low_ref[rows, :] = dh.astype(LOW)
        if part == 0:
            dh_ref[...] = dh


def mixed_back_kernel(
    info, pair_own, pair_other, out_w, mixed_ref, lse_ref, payload_ref, back_ref, stat_ref, branch_ref
):
    window, width = mixed_ref.shape
    heads = width // HEAD
    pieces = (pair_own[:CHUNK, :], pair_own[CHUNK:, :], pair_other[:CHUNK, :], pair_other[CHUNK:, :])
    for piece, spot in zip(pieces, place(info[0], info[1])):
        branch_ref[aligned(spot * CHUNK), :] = piece
    d_all = dot_nt(branch_ref[...], out_w[...]).astype(LOW)
    back_ref[...] = d_all
    pack_lanes(d_all, payload_ref)
    first = window + window // 2
    for a in range(window // CHUNK):
        rows = slice(a * CHUNK, (a + 1) * CHUNK)
        product = d_all[rows, :].astype(F32) * mixed_ref[rows, :]
        deltas = [jnp.sum(keep_head(product, h), axis=-1, keepdims=True) for h in range(heads)]
        stat = pack_columns(deltas, heads, lse_ref[rows, :])
        stat_ref[rows, :] = stat
        turned = stat.T[: 2 * heads, :]
        high = turned.astype(LOW).astype(F32)
        blank = jnp.zeros((EXTRA - 4 * heads, CHUNK), F32)
        block = jnp.concatenate([high, turned - high, blank], axis=0)
        payload_ref[first + a * EXTRA : first + (a + 1) * EXTRA, :] = block.astype(LOW)


def recall_kernel(
    info, q_ref, k_ref, qp_ref, kp_ref, lse_ref, bias, bias_t, seg_col, seg_row, own_ref, far_ref, near_ref
):
    window, width = q_ref.shape
    heads = width // HEAD
    queries, keys = q_ref[...], k_ref[...]
    for h in range(heads):
        own_ref[h] = dot_nt(keep_head(keys, h), queries)
    lse = lse_ref[...].T
    for h in range(heads):
        for a in range(window // CHUNK):
            rows = slice(a * CHUNK, (a + 1) * CHUNK)
            start = SPAN // 2 - a * CHUNK
            scores = own_ref[h, rows, :] + bias_t[h, :, start : start + window]
            scores = jnp.where(seg_col[rows, 0:1] == seg_row[...], scores, NEG)
            own_ref[h, rows, :] = jnp.exp(scores - lse[h : h + 1, :])

    @pl.when(info[3] == 1)
    def _():
        first = far_start(info, window)
        for h in range(heads):
            far_ref[h] = dot_nt(keep_head(queries, h), kp_ref[...])
            near_ref[h] = dot_nt(keep_head(keys, h), qp_ref[...])
        for h in range(heads):
            for a in range(window // CHUNK):
                rows = slice(a * CHUNK, (a + 1) * CHUNK)
                spot = pl.ds(pl.multiple_of(first - a * CHUNK, CHUNK), window)
                far_ref[h, rows, :] = jnp.exp(far_ref[h, rows, :] + bias[h, :, spot] - lse_ref[rows, h : h + 1])
                near_ref[h, rows, :] += bias_t[h, :, spot]


def bend(weights_of, products_ref, probs_ref, ds_ref, h, delta_of, fold_ref):
    window = products_ref.shape[1]
    steps = window // CHUNK
    for a in range(steps):
        rows = slice(a * CHUNK, (a + 1) * CHUNK)
        weights = weights_of(rows)
        d_scores = weights * (products_ref[h, rows, :] - delta_of(rows))
        ds_ref[h, rows, :] = d_scores.astype(LOW)
        if probs_ref is not None:
            probs_ref[h, rows, :] = weights.astype(LOW)
        if fold_ref is not None:
            at = (steps - a) * CHUNK
            if a == 0:
                fold_ref[h, :, :at] = jnp.zeros((CHUNK, at), F32)
                fold_ref[h, :, at:] = d_scores
            else:
                if a == steps - 1:
                    fold_ref[h, :, :CHUNK] = jnp.zeros((CHUNK, CHUNK), F32)
                fold_ref[h, :, at : at + window] += d_scores


def table_kernel(info, near_fold, far_fold, flipped_ref, bucket_ref, table_ref):
    window = near_fold.shape[2] // 2
    table_ref[...] = table_sums(near_fold, flipped_ref, SPAN // 2 - window, table_ref)

    @pl.when(info[3] == 1)
    def _():
        table_ref[...] += table_sums(far_fold, bucket_ref, far_start(info, window) - window, table_ref)


def table_sums(fold_ref, bucket_ref, start, table_ref):
    heads, buckets = table_ref.shape
    reach = fold_ref.shape[2]
    row = row_of(bucket_ref, start // CHUNK, reach // CHUNK)
    onehot = row == lax.broadcasted_iota(jnp.int32, (buckets, reach), 0)
    columns = []
    for h in range(heads):
        folded = fold_diagonals(fold_ref[h])
        columns.append(jnp.sum(jnp.where(onehot, folded, 0.0), axis=1, keepdims=True))
    return pack_columns(columns).T[:heads, :]


def own_back_kernel(
    own_ref,
    q_ref,
    k_ref,
    v_ref,
    back_ref,
    stat_ref,
    dq_ref,
    dk_ref,
    dv_ref,
    fold_ref,
    products_ref,
    probs_ref,
    ds_ref,
):
    window, width = q_ref.shape
    heads = width // HEAD
    queries, keys, values = q_ref[...], k_ref[...], v_ref[...]
    back = back_ref[...]
    stat = stat_ref[...].T
    for h in range(heads):
        products_ref[h] = dot_nt(keep_head(values, h), back)
    for h in range(heads):
        delta = stat[heads + h : heads + h + 1, :]
        bend(lambda rows: own_ref[h, rows, :], products_ref, probs_ref, ds_ref, h, lambda rows: delta, fold_ref)
    d_queries = dot_tn(ds_ref[0], keep_head(keys, 0))
    d_keys = dot_nn(ds_ref[0], keep_head(queries, 0))
    d_values = dot_nn(probs_ref[0], keep_head(back, 0))
    for h in range(1, heads):
        d_queries = d_queries + dot_tn(ds_ref[h], keep_head(keys, h))
        d_keys = d_keys + dot_nn(ds_ref[h], keep_head(queries, h))
        d_values = d_values + dot_nn(probs_ref[h], keep_head(back, h))
    dq_ref[...] = d_queries
    dk_ref[...] = d_keys
    dv_ref[...] = d_values


def far_back_kernel(
    info,
    far_ref,
    kp_ref,
    vp_ref,
    back_ref,
    stat_ref,
    dq_in,
    mixed_low,
    branch_ref,
    dq_ref,
    fold_ref,
    grad_ref,
    products_ref,
    ds_ref,
):
    grad_ref[...] = dot_tn(mixed_low[...], branch_ref[...]).astype(LOW)
    width = kp_ref.shape[1]
    heads = width // HEAD

    @pl.when(info[3] == 1)
    def _():
        keys, values = kp_ref[...], vp_ref[...]
        back = back_ref[...]
        for h in range(heads):
            products_ref[h] = dot_nt(keep_head(back, h), values)
        for h in range(heads):
            bend(
                lambda rows: far_ref[h, rows, :],
                products_ref,
                None,
                ds_ref,
                h,
                lambda rows: stat_ref[rows, heads + h : heads + h + 1],
                fold_ref,
            )
        d_queries = dq_in[...]
        for h in range(heads):
            d_queries = d_queries + dot_nn(ds_ref[h], keep_head(keys, h))
        dq_ref[...] = (d_queries * HEAD**-0.5).astype(LOW)

    @pl.when(info[3] == 0)
    def _():
        dq_ref[...] = (dq_in[...] * HEAD**-0.5).astype(LOW)


def partner_back_kernel(
    info,
    near_ref,
    v_ref,
    qp_ref,
    from_even,
    from_odd,
    dk_in,
    dv_in,
    dq_ref,
    normed_ref,
    x_all,
    gain,
    wq,
    wk,
    wv,
    grad_in,
    gain_in,
    one_send,
    one_keep,
    two_send,
    two_keep,
    send_ref,
    keep_ref,
    small_ref,
    d_all,
    products_ref,
    probs_ref,
    ds_ref,
):
    window, width = v_ref.shape
    heads = width // HEAD
    y, c = info[0], info[1]
    d_all[:, :width] = dq_ref[...]

    @pl.when(info[3] == 1)
    def _():
        payload = jnp.where(info[6] == 1, from_even[...], from_odd[...])
        queries, values = qp_ref[...], v_ref[...]
        back = unpack_lanes(payload, window)
        at = window + window // 2
        blocks = [payload[at + a * EXTRA : at + (a + 1) * EXTRA, :] for a in range(window // CHUNK)]
        columns = jnp.concatenate(blocks, axis=1).astype(F32)
        for h in range(heads):
            products_ref[h] = dot_nt(keep_head(values, h), back)
        for h in range(heads):
            at = h
            lse = columns[at : at + 1, :] + columns[at + 2 * heads : at + 2 * heads + 1, :]
            at = at + heads
            delta = columns[at : at + 1, :] + columns[at + 2 * heads : at + 2 * heads + 1, :]
            bend(
                lambda rows: jnp.exp(near_ref[h, rows, :] - lse),
                products_ref,
                probs_ref,
                ds_ref,
                h,
                lambda rows: delta,
                None,
            )
        d_keys, d_values = dk_in[...], dv_in[...]
        for h in range(heads):
            d_keys = d_keys + dot_nn(ds_ref[h], keep_head(queries, h))
            d_values = d_values + dot_nn(probs_ref[h], keep_head(back, h))
        d_all[:, width : 2 * width] = d_keys.astype(LOW)
        d_all[:, 2 * width :] = d_values.astype(LOW)

    @pl.when(info[3] == 0)
    def _():
        d_all[:, width : 2 * width] = dk_in[...].astype(LOW)
        d_all[:, 2 * width :] = dv_in[...].astype(LOW)

    joint = dot_tn(d_all[...], normed_ref[...]).astype(LOW)
    halves = (joint[:width, :], joint[width : 2 * width, :])
    for side in (0, 1):

        @pl.when(info[4] == side)
        def _():
            one_keep[...] = halves[side]
            one_send[...] = halves[1 - side]

    halves_two = (joint[2 * width :, :], grad_in[...])
    for side in (0, 1):

        @pl.when(info[5] == side)
        def _():
            two_keep[...] = halves_two[side]
            two_send[...] = halves_two[1 - side]

    gain_sum = jnp.zeros((1, x_all.shape[1]), F32)
    for part, core in enumerate((1 - c, c)):
        spots = (aligned((2 * y + core) * CHUNK), aligned((2 * (1 - y) + core) * CHUNK))
        mine = jnp.concatenate([d_all[spots[0], :], d_all[spots[1], :]], axis=0)
        d_normed = dot_nn(mine[:, :width], wq[...])
        d_normed = d_normed + dot_nn(mine[:, width : 2 * width], wk[...])
        d_normed = d_normed + dot_nn(mine[:, 2 * width :], wv[...])
        wide = jnp.concatenate([x_all[spots[0], :], x_all[spots[1], :]], axis=0).astype(F32)
        gain_sum = gain_sum + jnp.sum(d_normed * (wide * rows_norm(wide)), axis=0, keepdims=True)
        if part == 0:
            send_ref[: 2 * CHUNK, :] = d_normed.astype(LOW)
        else:
            keep_ref[...] = d_normed
    small = jnp.concatenate([gain_sum, gain_in[...], jnp.zeros((6, gain_sum.shape[1]), F32)], axis=0)
    small_ref[...] = small
    put_small(send_ref, 2 * CHUNK, small)


def put_small(target, start, small):
    high = small.astype(LOW).astype(F32)
    target[start : start + EXTRA, :] = jnp.concatenate([high, small - high], axis=0).astype(LOW)


def get_small(source, start):
    both = source[start : start + EXTRA, :].astype(F32)
    return both[: EXTRA // 2] + both[EXTRA // 2 :]


def first_merge_kernel(keep_ref, got_ref, small_in, send_ref, own_ref, small_ref):
    local = own_ref.shape[0]
    total = (keep_ref[...] + got_ref[: 2 * local, :].astype(F32)).astype(LOW)
    own_ref[...] = total[:local, :]
    send_ref[:local, :] = total[local:, :]
    small = small_in[...] + get_small(got_ref, 2 * local)
    small_ref[...] = small
    put_small(send_ref, local, small)


def input_back_kernel(own_ref, got_ref, x_ref, dh_ref, gain, small_in, table_ref, out_ref, small_ref):
    local = own_ref.shape[0]
    d_normed = own_ref[...].astype(F32) + got_ref[:local, :].astype(F32)
    wide = x_ref[...].astype(F32)
    inverse = rows_norm(wide)
    unit = wide * inverse
    scaled = d_normed * as_row(gain)
    back = inverse * (scaled - unit * jnp.mean(unit * scaled, axis=-1, keepdims=True))
    out_ref[...] = (dh_ref[...] + back).astype(LOW)
    small_ref[...] = small_in[...] + get_small(got_ref, local)
    heads, buckets = table_ref.shape
    small_ref[2 : 2 + heads, :buckets] = table_ref[...]


def halve_kernel(info, *refs, bits):
    count = len(bits)
    for k, bit in enumerate(bits):
        keep, got = refs[2 * k], refs[2 * k + 1]
        send_ref, keep_ref = refs[2 * count + 2 * k], refs[2 * count + 2 * k + 1]
        half = send_ref.shape[0]
        side = (info[7] >> bit) & 1
        for first, target in ((1 - side, send_ref), (side, keep_ref)):
            rows = pl.ds(pl.multiple_of(first * half, 16), half)
            target[...] = (keep[rows, :].astype(F32) + got[rows, :].astype(F32)).astype(LOW)


def sum_kernel(*refs, count, small):
    for k in range(count):
        keep, got = refs[2 * k], refs[2 * k + 1]
        target = refs[2 * count + small + k]
        rows = keep.shape[0]
        target[:rows, :] = (keep[...].astype(F32) + got[...].astype(F32)).astype(LOW)
        if small and k == 0:
            put_small(target, rows, refs[2 * count][...])


def pair_kernel(*refs, count, small):
    for k in range(count):
        mine, got, target = refs[2 * k], refs[2 * k + 1], refs[2 * count + k]
        extra = EXTRA if small and k == 0 else 0
        rows = mine.shape[0] - extra
        target[:rows, :] = (mine[:rows, :].astype(F32) + got[:rows, :].astype(F32)).astype(LOW)
        if extra:
            put_small(target, rows, get_small(mine, rows) + get_small(got, rows))


def double_kernel(info, *refs, bits, small):
    count = len(bits)
    for k, bit in enumerate(bits):
        mine, got, target = refs[2 * k], refs[2 * k + 1], refs[2 * count + k]
        extra = EXTRA if small and k == 0 else 0
        rows = mine.shape[0] - extra
        side = (info[7] >> bit) & 1
        target[pl.ds(pl.multiple_of(side * rows, 16), rows), :] = mine[:rows, :]
        target[pl.ds(pl.multiple_of((1 - side) * rows, 16), rows), :] = got[:rows, :]
        if extra:
            put_small(target, 2 * rows, get_small(mine, rows) + get_small(got, rows))


def attention_total_kernel(
    info,
    one,
    one_got,
    two,
    two_got,
    q_hbm,
    k_hbm,
    v_hbm,
    out_hbm,
    gain_one_ref,
    gain_two_ref,
    table_ref,
    q_ref,
    k_ref,
    v_ref,
    out_ref,
    sems,
):
    rows = q_ref.shape[0]
    pairs = ((q_ref, q_hbm), (k_ref, k_hbm), (v_ref, v_hbm), (out_ref, out_hbm))
    copies = [pltpu.make_async_copy(a, b, sems.at[k]) for k, (a, b) in enumerate(pairs)]
    first = info[4] == 0
    mine, got = one[:rows, :], one_got[:rows, :]
    q_ref[...] = jnp.where(first, mine, got).astype(F32)
    copies[0].start()
    k_ref[...] = jnp.where(first, got, mine).astype(F32)
    copies[1].start()
    first = info[5] == 0
    v_ref[...] = jnp.where(first, two[...], two_got[...]).astype(F32)
    copies[2].start()
    out_ref[...] = jnp.where(first, two_got[...], two[...]).astype(F32)
    copies[3].start()
    if one.shape[0] > rows:
        small = get_small(one, rows) + get_small(one_got, rows)
        for k in range(gain_one_ref.shape[0]):
            columns = slice(k * CHUNK, (k + 1) * CHUNK)
            gain_one_ref[k : k + 1, :] = small[0:1, columns]
            gain_two_ref[k : k + 1, :] = small[1:2, columns]
        heads, buckets = table_ref.shape
        table_ref[...] = small[2 : 2 + heads, :buckets]
    else:
        gain_one_ref[...] = jnp.zeros_like(gain_one_ref)
        gain_two_ref[...] = jnp.zeros_like(gain_two_ref)
        table_ref[...] = jnp.zeros_like(table_ref)
    for copy in copies:
        copy.wait()


def swap(values, axis, bit):
    return lax.ppermute(values, axis, [(i, i ^ bit) for i in range(lax.axis_size(axis))])


def swap_odd(values):
    ends = range(1, lax.axis_size("dp") - 1, 2)
    return lax.ppermute(values, "dp", [(i, i + 1) for i in ends] + [(i + 1, i) for i in ends])


def after(values, *others):
    return lax.optimization_barrier((values, *others))[0]


def spread(own, across=None):
    across = swap(own, "mp", 2) if across is None else across
    return own, across, swap(own, "mp", 1), swap(across, "mp", 1)


def cut(values, first, count):
    return lax.dynamic_slice_in_dim(values, first, count)


class Sums:
    def __init__(self, info, rank, orders, sends, keeps):
        self.info, self.rank, self.orders, self.keeps = info, rank, orders, list(keeps)
        self.bits = len(orders[0])
        self.tiled = all((k.shape[0] >> (self.bits - 2)) % 16 == 0 for k in keeps)
        self.step, self.small = 0, None
        self.exchange(sends)

    def exchange(self, sends):
        done = self.step if self.step < self.bits else 2 * self.bits - 2 - self.step
        self.now = [order[done] for order in self.orders]
        self.gots = [swap(v, "dp", 1 << bit) for v, bit in zip(sends, self.now)]
        self.step += 1

    def pairs(self):
        return [v for pair in zip(self.keeps, self.gots) for v in pair]

    def advance(self, token, small=None, micros=1):
        self.keeps[0] = after(self.keeps[0], token)
        count = len(self.keeps)
        if self.step < self.bits - 1:
            bits = [order[self.step] for order in self.orders]
            halves = [v.shape[0] // 2 for v in self.keeps]
            if self.tiled:
                out = call(
                    functools.partial(halve_kernel, bits=bits),
                    [shape((h, v.shape[1]), LOW) for h, v in zip(halves, self.keeps) for _ in range(2)],
                    [self.info, *self.pairs()],
                    micros=micros,
                )
                sends, self.keeps = out[0::2], list(out[1::2])
            else:
                sends, keeps = [], []
                for k, g, h, bit in zip(self.keeps, self.gots, halves, bits):
                    side = (self.rank >> bit) & 1
                    total = (k.astype(F32) + g.astype(F32)).astype(LOW)
                    sends.append(cut(total, (1 - side) * h, h))
                    keeps.append(cut(total, side * h, h))
                self.keeps = keeps
        elif self.step == self.bits - 1:
            if self.tiled:
                self.small = small
                rows = [v.shape[0] for v in self.keeps]
                if small is not None:
                    rows[0] += EXTRA
                sends = call(
                    functools.partial(sum_kernel, count=count, small=int(small is not None)),
                    [shape((r, v.shape[1]), LOW) for r, v in zip(rows, self.keeps)],
                    self.pairs() + ([small] if small is not None else []),
                    smem=0,
                    micros=micros,
                )
            else:
                sends = [(k.astype(F32) + g.astype(F32)).astype(LOW) for k, g in zip(self.keeps, self.gots)]
            self.keeps = list(sends)
        elif self.step == self.bits:
            if self.tiled:
                sends = call(
                    functools.partial(pair_kernel, count=count, small=self.small is not None),
                    [shape(v.shape, LOW) for v in self.keeps],
                    self.pairs(),
                    smem=0,
                    micros=micros,
                )
            else:
                sends = [(k.astype(F32) + g.astype(F32)).astype(LOW) for k, g in zip(self.keeps, self.gots)]
            self.keeps = list(sends)
        else:
            has = self.small is not None
            if self.tiled:
                rows = [2 * v.shape[0] for v in self.keeps]
                if has:
                    rows[0] -= EXTRA
                sends = call(
                    functools.partial(double_kernel, bits=self.now, small=has),
                    [shape((r, v.shape[1]), LOW) for r, v in zip(rows, self.keeps)],
                    [self.info, *self.pairs()],
                    micros=micros,
                )
            else:
                sends = []
                for k, g, bit in zip(self.keeps, self.gots, self.now):
                    side = (self.rank >> bit) & 1
                    sends.append(
                        jnp.where(side == 0, jnp.concatenate([k, g], axis=0), jnp.concatenate([g, k], axis=0))
                    )
            self.keeps = list(sends)
        self.exchange(sends)
        return sends[0]


def per_device(
    inputs,
    attention_gain,
    query_weight,
    key_weight,
    value_weight,
    out_weight,
    bias_table,
    feedforward_gain,
    gate_weight,
    up_weight,
    down_weight,
    segment,
    bucket,
    cotangent,
):
    parts = lax.axis_size("mp")
    groups = lax.axis_size("dp")
    local, d = inputs.shape
    window = local * parts
    width = query_weight.shape[1]
    heads = width // HEAD
    units = gate_weight.shape[1]
    buckets = bias_table.shape[0]
    half = 2 * local
    rank = lax.axis_index("dp")
    member = lax.axis_index("mp")
    bits = list(range(groups.bit_length() - 1))
    order_one = bits
    order_two = [bits[1], bits[0]] + bits[2:]

    x_across = swap(inputs, "mp", 2)
    from_even = swap(inputs, "dp", 1)
    from_odd = swap_odd(inputs)

    spot = jnp.stack([rank, member]).astype(jnp.int32)
    edge = jnp.full((1,), -1, jnp.int32)
    bucket_rows = jnp.concatenate([edge, bucket]).reshape(-1, CHUNK)
    table = bias_table.T
    gain_one, gain_two = attention_gain.reshape(-1, CHUNK), feedforward_gain.reshape(-1, CHUNK)
    band = shape((heads, CHUNK, SPAN), F32)
    segments = segment.reshape(-1, CHUNK)
    info, seg_row, seg_col, bias, table, gain_one, gain_two = call(
        functools.partial(setup_kernel, groups=groups, first_bits=(order_one[0], order_two[0])),
        [shape((8,), jnp.int32), shape((1, window), F32), shape((window, CHUNK), F32), band]
        + [shape(v.shape, F32) for v in (table, gain_one, gain_two)],
        [spot, bucket_rows] + [in_hbm(v) for v in (segments, table, gain_one, gain_two)],
        scratch=[pltpu.VMEM(segments.shape, jnp.int32), pltpu.SemaphoreType.DMA((4,))],
        hbm=4,
        out_smem=1,
        micros=3.0,
    )
    cot_across = swap(cotangent, "mp", 2)
    (near,) = call(near_kernel, [shape((local, d), LOW)], [info, after(from_even, x_across, cot_across), from_odd], micros=0.5)
    near_across = swap(near, "mp", 2)
    near_core = swap(near, "mp", 1)
    x_pieces = (inputs, x_across, swap(inputs, "mp", 1), swap(after(x_across, bias), "mp", 1))

    low_rows = shape((window, width), LOW)
    wide_rows = shape((window, width), F32)
    stats = shape((window, CHUNK), F32)
    square_wide = pltpu.VMEM((heads, window, window), F32)
    square_low = pltpu.VMEM((heads, window, window), LOW)
    weight = shape((width, d), LOW)
    x_all, normed, queries, keys, values, acc, top, total, wq, wk, wv = call(
        own_kernel,
        [shape((window, d), LOW)] * 2 + [low_rows] * 3 + [wide_rows, stats, stats] + [weight] * 3,
        [info, x_across, *x_pieces[2:], gain_one, bias, seg_col, seg_row]
        + [in_hbm(v) for v in (inputs, query_weight.T, key_weight.T, value_weight.T)],
        scratch=[square_wide, square_low, pltpu.VMEM((local, d), LOW), pltpu.SemaphoreType.DMA((4,))],
        hbm=4,
        micros=5.0,
    )
    near_pieces = (near, near_across, near_core, swap(after(near_across, acc), "mp", 1))
    mixed_low, packed, mixed, lse, queries_near, keys_near, values_near = call(
        partner_kernel,
        [low_rows, shape((window + window // 2, CHUNK), LOW), wide_rows, stats] + [low_rows] * 3,
        [info, *near_pieces, gain_one, wq, wk, wv, bias, queries, acc, top, total],
        scratch=[
            pltpu.VMEM((window, d), LOW),
            square_wide,
            square_low,
            pltpu.VMEM((window, width), F32),
            pltpu.VMEM((window, CHUNK), F32),
            pltpu.VMEM((window, CHUNK), F32),
        ],
        micros=300,
    )
    mixed_across = swap(packed, "mp", 2)
    mixed_core = swap(packed, "mp", 1)
    cot_pieces = (
        cotangent,
        cot_across,
        swap(after(cotangent, mixed_core), "mp", 1),
        swap(after(cot_across, mixed_core), "mp", 1),
    )
    out_across = swap(after(out_weight, near), "mp", 2)
    out_pieces = (
        out_weight,
        out_across,
        swap(after(out_weight, mixed_core), "mp", 1),
        swap(after(out_across, mixed_core), "mp", 1),
    )
    bias_t, flipped_rows = call(
        flipped_kernel,
        [band, shape(bucket_rows.shape, jnp.int32)],
        [after(bucket_rows, mixed_low), table],
        smem=0,
        micros=3.0,
    )
    cot_all, d_act = call(
        cotangent_kernel,
        [shape((window, d), LOW), shape((window, units), F32)],
        [*cot_pieces, after(down_weight, mixed_across)],
        smem=0,
        micros=1.0,
    )
    (base,) = call(
        base_kernel,
        [shape((window, d), F32)],
        [x_all, after(mixed_low, bias_t), out_weight],
        smem=0,
        micros=1.0,
    )
    mixed_pieces = (mixed_low, mixed_across, mixed_core, swap(after(mixed_across, bias_t, base), "mp", 1))
    second, hidden, act, d_gate, d_up, second_send, second_keep, gain_two_part = call(
        feed_kernel,
        [shape((window, d), LOW), shape((half, d), F32)]
        + [shape((window, units), LOW)] * 3
        + [shape((half, d), LOW), shape((half, d), F32), shape((1, d), F32)],
        [info, base, *mixed_pieces[1:], *out_pieces[1:], d_act, gain_two, gate_weight, up_weight],
        micros=5.0,
    )
    (second_sum,) = call(
        functools.partial(sum_kernel, count=1, small=0),
        [shape((half, d), LOW)],
        [second_keep, swap(second_send, "mp", 1)],
        smem=0,
        micros=1.0,
    )
    second_other = swap(second_sum, "mp", 2)
    rows = d + units // 2 + units // 4
    gate_send, gate_keep, up_send, up_keep = call(
        feed_grad_kernel,
        [shape((rows // 2, units), LOW)] * 4,
        [info, after(second, second_sum), d_gate, d_up, act, cot_all],
        scratch=[pltpu.VMEM((rows, units), LOW)] * 2,
        micros=3.0,
    )
    feed_sums = Sums(info, rank, (order_one, order_two), (gate_send, up_send), (gate_keep, up_keep))
    feed_send, feed_keep = call(
        feed_out_kernel, [shape((half, d), LOW)] * 2, [after(act, gate_send), down_weight], smem=0, micros=30
    )
    feed_got = swap(feed_send, "mp", 1)
    block = shape((heads, window, window), F32)
    own_probs, far_probs, near_scores = call(
        recall_kernel,
        [block] * 3,
        [
            info,
            after(queries, feed_send),
            keys,
            queries_near,
            keys_near,
            lse,
            bias,
            bias_t,
            seg_col,
            seg_row,
        ],
        micros=1.0,
    )
    second_other = after(second_other, own_probs)
    dh, branch_low = call(
        hidden_back_kernel,
        [shape((local, d), F32), shape((half, d), LOW)],
        [second_sum, second_other, hidden, cot_pieces[0], cot_pieces[1], gain_two],
        smem=0,
    )
    feed_own, feed_cross = call(
        feed_merge_kernel,
        [shape((local, d), LOW)] * 2,
        [after(feed_keep, branch_low), feed_got],
        smem=0,
        micros=100,
    )
    payload, back, stat_back, branch_all = call(
        mixed_back_kernel,
        [shape((window + window // 2 + window // CHUNK * EXTRA, CHUNK), LOW), low_rows, stats, shape((window, d), LOW)],
        [info, after(branch_low, feed_cross), swap(branch_low, "mp", 1), out_weight, mixed, lse],
    )
    payload_even = swap(payload, "dp", 1)
    payload_odd = swap_odd(payload)
    token = feed_sums.advance(payload)
    fold = shape((heads, CHUNK, 2 * window), F32)
    d_queries, d_keys, d_values, near_fold = call(
        own_back_kernel,
        [wide_rows, wide_rows, wide_rows, fold],
        [own_probs, after(queries, token), keys, values, back, stat_back],
        scratch=[square_wide, square_low, square_low],
        smem=0,
        micros=200,
    )
    d_queries, far_fold, out_grad = call(
        far_back_kernel,
        [low_rows, fold, shape((width, d), LOW)],
        [info, far_probs, keys_near, values_near, back, stat_back, d_queries, mixed_low, branch_all],
        scratch=[square_wide, square_low],
        micros=3.0,
    )
    one_send, one_keep, two_send, two_keep, first_send, first_keep, small = call(
        partner_back_kernel,
        [shape((width, d), LOW)] * 4
        + [shape((half + EXTRA, d), LOW), shape((half, d), F32), shape((EXTRA // 2, d), F32)],
        [
            info,
            near_scores,
            values,
            queries_near,
            payload_even,
            payload_odd,
            d_keys,
            d_values,
            d_queries,
            normed,
            x_all,
            gain_one,
            wq,
            wk,
            wv,
            out_grad,
            gain_two_part,
        ],
        scratch=[pltpu.VMEM((window, 3 * width), LOW), square_wide, square_low, square_low],
        micros=300,
    )
    token = feed_sums.advance(one_send, micros=300)
    joint_sums = Sums(info, rank, (order_one, order_two), (after(one_send, token), two_send), (one_keep, two_keep))
    first_send, first_own, small = call(
        first_merge_kernel,
        [shape((local + EXTRA, d), LOW), shape((local, d), LOW), shape((EXTRA // 2, d), F32)],
        [after(first_keep, token), swap(first_send, "mp", 1), small],
        smem=0,
        micros=1,
    )
    first_got = swap(first_send, "mp", 2)
    token = joint_sums.advance(first_send)
    (table_part,) = call(
        table_kernel,
        [shape((heads, CHUNK), F32)],
        [info, after(near_fold, token), far_fold, flipped_rows, bucket_rows],
        micros=1.0,
    )
    input_grad, small = call(
        input_back_kernel,
        [shape((local, d), LOW), shape((EXTRA // 2, d), F32)],
        [first_own, first_got, inputs, after(dh, token), gain_one, small, table_part],
        smem=0,
        micros=1,
    )
    token = joint_sums.advance(small, small)
    token = feed_sums.advance(token)
    feed_got = swap(after(feed_cross, token), "mp", 2)
    token = joint_sums.advance(token, small, micros=1)
    token = feed_sums.advance(token)
    last = 2 * len(bits) - 1
    while joint_sums.step < last or feed_sums.step < last:
        if joint_sums.step < last:
            token = joint_sums.advance(token, small, micros=300)
        if feed_sums.step < last:
            token = feed_sums.advance(token)
    (layer_out,) = call(
        layer_out_kernel,
        [shape((local, d), LOW)],
        [after(hidden, token), feed_own, feed_got],
        smem=0,
        micros=40,
    )
    ready = feed_sums.pairs()
    gate_grad, up_grad, down_grad = call(
        feed_total_kernel,
        [shape((d, units), F32)] * 2 + [shape((units, d), F32)],
        [info, after(ready[0], layer_out), *ready[1:]],
        scratch=[pltpu.VMEM((rows, units), LOW)],
        micros=2.0,
    )
    ready = joint_sums.pairs()
    query_grad, key_grad, value_grad, out_total, gain_one_total, gain_two_total, table_total = call(
        attention_total_kernel,
        [shape((width, d), F32)] * 4 + [shape((d // CHUNK, CHUNK), F32)] * 2 + [shape((heads, buckets), F32)],
        [info, after(ready[0], down_grad), *ready[1:]],
        scratch=[pltpu.VMEM((width, d), F32)] * 4 + [pltpu.SemaphoreType.DMA((4,))],
        out_hbm=4,
        micros=2.0,
    )
    if not joint_sums.tiled:
        small = lax.psum(small, "dp")
        gain_one_total, gain_two_total = small[0].reshape(-1, CHUNK), small[1].reshape(-1, CHUNK)
        table_total = small[2 : 2 + heads, :buckets]
    return (
        layer_out,
        input_grad,
        gain_one_total.reshape(-1),
        query_grad.T,
        key_grad.T,
        value_grad.T,
        out_total,
        table_total.T,
        gain_two_total.reshape(-1),
        gate_grad,
        up_grad,
        down_grad,
    )


def solution(mesh):
    rows = P(("dp", "mp"), None)
    in_specs = (
        rows,
        P(),
        P(None, "mp"),
        P(None, "mp"),
        P(None, "mp"),
        P("mp", None),
        P(None, "mp"),
        P(),
        P(None, "mp"),
        P(None, "mp"),
        P("mp", None),
        P(),
        P(),
        rows,
    )
    out_specs = (
        rows,
        rows,
        P(),
        P(None, "mp"),
        P(None, "mp"),
        P(None, "mp"),
        P("mp", None),
        P(None, "mp"),
        P(),
        P(None, "mp"),
        P(None, "mp"),
        P("mp", None),
    )
    return jax.shard_map(
        per_device, mesh=mesh, in_specs=in_specs, out_specs=out_specs, check_vma=False
    )
```
